32 devices in a mesh: scan: 2 (over x), slab: 16 (over z, y, core).
Axes of the slice: x: 2, y: 2, z: 4, core: 2. Of those that a mesh axis runs over, the one named last changes fastest.
Arguments:
- sinogram: bfloat16 [1024, 8, 128], P(('scan', 'slab')), parts along dimension 0, may hold values from -144 to 144
- start_volume: float32 [512, 8, 128], P(('scan', 'slab')), parts along dimension 0, may hold values from -6 to 6
- slot_voxel: int32 [8192, 4], P(('scan', 'slab')), parts along dimension 0, may hold values from 0 to 15
- slot_ray: int32 [8192], P(('scan', 'slab')), parts along dimension 0, may hold values from 0 to 31
- live_count: int32 [512], P(('scan', 'slab')), parts along dimension 0, may hold values from 0 to 16, as said below
- block_slope: float32 [8192, 4], P(('scan', 'slab')), parts along dimension 0, may hold values from 0.8 to 1.25
- block_offset: float32 [8192, 4], P(('scan', 'slab')), parts along dimension 0, may hold values from -8 to 8
Outputs:
- recon_volume: float32 [512, 8, 128], P(('scan', 'slab')), parts along dimension 0
The draws below stay inside these ranges and needn't reach their ends.
There are 2 independent parts, one for each index of `scan`. The reference program is written for one: setup_inputs(seed, part) draws one part's arguments, and reference() takes and returns one part's arrays. A program takes and returns all parts, laid end to end along the dimension named above; each array names one. Nothing has to cross between parts.
Inputs may be any that keep to these rules, and one draw needn't show every extreme that they name: `live_count`: every device's 16 slots to itself are all live.
All inputs are finite; a program needn't handle non-finite values.
Results may differ from the reference program's by a relative error of at most 0.0039.
Values may be sent and summed in bfloat16 or wider, within the bound.
No kernel may reach another device: no remote copies, remote signals or barrier semaphores. Data moves between devices by JAX's collectives and lax.ppermute only.
A program may use at most 64 MiB of HBM per device.

```python
import math
import jax
import jax.numpy as jnp
import numpy as np
from jax import lax

TILE = 128
FRAMES = 8
VT_DEV = 16
RT_DEV = 32
SLOT_DEV = 256
DEPTH = 4
ITERS = 2
CAP = 16
VOXEL_TILES = 256
RAY_TILES = 512
SLOTS = 4096
N_SLAB = 16


def draw_live_count(key, part):
    key = jax.random.fold_in(key, 7)
    position = jnp.arange(N_SLAB * N_SLAB, dtype=jnp.int32)
    source = position // N_SLAB
    target = position % N_SLAB
    capacity = SLOT_DEV // N_SLAB
    spread = jax.random.randint(key, (N_SLAB * N_SLAB,), 0, capacity + 1)
    return jnp.where(source == target, capacity, spread).astype(jnp.int32)


def touch_ends(values, key, smallest, top_value):
    spot = [jax.random.randint(jax.random.fold_in(key, axis), (), 0, length) for axis, length in enumerate(values.shape)]
    widest = values.shape.index(max(values.shape))
    neighbour = spot[:widest] + [(spot[widest] + 1) % values.shape[widest]] + spot[widest + 1:]
    return values.at[tuple(spot)].set(smallest).at[tuple(neighbour)].set(top_value)


def levels(own_key, shape, split, smallest, largest):
    def one(dim, shards_of):
        draws = jax.random.uniform(jax.random.fold_in(jax.random.fold_in(own_key, 6), dim), (shards_of,), jnp.float32, smallest / len(split), largest / len(split))
        return jnp.repeat(jnp.exp(draws), shape[dim] // shards_of).reshape((-1,) + (1,) * (len(shape) - dim - 1))

    factor_of = one(*split[0])
    for cut in split[1:]:
        factor_of = factor_of * one(*cut)
    return factor_of


def rank_bounds(number_of, lean):
    portions = [(1 << 20) // math.isqrt(rank ** lean) + 1 for rank in range(1, number_of + 1)]
    width = 1 + sum(portions) // (1 << 30)
    return np.cumsum(np.array([max(1, weight // width) for weight in portions]))


def ranked_ids(rng, shape, number_of, skew):
    table = rank_bounds(number_of, skew)
    pick = jax.random.randint(jax.random.fold_in(rng, 1), shape, 0, int(table[number_of - 1]))
    rank = jnp.searchsorted(jnp.asarray(table, jnp.int32), pick, side="right")
    return jax.random.permutation(jax.random.fold_in(rng, 2), number_of)[rank].astype(jnp.int32)


def centred(own_key, dims, scale, limit, cuts=(), kind=jnp.bfloat16):
    loudness = levels(own_key, dims, cuts, -0.22, 0.18) if cuts else 1.0
    result = jax.random.normal(own_key, dims, jnp.float32) * scale * loudness
    return jnp.minimum(jnp.maximum(result, -limit), limit).astype(kind)


def setup_inputs(seed: int = 0, part: int = 0) -> dict:
    keys = jax.random.split(jax.random.key(seed), 8)
    part_splits = jax.random.split(jax.random.fold_in(keys[7], part), 8)
    return {
        "sinogram": centred(part_splits[0], (RAY_TILES, FRAMES, TILE), 24.0, 144.0, ((0, 16),)),
        "start_volume": centred(part_splits[1], (VOXEL_TILES, FRAMES, TILE), 1.0, 6.0, ((0, 16),), jnp.float32),
        "slot_voxel": touch_ends(ranked_ids(part_splits[2], (SLOTS, DEPTH), VT_DEV, 3), jax.random.fold_in(part_splits[2], 3), 0, VT_DEV - 1).astype(jnp.int32),
        "slot_ray": touch_ends(jax.random.randint(part_splits[3], (SLOTS,), 0, RT_DEV), jax.random.fold_in(part_splits[3], 1), 0, RT_DEV - 1).astype(jnp.int32),
        "live_count": draw_live_count(jax.random.fold_in(jax.random.fold_in(keys[7], part), 71), part),
        "block_slope": jnp.clip(0.8 + 0.45 * jax.random.uniform(part_splits[5], (SLOTS, DEPTH), jnp.float32) ** levels(part_splits[5], (SLOTS, DEPTH), ((0, 16),), -0.2, 0.2), 0.8, 1.25),
        "block_offset": jnp.clip(jax.random.uniform(part_splits[6], (SLOTS, DEPTH), jnp.float32, -8.0, 8.0) * levels(part_splits[6], (SLOTS, DEPTH), ((0, 16),), -0.4, 0.0), -8.0, 8.0),
    }


def footprint(slope_part, offset_part, alive, extent):
    position = jnp.arange(extent, dtype=jnp.float32)
    centre = offset_part[:, :, None] + slope_part[:, :, None] * position[None, None, :]
    distance = jnp.abs(position[None, None, :, None] - centre[:, :, None, :])
    weight = jnp.maximum(0.0, 1.0 - distance) * alive[:, None, None, None]
    return weight.astype(jnp.bfloat16)


def reference(sinogram, start_volume, slot_voxel, slot_ray, live_count, block_slope, block_offset):
    extent = sinogram.shape[2]
    voxel_index = slot_voxel.reshape(N_SLAB, SLOT_DEV, DEPTH)
    ray_index = slot_ray.reshape(N_SLAB, SLOT_DEV)
    counts = live_count.reshape(N_SLAB, N_SLAB)
    slopes = block_slope.reshape(N_SLAB, SLOT_DEV, DEPTH)
    offsets = block_offset.reshape(N_SLAB, SLOT_DEV, DEPTH)
    sources = jnp.arange(N_SLAB, dtype=jnp.int32)
    targets = jnp.arange(SLOT_DEV, dtype=jnp.int32) // CAP
    within = jnp.arange(SLOT_DEV, dtype=jnp.int32) % CAP
    highest = lax.Precision.HIGHEST

    def tiles_of(source):
        alive = (within < counts[source][targets]).astype(jnp.float32)
        return footprint(slopes[source], offsets[source], alive, extent).astype(jnp.float32)

    def rays_of(source):
        return (targets * RT_DEV + ray_index[source]).astype(jnp.int32)

    def setup(row_sum, source):
        tiles = tiles_of(source)
        row_sum = row_sum.at[rays_of(source)].add(jnp.sum(tiles, axis=(1, 3)))
        column = jnp.zeros((VT_DEV, extent), jnp.float32).at[voxel_index[source].reshape(-1)].add(
            jnp.sum(tiles, axis=2).reshape(SLOT_DEV * DEPTH, extent))
        return row_sum, column

    row_sum, column_sum = lax.scan(setup, jnp.zeros((RT_DEV * N_SLAB, extent), jnp.float32), sources)
    row_weight = 1.0 / jnp.maximum(row_sum, 1.0)
    column_weight = 1.0 / jnp.maximum(column_sum, 1.0)
    volume = start_volume.reshape(N_SLAB, VT_DEV, FRAMES, extent)
    for sweep in range(ITERS):
        volume_bf = volume.astype(jnp.bfloat16).reshape(N_SLAB * VT_DEV, FRAMES, extent)

        def forward(projection, source):
            tiles = tiles_of(source)
            picked = volume_bf[(source * VT_DEV + voxel_index[source]).astype(jnp.int32)].astype(jnp.float32)
            terms = jnp.einsum("sdrv,sdfv->sfr", tiles, picked, precision=highest).astype(jnp.bfloat16)
            return projection.at[rays_of(source)].add(terms.astype(jnp.float32)), None

        projection, unused = lax.scan(forward, jnp.zeros((RT_DEV * N_SLAB, FRAMES, extent), jnp.float32), sources)
        residual = ((sinogram.astype(jnp.float32) - projection) * row_weight[:, None, :]).astype(jnp.bfloat16)

        def backward(source):
            tiles = tiles_of(source)
            picked = residual[rays_of(source)].astype(jnp.float32)
            contrib = jnp.einsum("sdrv,sfr->sdfv", tiles, picked, precision=highest)
            back = jnp.zeros((VT_DEV, FRAMES, extent), jnp.float32).at[voxel_index[source].reshape(-1)].add(
                contrib.reshape(SLOT_DEV * DEPTH, FRAMES, extent))
            return volume[source] + column_weight[source][:, None, :] * back

        volume = lax.map(backward, sources)
    return volume.reshape(N_SLAB * VT_DEV, FRAMES, extent)
```

```python
import functools

import jax
import jax.numpy as jnp
from jax import lax
from jax.experimental import pallas as pl
from jax.experimental.pallas import tpu as pltpu
from jax.sharding import PartitionSpec as P

ITERS = 2
FAR = 1.0e6
PARAMS = pltpu.CompilerParams(vmem_limit_bytes=48 * 1024 * 1024)
VMEM = pl.BlockSpec(memory_space=pltpu.VMEM)
SMEM = pl.BlockSpec(memory_space=pltpu.SMEM)


def hat(ray, offset, slope, voxel):
    return jnp.maximum(0.0, 1.0 - jnp.abs(ray - (offset + slope * voxel))).astype(jnp.bfloat16)


def row_taps(offset, slope, extent):
    shape = (offset.shape[0], extent)
    ray = lax.broadcasted_iota(jnp.int32, shape, 1).astype(jnp.float32)
    offset = jnp.broadcast_to(offset, shape)
    slope = jnp.broadcast_to(slope, shape)
    middle = jnp.floor((ray - offset) / slope + 0.5)
    middle = jnp.minimum(jnp.maximum(middle, 1.0), extent - 2.0)
    weights = [hat(ray, offset, slope, middle + step) for step in (-1.0, 0.0, 1.0)]
    return middle.astype(jnp.int32), weights


def column_taps(offset, slope, extent):
    shape = (offset.shape[0], extent)
    voxel = lax.broadcasted_iota(jnp.int32, shape, 1).astype(jnp.float32)
    centre = jnp.broadcast_to(offset, shape) + jnp.broadcast_to(slope, shape) * voxel
    first = jnp.minimum(jnp.maximum(jnp.floor(centre), 0.0), extent - 2.0)
    weights = [
        jnp.maximum(0.0, 1.0 - jnp.abs(first + step - centre)).astype(jnp.bfloat16)
        for step in (0.0, 1.0)
    ]
    return first.astype(jnp.int32), weights


def target_setup(fields, n_slab, group, capacity, extent, frames, got_ref, index_ref, *rest):
    weight_refs, row_ref = rest[:3], rest[3]
    columns = got_ref[...].T
    ray_tiles = row_ref.shape[0] // frames
    total = jnp.zeros((ray_tiles, extent), jnp.float32)
    depth = group // capacity
    for source in range(n_slab):
        offset = columns[0:group, source:source + 1]
        slope = columns[group:2 * group, source:source + 1]
        middle, weights = row_taps(offset, slope, extent)
        rows = pl.ds(source * group, group)
        index_ref[rows, :] = middle
        for ref, weight in zip(weight_refs, weights):
            ref[rows, :] = weight.astype(jnp.float32)
        summed = sum(weight.astype(jnp.float32) for weight in weights)
        tile_of = jnp.broadcast_to(
            got_ref[source:source + 1, 4 * group:5 * group], (ray_tiles, group))
        match = tile_of == lax.broadcasted_iota(
            jnp.int32, (ray_tiles, group), 0).astype(jnp.float32)
        hot = match.astype(jnp.float32)
        total += jnp.dot(hot, summed, precision=lax.Precision.HIGHEST,
                         preferred_element_type=jnp.float32)
    weight = 1.0 / jnp.maximum(total, 1.0)
    for tile in range(ray_tiles):
        row_ref[tile * frames:(tile + 1) * frames, :] = jnp.broadcast_to(
            weight[tile:tile + 1, :], (frames, extent))


def source_setup(extent, frames, offset_ref, slope_ref, voxel_ref, index_ref, first_ref, second_ref,
                 column_ref):
    offsets = offset_ref[...].T
    slopes = slope_ref[...].T
    voxel_tiles = column_ref.shape[0] // frames
    total = jnp.zeros((voxel_tiles, extent), jnp.float32)
    for part in range(offset_ref.shape[0]):
        first, weights = column_taps(offsets[:, part:part + 1], slopes[:, part:part + 1], extent)
        rows = pl.ds(part * extent, extent)
        index_ref[rows, :] = first
        first_ref[rows, :] = weights[0].astype(jnp.float32)
        second_ref[rows, :] = weights[1].astype(jnp.float32)
        summed = weights[0].astype(jnp.float32) + weights[1].astype(jnp.float32)
        tile_of = jnp.broadcast_to(voxel_ref[part:part + 1, :], (voxel_tiles, extent))
        hot = (tile_of == lax.broadcasted_iota(jnp.int32, (voxel_tiles, extent), 0)).astype(jnp.float32)
        total += jnp.dot(hot, summed, precision=lax.Precision.HIGHEST,
                         preferred_element_type=jnp.float32)
    weight = 1.0 / jnp.maximum(total, 1.0)
    for tile in range(voxel_tiles):
        column_ref[tile * frames:(tile + 1) * frames, :] = jnp.broadcast_to(
            weight[tile:tile + 1, :], (frames, extent))


def pick(values, index):
    return jnp.take_along_axis(values, index, axis=1, mode="promise_in_bounds")


def spread(ref, row, frames):
    return jnp.broadcast_to(ref[pl.ds(row, 1), :], (frames, ref.shape[1]))


def forward_kernel(n_slab, group, capacity, tiles, frames, chunk,
                   meta_ref, volume_ref, sinogram_ref, row_ref, index_ref, w0_ref, w1_ref, w2_ref,
                   out_ref, wide, projection):
    depth = group // capacity
    wide[...] = volume_ref[...].astype(jnp.float32)
    projection[...] = jnp.zeros_like(projection)

    def from_source(source, carry):
        count = meta_ref[source, 2 * group + capacity]

        def some(step, carry):
            for place in range(chunk):
                slot = step * chunk + place
                total = None
                for level in range(depth):
                    block = slot * depth + level
                    voxel = source * tiles + meta_ref[source, group + block]
                    row = source * group + block
                    values = wide[pl.ds(pl.multiple_of(voxel * frames, frames), frames), :]
                    index = spread(index_ref, row, frames)
                    for ref, shift in ((w0_ref, -1), (w1_ref, 0), (w2_ref, 1)):
                        term = spread(ref, row, frames) * pick(values, index + shift)
                        total = term if total is None else total + term
                ray = meta_ref[source, 2 * group + slot]
                at = pl.ds(pl.multiple_of(ray * frames, frames), frames)
                projection[at, :] += total.astype(jnp.bfloat16).astype(jnp.float32)
            return carry

        return lax.fori_loop(0, lax.div(count + (chunk - 1), chunk), some, carry)

    lax.fori_loop(0, n_slab, from_source, 0)
    residual = (sinogram_ref[...].astype(jnp.float32) - projection[...]) * row_ref[...]
    out_ref[...] = residual.astype(jnp.bfloat16)


def backward_kernel(n_slab, group, capacity, tiles, frames, chunk,
                    count_ref, voxel_ref, ray_ref, residual_ref, volume_ref, column_ref, index_ref,
                    w0_ref, w1_ref, out_ref, rounded_ref, wide, *banks):
    depth = group // capacity
    wide[...] = residual_ref[...].astype(jnp.float32)
    for bank in banks:
        bank[...] = jnp.zeros_like(bank)

    def to_target(target, carry):
        count = count_ref[target]

        def some(step, carry):
            for place in range(chunk):
                slot = target * capacity + step * chunk + place
                ray = target * tiles + ray_ref[slot]
                values = wide[pl.ds(pl.multiple_of(ray * frames, frames), frames), :]
                for level in range(depth):
                    row = slot * depth + level
                    index = spread(index_ref, row, frames)
                    term = (spread(w0_ref, row, frames) * pick(values, index)
                            + spread(w1_ref, row, frames) * pick(values, index + 1))
                    at = pl.ds(pl.multiple_of(voxel_ref[row] * frames, frames), frames)
                    banks[level][at, :] += term
            return carry

        return lax.fori_loop(0, lax.div(count + (chunk - 1), chunk), some, carry)

    lax.fori_loop(0, n_slab, to_target, 0)
    back = banks[0][...]
    for bank in banks[1:]:
        back = back + bank[...]
    volume = volume_ref[...] + column_ref[...] * back
    out_ref[...] = volume
    rounded_ref[...] = volume.astype(jnp.bfloat16)


def shards(sinogram, start_volume, slot_voxel, slot_ray, live_count, block_slope, block_offset):
    n_slab = lax.axis_size("slab")
    n_slots, depth = slot_voxel.shape
    capacity = n_slots // n_slab
    group = capacity * depth
    ray_tiles, frames, extent = sinogram.shape
    voxel_tiles = start_volume.shape[0]
    blocks = n_slots * depth
    chunk = min(4, capacity)
    f32, bf16 = jnp.float32, jnp.bfloat16
    shape = jax.ShapeDtypeStruct

    volume = start_volume.reshape(voxel_tiles * frames, extent)
    gathered = lax.all_gather(volume.astype(bf16), "slab", axis=0, tiled=True)

    alive = (jnp.arange(capacity)[None, :] < live_count[:, None]).reshape(n_slots, 1)
    offset = jnp.where(alive, block_offset, FAR)
    width = -(-(5 * group + capacity + 1) // extent) * extent
    used = 5 * group + capacity + 1
    packed = jnp.concatenate(
        [
            offset.reshape(n_slab, group),
            block_slope.reshape(n_slab, group),
            slot_voxel.astype(f32).reshape(n_slab, group),
            jnp.zeros((n_slab, group), f32),
            jnp.repeat(slot_ray.astype(f32), depth).reshape(n_slab, group),
            slot_ray.astype(f32).reshape(n_slab, capacity),
            live_count.astype(f32).reshape(n_slab, 1),
            jnp.zeros((n_slab, width - used), f32),
        ],
        axis=1,
    )
    got = lax.all_to_all(packed, "slab", split_axis=0, concat_axis=0, tiled=True)
    meta = jnp.concatenate(
        [got[:, 4 * group:5 * group], got[:, 2 * group:3 * group], got[:, 5 * group:used]], axis=1
    ).astype(jnp.int32)

    fwd_index, fwd0, fwd1, fwd2, row_weight = pl.pallas_call(
        functools.partial(target_setup, None, n_slab, group, capacity, extent, frames),
        out_shape=[shape((blocks, extent), jnp.int32)] + [shape((blocks, extent), f32)] * 3
        + [shape((ray_tiles * frames, extent), f32)],
        in_specs=[VMEM],
        out_specs=[VMEM] * 5,
        compiler_params=PARAMS,
        name="target_setup",
    )(got)
    meta = meta[:, :]

    voxel_flat = slot_voxel.reshape(blocks)
    bwd_index, bwd0, bwd1, column_weight = pl.pallas_call(
        functools.partial(source_setup, extent, frames),
        out_shape=[shape((blocks, extent), jnp.int32)] + [shape((blocks, extent), f32)] * 2
        + [shape((voxel_tiles * frames, extent), f32)],
        in_specs=[VMEM] * 3,
        out_specs=[VMEM] * 4,
        compiler_params=PARAMS,
        name="source_setup",
    )(
        offset.reshape(blocks // extent, extent),
        block_slope.reshape(blocks // extent, extent),
        voxel_flat.reshape(blocks // extent, extent),
    )

    forward = pl.pallas_call(
        functools.partial(forward_kernel, n_slab, group, capacity, voxel_tiles, frames, chunk),
        out_shape=shape((ray_tiles * frames, extent), bf16),
        in_specs=[SMEM] + [VMEM] * 7,
        out_specs=VMEM,
        scratch_shapes=[
            pltpu.VMEM((n_slab * voxel_tiles * frames, extent), f32),
            pltpu.VMEM((ray_tiles * frames, extent), f32),
        ],
        compiler_params=PARAMS,
        name="forward",
    )
    backward = pl.pallas_call(
        functools.partial(backward_kernel, n_slab, group, capacity, ray_tiles, frames, chunk),
        out_shape=[shape(volume.shape, f32), shape(volume.shape, bf16)],
        in_specs=[SMEM] * 3 + [VMEM] * 6,
        out_specs=[VMEM] * 2,
        scratch_shapes=[pltpu.VMEM((n_slab * ray_tiles * frames, extent), f32)]
        + [pltpu.VMEM(volume.shape, f32)] * depth,
        compiler_params=PARAMS,
        name="backward",
    )
    sino = sinogram.reshape(ray_tiles * frames, extent)
    for sweep in range(ITERS):
        residual = forward(meta, gathered, sino, row_weight, fwd_index, fwd0, fwd1, fwd2)
        spread_out = lax.all_gather(residual, "slab", axis=0, tiled=True)
        volume, rounded = backward(
            live_count, voxel_flat, slot_ray, spread_out, volume, column_weight, bwd_index, bwd0, bwd1
        )
        if sweep + 1 < ITERS:
            gathered = lax.all_gather(rounded, "slab", axis=0, tiled=True)
    return volume.reshape(start_volume.shape)


def solution(mesh):
    in_specs = (
        P(("scan", "slab"), None, None),
        P(("scan", "slab"), None, None),
        P(("scan", "slab"), None),
        P(("scan", "slab")),
        P(("scan", "slab")),
        P(("scan", "slab"), None),
        P(("scan", "slab"), None),
    )
    out_specs = P(("scan", "slab"), None, None)
    return jax.shard_map(shards, mesh=mesh, in_specs=in_specs, out_specs=out_specs, check_vma=False)
```

```python
import functools

import jax
import jax.numpy as jnp
from jax import lax
from jax.experimental import pallas as pl
from jax.experimental.pallas import tpu as pltpu
from jax.sharding import PartitionSpec as P

ITERS = 2
FAR = 1.0e6
PARAMS = pltpu.CompilerParams(vmem_limit_bytes=48 * 1024 * 1024)
VMEM = pl.BlockSpec(memory_space=pltpu.VMEM)
SMEM = pl.BlockSpec(memory_space=pltpu.SMEM)


def hat(ray, offset, slope, voxel):
    return jnp.maximum(0.0, 1.0 - jnp.abs(ray - (offset + slope * voxel))).astype(jnp.bfloat16)


def row_taps(offset, slope, extent):
    shape = (offset.shape[0], extent)
    ray = lax.broadcasted_iota(jnp.int32, shape, 1).astype(jnp.float32)
    offset = jnp.broadcast_to(offset, shape)
    slope = jnp.broadcast_to(slope, shape)
    middle = jnp.floor((ray - offset) / slope + 0.5)
    middle = jnp.minimum(jnp.maximum(middle, 1.0), extent - 2.0)
    weights = [hat(ray, offset, slope, middle + step) for step in (-1.0, 0.0, 1.0)]
    return middle.astype(jnp.int32), weights


def column_taps(offset, slope, extent):
    shape = (offset.shape[0], extent)
    voxel = lax.broadcasted_iota(jnp.int32, shape, 1).astype(jnp.float32)
    centre = jnp.broadcast_to(offset, shape) + jnp.broadcast_to(slope, shape) * voxel
    first = jnp.minimum(jnp.maximum(jnp.floor(centre), 0.0), extent - 2.0)
    weights = [
        jnp.maximum(0.0, 1.0 - jnp.abs(first + step - centre)).astype(jnp.bfloat16)
        for step in (0.0, 1.0)
    ]
    return first.astype(jnp.int32), weights


def target_setup(n_slab, group, capacity, extent, frames, got_ref, index_ref, *rest):
    weight_refs, row_ref = rest[:3], rest[3]
    columns = got_ref[...].T
    ray_tiles = row_ref.shape[0] // frames
    total = jnp.zeros((ray_tiles, extent), jnp.float32)
    depth = group // capacity
    for source in range(n_slab):
        offset = columns[0:group, source:source + 1]
        slope = columns[group:2 * group, source:source + 1]
        middle, weights = row_taps(offset, slope, extent)
        rows = pl.ds(source * group, group)
        index_ref[rows, :] = middle
        for ref, weight in zip(weight_refs, weights):
            ref[rows, :] = weight.astype(jnp.float32)
        summed = sum(weight.astype(jnp.float32) for weight in weights)
        tile_of = jnp.broadcast_to(
            got_ref[source:source + 1, 4 * group:5 * group], (ray_tiles, group))
        match = tile_of == lax.broadcasted_iota(
            jnp.int32, (ray_tiles, group), 0).astype(jnp.float32)
        hot = match.astype(jnp.float32)
        total += jnp.dot(hot, summed, precision=lax.Precision.HIGHEST,
                         preferred_element_type=jnp.float32)
    weight = 1.0 / jnp.maximum(total, 1.0)
    for tile in range(ray_tiles):
        row_ref[tile * frames:(tile + 1) * frames, :] = jnp.broadcast_to(
            weight[tile:tile + 1, :], (frames, extent))


def source_setup(extent, frames, offset_ref, slope_ref, voxel_ref, index_ref, first_ref, second_ref,
                 column_ref):
    offsets = offset_ref[...].T
    slopes = slope_ref[...].T
    voxel_tiles = column_ref.shape[0] // frames
    total = jnp.zeros((voxel_tiles, extent), jnp.float32)
    for part in range(offset_ref.shape[0]):
        first, weights = column_taps(offsets[:, part:part + 1], slopes[:, part:part + 1], extent)
        rows = pl.ds(part * extent, extent)
        index_ref[rows, :] = first
        first_ref[rows, :] = weights[0].astype(jnp.float32)
        second_ref[rows, :] = weights[1].astype(jnp.float32)
        summed = weights[0].astype(jnp.float32) + weights[1].astype(jnp.float32)
        tile_of = jnp.broadcast_to(voxel_ref[part:part + 1, :], (voxel_tiles, extent))
        hot = (tile_of == lax.broadcasted_iota(jnp.int32, (voxel_tiles, extent), 0)).astype(jnp.float32)
        total += jnp.dot(hot, summed, precision=lax.Precision.HIGHEST,
                         preferred_element_type=jnp.float32)
    weight = 1.0 / jnp.maximum(total, 1.0)
    for tile in range(voxel_tiles):
        column_ref[tile * frames:(tile + 1) * frames, :] = jnp.broadcast_to(
            weight[tile:tile + 1, :], (frames, extent))


def pick(values, index):
    return jnp.take_along_axis(values, index, axis=1, mode="promise_in_bounds")


def spread(ref, row, frames):
    return jnp.broadcast_to(ref[pl.ds(row, 1), :], (frames, ref.shape[1]))


def forward_kernel(n_slab, group, capacity, tiles, frames, chunk,
                   me_ref, meta_ref, volume_ref, sinogram_ref, row_ref, index_ref, w0_ref, w1_ref,
                   w2_ref, out_ref, before, wide, after, projection):
    depth = group // capacity
    me = me_ref[0]
    rows = tiles * frames

    def widen(source, carry):
        at = pl.ds(pl.multiple_of(source * rows, rows), rows)
        values = volume_ref[at, :].astype(jnp.float32)
        wide[at, :] = values
        before[at, :] = pltpu.roll(values, 1, axis=1)
        after[at, :] = pltpu.roll(values, values.shape[1] - 1, axis=1)
        return carry

    lax.fori_loop(0, n_slab, widen, 0)
    projection[...] = jnp.zeros_like(projection)

    def from_source(source, carry):
        count = meta_ref[source, 2 * group + capacity]

        def some(step, carry):
            for place in range(chunk):
                slot = step * chunk + place
                total = None
                for level in range(depth):
                    block = slot * depth + level
                    voxel = lax.bitwise_xor(source, me) * tiles + meta_ref[source, group + block]
                    row = source * group + block
                    at = pl.ds(pl.multiple_of(voxel * frames, frames), frames)
                    index = spread(index_ref, row, frames)
                    for ref, values in ((w0_ref, before), (w1_ref, wide), (w2_ref, after)):
                        term = spread(ref, row, frames) * pick(values[at, :], index)
                        total = term if total is None else total + term
                ray = meta_ref[source, 2 * group + slot]
                at = pl.ds(pl.multiple_of(ray * frames, frames), frames)
                projection[at, :] += total.astype(jnp.bfloat16).astype(jnp.float32)
            return carry

        return lax.fori_loop(0, lax.div(count + (chunk - 1), chunk), some, carry)

    lax.fori_loop(0, n_slab, from_source, 0)
    residual = (sinogram_ref[...].astype(jnp.float32) - projection[...]) * row_ref[...]
    out_ref[...] = residual.astype(jnp.bfloat16)


def backward_kernel(n_slab, group, capacity, tiles, frames, chunk,
                    me_ref, count_ref, voxel_ref, ray_ref, even_ref, odd_ref, volume_ref, column_ref,
                    index_ref, w0_ref, w1_ref, out_ref, rounded_ref, wide, *banks):
    depth = group // capacity
    me = me_ref[0]
    rows = tiles * frames

    def widen(pair, carry):
        at = pl.ds(pl.multiple_of(pair * rows, rows), rows)
        twice = pl.multiple_of(pair * (2 * rows), rows)
        wide[pl.ds(twice, rows), :] = even_ref[at, :].astype(jnp.float32)
        wide[pl.ds(twice + rows, rows), :] = odd_ref[at, :].astype(jnp.float32)
        return carry

    lax.fori_loop(0, n_slab // 2, widen, 0)
    for bank in banks:
        bank[...] = jnp.zeros_like(bank)

    def to_target(target, carry):
        count = count_ref[target]

        def some(step, carry):
            for place in range(chunk):
                slot = target * capacity + step * chunk + place
                ray = lax.bitwise_xor(target, me) * tiles + ray_ref[slot]
                values = wide[pl.ds(pl.multiple_of(ray * frames, frames), frames), :]
                after = pltpu.roll(values, values.shape[1] - 1, axis=1)
                for level in range(depth):
                    row = slot * depth + level
                    index = spread(index_ref, row, frames)
                    term = (spread(w0_ref, row, frames) * pick(values, index)
                            + spread(w1_ref, row, frames) * pick(after, index))
                    at = pl.ds(pl.multiple_of(voxel_ref[row] * frames, frames), frames)
                    banks[level][at, :] += term
            return carry

        return lax.fori_loop(0, lax.div(count + (chunk - 1), chunk), some, carry)

    lax.fori_loop(0, n_slab, to_target, 0)
    back = banks[0][...]
    for bank in banks[1:]:
        back = back + bank[...]
    volume = volume_ref[...] + column_ref[...] * back
    out_ref[...] = volume
    rounded_ref[...] = volume.astype(jnp.bfloat16)


def exchange(values, n_slab, distance):
    pairs = [(device, device ^ distance) for device in range(n_slab)]
    return lax.ppermute(values, "slab", pairs)


def gather_tree(values, n_slab):
    rows, extent = values.shape
    held = values.reshape(1, rows, extent)
    distance = n_slab // 2
    while distance:
        got = exchange(held, n_slab, distance)
        held = jnp.stack([held, got], axis=1).reshape(-1, rows, extent)
        distance //= 2
    return held.reshape(-1, extent)


def gather_direct(values, n_slab):
    even = jnp.concatenate(
        [values] + [exchange(values, n_slab, distance) for distance in range(2, n_slab, 2)], axis=0)
    return even, exchange(even, n_slab, 1)


def shards(sinogram, start_volume, slot_voxel, slot_ray, live_count, block_slope, block_offset):
    n_slab = lax.axis_size("slab")
    n_slots, depth = slot_voxel.shape
    capacity = n_slots // n_slab
    group = capacity * depth
    ray_tiles, frames, extent = sinogram.shape
    voxel_tiles = start_volume.shape[0]
    blocks = n_slots * depth
    chunk = min(4, capacity)
    f32, bf16 = jnp.float32, jnp.bfloat16
    shape = jax.ShapeDtypeStruct

    volume = start_volume.reshape(voxel_tiles * frames, extent)
    me = lax.axis_index("slab").astype(jnp.int32).reshape(1)
    gathered = gather_tree(volume.astype(bf16), n_slab)

    alive = (jnp.arange(capacity)[None, :] < live_count[:, None]).reshape(n_slots, 1)
    offset = jnp.where(alive, block_offset, FAR)
    width = -(-(5 * group + capacity + 1) // extent) * extent
    used = 5 * group + capacity + 1
    packed = jnp.concatenate(
        [
            offset.reshape(n_slab, group),
            block_slope.reshape(n_slab, group),
            slot_voxel.astype(f32).reshape(n_slab, group),
            jnp.zeros((n_slab, group), f32),
            jnp.repeat(slot_ray.astype(f32), depth).reshape(n_slab, group),
            slot_ray.astype(f32).reshape(n_slab, capacity),
            live_count.astype(f32).reshape(n_slab, 1),
            jnp.zeros((n_slab, width - used), f32),
        ],
        axis=1,
    )
    got = lax.all_to_all(packed, "slab", split_axis=0, concat_axis=0, tiled=True)
    meta = jnp.concatenate(
        [got[:, 4 * group:5 * group], got[:, 2 * group:3 * group], got[:, 5 * group:used]], axis=1
    ).astype(jnp.int32)

    fwd_index, fwd0, fwd1, fwd2, row_weight = pl.pallas_call(
        functools.partial(target_setup, n_slab, group, capacity, extent, frames),
        out_shape=[shape((blocks, extent), jnp.int32)] + [shape((blocks, extent), f32)] * 3
        + [shape((ray_tiles * frames, extent), f32)],
        in_specs=[VMEM],
        out_specs=[VMEM] * 5,
        compiler_params=PARAMS,
        name="target_setup",
    )(got)

    voxel_flat = slot_voxel.reshape(blocks)
    bwd_index, bwd0, bwd1, column_weight = pl.pallas_call(
        functools.partial(source_setup, extent, frames),
        out_shape=[shape((blocks, extent), jnp.int32)] + [shape((blocks, extent), f32)] * 2
        + [shape((voxel_tiles * frames, extent), f32)],
        in_specs=[VMEM] * 3,
        out_specs=[VMEM] * 4,
        compiler_params=PARAMS,
        name="source_setup",
    )(
        offset.reshape(blocks // extent, extent),
        block_slope.reshape(blocks // extent, extent),
        voxel_flat.reshape(blocks // extent, extent),
    )

    forward = pl.pallas_call(
        functools.partial(forward_kernel, n_slab, group, capacity, voxel_tiles, frames, chunk),
        out_shape=shape((ray_tiles * frames, extent), bf16),
        in_specs=[SMEM] * 2 + [VMEM] * 7,
        out_specs=VMEM,
        scratch_shapes=[pltpu.VMEM((n_slab * voxel_tiles * frames, extent), f32)] * 3
        + [
            pltpu.VMEM((ray_tiles * frames, extent), f32),
        ],
        compiler_params=PARAMS,
        name="forward",
    )
    backward = pl.pallas_call(
        functools.partial(backward_kernel, n_slab, group, capacity, ray_tiles, frames, chunk),
        out_shape=[shape(volume.shape, f32), shape(volume.shape, bf16)],
        in_specs=[SMEM] * 4 + [VMEM] * 7,
        out_specs=[VMEM] * 2,
        scratch_shapes=[pltpu.VMEM((n_slab * ray_tiles * frames, extent), f32)]
        + [pltpu.VMEM(volume.shape, f32)] * depth,
        compiler_params=PARAMS,
        name="backward",
    )
    sino = sinogram.reshape(ray_tiles * frames, extent)
    for sweep in range(ITERS):
        residual = forward(me, meta, gathered, sino, row_weight, fwd_index, fwd0, fwd1, fwd2)
        even, odd = gather_direct(residual, n_slab)
        volume, rounded = backward(
            me, live_count, voxel_flat, slot_ray, even, odd, volume, column_weight, bwd_index, bwd0, bwd1
        )
        if sweep + 1 < ITERS:
            gathered = gather_tree(rounded, n_slab)
    return volume.reshape(start_volume.shape)


def solution(mesh):
    in_specs = (
        P(("scan", "slab"), None, None),
        P(("scan", "slab"), None, None),
        P(("scan", "slab"), None),
        P(("scan", "slab")),
        P(("scan", "slab")),
        P(("scan", "slab"), None),
        P(("scan", "slab"), None),
    )
    out_specs = P(("scan", "slab"), None, None)
    return jax.shard_map(shards, mesh=mesh, in_specs=in_specs, out_specs=out_specs, check_vma=False)
```

```python
import functools

import jax
import jax.numpy as jnp
from jax import lax
from jax.experimental import pallas as pl
from jax.experimental.pallas import tpu as pltpu
from jax.sharding import PartitionSpec as P

ITERS = 2
FAR = 1.0e6
CHUNK = 8
F32 = jnp.float32
BF16 = jnp.bfloat16
I32 = jnp.int32
VMEM = pl.BlockSpec(memory_space=pltpu.VMEM)
SMEM = pl.BlockSpec(memory_space=pltpu.SMEM)


def params(mib):
    return pltpu.CompilerParams(vmem_limit_bytes=mib * 1024 * 1024)


def hat(ray, centre):
    return jnp.maximum(0.0, 1.0 - jnp.abs(ray - centre)).astype(BF16)


def row_taps(offset, slope, extent):
    shape = (offset.shape[0], extent)
    ray = lax.broadcasted_iota(I32, shape, 1).astype(F32)
    offset = jnp.broadcast_to(offset, shape)
    slope = jnp.broadcast_to(slope, shape)
    middle = jnp.floor((ray - offset) / slope + 0.5)
    middle = jnp.minimum(jnp.maximum(middle, 1.0), extent - 2.0)
    weights = [hat(ray, offset + slope * (middle + step)) for step in (-1.0, 0.0, 1.0)]
    return middle.astype(I32), weights


def column_taps(offset, slope, extent):
    shape = (offset.shape[0], extent)
    voxel = lax.broadcasted_iota(I32, shape, 1).astype(F32)
    centre = jnp.broadcast_to(offset, shape) + jnp.broadcast_to(slope, shape) * voxel
    first = jnp.minimum(jnp.maximum(jnp.floor(centre), 0.0), extent - 2.0)
    weights = [hat(first + step, centre) for step in (0.0, 1.0)]
    return first.astype(I32), weights


def repeat_rows(values, times):
    return jnp.concatenate(
        [jnp.broadcast_to(values[row:row + 1, :], (times, values.shape[1]))
         for row in range(values.shape[0])], axis=0)


def setup_kernel(paired, n_slab, capacity, depth, tiles, frames, extent,
                 me_ref, meta_ref, got_ref,
                 total_ref, line_ref, ray_ref, voxel_ref,
                 row_ref, fi_ref, f0_ref, f1_ref, f2_ref, bi_ref, b0_ref, b1_ref):
    group = capacity * depth
    ray_tiles = row_ref.shape[0] // frames
    tables = (fi_ref, f0_ref, f1_ref, f2_ref, bi_ref, b0_ref, b1_ref)
    me = me_ref[0]
    half = n_slab // 2

    def from_source(source, found):
        place = source
        if paired:
            entry = lax.bitwise_xor(source, me)
            place = lax.shift_right_logical(entry, 1) + lax.bitwise_and(entry, 1) * half

        def slot(k, found):
            line_ref[found] = source * group + k
            ray_ref[found] = meta_ref[source, depth * capacity + k] * frames
            for level in range(depth):
                tile = place * tiles + meta_ref[source, level * capacity + k]
                voxel_ref[found * depth + level] = tile * frames
            return found + 1

        return lax.fori_loop(0, meta_ref[source, (depth + 1) * capacity], slot, found)

    found = lax.fori_loop(0, n_slab, from_source, 0)
    total_ref[0] = found
    for spare in range(CHUNK):
        line_ref[found + spare] = n_slab * group
        ray_ref[found + spare] = 0
        for level in range(depth):
            voxel_ref[(found + spare) * depth + level] = 0

    def build(source, total):
        fields = got_ref[source]
        columns = fields.T
        summed = None
        for level in range(depth):
            offset = columns[0:capacity, level:level + 1]
            slope = columns[0:capacity, depth + level:depth + level + 1]
            middle, weights = row_taps(offset, slope, extent)
            first, pair = column_taps(offset, slope, extent)
            wide = [weight.astype(F32) for weight in weights]
            values = [middle] + wide + [first] + [weight.astype(F32) for weight in pair]
            at = source * group
            if not isinstance(at, int):
                at = pl.multiple_of(at, 8)
            at = pl.ds(at + level * capacity, capacity)
            for ref, value in zip(tables, values):
                ref[at, :] = value
            part = (wide[0] + wide[1]) + wide[2]
            summed = part if summed is None else summed + part
        tile_of = jnp.broadcast_to(fields[3 * depth:3 * depth + 1, 0:capacity], (ray_tiles, capacity))
        hot = tile_of == lax.broadcasted_iota(I32, (ray_tiles, capacity), 0).astype(F32)
        return total + jnp.dot(hot.astype(F32), summed, precision=lax.Precision.HIGHEST,
                               preferred_element_type=F32)

    total = jnp.zeros((ray_tiles, extent), F32)
    if paired:
        for source in range(n_slab):
            total = build(source, total)
    else:
        total = lax.fori_loop(0, n_slab, build, total)
    for ref in tables:
        ref[n_slab * group:, :] = jnp.zeros((group, extent), ref.dtype)
    row_ref[...] = repeat_rows(1.0 / jnp.maximum(total, 1.0), frames)


def column_kernel(frames, offset_ref, slope_ref, voxel_ref, out_ref):
    tiles = out_ref.shape[0] // frames
    depth, slots = offset_ref.shape
    extent = out_ref.shape[1]
    offsets = offset_ref[...].T
    slopes = slope_ref[...].T
    total = jnp.zeros((tiles, extent), F32)
    for level in range(depth):
        unused, pair = column_taps(
            offsets[:, level:level + 1], slopes[:, level:level + 1], extent)
        tile_of = jnp.broadcast_to(voxel_ref[level:level + 1, :], (tiles, slots))
        hot = (tile_of == lax.broadcasted_iota(I32, (tiles, slots), 0)).astype(F32).astype(BF16)
        for weight in pair:
            total += jnp.dot(hot, weight, preferred_element_type=F32)
    out_ref[...] = repeat_rows(1.0 / jnp.maximum(total, 1.0), frames)


def pick(values, index):
    return jnp.take_along_axis(values, index, axis=1, mode="promise_in_bounds")


def spread(ref, row, frames):
    return jnp.broadcast_to(ref[pl.ds(row, 1), :], (frames, ref.shape[1]))


def sweep_kernel(capacity, depth, frames, n_wide, n_bank,
                 total_ref, line_ref, ray_ref, voxel_ref, near_ref, far_ref, sinogram_ref, row_ref,
                 fi_ref, f0_ref, f1_ref, f2_ref, bi_ref, b0_ref, b1_ref,
                 near_out, far_out, projection, *scratch):
    wides, banks = scratch[:n_wide], scratch[n_wide:]
    half, extent = near_ref.shape
    step_rows = 128
    steps = half // step_rows

    def widen(step, carry):
        at = pl.multiple_of(step * step_rows, step_rows)
        for ref, base in ((near_ref, 0), (far_ref, half)):
            values = ref[pl.ds(at, step_rows), :].astype(F32)
            to = pl.ds(base + at, step_rows)
            wides[0][to, :] = values
            if n_wide == 3:
                wides[1][to, :] = pltpu.roll(values, 1, axis=1)
                wides[2][to, :] = pltpu.roll(values, extent - 1, axis=1)
            for bank in banks:
                bank[to, :] = jnp.zeros_like(values)
        return carry

    lax.fori_loop(0, steps, widen, 0)
    projection[...] = jnp.zeros_like(projection)
    rounds = lax.div(total_ref[0] + (CHUNK - 1), CHUNK)

    def tile_at(start):
        return pl.ds(pl.multiple_of(start, frames), frames)

    def forward(step, carry):
        for place in range(CHUNK):
            slot = step * CHUNK + place
            line = line_ref[slot]
            total = None
            for level in range(depth):
                at = tile_at(voxel_ref[slot * depth + level])
                row = line + level * capacity
                index = spread(fi_ref, row, frames)
                if n_wide == 3:
                    taps = [pick(ref[at, :], index) for ref in (wides[1], wides[0], wides[2])]
                else:
                    values = wides[0][at, :]
                    taps = [pick(values, index + shift) for shift in (-1, 0, 1)]
                for ref, tap in zip((f0_ref, f1_ref, f2_ref), taps):
                    term = spread(ref, row, frames) * tap
                    total = term if total is None else total + term
            projection[tile_at(ray_ref[slot]), :] += total.astype(BF16).astype(F32)
        return carry

    lax.fori_loop(0, rounds, forward, 0)
    residual = (sinogram_ref[...].astype(F32) - projection[...]) * row_ref[...]
    projection[...] = residual.astype(BF16).astype(F32)

    def backward(step, carry):
        for place in range(CHUNK):
            slot = step * CHUNK + place
            line = line_ref[slot]
            values = projection[tile_at(ray_ref[slot]), :]
            for level in range(depth):
                row = line + level * capacity
                index = spread(bi_ref, row, frames)
                term = (spread(b0_ref, row, frames) * pick(values, index)
                        + spread(b1_ref, row, frames) * pick(values, index + 1))
                bank = banks[level % n_bank]
                bank[tile_at(voxel_ref[slot * depth + level]), :] += term
        return carry

    lax.fori_loop(0, rounds, backward, 0)

    def finish(step, carry):
        at = pl.multiple_of(step * step_rows, step_rows)
        here, there = pl.ds(at, step_rows), pl.ds(half + at, step_rows)
        near_out[here, :] = sum(bank[here, :] for bank in banks[1:]) + banks[0][here, :]
        far = sum(bank[there, :] for bank in banks[1:]) + banks[0][there, :]
        far_out[here, :] = far.astype(BF16)
        return carry

    lax.fori_loop(0, steps, finish, 0)


def combine_kernel(near_ref, got_ref, own_ref, *piece_refs):
    rows = own_ref.shape[0]
    own_ref[...] = near_ref[0:rows, :] + got_ref[0:rows, :].astype(F32)
    for place, ref in enumerate(piece_refs):
        at = pl.ds((place + 1) * rows, rows)
        ref[...] = (near_ref[at, :] + got_ref[at, :].astype(F32)).astype(BF16)


def update_kernel(n_pieces, volume_ref, column_ref, own_ref, *refs):
    back = own_ref[...]
    for ref in refs[:n_pieces]:
        back = back + ref[...].astype(F32)
    volume = volume_ref[...] + column_ref[...] * back
    outs = refs[n_pieces:]
    outs[0][...] = volume
    if len(outs) > 1:
        outs[1][...] = volume.astype(BF16)


def exchange(values, n_slab, distance):
    pairs = [(device, device ^ distance) for device in range(n_slab)]
    return lax.ppermute(values, "slab", pairs)


def gather(values, n_slab, paired):
    if not paired:
        whole = lax.all_gather(values, "slab", axis=0, tiled=True)
        middle = whole.shape[0] // 2
        return whole[:middle], whole[middle:]
    near = jnp.concatenate(
        [values] + [exchange(values, n_slab, distance) for distance in range(2, n_slab, 2)], axis=0)
    return near, exchange(near, n_slab, 1)


def shards(sinogram, start_volume, slot_voxel, slot_ray, live_count, block_slope, block_offset):
    n_slab = lax.axis_size("slab")
    n_slots, depth = slot_voxel.shape
    capacity = n_slots // n_slab
    ray_tiles, frames, extent = sinogram.shape
    voxel_tiles = start_volume.shape[0]
    lines = n_slots * depth + capacity * depth
    rows = voxel_tiles * frames
    half = n_slab // 2
    paired = n_slab <= 32
    n_wide, n_bank = (3, 2) if paired else (1, 1)
    shape = jax.ShapeDtypeStruct

    volume = start_volume.reshape(rows, extent)
    near, far = gather(volume.astype(BF16), n_slab, paired)
    me = lax.axis_index("slab").astype(I32).reshape(1)

    alive = (jnp.arange(capacity)[None, :] < live_count[:, None]).reshape(1, n_slots)
    offset = jnp.where(alive, block_offset.T, FAR)
    slope = block_slope.T
    voxel = slot_voxel.T
    count = jnp.broadcast_to(live_count[:, None], (n_slab, capacity)).reshape(1, n_slots)
    fields = jnp.concatenate(
        [offset, slope, voxel.astype(F32), slot_ray.astype(F32).reshape(1, n_slots), count.astype(F32)],
        axis=0)
    n_fields = 3 * depth + 2
    packed = fields.reshape(n_fields, n_slab, capacity).transpose(1, 0, 2)
    padding = ((0, 0), (0, -n_fields % 8), (0, extent - capacity))
    got = lax.all_to_all(
        jnp.pad(packed, padding), "slab", split_axis=0, concat_axis=0, tiled=True)
    meta = got[:, 2 * depth:n_fields, :capacity].astype(I32).reshape(n_slab, (depth + 2) * capacity)

    table = [shape((lines, extent), I32)] + [shape((lines, extent), F32)] * 3
    table += [shape((lines, extent), I32)] + [shape((lines, extent), F32)] * 2
    spare = n_slots + CHUNK
    lists = [shape((1,), I32), shape((spare,), I32), shape((spare,), I32), shape((spare * depth,), I32)]
    prepared = pl.pallas_call(
        functools.partial(setup_kernel, paired, n_slab, capacity, depth, voxel_tiles, frames, extent),
        out_shape=lists + [shape((ray_tiles * frames, extent), F32)] + table,
        in_specs=[SMEM, SMEM, VMEM],
        out_specs=[SMEM] * 4 + [VMEM] * 8,
        compiler_params=params(32),
        name="setup",
    )(me, meta, got)
    lists, row_weight, table = prepared[:4], prepared[4], prepared[5:]

    column_weight = pl.pallas_call(
        functools.partial(column_kernel, frames),
        out_shape=shape((rows, extent), F32),
        in_specs=[VMEM] * 3,
        out_specs=VMEM,
        compiler_params=params(16),
        name="column_weight",
    )(offset, slope, voxel)

    sweep = pl.pallas_call(
        functools.partial(sweep_kernel, capacity, depth, frames, n_wide, n_bank),
        out_shape=[shape((half * rows, extent), F32), shape((half * rows, extent), BF16)],
        in_specs=[SMEM] * 4 + [VMEM] * 11,
        out_specs=[VMEM] * 2,
        scratch_shapes=[pltpu.VMEM((ray_tiles * frames, extent), F32)]
        + [pltpu.VMEM((n_slab * rows, extent), F32)] * (n_wide + n_bank),
        compiler_params=params(40 if n_slab > 32 else 24),
        name="sweep",
    )
    combine = pl.pallas_call(
        combine_kernel,
        out_shape=[shape((rows, extent), F32)] + [shape((rows, extent), BF16)] * (half - 1),
        in_specs=[VMEM] * 2,
        out_specs=[VMEM] * half,
        compiler_params=params(24),
        name="combine",
    )
    sino = sinogram.reshape(ray_tiles * frames, extent)
    for turn in range(ITERS):
        last = turn + 1 == ITERS
        near_sum, far_sum = sweep(*lists, near, far, sino, row_weight, *table)
        if paired:
            own, *pieces = combine(near_sum, exchange(far_sum, n_slab, 1))
            pieces = [exchange(piece, n_slab, 2 * (place + 1)) for place, piece in enumerate(pieces)]
        else:
            both = jnp.concatenate([near_sum.astype(BF16), far_sum], axis=0)
            parts = lax.all_to_all(
                both.reshape(n_slab, rows, extent), "slab", split_axis=0, concat_axis=0, tiled=True)
            own, pieces = jnp.sum(parts.astype(F32), axis=0), []
        updated = pl.pallas_call(
            functools.partial(update_kernel, len(pieces)),
            out_shape=[shape((rows, extent), F32)] + ([] if last else [shape((rows, extent), BF16)]),
            in_specs=[VMEM] * (len(pieces) + 3),
            out_specs=[VMEM] * (1 if last else 2),
            compiler_params=params(16),
            name="update",
        )(volume, column_weight, own, *pieces)
        volume = updated[0]
        if not last:
            near, far = gather(updated[1], n_slab, paired)
    return volume.reshape(start_volume.shape)


def solution(mesh):
    in_specs = (
        P(("scan", "slab"), None, None),
        P(("scan", "slab"), None, None),
        P(("scan", "slab"), None),
        P(("scan", "slab")),
        P(("scan", "slab")),
        P(("scan", "slab"), None),
        P(("scan", "slab"), None),
    )
    out_specs = P(("scan", "slab"), None, None)
    return jax.shard_map(shards, mesh=mesh, in_specs=in_specs, out_specs=out_specs, check_vma=False)
```

```python
import functools

import jax
import jax.numpy as jnp
from jax import lax
from jax.experimental import pallas as pl
from jax.experimental.pallas import tpu as pltpu
from jax.sharding import PartitionSpec as P

ITERS = 2
FAR = 1.0e6
CHUNK = 8
F32 = jnp.float32
BF16 = jnp.bfloat16
I32 = jnp.int32
HIGHEST = lax.Precision.HIGHEST
VMEM = pl.BlockSpec(memory_space=pltpu.VMEM)
SMEM = pl.BlockSpec(memory_space=pltpu.SMEM)


def params(mib):
    return pltpu.CompilerParams(vmem_limit_bytes=mib * 1024 * 1024)


def hat(ray, centre):
    return jnp.maximum(0.0, 1.0 - jnp.abs(ray - centre)).astype(BF16)


def row_taps(offset, slope, extent):
    shape = (offset.shape[0], extent)
    ray = lax.broadcasted_iota(I32, shape, 1).astype(F32)
    offset = jnp.broadcast_to(offset, shape)
    slope = jnp.broadcast_to(slope, shape)
    middle = jnp.floor((ray - offset) / slope + 0.5)
    middle = jnp.minimum(jnp.maximum(middle, 1.0), extent - 2.0)
    weights = [hat(ray, offset + slope * (middle + step)) for step in (-1.0, 0.0, 1.0)]
    return middle.astype(I32), weights


def column_taps(offset, slope, extent):
    shape = (offset.shape[0], extent)
    voxel = lax.broadcasted_iota(I32, shape, 1).astype(F32)
    centre = jnp.broadcast_to(offset, shape) + jnp.broadcast_to(slope, shape) * voxel
    first = jnp.minimum(jnp.maximum(jnp.floor(centre), 0.0), extent - 2.0)
    weights = [hat(first + step, centre) for step in (0.0, 1.0)]
    return first.astype(I32), weights


def repeat_rows(values, times):
    return jnp.concatenate(
        [jnp.broadcast_to(values[row:row + 1, :], (times, values.shape[1]))
         for row in range(values.shape[0])], axis=0)


def contract_lanes(left, right):
    return lax.dot_general(
        left, right, (((1,), (1,)), ((), ())), precision=HIGHEST, preferred_element_type=F32)


def setup_kernel(n_slab, capacity, depth, tiles, frames, extent,
                 me_ref, line_up_ref, got_ref,
                 near_list, far_list, row_ref, fi_ref, f0_ref, f1_ref, f2_ref, bi_ref, b0_ref, b1_ref):
    group = capacity * depth
    slots = n_slab * capacity
    dead = n_slab * group
    ray_tiles = row_ref.shape[0] // frames
    tables = (fi_ref, f0_ref, f1_ref, f2_ref, bi_ref, b0_ref, b1_ref)

    slot = lax.broadcasted_iota(I32, (1, slots), 1)
    source = lax.div(slot, capacity)
    within = lax.rem(slot, capacity)
    line = (source * group + within - dead).astype(F32)
    ray = line_up_ref[depth:depth + 1, :] * frames
    base = lax.shift_right_logical(source, 1).astype(F32) * tiles
    voxels = [(line_up_ref[level:level + 1, :] + base) * frames for level in range(depth)]
    table = jnp.concatenate(
        [line, ray] + voxels + [jnp.zeros((8 - 2 - depth, slots), F32)], axis=0)
    alive = within.astype(F32) < line_up_ref[depth + 1:depth + 2, :]
    same = lax.bitwise_and(lax.bitwise_xor(source, me_ref[0]), 1) == 0
    order = lax.broadcasted_iota(I32, (slots, slots), 0)
    earlier = (lax.broadcasted_iota(I32, (slots, slots), 1) < order).astype(F32)
    kind = lax.broadcasted_iota(I32, (8, slots), 0)
    for ref, wanted in ((near_list, same), (far_list, jnp.logical_not(same))):
        room = ref.shape[1]
        taken = jnp.logical_and(alive, wanted).astype(F32)
        position = contract_lanes(jnp.broadcast_to(taken, (8, slots)), earlier)[0:1, :]
        position = jnp.where(taken > 0.0, position, -1.0).astype(I32)
        choose = jnp.broadcast_to(position, (room, slots)) == order[:room, :]
        packed = contract_lanes(table, choose.astype(F32))
        total = jnp.sum(taken, axis=1, keepdims=True)
        extra = jnp.where(kind == 0, float(dead), jnp.where(kind == 7, total, 0.0))[:, :room]
        ref[...] = (packed + extra + 0.5).astype(I32)

    def build(source, total):
        fields = got_ref[source]
        columns = fields.T
        summed = None
        for level in range(depth):
            offset = columns[0:capacity, level:level + 1]
            slope = columns[0:capacity, depth + level:depth + level + 1]
            middle, weights = row_taps(offset, slope, extent)
            first, pair = column_taps(offset, slope, extent)
            wide = [weight.astype(F32) for weight in weights]
            values = [middle] + wide + [first] + [weight.astype(F32) for weight in pair]
            at = source * group
            if not isinstance(at, int):
                at = pl.multiple_of(at, 8)
            at = pl.ds(at + level * capacity, capacity)
            for ref, value in zip(tables, values):
                ref[at, :] = value
            part = (wide[0] + wide[1]) + wide[2]
            summed = part if summed is None else summed + part
        tile_of = jnp.broadcast_to(fields[3 * depth:3 * depth + 1, 0:capacity], (ray_tiles, capacity))
        hot = tile_of == lax.broadcasted_iota(I32, (ray_tiles, capacity), 0).astype(F32)
        return total + jnp.dot(hot.astype(F32), summed, precision=HIGHEST, preferred_element_type=F32)

    total = jnp.zeros((ray_tiles, extent), F32)
    if n_slab <= 32:
        for source in range(n_slab):
            total = build(source, total)
    else:
        total = lax.fori_loop(0, n_slab, build, total)
    for ref in tables:
        ref[dead:, :] = jnp.zeros((group, extent), ref.dtype)
    row_ref[...] = repeat_rows(1.0 / jnp.maximum(total, 1.0), frames)


def column_kernel(frames, offset_ref, slope_ref, voxel_ref, out_ref):
    tiles = out_ref.shape[0] // frames
    depth, slots = offset_ref.shape
    extent = out_ref.shape[1]
    offsets = offset_ref[...].T
    slopes = slope_ref[...].T
    total = jnp.zeros((tiles, extent), F32)
    for level in range(depth):
        unused, pair = column_taps(
            offsets[:, level:level + 1], slopes[:, level:level + 1], extent)
        tile_of = jnp.broadcast_to(voxel_ref[level:level + 1, :], (tiles, slots))
        hot = (tile_of == lax.broadcasted_iota(I32, (tiles, slots), 0)).astype(F32).astype(BF16)
        for weight in pair:
            total += jnp.dot(hot, weight, preferred_element_type=F32)
    out_ref[...] = repeat_rows(1.0 / jnp.maximum(total, 1.0), frames)


def pick(values, index):
    return jnp.take_along_axis(values, index, axis=1, mode="promise_in_bounds")


def spread(ref, row, frames):
    return jnp.broadcast_to(ref[pl.ds(row, 1), :], (frames, ref.shape[1]))


def tile_at(start, frames):
    return pl.ds(pl.multiple_of(start, frames), frames)


def for_slots(list_ref, body):
    def some(step, carry):
        for place in range(CHUNK):
            body(step * CHUNK + place)
        return carry

    lax.fori_loop(0, lax.div(list_ref[7, 0] + (CHUNK - 1), CHUNK), some, 0)


def for_rows(rows, body):
    step = 128

    def some(number, carry):
        body(pl.ds(pl.multiple_of(number * step, step), step))
        return carry

    lax.fori_loop(0, rows // step, some, 0)


def project(capacity, depth, frames, list_ref, values_ref, tables, projection, wides):
    extent = values_ref.shape[1]

    def widen(at):
        values = values_ref[at, :].astype(F32)
        wides[0][at, :] = values
        if len(wides) == 3:
            wides[1][at, :] = pltpu.roll(values, 1, axis=1)
            wides[2][at, :] = pltpu.roll(values, extent - 1, axis=1)

    for_rows(values_ref.shape[0], widen)

    def one(slot):
        line = list_ref[0, slot]
        total = None
        for level in range(depth):
            at = tile_at(list_ref[2 + level, slot], frames)
            row = line + level * capacity
            index = spread(tables[0], row, frames)
            if len(wides) == 3:
                taps = [pick(ref[at, :], index) for ref in (wides[1], wides[0], wides[2])]
            else:
                values = wides[0][at, :]
                taps = [pick(values, index + shift) for shift in (-1, 0, 1)]
            for ref, tap in zip(tables[1:], taps):
                term = spread(ref, row, frames) * tap
                total = term if total is None else total + term
        projection[tile_at(list_ref[1, slot], frames), :] += total.astype(BF16).astype(F32)

    for_slots(list_ref, one)


def backproject(capacity, depth, frames, list_ref, residual, tables, banks):
    def clear(at):
        for bank in banks:
            bank[at, :] = jnp.zeros((at.size, bank.shape[1]), F32)

    for_rows(banks[0].shape[0], clear)

    def one(slot):
        line = list_ref[0, slot]
        values = residual[tile_at(list_ref[1, slot], frames), :]
        for level in range(depth):
            row = line + level * capacity
            index = spread(tables[0], row, frames)
            term = (spread(tables[1], row, frames) * pick(values, index)
                    + spread(tables[2], row, frames) * pick(values, index + 1))
            banks[level % len(banks)][tile_at(list_ref[2 + level, slot], frames), :] += term

    for_slots(list_ref, one)


def near_forward(sizes, list_ref, values_ref, *refs):
    tables, projection, wides = refs[:4], refs[4], refs[5:]
    projection[...] = jnp.zeros_like(projection)
    project(*sizes, list_ref, values_ref, tables, projection, wides)


def far_both(sizes, n_wide, list_ref, values_ref, partial_ref, sinogram_ref, row_ref, *refs):
    forward, backward = refs[:4], refs[4:7]
    out_ref, residual, scratch = refs[7], refs[8], refs[9:]
    projection, wides, banks = scratch[0], scratch[1:1 + n_wide], scratch[1 + n_wide:]
    projection[...] = partial_ref[...]
    project(*sizes, list_ref, values_ref, forward, projection, wides)
    scaled = (sinogram_ref[...].astype(F32) - projection[...]) * row_ref[...]
    residual[...] = scaled.astype(BF16).astype(F32)
    backproject(*sizes, list_ref, residual, backward, banks)

    def finish(at):
        out_ref[at, :] = sum([bank[at, :] for bank in banks[1:]], banks[0][at, :]).astype(BF16)

    for_rows(out_ref.shape[0], finish)


def near_backward(sizes, list_ref, residual, *refs):
    tables, out_ref, banks = refs[:3], refs[3], refs[4:]
    backproject(*sizes, list_ref, residual, tables, (out_ref,) + banks)

    def finish(at):
        out_ref[at, :] = sum([bank[at, :] for bank in banks], out_ref[at, :])

    if banks:
        for_rows(out_ref.shape[0], finish)


def combine_kernel(near_ref, got_ref, out_ref):
    def add(at):
        out_ref[at, :] = (near_ref[at, :] + got_ref[at, :].astype(F32)).astype(BF16)

    for_rows(out_ref.shape[0], add)


def update_kernel(volume_ref, column_ref, parts_ref, out_ref, *copies_ref):
    rows = volume_ref.shape[0]
    pieces = parts_ref.shape[0] // rows
    back = parts_ref[0:rows, :].astype(F32)
    for piece in range(1, pieces):
        back = back + parts_ref[piece * rows:(piece + 1) * rows, :].astype(F32)
    volume = volume_ref[...] + column_ref[...] * back
    out_ref[...] = volume
    for ref in copies_ref:
        for piece in range(pieces):
            ref[piece * rows:(piece + 1) * rows, :] = volume.astype(BF16)


def exchange_cores(values, n_slab):
    return lax.ppermute(values, "slab", [(device, device ^ 1) for device in range(n_slab)])


def across(values, n_slab):
    groups = [list(range(core, n_slab, 2)) for core in (0, 1)]
    return lax.all_to_all(
        values, "slab", split_axis=0, concat_axis=0, axis_index_groups=groups, tiled=True)


def shards(sinogram, start_volume, slot_voxel, slot_ray, live_count, block_slope, block_offset):
    n_slab = lax.axis_size("slab")
    n_slots, depth = slot_voxel.shape
    capacity = n_slots // n_slab
    ray_tiles, frames, extent = sinogram.shape
    voxel_tiles = start_volume.shape[0]
    lines = n_slots * depth + capacity * depth
    rows = voxel_tiles * frames
    half = n_slab // 2
    n_wide, n_bank = (3, 2) if n_slab <= 32 else (1, 1)
    shape = jax.ShapeDtypeStruct
    sizes = (capacity, depth, frames)

    volume = start_volume.reshape(rows, extent)
    rounded = jnp.broadcast_to(volume.astype(BF16)[None], (half, rows, extent))
    near = across(rounded.reshape(half * rows, extent), n_slab)
    me = lax.axis_index("slab").astype(I32).reshape(1)

    alive = (jnp.arange(capacity)[None, :] < live_count[:, None]).reshape(1, n_slots)
    offset = jnp.where(alive, block_offset.T, FAR)
    slope = block_slope.T
    voxel = slot_voxel.T
    count = jnp.broadcast_to(live_count[:, None], (n_slab, capacity)).reshape(1, n_slots)
    fields = jnp.concatenate(
        [offset, slope, voxel.astype(F32), slot_ray.astype(F32).reshape(1, n_slots), count.astype(F32)],
        axis=0)
    n_fields = 3 * depth + 2
    packed = fields.reshape(n_fields, n_slab, capacity).transpose(1, 0, 2)
    padding = ((0, 0), (0, -n_fields % 8), (0, extent - capacity))
    got = lax.all_to_all(
        jnp.pad(packed, padding), "slab", split_axis=0, concat_axis=0, tiled=True)
    line_up = got[:, 2 * depth:n_fields, :capacity].transpose(1, 0, 2).reshape(depth + 2, n_slots)

    table = [shape((lines, extent), I32)] + [shape((lines, extent), F32)] * 3
    table += [shape((lines, extent), I32)] + [shape((lines, extent), F32)] * 2
    lists = [shape((8, n_slots // 2), I32)] * 2
    near_list, far_list, row_weight, *table = pl.pallas_call(
        functools.partial(setup_kernel, n_slab, capacity, depth, voxel_tiles, frames, extent),
        out_shape=lists + [shape((ray_tiles * frames, extent), F32)] + table,
        in_specs=[SMEM, VMEM, VMEM],
        out_specs=[VMEM] * 10,
        compiler_params=params(32),
        name="setup",
    )(me, line_up, got)

    column_weight = pl.pallas_call(
        functools.partial(column_kernel, frames),
        out_shape=shape((rows, extent), F32),
        in_specs=[VMEM] * 3,
        out_specs=VMEM,
        compiler_params=params(16),
        name="column_weight",
    )(offset, slope, voxel)

    rays = shape((ray_tiles * frames, extent), F32)
    wide = pltpu.VMEM((half * rows, extent), F32)
    forward_near = pl.pallas_call(
        functools.partial(near_forward, sizes),
        out_shape=rays,
        in_specs=[SMEM] + [VMEM] * 5,
        out_specs=VMEM,
        scratch_shapes=[wide] * n_wide,
        compiler_params=params(24),
        name="near_forward",
    )
    both_far = pl.pallas_call(
        functools.partial(far_both, sizes, n_wide),
        out_shape=[shape((half * rows, extent), BF16), rays],
        in_specs=[SMEM] + [VMEM] * 11,
        out_specs=[VMEM] * 2,
        scratch_shapes=[pltpu.VMEM(rays.shape, F32)] + [wide] * (n_wide + n_bank),
        compiler_params=params(28),
        name="far_both",
    )
    backward_near = pl.pallas_call(
        functools.partial(near_backward, sizes),
        out_shape=shape((half * rows, extent), F32),
        in_specs=[SMEM] + [VMEM] * 4,
        out_specs=VMEM,
        scratch_shapes=[wide] * (n_bank - 1),
        compiler_params=params(24),
        name="near_backward",
    )
    combine = pl.pallas_call(
        combine_kernel,
        out_shape=shape((half * rows, extent), BF16),
        in_specs=[VMEM] * 2,
        out_specs=VMEM,
        compiler_params=params(24),
        name="combine",
    )
    sino = sinogram.reshape(rays.shape)
    for turn in range(ITERS):
        copies = [shape((half * rows, extent), BF16)] if turn + 1 < ITERS else []
        far = exchange_cores(near, n_slab)
        partial = forward_near(near_list, near, *table[:4])
        far_sum, residual = both_far(far_list, far, partial, sino, row_weight, *table)
        swapped = exchange_cores(far_sum, n_slab)
        near_sum = backward_near(near_list, residual, *table[4:])
        parts = across(combine(near_sum, swapped), n_slab)
        volume, *rounded = pl.pallas_call(
            update_kernel,
            out_shape=[shape((rows, extent), F32)] + copies,
            in_specs=[VMEM] * 3,
            out_specs=[VMEM] * (1 + len(copies)),
            compiler_params=params(16),
            name="update",
        )(volume, column_weight, parts)
        if copies:
            near = across(rounded[0], n_slab)
    return volume.reshape(start_volume.shape)


def solution(mesh):
    in_specs = (
        P(("scan", "slab"), None, None),
        P(("scan", "slab"), None, None),
        P(("scan", "slab"), None),
        P(("scan", "slab")),
        P(("scan", "slab")),
        P(("scan", "slab"), None),
        P(("scan", "slab"), None),
    )
    out_specs = P(("scan", "slab"), None, None)
    return jax.shard_map(shards, mesh=mesh, in_specs=in_specs, out_specs=out_specs, check_vma=False)
```

```python
import functools

import jax
import jax.numpy as jnp
from jax import lax
from jax.experimental import pallas as pl
from jax.experimental.pallas import tpu as pltpu
from jax.sharding import PartitionSpec as P

ITERS = 2
FAR = 1.0e6
CHUNK = 8
F32 = jnp.float32
BF16 = jnp.bfloat16
I32 = jnp.int32
HIGHEST = lax.Precision.HIGHEST
VMEM = pl.BlockSpec(memory_space=pltpu.VMEM)
SMEM = pl.BlockSpec(memory_space=pltpu.SMEM)


def hat(ray, centre):
    return jnp.maximum(0.0, 1.0 - jnp.abs(ray - centre)).astype(BF16)


def row_taps(offset, slope, extent):
    shape = (offset.shape[0], extent)
    ray = lax.broadcasted_iota(I32, shape, 1).astype(F32)
    offset = jnp.broadcast_to(offset, shape)
    slope = jnp.broadcast_to(slope, shape)
    middle = jnp.floor((ray - offset) / slope + 0.5)
    middle = jnp.minimum(jnp.maximum(middle, 1.0), extent - 2.0)
    weights = [hat(ray, offset + slope * (middle + step)) for step in (-1.0, 0.0, 1.0)]
    return middle.astype(I32), weights


def column_taps(offset, slope, extent):
    shape = (offset.shape[0], extent)
    voxel = lax.broadcasted_iota(I32, shape, 1).astype(F32)
    centre = jnp.broadcast_to(offset, shape) + jnp.broadcast_to(slope, shape) * voxel
    first = jnp.minimum(jnp.maximum(jnp.floor(centre), 0.0), extent - 2.0)
    weights = [hat(first + step, centre) for step in (0.0, 1.0)]
    return first.astype(I32), weights


def repeat_rows(values, times):
    return jnp.concatenate(
        [jnp.broadcast_to(values[row:row + 1, :], (times, values.shape[1]))
         for row in range(values.shape[0])], axis=0)


def contract_lanes(left, right):
    return lax.dot_general(
        left, right, (((1,), (1,)), ((), ())), precision=HIGHEST, preferred_element_type=F32)


def pack_kernel(capacity, volume_ref, offset_ref, slope_ref, voxel_ref, ray_ref, live_ref, out_ref):
    rows, extent = volume_ref.shape
    out_ref[0:rows, :] = volume_ref[...].astype(BF16)
    slots = ray_ref.shape[1]
    fields = []
    for ref in (offset_ref, slope_ref):
        left = ref[...]
        for addend in range(3):
            part = left.astype(BF16).astype(F32)
            fields.append(part)
            left = left - part
    fields.append(voxel_ref[...].astype(F32))
    fields.append(ray_ref[...].astype(F32))
    fields.append(per_slot(live_ref, slots, capacity))
    used = sum(field.shape[0] for field in fields)
    fields.append(jnp.zeros((-used % 16, slots), F32))
    fields = jnp.concatenate(fields, axis=0)
    height = fields.shape[0]
    for part in range(slots // extent):
        at = pl.ds(rows + part * height, height)
        out_ref[at, :] = fields[:, part * extent:(part + 1) * extent].astype(BF16)


def per_slot(live_ref, slots, capacity):
    targets = live_ref.shape[1]
    slot = lax.broadcasted_iota(I32, (targets, slots), 1)
    owner = lax.broadcasted_iota(I32, (targets, slots), 0)
    expand = (lax.div(slot, capacity) == owner).astype(F32)
    return jnp.dot(live_ref[...].astype(F32), expand, precision=HIGHEST, preferred_element_type=F32)


def setup_kernel(members, stride, sizes, tiles, me_ref, payload_ref,
                 list_ref, row_ref, fi_ref, f0_ref, f1_ref, f2_ref, bi_ref, b0_ref, b1_ref):
    capacity, depth, frames = sizes
    group = capacity * depth
    dead = members * group
    ray_tiles, extent = row_ref.shape
    height = -(-(7 * depth + 2) // 16) * 16
    tables = (fi_ref, f0_ref, f1_ref, f2_ref, bi_ref, b0_ref, b1_ref)
    lanes = list_ref.shape[1]
    first_slot = me_ref[0] * capacity
    part = lax.div(first_slot, extent)
    shift = lax.rem(extent - lax.rem(first_slot, extent), extent)

    def build(member, carry):
        total, lined = carry
        at = member * stride + tiles * frames + part * height
        raw = payload_ref[pl.ds(pl.multiple_of(at, 16), height), :].astype(F32)
        offset = (raw[0:depth] + raw[depth:2 * depth]) + raw[2 * depth:3 * depth]
        slope = (raw[3 * depth:4 * depth] + raw[4 * depth:5 * depth]) + raw[5 * depth:6 * depth]
        rest = raw[6 * depth:7 * depth + 2]
        fields = jnp.concatenate(
            [offset, slope, rest, jnp.zeros((16 - 3 * depth - 2, extent), F32)], axis=0)
        fields = pltpu.roll(fields, shift, axis=1)
        columns = fields.T
        summed = None
        for level in range(depth):
            offset = columns[0:capacity, level:level + 1]
            slope = columns[0:capacity, depth + level:depth + level + 1]
            middle, weights = row_taps(offset, slope, extent)
            first, pair = column_taps(offset, slope, extent)
            wide = [weight.astype(F32) for weight in weights]
            values = [middle] + wide + [first] + [weight.astype(F32) for weight in pair]
            at = member * group
            if not isinstance(at, int):
                at = pl.multiple_of(at, 8)
            at = pl.ds(at + level * capacity, capacity)
            for ref, value in zip(tables, values):
                ref[at, :] = value
            parts = (wide[0] + wide[1]) + wide[2]
            summed = parts if summed is None else summed + parts
        row = 3 * depth
        tile_of = jnp.broadcast_to(fields[row:row + 1, 0:capacity], (ray_tiles, capacity))
        count = jnp.broadcast_to(fields[row + 1:row + 2, 0:capacity], (ray_tiles, capacity))
        tile = lax.broadcasted_iota(I32, (ray_tiles, capacity), 0).astype(F32)
        within = lax.broadcasted_iota(I32, (ray_tiles, capacity), 1).astype(F32)
        hot = jnp.logical_and(tile_of == tile, within < count).astype(F32)
        total = total + jnp.dot(hot, summed, precision=HIGHEST, preferred_element_type=F32)
        lane = lax.broadcasted_iota(I32, fields.shape, 1)
        own = jnp.where(lane < capacity, fields, 0.0)
        if lanes > extent:
            own = jnp.concatenate(
                [own, jnp.zeros((fields.shape[0], lanes - extent), F32)], axis=1)
        return total, lined + pltpu.roll(own, member * capacity, axis=1)

    carry = jnp.zeros((ray_tiles, extent), F32), jnp.zeros((16, lanes), F32)
    if members <= 16:
        for member in range(members):
            carry = build(member, carry)
    else:
        carry = lax.fori_loop(0, members, build, carry)
    row_ref[...], lined = carry
    for ref in tables:
        ref[dead:, :] = jnp.zeros((group, extent), ref.dtype)

    slot = lax.broadcasted_iota(I32, (1, lanes), 1)
    member = lax.div(slot, capacity)
    within = lax.rem(slot, capacity)
    line = (member * group + within - dead).astype(F32)
    row = 2 * depth
    base = member.astype(F32) * tiles
    voxels = [(lined[row + level:row + level + 1] + base) * frames for level in range(depth)]
    ray = lined[3 * depth:3 * depth + 1] * frames
    table = jnp.concatenate([line, ray] + voxels + [jnp.zeros((6 - depth, lanes), F32)], axis=0)
    alive = jnp.logical_and(
        within.astype(F32) < lined[3 * depth + 1:3 * depth + 2], member < members).astype(F32)
    order = lax.broadcasted_iota(I32, (lanes, lanes), 0)
    earlier = (lax.broadcasted_iota(I32, (lanes, lanes), 1) < order).astype(F32)
    position = contract_lanes(jnp.broadcast_to(alive, (8, lanes)), earlier)[0:1]
    position = jnp.where(alive > 0.0, position, -1.0).astype(I32)
    choose = jnp.broadcast_to(position, (lanes, lanes)) == order
    packed = contract_lanes(table, choose.astype(F32))
    kind = lax.broadcasted_iota(I32, (8, lanes), 0)
    total = jnp.sum(alive, axis=1, keepdims=True)
    extra = jnp.where(kind == 0, float(dead), jnp.where(kind == 7, total, 0.0))
    list_ref[...] = (packed + extra + 0.5).astype(I32)


def column_kernel(sizes, offset_ref, slope_ref, voxel_ref, live_ref, out_ref):
    capacity, depth, frames = sizes
    tiles = out_ref.shape[0] // frames
    slots = offset_ref.shape[1]
    extent = out_ref.shape[1]
    offsets = offset_ref[...].T
    slopes = slope_ref[...].T
    within = lax.rem(lax.broadcasted_iota(I32, (1, slots), 1), capacity).astype(F32)
    alive = jnp.broadcast_to(within, (tiles, slots)) < per_slot(live_ref, slots, capacity)
    total = jnp.zeros((tiles, extent), F32)
    for level in range(depth):
        unused, pair = column_taps(
            offsets[:, level:level + 1], slopes[:, level:level + 1], extent)
        tile_of = jnp.broadcast_to(voxel_ref[level:level + 1, :], (tiles, slots))
        match = tile_of == lax.broadcasted_iota(I32, (tiles, slots), 0)
        hot = jnp.logical_and(match, alive).astype(F32).astype(BF16)
        for weight in pair:
            total += jnp.dot(hot, weight, preferred_element_type=F32)
    out_ref[...] = repeat_rows(1.0 / jnp.maximum(total, 1.0), frames)


def pick(values, index):
    return jnp.take_along_axis(values, index, axis=1, mode="promise_in_bounds")


def spread(ref, row, frames):
    return jnp.broadcast_to(ref[pl.ds(row, 1), :], (frames, ref.shape[1]))


def tile_at(start, frames):
    return pl.ds(pl.multiple_of(start, frames), frames)


def for_slots(list_ref, body):
    def some(step, carry):
        for place in range(CHUNK):
            body(step * CHUNK + place)
        return carry

    lax.fori_loop(0, lax.div(list_ref[7, 0] + (CHUNK - 1), CHUNK), some, 0)


def for_rows(rows, body):
    step = 128

    def some(number, carry):
        body(pl.ds(pl.multiple_of(number * step, step), step))
        return carry

    lax.fori_loop(0, rows // step, some, 0)


def project(sizes, stride, list_ref, values_ref, tables, projection, wides):
    capacity, depth, frames = sizes
    members = values_ref.shape[0] // stride
    rows = wides[0].shape[0] // members
    extent = values_ref.shape[1]

    def widen(member, carry):
        values = values_ref[pl.ds(pl.multiple_of(member * stride, 16), rows), :].astype(F32)
        at = pl.ds(pl.multiple_of(member * rows, rows), rows)
        wides[0][at, :] = values
        if len(wides) == 3:
            wides[1][at, :] = pltpu.roll(values, 1, axis=1)
            wides[2][at, :] = pltpu.roll(values, extent - 1, axis=1)
        return carry

    lax.fori_loop(0, members, widen, 0)

    def one(slot):
        line = list_ref[0, slot]
        total = None
        for level in range(depth):
            at = tile_at(list_ref[2 + level, slot], frames)
            row = line + level * capacity
            index = spread(tables[0], row, frames)
            if len(wides) == 3:
                taps = [pick(ref[at, :], index) for ref in (wides[1], wides[0], wides[2])]
            else:
                values = wides[0][at, :]
                taps = [pick(values, index + shift) for shift in (-1, 0, 1)]
            for ref, tap in zip(tables[1:], taps):
                term = spread(ref, row, frames) * tap
                total = term if total is None else total + term
        projection[tile_at(list_ref[1, slot], frames), :] += total.astype(BF16).astype(F32)

    for_slots(list_ref, one)


def backproject(sizes, list_ref, residual, tables, banks):
    capacity, depth, frames = sizes

    def clear(at):
        for bank in banks:
            bank[at, :] = jnp.zeros((at.size, bank.shape[1]), F32)

    for_rows(banks[0].shape[0], clear)

    def one(slot):
        line = list_ref[0, slot]
        values = residual[tile_at(list_ref[1, slot], frames), :]
        for level in range(depth):
            row = line + level * capacity
            index = spread(tables[0], row, frames)
            term = (spread(tables[1], row, frames) * pick(values, index)
                    + spread(tables[2], row, frames) * pick(values, index + 1))
            banks[level % len(banks)][tile_at(list_ref[2 + level, slot], frames), :] += term

    for_slots(list_ref, one)


def forward_kernel(sizes, stride, first, list_ref, values_ref, *refs):
    tables, refs = refs[:4], refs[4:]
    if not first:
        start_ref, refs = refs[0], refs[1:]
    projection, wides = refs[0], refs[1:]
    projection[...] = jnp.zeros_like(projection) if first else start_ref[...]
    project(sizes, stride, list_ref, values_ref, tables, projection, wides)


def residual_of(sizes, projection, sinogram_ref, row_refs):
    total = sum([ref[...] for ref in row_refs[1:]], row_refs[0][...])
    weight = repeat_rows(1.0 / jnp.maximum(total, 1.0), sizes[2])
    scaled = (sinogram_ref[...].astype(F32) - projection[...]) * weight
    return scaled.astype(BF16).astype(F32)


def turn_kernel(sizes, stride, n_rows, n_wide, first, list_ref, values_ref, *refs):
    forward, backward, refs = refs[:4], refs[4:7], refs[7:]
    sinogram_ref, row_refs, refs = refs[0], refs[1:1 + n_rows], refs[1 + n_rows:]
    if not first:
        start_ref, refs = refs[0], refs[1:]
    out_ref, residual, projection = refs[:3]
    wides, banks = refs[3:3 + n_wide], refs[3 + n_wide:]
    projection[...] = jnp.zeros_like(projection) if first else start_ref[...]
    project(sizes, stride, list_ref, values_ref, forward, projection, wides)
    residual[...] = residual_of(sizes, projection, sinogram_ref, row_refs)
    backproject(sizes, list_ref, residual, backward, banks)

    def finish(at):
        out_ref[at, :] = sum([bank[at, :] for bank in banks[1:]], banks[0][at, :]).astype(BF16)

    for_rows(out_ref.shape[0], finish)


def backward_kernel(sizes, list_ref, residual, *refs):
    tables, out_ref, banks = refs[:3], refs[3], refs[4:]
    backproject(sizes, list_ref, residual, tables, (out_ref,) + banks)

    def finish(at):
        out_ref[at, :] = sum([bank[at, :] for bank in banks], out_ref[at, :])

    if banks:
        for_rows(out_ref.shape[0], finish)


def combine_y_kernel(sum_ref, core_ref, out_ref):
    rows = sum_ref.shape[0]
    out_ref[...] = (sum_ref[...] + core_ref[rows:2 * rows, :].astype(F32)).astype(BF16)


def combine_z_kernel(sum_ref, core_ref, y_ref, own_ref, *piece_refs):
    rows = own_ref.shape[0]
    for place, ref in enumerate((own_ref,) + piece_refs):
        at = pl.ds(place * rows, rows)
        total = sum_ref[at, :] + core_ref[at, :].astype(F32) + y_ref[at, :].astype(F32)
        ref[...] = total.astype(ref.dtype)


def update_kernel(n_pieces, volume_ref, column_ref, *refs):
    back = refs[0][...]
    for ref in refs[1:n_pieces]:
        back = back + ref[...].astype(F32)
    volume = volume_ref[...] + column_ref[...] * back
    for ref in refs[n_pieces:]:
        ref[...] = volume.astype(ref.dtype)


def call(kernel, name, mib, in_specs, out_shape, *operands, scratch=()):
    one = not isinstance(out_shape, list)
    return pl.pallas_call(
        kernel,
        out_shape=out_shape,
        in_specs=in_specs,
        out_specs=VMEM if one else [VMEM] * len(out_shape),
        scratch_shapes=list(scratch),
        compiler_params=pltpu.CompilerParams(vmem_limit_bytes=mib * 1024 * 1024),
        name=name,
    )(*operands)


def exchange(values, n_slab, distance):
    return lax.ppermute(
        values, "slab", [(device, device ^ distance) for device in range(n_slab)])


def shards(sinogram, start_volume, slot_voxel, slot_ray, live_count, block_slope, block_offset):
    n_slab = lax.axis_size("slab")
    n_slots, depth = slot_voxel.shape
    capacity = n_slots // n_slab
    ray_tiles, frames, extent = sinogram.shape
    voxel_tiles = start_volume.shape[0]
    rows = voxel_tiles * frames
    sizes = (capacity, depth, frames)
    paired = n_slab == 16
    n_wide, n_bank = (3, 2) if paired else (1, 1)
    shape = jax.ShapeDtypeStruct
    rays = shape((ray_tiles * frames, extent), F32)
    volume = start_volume.reshape(rows, extent)
    sino = sinogram.reshape(rays.shape)
    me = lax.axis_index("slab").astype(I32).reshape(1)
    slots_by_depth = (block_offset.T, block_slope.T, slot_voxel.T)
    live = live_count.reshape(1, n_slab)
    height = -(-(7 * depth + 2) // 16) * 16 * (n_slots // extent)
    payload = call(
        functools.partial(pack_kernel, capacity), "pack", 16, [VMEM] * 6,
        shape((rows + height, extent), BF16),
        volume, *slots_by_depth, slot_ray.reshape(1, n_slots), live)

    def setup(values, members):
        group = capacity * depth
        lines = (members + 1) * group
        lanes = -(-members * capacity // 128) * 128
        table = [shape((lines, extent), I32)] + [shape((lines, extent), F32)] * 3
        table += [shape((lines, extent), I32)] + [shape((lines, extent), F32)] * 2
        out = [shape((8, lanes), I32), shape((ray_tiles, extent), F32)] + table
        stride = values.shape[0] // members
        found = call(
            functools.partial(setup_kernel, members, stride, sizes, voxel_tiles), "setup", 24,
            [SMEM, VMEM], out, me, values)
        return found[0], found[1], found[2:6], found[6:9]

    def wide(members):
        return pltpu.VMEM((members * rows, extent), F32)

    def forward(values, group, start, members):
        operands = [values, *group[2]] + ([] if start is None else [start])
        return call(
            functools.partial(forward_kernel, sizes, values.shape[0] // members, start is None),
            "forward", 16, [SMEM] + [VMEM] * len(operands), rays,
            group[0], *operands, scratch=[wide(members)] * n_wide)

    def turn(values, group, row_sums, start, members):
        operands = [values, *group[2], *group[3], sino, *row_sums] + ([] if start is None else [start])
        return call(
            functools.partial(turn_kernel, sizes, values.shape[0] // members, len(row_sums), n_wide,
                              start is None),
            "turn", 24 if paired else 40, [SMEM] + [VMEM] * len(operands),
            [shape((members * rows, extent), BF16), rays],
            group[0], *operands,
            scratch=[pltpu.VMEM(rays.shape, F32)] + [wide(members)] * (n_wide + n_bank))

    def backward(residual, group, members):
        return call(
            functools.partial(backward_kernel, sizes), "backward", 16, [SMEM] + [VMEM] * 4,
            shape((members * rows, extent), F32), group[0], residual, *group[3],
            scratch=[wide(members)] * (n_bank - 1))

    def update(volume, pieces, last):
        out = [shape((rows, extent), F32)] + ([] if last else [shape((rows, extent), BF16)])
        return call(
            functools.partial(update_kernel, len(pieces)), "update", 16,
            [VMEM] * (2 + len(pieces)), out, volume, column_weight, *pieces)

    column_weight = call(
        functools.partial(column_kernel, sizes), "column_weight", 16, [VMEM] * 4,
        shape((rows, extent), F32), *slots_by_depth, live)

    groups = None
    for sweep in range(ITERS):
        last = sweep + 1 == ITERS
        if paired:
            along_z = jnp.concatenate(
                [payload] + [exchange(payload, n_slab, distance) for distance in (4, 8, 12)], axis=0)
            along_y = exchange(along_z, n_slab, 2)
            other = exchange(jnp.concatenate([along_z, along_y], axis=0), n_slab, 1)
            if groups is None:
                groups = [setup(along_z, 4), setup(along_y, 4), setup(other, 8)]
                row_sums = [group[1] for group in groups]
            projection = forward(along_z, groups[0], None, 4)
            projection = forward(along_y, groups[1], projection, 4)
            other_sum, residual = turn(other, groups[2], row_sums, projection, 8)
            core_part = exchange(other_sum, n_slab, 1)
            y_sum = backward(residual, groups[1], 4)
            y_part = exchange(
                call(combine_y_kernel, "combine_y", 16, [VMEM] * 2,
                     shape((4 * rows, extent), BF16), y_sum, core_part), n_slab, 2)
            z_sum = backward(residual, groups[0], 4)
            own, *pieces = call(
                combine_z_kernel, "combine_z", 16, [VMEM] * 3,
                [shape((rows, extent), F32)] + [shape((rows, extent), BF16)] * 3,
                z_sum, core_part, y_part)
            pieces = [own] + [
                exchange(piece, n_slab, distance) for piece, distance in zip(pieces, (4, 8, 12))]
        else:
            everyone = lax.all_gather(payload, "slab", axis=0, tiled=True)
            if groups is None:
                groups = [setup(everyone, n_slab)]
                row_sums = [groups[0][1]]
            sums, residual = turn(everyone, groups[0], row_sums, None, n_slab)
            parts = lax.all_to_all(
                sums.reshape(n_slab, rows, extent), "slab", split_axis=0, concat_axis=0, tiled=True)
            pieces = [jnp.sum(parts.astype(F32), axis=0)]
        volume, *rounded = update(volume, pieces, last)
        if not last:
            payload = rounded[0]
    return volume.reshape(start_volume.shape)


def solution(mesh):
    in_specs = (
        P(("scan", "slab"), None, None),
        P(("scan", "slab"), None, None),
        P(("scan", "slab"), None),
        P(("scan", "slab")),
        P(("scan", "slab")),
        P(("scan", "slab"), None),
        P(("scan", "slab"), None),
    )
    out_specs = P(("scan", "slab"), None, None)
    return jax.shard_map(shards, mesh=mesh, in_specs=in_specs, out_specs=out_specs, check_vma=False)
```

```python
import functools

import jax
import jax.numpy as jnp
from jax import lax
from jax.experimental import pallas as pl
from jax.experimental.pallas import tpu as pltpu
from jax.sharding import PartitionSpec as P

ITERS = 2
FAR = 1.0e6
CHUNK = 8
F32 = jnp.float32
BF16 = jnp.bfloat16
I32 = jnp.int32
HIGHEST = lax.Precision.HIGHEST
VMEM = pl.BlockSpec(memory_space=pltpu.VMEM)
SMEM = pl.BlockSpec(memory_space=pltpu.SMEM)
ANY = pl.BlockSpec(memory_space=pl.ANY)


def hat(ray, centre):
    return jnp.maximum(0.0, 1.0 - jnp.abs(ray - centre)).astype(BF16)


def row_taps(offset, slope, extent):
    shape = (offset.shape[0], extent)
    ray = lax.broadcasted_iota(I32, shape, 1).astype(F32)
    offset = jnp.broadcast_to(offset, shape)
    slope = jnp.broadcast_to(slope, shape)
    middle = jnp.floor((ray - offset) / slope + 0.5)
    middle = jnp.minimum(jnp.maximum(middle, 1.0), extent - 2.0)
    weights = [hat(ray, offset + slope * (middle + step)) for step in (-1.0, 0.0, 1.0)]
    return middle.astype(I32), weights


def column_taps(offset, slope, extent):
    shape = (offset.shape[0], extent)
    voxel = lax.broadcasted_iota(I32, shape, 1).astype(F32)
    centre = jnp.broadcast_to(offset, shape) + jnp.broadcast_to(slope, shape) * voxel
    first = jnp.minimum(jnp.maximum(jnp.floor(centre), 0.0), extent - 2.0)
    weights = [hat(first + step, centre) for step in (0.0, 1.0)]
    return first.astype(I32), weights


def repeat_rows(values, times):
    return jnp.concatenate(
        [jnp.broadcast_to(values[row:row + 1, :], (times, values.shape[1]))
         for row in range(values.shape[0])], axis=0)


def contract_lanes(left, right):
    return lax.dot_general(
        left, right, (((1,), (1,)), ((), ())), precision=HIGHEST, preferred_element_type=F32)


def pack_kernel(capacity, *refs):
    sources, out_ref, loaded, arrived = refs[:6], refs[6], refs[7:13], refs[13]
    copies = [
        pltpu.make_async_copy(source, ref, arrived.at[place])
        for place, (source, ref) in enumerate(zip(sources, loaded))]
    for copy in copies:
        copy.start()
    for copy in copies:
        copy.wait()
    volume_ref, offset_ref, slope_ref, voxel_ref, ray_ref, live_ref = loaded
    rows, extent = volume_ref.shape
    out_ref[0:rows, :] = volume_ref[...].astype(BF16)
    slots = ray_ref.shape[1]
    fields = []
    for ref in (offset_ref, slope_ref):
        left = ref[...]
        for addend in range(3):
            part = left.astype(BF16).astype(F32)
            fields.append(part)
            left = left - part
    fields.append(voxel_ref[...].astype(F32))
    fields.append(ray_ref[...].astype(F32))
    fields.append(per_slot(live_ref, slots, capacity))
    used = sum(field.shape[0] for field in fields)
    fields.append(jnp.zeros((-used % 16, slots), F32))
    fields = jnp.concatenate(fields, axis=0)
    height = fields.shape[0]
    for part in range(slots // extent):
        at = pl.ds(rows + part * height, height)
        out_ref[at, :] = fields[:, part * extent:(part + 1) * extent].astype(BF16)


def per_slot(live_ref, slots, capacity):
    targets = live_ref.shape[1]
    slot = lax.broadcasted_iota(I32, (targets, slots), 1)
    owner = lax.broadcasted_iota(I32, (targets, slots), 0)
    expand = (lax.div(slot, capacity) == owner).astype(F32)
    return jnp.dot(live_ref[...].astype(F32), expand, precision=HIGHEST, preferred_element_type=F32)


def setup_kernel(members, stride, sizes, tiles, me_ref, payload_ref,
                 list_ref, row_ref, fi_ref, f0_ref, f1_ref, f2_ref, bi_ref, b0_ref, b1_ref):
    capacity, depth, frames = sizes
    group = capacity * depth
    dead = members * group
    ray_tiles, extent = row_ref.shape
    height = -(-(7 * depth + 2) // 16) * 16
    tables = (fi_ref, f0_ref, f1_ref, f2_ref, bi_ref, b0_ref, b1_ref)
    lanes = list_ref.shape[1]
    first_slot = me_ref[0] * capacity
    part = lax.div(first_slot, extent)
    shift = lax.rem(extent - lax.rem(first_slot, extent), extent)

    def build(member, carry):
        total, lined = carry
        at = member * stride + tiles * frames + part * height
        raw = payload_ref[pl.ds(pl.multiple_of(at, 16), height), :].astype(F32)
        offset = (raw[0:depth] + raw[depth:2 * depth]) + raw[2 * depth:3 * depth]
        slope = (raw[3 * depth:4 * depth] + raw[4 * depth:5 * depth]) + raw[5 * depth:6 * depth]
        rest = raw[6 * depth:7 * depth + 2]
        fields = jnp.concatenate(
            [offset, slope, rest, jnp.zeros((16 - 3 * depth - 2, extent), F32)], axis=0)
        fields = pltpu.roll(fields, shift, axis=1)
        columns = fields.T
        summed = None
        for level in range(depth):
            offset = columns[0:capacity, level:level + 1]
            slope = columns[0:capacity, depth + level:depth + level + 1]
            middle, weights = row_taps(offset, slope, extent)
            first, pair = column_taps(offset, slope, extent)
            wide = [weight.astype(F32) for weight in weights]
            values = [middle] + wide + [first] + [weight.astype(F32) for weight in pair]
            at = member * group
            if not isinstance(at, int):
                at = pl.multiple_of(at, 8)
            at = pl.ds(at + level * capacity, capacity)
            for ref, value in zip(tables, values):
                ref[at, :] = value
            parts = (wide[0] + wide[1]) + wide[2]
            summed = parts if summed is None else summed + parts
        row = 3 * depth
        tile_of = jnp.broadcast_to(fields[row:row + 1, 0:capacity], (ray_tiles, capacity))
        count = jnp.broadcast_to(fields[row + 1:row + 2, 0:capacity], (ray_tiles, capacity))
        tile = lax.broadcasted_iota(I32, (ray_tiles, capacity), 0).astype(F32)
        within = lax.broadcasted_iota(I32, (ray_tiles, capacity), 1).astype(F32)
        hot = jnp.logical_and(tile_of == tile, within < count).astype(F32)
        total = total + jnp.dot(hot, summed, precision=HIGHEST, preferred_element_type=F32)
        lane = lax.broadcasted_iota(I32, fields.shape, 1)
        own = jnp.where(lane < capacity, fields, 0.0)
        if lanes > extent:
            own = jnp.concatenate(
                [own, jnp.zeros((fields.shape[0], lanes - extent), F32)], axis=1)
        return total, lined + pltpu.roll(own, member * capacity, axis=1)

    carry = jnp.zeros((ray_tiles, extent), F32), jnp.zeros((16, lanes), F32)
    if members <= 16:
        for member in range(members):
            carry = build(member, carry)
    else:
        carry = lax.fori_loop(0, members, build, carry)
    row_ref[...], lined = carry
    for ref in tables:
        ref[dead:, :] = jnp.zeros((group, extent), ref.dtype)

    slot = lax.broadcasted_iota(I32, (1, lanes), 1)
    member = lax.div(slot, capacity)
    within = lax.rem(slot, capacity)
    line = (member * group + within - dead).astype(F32)
    row = 2 * depth
    base = member.astype(F32) * tiles
    voxels = [(lined[row + level:row + level + 1] + base) * frames for level in range(depth)]
    ray = lined[3 * depth:3 * depth + 1] * frames
    table = jnp.concatenate([line, ray] + voxels + [jnp.zeros((6 - depth, lanes), F32)], axis=0)
    alive = jnp.logical_and(
        within.astype(F32) < lined[3 * depth + 1:3 * depth + 2], member < members).astype(F32)
    order = lax.broadcasted_iota(I32, (lanes, lanes), 0)
    earlier = (lax.broadcasted_iota(I32, (lanes, lanes), 1) < order).astype(F32)
    position = contract_lanes(jnp.broadcast_to(alive, (8, lanes)), earlier)[0:1]
    position = jnp.where(alive > 0.0, position, -1.0).astype(I32)
    choose = jnp.broadcast_to(position, (lanes, lanes)) == order
    packed = contract_lanes(table, choose.astype(F32))
    kind = lax.broadcasted_iota(I32, (8, lanes), 0)
    total = jnp.sum(alive, axis=1, keepdims=True)
    extra = jnp.where(kind == 0, float(dead), jnp.where(kind == 7, total, 0.0))
    list_ref[...] = (packed + extra + 0.5).astype(I32)


def column_kernel(sizes, offset_ref, slope_ref, voxel_ref, live_ref, out_ref):
    capacity, depth, frames = sizes
    tiles = out_ref.shape[0] // frames
    slots = offset_ref.shape[1]
    extent = out_ref.shape[1]
    offsets = offset_ref[...].T
    slopes = slope_ref[...].T
    within = lax.rem(lax.broadcasted_iota(I32, (1, slots), 1), capacity).astype(F32)
    alive = jnp.broadcast_to(within, (tiles, slots)) < per_slot(live_ref, slots, capacity)
    total = jnp.zeros((tiles, extent), F32)
    for level in range(depth):
        unused, pair = column_taps(
            offsets[:, level:level + 1], slopes[:, level:level + 1], extent)
        tile_of = jnp.broadcast_to(voxel_ref[level:level + 1, :], (tiles, slots))
        match = tile_of == lax.broadcasted_iota(I32, (tiles, slots), 0)
        hot = jnp.logical_and(match, alive).astype(F32).astype(BF16)
        for weight in pair:
            total += jnp.dot(hot, weight, preferred_element_type=F32)
    out_ref[...] = repeat_rows(1.0 / jnp.maximum(total, 1.0), frames)


def pick(values, index):
    return jnp.take_along_axis(values, index, axis=1, mode="promise_in_bounds")


def spread(ref, row, frames):
    return jnp.broadcast_to(ref[pl.ds(row, 1), :], (frames, ref.shape[1]))


def tile_at(start, frames):
    return pl.ds(pl.multiple_of(start, frames), frames)


def for_slots(list_ref, body):
    def some(step, carry):
        for place in range(CHUNK):
            body(step * CHUNK + place)
        return carry

    lax.fori_loop(0, lax.div(list_ref[7, 0] + (CHUNK - 1), CHUNK), some, 0)


def for_rows(rows, body):
    step = 128

    def some(number, carry):
        body(pl.ds(pl.multiple_of(number * step, step), step))
        return carry

    lax.fori_loop(0, rows // step, some, 0)


def project(sizes, stride, list_ref, values_ref, tables, projection, wides):
    capacity, depth, frames = sizes
    members = values_ref.shape[0] // stride
    rows = wides[0].shape[0] // members
    extent = values_ref.shape[1]

    def widen(member, carry):
        values = values_ref[pl.ds(pl.multiple_of(member * stride, 16), rows), :].astype(F32)
        at = pl.ds(pl.multiple_of(member * rows, rows), rows)
        wides[0][at, :] = values
        if len(wides) == 3:
            wides[1][at, :] = pltpu.roll(values, 1, axis=1)
            wides[2][at, :] = pltpu.roll(values, extent - 1, axis=1)
        return carry

    lax.fori_loop(0, members, widen, 0)

    def one(slot):
        line = list_ref[0, slot]
        total = None
        for level in range(depth):
            at = tile_at(list_ref[2 + level, slot], frames)
            row = line + level * capacity
            index = spread(tables[0], row, frames)
            if len(wides) == 3:
                taps = [pick(ref[at, :], index) for ref in (wides[1], wides[0], wides[2])]
            else:
                values = wides[0][at, :]
                taps = [pick(values, index + shift) for shift in (-1, 0, 1)]
            for ref, tap in zip(tables[1:], taps):
                term = spread(ref, row, frames) * tap
                total = term if total is None else total + term
        projection[tile_at(list_ref[1, slot], frames), :] += total.astype(BF16).astype(F32)

    for_slots(list_ref, one)


def backproject(sizes, list_ref, residual, tables, banks):
    capacity, depth, frames = sizes

    def clear(at):
        for bank in banks:
            bank[at, :] = jnp.zeros((at.size, bank.shape[1]), F32)

    for_rows(banks[0].shape[0], clear)

    def one(slot):
        line = list_ref[0, slot]
        values = residual[tile_at(list_ref[1, slot], frames), :]
        for level in range(depth):
            row = line + level * capacity
            index = spread(tables[0], row, frames)
            term = (spread(tables[1], row, frames) * pick(values, index)
                    + spread(tables[2], row, frames) * pick(values, index + 1))
            banks[level % len(banks)][tile_at(list_ref[2 + level, slot], frames), :] += term

    for_slots(list_ref, one)


def forward_kernel(sizes, stride, first, list_ref, values_ref, *refs):
    tables, refs = refs[:4], refs[4:]
    if not first:
        start_ref, refs = refs[0], refs[1:]
    projection, wides = refs[0], refs[1:]
    projection[...] = jnp.zeros_like(projection) if first else start_ref[...]
    project(sizes, stride, list_ref, values_ref, tables, projection, wides)


def residual_of(sizes, projection, sinogram_ref, row_refs):
    total = sum([ref[...] for ref in row_refs[1:]], row_refs[0][...])
    weight = repeat_rows(1.0 / jnp.maximum(total, 1.0), sizes[2])
    scaled = (sinogram_ref[...].astype(F32) - projection[...]) * weight
    return scaled.astype(BF16).astype(F32)


def turn_kernel(sizes, stride, n_rows, n_wide, first, list_ref, values_ref, *refs):
    forward, backward, refs = refs[:4], refs[4:7], refs[7:]
    sinogram_ref, row_refs, refs = refs[0], refs[1:1 + n_rows], refs[1 + n_rows:]
    if not first:
        start_ref, refs = refs[0], refs[1:]
    out_ref, residual, projection = refs[:3]
    wides, banks = refs[3:3 + n_wide], refs[3 + n_wide:]
    projection[...] = jnp.zeros_like(projection) if first else start_ref[...]
    project(sizes, stride, list_ref, values_ref, forward, projection, wides)
    residual[...] = residual_of(sizes, projection, sinogram_ref, row_refs)
    backproject(sizes, list_ref, residual, backward, banks)

    def finish(at):
        out_ref[at, :] = sum([bank[at, :] for bank in banks[1:]], banks[0][at, :]).astype(BF16)

    for_rows(out_ref.shape[0], finish)


def backward_kernel(sizes, list_ref, residual, *refs):
    tables, out_ref, banks = refs[:3], refs[3], refs[4:]
    backproject(sizes, list_ref, residual, tables, (out_ref,) + banks)

    def finish(at):
        out_ref[at, :] = sum([bank[at, :] for bank in banks], out_ref[at, :])

    if banks:
        for_rows(out_ref.shape[0], finish)


def combine_y_kernel(sum_ref, core_ref, out_ref):
    rows = sum_ref.shape[0]
    out_ref[...] = (sum_ref[...] + core_ref[rows:2 * rows, :].astype(F32)).astype(BF16)


def combine_z_kernel(sum_ref, core_ref, y_ref, out_ref):
    def add(at):
        out_ref[at, :] = sum_ref[at, :] + core_ref[at, :].astype(F32) + y_ref[at, :].astype(F32)

    for_rows(out_ref.shape[0], add)


def join_kernel(z_ref, y_ref, after_ref, out_ref):
    del after_ref
    rows = z_ref.shape[0]
    out_ref[0:rows, :] = z_ref[...]
    out_ref[rows:2 * rows, :] = y_ref[...]


def update_kernel(n_pieces, volume_ref, column_ref, *refs):
    back = refs[0][...]
    for ref in refs[1:n_pieces]:
        back = back + ref[...].astype(F32)
    volume = volume_ref[...] + column_ref[...] * back
    for ref in refs[n_pieces:]:
        ref[...] = volume.astype(ref.dtype)


def call(kernel, name, mib, in_specs, out_shape, *operands, scratch=()):
    one = not isinstance(out_shape, list)
    return pl.pallas_call(
        kernel,
        out_shape=out_shape,
        in_specs=in_specs,
        out_specs=VMEM if one else [VMEM] * len(out_shape),
        scratch_shapes=list(scratch),
        compiler_params=pltpu.CompilerParams(vmem_limit_bytes=mib * 1024 * 1024),
        name=name,
    )(*operands)


def exchange(values, n_slab, distance):
    return lax.ppermute(
        values, "slab", [(device, device ^ distance) for device in range(n_slab)])


def shards(sinogram, start_volume, slot_voxel, slot_ray, live_count, block_slope, block_offset):
    n_slab = lax.axis_size("slab")
    n_slots, depth = slot_voxel.shape
    capacity = n_slots // n_slab
    ray_tiles, frames, extent = sinogram.shape
    voxel_tiles = start_volume.shape[0]
    rows = voxel_tiles * frames
    sizes = (capacity, depth, frames)
    paired = n_slab == 16
    n_wide, n_bank = (3, 2) if paired else (1, 1)
    shape = jax.ShapeDtypeStruct
    rays = shape((ray_tiles * frames, extent), F32)
    volume = start_volume.reshape(rows, extent)
    sino = sinogram.reshape(rays.shape)
    me = lax.axis_index("slab").astype(I32).reshape(1)
    slots_by_depth = (block_offset.T, block_slope.T, slot_voxel.T)
    live = live_count.reshape(1, n_slab)
    height = -(-(7 * depth + 2) // 16) * 16 * (n_slots // extent)
    operands = (volume, *slots_by_depth, slot_ray.reshape(1, n_slots), live)
    payload = call(
        functools.partial(pack_kernel, capacity), "pack", 16, [ANY] * 6,
        shape((rows + height, extent), BF16), *operands,
        scratch=[pltpu.VMEM(operand.shape, operand.dtype) for operand in operands]
        + [pltpu.SemaphoreType.DMA((6,))])

    def setup(values, members):
        group = capacity * depth
        lines = (members + 1) * group
        lanes = -(-members * capacity // 128) * 128
        table = [shape((lines, extent), I32)] + [shape((lines, extent), F32)] * 3
        table += [shape((lines, extent), I32)] + [shape((lines, extent), F32)] * 2
        out = [shape((8, lanes), I32), shape((ray_tiles, extent), F32)] + table
        stride = values.shape[0] // members
        found = call(
            functools.partial(setup_kernel, members, stride, sizes, voxel_tiles), "setup", 24,
            [SMEM, VMEM], out, me, values)
        return found[0], found[1], found[2:6], found[6:9]

    def wide(members):
        return pltpu.VMEM((members * rows, extent), F32)

    def forward(values, group, start, members):
        operands = [values, *group[2]] + ([] if start is None else [start])
        return call(
            functools.partial(forward_kernel, sizes, values.shape[0] // members, start is None),
            "forward", 16, [SMEM] + [VMEM] * len(operands), rays,
            group[0], *operands, scratch=[wide(members)] * n_wide)

    def turn(values, group, row_sums, start, members):
        operands = [values, *group[2], *group[3], sino, *row_sums] + ([] if start is None else [start])
        return call(
            functools.partial(turn_kernel, sizes, values.shape[0] // members, len(row_sums), n_wide,
                              start is None),
            "turn", 24 if paired else 40, [SMEM] + [VMEM] * len(operands),
            [shape((members * rows, extent), BF16), rays],
            group[0], *operands,
            scratch=[pltpu.VMEM(rays.shape, F32)] + [wide(members)] * (n_wide + n_bank))

    def backward(residual, group, members):
        return call(
            functools.partial(backward_kernel, sizes), "backward", 16, [SMEM] + [VMEM] * 4,
            shape((members * rows, extent), F32), group[0], residual, *group[3],
            scratch=[wide(members)] * (n_bank - 1))

    def update(volume, pieces, last):
        out = [shape((rows, extent), F32)] + ([] if last else [shape((rows, extent), BF16)])
        return call(
            functools.partial(update_kernel, len(pieces)), "update", 16,
            [VMEM] * (2 + len(pieces)), out, volume, column_weight, *pieces)

    column_weight = call(
        functools.partial(column_kernel, sizes), "column_weight", 16, [VMEM] * 4,
        shape((rows, extent), F32), *slots_by_depth, live)

    groups = None
    for sweep in range(ITERS):
        last = sweep + 1 == ITERS
        if paired:
            columns = [list(range(place, n_slab, 4)) for place in range(4)]
            along_z = lax.all_gather(
                payload, "slab", axis=0, axis_index_groups=columns, tiled=True)
            along_y = exchange(along_z, n_slab, 2)
            if sweep == 0:
                groups = [setup(along_z, 4)]
            projection = forward(along_z, groups[0], None, 4)
            stride = along_z.shape[0]
            other = exchange(
                call(join_kernel, "join", 16, [VMEM, VMEM, ANY],
                     shape((2 * stride, extent), BF16), along_z, along_y, projection), n_slab, 1)
            if sweep == 0:
                groups += [setup(along_y, 4), setup(other, 8)]
                row_sums = [group[1] for group in groups]
            projection = forward(along_y, groups[1], projection, 4)
            other_sum, residual = turn(other, groups[2], row_sums, projection, 8)
            core_part = exchange(other_sum, n_slab, 1)
            y_sum = backward(residual, groups[1], 4)
            y_part = exchange(
                call(combine_y_kernel, "combine_y", 16, [VMEM] * 2,
                     shape((4 * rows, extent), BF16), y_sum, core_part), n_slab, 2)
            z_sum = backward(residual, groups[0], 4)
            total = call(
                combine_z_kernel, "combine_z", 16, [VMEM] * 3, shape((4 * rows, extent), F32),
                z_sum, core_part, y_part)
            pieces = [lax.psum_scatter(
                total, "slab", scatter_dimension=0, axis_index_groups=columns, tiled=True)]
        else:
            everyone = lax.all_gather(payload, "slab", axis=0, tiled=True)
            if groups is None:
                groups = [setup(everyone, n_slab)]
                row_sums = [groups[0][1]]
            sums, residual = turn(everyone, groups[0], row_sums, None, n_slab)
            parts = lax.all_to_all(
                sums.reshape(n_slab, rows, extent), "slab", split_axis=0, concat_axis=0, tiled=True)
            pieces = [jnp.sum(parts.astype(F32), axis=0)]
        volume, *rounded = update(volume, pieces, last)
        if not last:
            payload = rounded[0]
    return volume.reshape(start_volume.shape)


def solution(mesh):
    in_specs = (
        P(("scan", "slab"), None, None),
        P(("scan", "slab"), None, None),
        P(("scan", "slab"), None),
        P(("scan", "slab")),
        P(("scan", "slab")),
        P(("scan", "slab"), None),
        P(("scan", "slab"), None),
    )
    out_specs = P(("scan", "slab"), None, None)
    return jax.shard_map(shards, mesh=mesh, in_specs=in_specs, out_specs=out_specs, check_vma=False)
```

```python
import functools

import jax
import jax.numpy as jnp
from jax import lax
from jax.experimental import pallas as pl
from jax.experimental.pallas import tpu as pltpu
from jax.sharding import PartitionSpec as P

ITERS = 2
FAR = 1.0e6
CHUNK = 8
F32 = jnp.float32
BF16 = jnp.bfloat16
I32 = jnp.int32
HIGHEST = lax.Precision.HIGHEST
VMEM = pl.BlockSpec(memory_space=pltpu.VMEM)
SMEM = pl.BlockSpec(memory_space=pltpu.SMEM)
ANY = pl.BlockSpec(memory_space=pl.ANY)


def hat(ray, centre):
    return jnp.maximum(0.0, 1.0 - jnp.abs(ray - centre)).astype(BF16)


def row_taps(offset, slope, extent):
    shape = (offset.shape[0], extent)
    ray = lax.broadcasted_iota(I32, shape, 1).astype(F32)
    offset = jnp.broadcast_to(offset, shape)
    slope = jnp.broadcast_to(slope, shape)
    middle = jnp.floor((ray - offset) / slope + 0.5)
    middle = jnp.minimum(jnp.maximum(middle, 1.0), extent - 2.0)
    weights = [hat(ray, offset + slope * (middle + step)) for step in (-1.0, 0.0, 1.0)]
    return middle, weights


def column_taps(offset, slope, extent):
    shape = (offset.shape[0], extent)
    voxel = lax.broadcasted_iota(I32, shape, 1).astype(F32)
    centre = jnp.broadcast_to(offset, shape) + jnp.broadcast_to(slope, shape) * voxel
    first = jnp.minimum(jnp.maximum(jnp.floor(centre), 0.0), extent - 2.0)
    weights = [hat(first + step, centre) for step in (0.0, 1.0)]
    return first.astype(I32), weights


def repeat_rows(values, times):
    return jnp.concatenate(
        [jnp.broadcast_to(values[row:row + 1, :], (times, values.shape[1]))
         for row in range(values.shape[0])], axis=0)


def contract_lanes(left, right):
    return lax.dot_general(
        left, right, (((1,), (1,)), ((), ())), precision=HIGHEST, preferred_element_type=F32)


def pack_kernel(capacity, *refs):
    sources, out_ref, loaded, arrived = refs[:6], refs[6], refs[7:13], refs[13]
    copies = [
        pltpu.make_async_copy(source, ref, arrived.at[place])
        for place, (source, ref) in enumerate(zip(sources, loaded))]
    for copy in copies:
        copy.start()
    for copy in copies:
        copy.wait()
    volume_ref, offset_ref, slope_ref, voxel_ref, ray_ref, live_ref = loaded
    rows, extent = volume_ref.shape
    out_ref[0:rows, :] = volume_ref[...].astype(BF16)
    slots = ray_ref.shape[1]
    fields = []
    for ref in (offset_ref, slope_ref):
        left = ref[...]
        for addend in range(3):
            part = left.astype(BF16).astype(F32)
            fields.append(part)
            left = left - part
    fields.append(voxel_ref[...].astype(F32))
    fields.append(ray_ref[...].astype(F32))
    fields.append(per_slot(live_ref, slots, capacity))
    used = sum(field.shape[0] for field in fields)
    fields.append(jnp.zeros((-used % 16, slots), F32))
    fields = jnp.concatenate(fields, axis=0)
    height = fields.shape[0]
    for part in range(slots // extent):
        at = pl.ds(rows + part * height, height)
        out_ref[at, :] = fields[:, part * extent:(part + 1) * extent].astype(BF16)


def per_slot(live_ref, slots, capacity):
    targets = live_ref.shape[1]
    slot = lax.broadcasted_iota(I32, (targets, slots), 1)
    owner = lax.broadcasted_iota(I32, (targets, slots), 0)
    expand = (lax.div(slot, capacity) == owner).astype(F32)
    return jnp.dot(live_ref[...].astype(F32), expand, precision=HIGHEST, preferred_element_type=F32)


def setup_kernel(members, stride, sizes, tiles, me_ref, payload_ref,
                 list_ref, row_ref, fi_ref, f0_ref, f1_ref, f2_ref, bi_ref, b0_ref, b1_ref):
    capacity, depth, frames = sizes
    group = capacity * depth
    dead = members * group
    ray_tiles, extent = row_ref.shape
    height = -(-(7 * depth + 2) // 16) * 16
    tables = (fi_ref, f0_ref, f1_ref, f2_ref, bi_ref, b0_ref, b1_ref)
    lanes = list_ref.shape[1]
    first_slot = me_ref[0] * capacity
    part = lax.div(first_slot, extent)
    shift = lax.rem(extent - lax.rem(first_slot, extent), extent)

    def build(member, carry):
        total, lined = carry
        at = member * stride + tiles * frames + part * height
        raw = payload_ref[pl.ds(pl.multiple_of(at, 16), height), :].astype(F32)
        offset = (raw[0:depth] + raw[depth:2 * depth]) + raw[2 * depth:3 * depth]
        slope = (raw[3 * depth:4 * depth] + raw[4 * depth:5 * depth]) + raw[5 * depth:6 * depth]
        rest = raw[6 * depth:7 * depth + 2]
        fields = jnp.concatenate(
            [offset, slope, rest, jnp.zeros((16 - 3 * depth - 2, extent), F32)], axis=0)
        fields = pltpu.roll(fields, shift, axis=1)
        columns = fields.T
        summed = None
        for level in range(depth):
            offset = columns[0:capacity, level:level + 1]
            slope = columns[0:capacity, depth + level:depth + level + 1]
            middle, weights = row_taps(offset, slope, extent)
            first, pair = column_taps(offset, slope, extent)
            wide = [weight.astype(F32) for weight in weights]
            values = [middle] + wide + [first] + [weight.astype(F32) for weight in pair]
            at = member * group
            if not isinstance(at, int):
                at = pl.multiple_of(at, 8)
            at = pl.ds(at + level * capacity, capacity)
            for ref, value in zip(tables, values):
                ref[at, :] = value
            parts = (wide[0] + wide[1]) + wide[2]
            summed = parts if summed is None else summed + parts
        row = 3 * depth
        tile_of = jnp.broadcast_to(fields[row:row + 1, 0:capacity], (ray_tiles, capacity))
        count = jnp.broadcast_to(fields[row + 1:row + 2, 0:capacity], (ray_tiles, capacity))
        tile = lax.broadcasted_iota(I32, (ray_tiles, capacity), 0).astype(F32)
        within = lax.broadcasted_iota(I32, (ray_tiles, capacity), 1).astype(F32)
        hot = jnp.logical_and(tile_of == tile, within < count).astype(F32)
        total = total + jnp.dot(hot, summed, precision=HIGHEST, preferred_element_type=F32)
        lane = lax.broadcasted_iota(I32, fields.shape, 1)
        own = jnp.where(lane < capacity, fields, 0.0)
        if lanes > extent:
            own = jnp.concatenate(
                [own, jnp.zeros((fields.shape[0], lanes - extent), F32)], axis=1)
        return total, lined + pltpu.roll(own, member * capacity, axis=1)

    carry = jnp.zeros((ray_tiles, extent), F32), jnp.zeros((16, lanes), F32)
    if members <= 16:
        for member in range(members):
            carry = build(member, carry)
    else:
        carry = lax.fori_loop(0, members, build, carry)
    row_ref[...], lined = carry
    for ref in tables:
        ref[dead:, :] = jnp.zeros((group, extent), ref.dtype)

    slot = lax.broadcasted_iota(I32, (1, lanes), 1)
    member = lax.div(slot, capacity)
    within = lax.rem(slot, capacity)
    line = (member * group + within - dead).astype(F32)
    row = 2 * depth
    base = member.astype(F32) * tiles
    voxels = [(lined[row + level:row + level + 1] + base) * frames for level in range(depth)]
    ray = lined[3 * depth:3 * depth + 1] * frames
    table = jnp.concatenate([line, ray] + voxels + [jnp.zeros((6 - depth, lanes), F32)], axis=0)
    alive = jnp.logical_and(
        within.astype(F32) < lined[3 * depth + 1:3 * depth + 2], member < members).astype(F32)
    order = lax.broadcasted_iota(I32, (lanes, lanes), 0)
    earlier = (lax.broadcasted_iota(I32, (lanes, lanes), 1) < order).astype(F32)
    position = contract_lanes(jnp.broadcast_to(alive, (8, lanes)), earlier)[0:1]
    position = jnp.where(alive > 0.0, position, -1.0).astype(I32)
    choose = jnp.broadcast_to(position, (lanes, lanes)) == order
    packed = contract_lanes(table, choose.astype(F32))
    kind = lax.broadcasted_iota(I32, (8, lanes), 0)
    total = jnp.sum(alive, axis=1, keepdims=True)
    extra = jnp.where(kind == 0, float(dead), jnp.where(kind == 7, total, 0.0))
    list_ref[...] = (packed + extra + 0.5).astype(I32)


def column_kernel(sizes, offset_ref, slope_ref, voxel_ref, live_ref, out_ref):
    capacity, depth, frames = sizes
    tiles = out_ref.shape[0] // frames
    slots = offset_ref.shape[1]
    extent = out_ref.shape[1]
    offsets = offset_ref[...].T
    slopes = slope_ref[...].T
    within = lax.rem(lax.broadcasted_iota(I32, (1, slots), 1), capacity).astype(F32)
    alive = jnp.broadcast_to(within, (tiles, slots)) < per_slot(live_ref, slots, capacity)
    total = jnp.zeros((tiles, extent), F32)
    for level in range(depth):
        unused, pair = column_taps(
            offsets[:, level:level + 1], slopes[:, level:level + 1], extent)
        tile_of = jnp.broadcast_to(voxel_ref[level:level + 1, :], (tiles, slots))
        match = tile_of == lax.broadcasted_iota(I32, (tiles, slots), 0)
        hot = jnp.logical_and(match, alive).astype(F32).astype(BF16)
        for weight in pair:
            total += jnp.dot(hot, weight, preferred_element_type=F32)
    out_ref[...] = repeat_rows(1.0 / jnp.maximum(total, 1.0), frames)


def pick(values, index):
    numbers = lax.GatherDimensionNumbers(
        offset_dims=(), collapsed_slice_dims=(1,), start_index_map=(1,),
        operand_batching_dims=(0,), start_indices_batching_dims=(0,))
    return lax.gather(
        values, index[:, :, None], numbers, slice_sizes=(1, 1),
        mode=lax.GatherScatterMode.PROMISE_IN_BOUNDS)


def spread(ref, row, frames):
    return jnp.broadcast_to(ref[pl.ds(row, 1), :], (frames, ref.shape[1]))


def tile_at(start, frames):
    return pl.ds(pl.multiple_of(start, frames), frames)


def for_slots(list_ref, body):
    def some(step, carry):
        for place in range(CHUNK):
            body(step * CHUNK + place)
        return carry

    lax.fori_loop(0, lax.div(list_ref[7, 0] + (CHUNK - 1), CHUNK), some, 0)


def for_rows(rows, body):
    step = 128

    def some(number, carry):
        body(pl.ds(pl.multiple_of(number * step, step), step))
        return carry

    lax.fori_loop(0, rows // step, some, 0)


def project(sizes, stride, list_ref, values_ref, tables, projection, taps_ref):
    capacity, depth, frames = sizes
    members = values_ref.shape[0] // stride
    room = 4 * frames
    tiles = taps_ref.shape[0] // (members * room)
    extent = values_ref.shape[1]

    def widen(member, carry):
        rows = pl.ds(pl.multiple_of(member * stride, 16), tiles * frames)
        values = values_ref[rows, :].astype(F32)
        before = pltpu.roll(values, 1, axis=1)
        after = pltpu.roll(values, extent - 1, axis=1)
        for tile in range(tiles):
            at = slice(tile * frames, (tile + 1) * frames)
            taps = jnp.concatenate([before[at], values[at], after[at], values[at]], axis=0)
            to = pl.multiple_of((member * tiles + tile) * room, room)
            taps_ref[pl.ds(to, room), :] = taps.astype(BF16)
        return carry

    lax.fori_loop(0, members, widen, 0)
    step = 16
    voxel = lax.broadcasted_iota(I32, (step, extent), 0)
    voxels = [(voxel + start).astype(F32).astype(BF16) for start in range(0, extent, step)]
    one_hot, zero = jnp.ones((step, extent), BF16), jnp.zeros((step, extent), BF16)

    def one(slot):
        line = list_ref[0, slot]
        total = None
        for level in range(depth):
            row = line + level * capacity
            at = pl.ds(pl.multiple_of(list_ref[2 + level, slot] * 4, room), room)
            middle = spread(tables[0], row, step).astype(BF16)
            choose = jnp.concatenate(
                [jnp.where(voxel == middle, one_hot, zero) for voxel in voxels], axis=0)
            taps = jnp.dot(taps_ref[at, :], choose, preferred_element_type=F32)
            for place, ref in enumerate(tables[1:]):
                term = spread(ref, row, frames) * taps[place * frames:(place + 1) * frames]
                total = term if total is None else total + term
        projection[tile_at(list_ref[1, slot], frames), :] += total.astype(BF16).astype(F32)

    for_slots(list_ref, one)


def backproject(sizes, list_ref, residual, tables, banks):
    capacity, depth, frames = sizes

    def clear(at):
        for bank in banks:
            bank[at, :] = jnp.zeros((at.size, bank.shape[1]), F32)

    for_rows(banks[0].shape[0], clear)

    def one(slot):
        line = list_ref[0, slot]
        values = residual[tile_at(list_ref[1, slot], frames), :]
        twice = jnp.concatenate([values, values], axis=0).astype(BF16)
        for level in range(depth):
            row = line + level * capacity
            first = spread(tables[0], row, frames)
            index = jnp.concatenate([first, first + 1], axis=0).astype(jnp.int16)
            taps = pick(twice, index).astype(F32)
            term = (spread(tables[1], row, frames) * taps[0:frames]
                    + spread(tables[2], row, frames) * taps[frames:2 * frames])
            banks[level % len(banks)][tile_at(list_ref[2 + level, slot], frames), :] += term

    for_slots(list_ref, one)


def forward_kernel(sizes, stride, first, list_ref, values_ref, *refs):
    tables, refs = refs[:4], refs[4:]
    if not first:
        start_ref, refs = refs[0], refs[1:]
    projection, taps_ref = refs
    projection[...] = jnp.zeros_like(projection) if first else start_ref[...]
    project(sizes, stride, list_ref, values_ref, tables, projection, taps_ref)


def residual_of(sizes, projection, sinogram_ref, row_refs):
    total = sum([ref[...] for ref in row_refs[1:]], row_refs[0][...])
    weight = repeat_rows(1.0 / jnp.maximum(total, 1.0), sizes[2])
    scaled = (sinogram_ref[...].astype(F32) - projection[...]) * weight
    return scaled.astype(BF16).astype(F32)


def turn_kernel(sizes, stride, n_rows, first, list_ref, values_ref, *refs):
    forward, backward, refs = refs[:4], refs[4:7], refs[7:]
    sinogram_ref, row_refs, refs = refs[0], refs[1:1 + n_rows], refs[1 + n_rows:]
    if not first:
        start_ref, refs = refs[0], refs[1:]
    out_ref, residual, projection = refs[:3]
    taps_ref, banks = refs[3], refs[4:]
    projection[...] = jnp.zeros_like(projection) if first else start_ref[...]
    project(sizes, stride, list_ref, values_ref, forward, projection, taps_ref)
    residual[...] = residual_of(sizes, projection, sinogram_ref, row_refs)
    backproject(sizes, list_ref, residual, backward, banks)

    def finish(at):
        out_ref[at, :] = sum([bank[at, :] for bank in banks[1:]], banks[0][at, :]).astype(BF16)

    for_rows(out_ref.shape[0], finish)


def backward_kernel(sizes, list_ref, residual, *refs):
    tables, out_ref, banks = refs[:3], refs[3], refs[4:]
    backproject(sizes, list_ref, residual, tables, (out_ref,) + banks)

    def finish(at):
        out_ref[at, :] = sum([bank[at, :] for bank in banks], out_ref[at, :])

    if banks:
        for_rows(out_ref.shape[0], finish)


def combine_y_kernel(sum_ref, core_ref, out_ref):
    rows = sum_ref.shape[0]
    out_ref[...] = (sum_ref[...] + core_ref[rows:2 * rows, :].astype(F32)).astype(BF16)


def combine_z_kernel(sum_ref, core_ref, y_ref, own_ref, *piece_refs):
    rows = own_ref.shape[0]
    for place, ref in enumerate((own_ref,) + piece_refs):
        at = pl.ds(place * rows, rows)
        total = sum_ref[at, :] + core_ref[at, :].astype(F32) + y_ref[at, :].astype(F32)
        ref[...] = total.astype(ref.dtype)


def join_kernel(z_ref, y_ref, after_ref, out_ref):
    del after_ref
    rows = z_ref.shape[0]
    out_ref[0:rows, :] = z_ref[...]
    out_ref[rows:2 * rows, :] = y_ref[...]


def update_kernel(n_pieces, volume_ref, column_ref, *refs):
    back = refs[0][...]
    for ref in refs[1:n_pieces]:
        back = back + ref[...].astype(F32)
    volume = volume_ref[...] + column_ref[...] * back
    for ref in refs[n_pieces:]:
        ref[...] = volume.astype(ref.dtype)


def call(kernel, name, mib, in_specs, out_shape, *operands, scratch=()):
    one = not isinstance(out_shape, list)
    return pl.pallas_call(
        kernel,
        out_shape=out_shape,
        in_specs=in_specs,
        out_specs=VMEM if one else [VMEM] * len(out_shape),
        scratch_shapes=list(scratch),
        compiler_params=pltpu.CompilerParams(vmem_limit_bytes=mib * 1024 * 1024),
        name=name,
    )(*operands)


def exchange(values, n_slab, distance):
    return lax.ppermute(
        values, "slab", [(device, device ^ distance) for device in range(n_slab)])


def shards(sinogram, start_volume, slot_voxel, slot_ray, live_count, block_slope, block_offset):
    n_slab = lax.axis_size("slab")
    n_slots, depth = slot_voxel.shape
    capacity = n_slots // n_slab
    ray_tiles, frames, extent = sinogram.shape
    voxel_tiles = start_volume.shape[0]
    rows = voxel_tiles * frames
    sizes = (capacity, depth, frames)
    paired = n_slab == 16
    n_bank = 2 if paired else 1
    shape = jax.ShapeDtypeStruct
    rays = shape((ray_tiles * frames, extent), F32)
    volume = start_volume.reshape(rows, extent)
    sino = sinogram.reshape(rays.shape)
    me = lax.axis_index("slab").astype(I32).reshape(1)
    slots_by_depth = (block_offset.T, block_slope.T, slot_voxel.T)
    live = live_count.reshape(1, n_slab)
    height = -(-(7 * depth + 2) // 16) * 16 * (n_slots // extent)
    operands = (volume, *slots_by_depth, slot_ray.reshape(1, n_slots), live)
    payload = call(
        functools.partial(pack_kernel, capacity), "pack", 60, [ANY] * 6,
        shape((rows + height, extent), BF16), *operands,
        scratch=[pltpu.VMEM(operand.shape, operand.dtype) for operand in operands]
        + [pltpu.SemaphoreType.DMA((6,))])

    def setup(values, members):
        group = capacity * depth
        lines = (members + 1) * group
        lanes = -(-members * capacity // 128) * 128
        table = [shape((lines, extent), F32)] * 4
        table += [shape((lines, extent), I32)] + [shape((lines, extent), F32)] * 2
        out = [shape((8, lanes), I32), shape((ray_tiles, extent), F32)] + table
        stride = values.shape[0] // members
        found = call(
            functools.partial(setup_kernel, members, stride, sizes, voxel_tiles), "setup", 24,
            [SMEM, VMEM], out, me, values)
        return found[0], found[1], found[2:6], found[6:9]

    def wide(members):
        return pltpu.VMEM((members * rows, extent), F32)

    def taps(members):
        return pltpu.VMEM((members * rows * 4, extent), BF16)

    def forward(values, group, start, members):
        operands = [values, *group[2]] + ([] if start is None else [start])
        return call(
            functools.partial(forward_kernel, sizes, values.shape[0] // members, start is None),
            "forward", 16, [SMEM] + [VMEM] * len(operands), rays,
            group[0], *operands, scratch=[taps(members)])

    def turn(values, group, row_sums, start, members):
        operands = [values, *group[2], *group[3], sino, *row_sums] + ([] if start is None else [start])
        return call(
            functools.partial(turn_kernel, sizes, values.shape[0] // members, len(row_sums),
                              start is None),
            "turn", 24 if paired else 40, [SMEM] + [VMEM] * len(operands),
            [shape((members * rows, extent), BF16), rays],
            group[0], *operands,
            scratch=[pltpu.VMEM(rays.shape, F32), taps(members)] + [wide(members)] * n_bank)

    def backward(residual, group, members):
        return call(
            functools.partial(backward_kernel, sizes), "backward", 16, [SMEM] + [VMEM] * 4,
            shape((members * rows, extent), F32), group[0], residual, *group[3],
            scratch=[wide(members)] * (n_bank - 1))

    def update(volume, pieces, last):
        out = [shape((rows, extent), F32)] + ([] if last else [shape((rows, extent), BF16)])
        return call(
            functools.partial(update_kernel, len(pieces)), "update", 16,
            [VMEM] * (2 + len(pieces)), out, volume, column_weight, *pieces)

    column_weight = call(
        functools.partial(column_kernel, sizes), "column_weight", 16, [VMEM] * 4,
        shape((rows, extent), F32), *slots_by_depth, live)

    groups = None
    for sweep in range(ITERS):
        last = sweep + 1 == ITERS
        if paired:
            along_z = jnp.concatenate(
                [payload] + [exchange(payload, n_slab, distance) for distance in (8, 12, 4)], axis=0)
            along_y = exchange(along_z, n_slab, 2)
            if sweep == 0:
                groups = [setup(along_z, 4)]
            projection = forward(along_z, groups[0], None, 4)
            stride = along_z.shape[0]
            other = exchange(
                call(join_kernel, "join", 16, [VMEM, VMEM, ANY],
                     shape((2 * stride, extent), BF16), along_z, along_y, projection), n_slab, 1)
            if sweep == 0:
                groups += [setup(along_y, 4), setup(other, 8)]
                row_sums = [group[1] for group in groups]
            projection = forward(along_y, groups[1], projection, 4)
            other_sum, residual = turn(other, groups[2], row_sums, projection, 8)
            core_part = exchange(other_sum, n_slab, 1)
            y_sum = backward(residual, groups[1], 4)
            y_part = exchange(
                call(combine_y_kernel, "combine_y", 16, [VMEM] * 2,
                     shape((4 * rows, extent), BF16), y_sum, core_part), n_slab, 2)
            z_sum = backward(residual, groups[0], 4)
            own, *pieces = call(
                combine_z_kernel, "combine_z", 16, [VMEM] * 3,
                [shape((rows, extent), F32)] + [shape((rows, extent), BF16)] * 3,
                z_sum, core_part, y_part)
            pieces = [own] + [
                exchange(piece, n_slab, distance) for piece, distance in zip(pieces, (8, 12, 4))]
        else:
            everyone = lax.all_gather(payload, "slab", axis=0, tiled=True)
            if groups is None:
                groups = [setup(everyone, n_slab)]
                row_sums = [groups[0][1]]
            sums, residual = turn(everyone, groups[0], row_sums, None, n_slab)
            parts = lax.all_to_all(
                sums.reshape(n_slab, rows, extent), "slab", split_axis=0, concat_axis=0, tiled=True)
            pieces = [jnp.sum(parts.astype(F32), axis=0)]
        volume, *rounded = update(volume, pieces, last)
        if not last:
            payload = rounded[0]
    return volume.reshape(start_volume.shape)


def solution(mesh):
    in_specs = (
        P(("scan", "slab"), None, None),
        P(("scan", "slab"), None, None),
        P(("scan", "slab"), None),
        P(("scan", "slab")),
        P(("scan", "slab")),
        P(("scan", "slab"), None),
        P(("scan", "slab"), None),
    )
    out_specs = P(("scan", "slab"), None, None)
    return jax.shard_map(shards, mesh=mesh, in_specs=in_specs, out_specs=out_specs, check_vma=False)
```

```python
import functools

import jax
import jax.numpy as jnp
from jax import lax
from jax.experimental import pallas as pl
from jax.experimental.pallas import tpu as pltpu
from jax.sharding import PartitionSpec as P

ITERS = 2
FAR = 1.0e6
CHUNK = 8
F32 = jnp.float32
BF16 = jnp.bfloat16
I32 = jnp.int32
HIGHEST = lax.Precision.HIGHEST
VMEM = pl.BlockSpec(memory_space=pltpu.VMEM)
SMEM = pl.BlockSpec(memory_space=pltpu.SMEM)
ANY = pl.BlockSpec(memory_space=pl.ANY)


def hat(ray, centre):
    return jnp.maximum(0.0, 1.0 - jnp.abs(ray - centre)).astype(BF16)


def row_taps(offset, slope, extent):
    shape = (offset.shape[0], extent)
    ray = lax.broadcasted_iota(I32, shape, 1).astype(F32)
    offset = jnp.broadcast_to(offset, shape)
    slope = jnp.broadcast_to(slope, shape)
    middle = jnp.floor((ray - offset) / slope + 0.5)
    middle = jnp.minimum(jnp.maximum(middle, 1.0), extent - 2.0)
    weights = [hat(ray, offset + slope * (middle + step)) for step in (-1.0, 0.0, 1.0)]
    return middle.astype(I32), weights


def column_taps(offset, slope, extent):
    shape = (offset.shape[0], extent)
    voxel = lax.broadcasted_iota(I32, shape, 1).astype(F32)
    centre = jnp.broadcast_to(offset, shape) + jnp.broadcast_to(slope, shape) * voxel
    first = jnp.minimum(jnp.maximum(jnp.floor(centre), 0.0), extent - 2.0)
    weights = [hat(first + step, centre) for step in (0.0, 1.0)]
    return first.astype(I32), weights


def repeat_rows(values, times):
    return jnp.concatenate(
        [jnp.broadcast_to(values[row:row + 1, :], (times, values.shape[1]))
         for row in range(values.shape[0])], axis=0)


def contract_lanes(left, right):
    return lax.dot_general(
        left, right, (((1,), (1,)), ((), ())), precision=HIGHEST, preferred_element_type=F32)


def pack_kernel(capacity, *refs):
    sources, out_ref, loaded, arrived = refs[:6], refs[6], refs[7:13], refs[13]
    copies = [
        pltpu.make_async_copy(source, ref, arrived.at[place])
        for place, (source, ref) in enumerate(zip(sources, loaded))]
    for copy in copies:
        copy.start()
    for copy in copies:
        copy.wait()
    volume_ref, offset_ref, slope_ref, voxel_ref, ray_ref, live_ref = loaded
    rows, extent = volume_ref.shape
    out_ref[0:rows, :] = volume_ref[...].astype(BF16)
    slots = ray_ref.shape[1]
    fields = []
    for ref in (offset_ref, slope_ref):
        left = ref[...]
        for addend in range(3):
            part = left.astype(BF16).astype(F32)
            fields.append(part)
            left = left - part
    fields.append(voxel_ref[...].astype(F32))
    fields.append(ray_ref[...].astype(F32))
    fields.append(per_slot(live_ref, slots, capacity))
    used = sum(field.shape[0] for field in fields)
    fields.append(jnp.zeros((-used % 16, slots), F32))
    fields = jnp.concatenate(fields, axis=0)
    height = fields.shape[0]
    for part in range(slots // extent):
        at = pl.ds(rows + part * height, height)
        out_ref[at, :] = fields[:, part * extent:(part + 1) * extent].astype(BF16)


def per_slot(live_ref, slots, capacity):
    targets = live_ref.shape[1]
    slot = lax.broadcasted_iota(I32, (targets, slots), 1)
    owner = lax.broadcasted_iota(I32, (targets, slots), 0)
    expand = (lax.div(slot, capacity) == owner).astype(F32)
    return jnp.dot(live_ref[...].astype(F32), expand, precision=HIGHEST, preferred_element_type=F32)


def setup_kernel(members, stride, sizes, tiles, me_ref, payload_ref,
                 list_ref, row_ref, fi_ref, f0_ref, f1_ref, f2_ref, bi_ref, b0_ref, b1_ref):
    capacity, depth, frames = sizes
    group = capacity * depth
    dead = members * group
    ray_tiles, extent = row_ref.shape
    height = -(-(7 * depth + 2) // 16) * 16
    tables = (fi_ref, f0_ref, f1_ref, f2_ref, bi_ref, b0_ref, b1_ref)
    lanes = list_ref.shape[1]
    first_slot = me_ref[0] * capacity
    part = lax.div(first_slot, extent)
    shift = lax.rem(extent - lax.rem(first_slot, extent), extent)

    def build(member, carry):
        total, lined = carry
        at = member * stride + tiles * frames + part * height
        raw = payload_ref[pl.ds(pl.multiple_of(at, 16), height), :].astype(F32)
        offset = (raw[0:depth] + raw[depth:2 * depth]) + raw[2 * depth:3 * depth]
        slope = (raw[3 * depth:4 * depth] + raw[4 * depth:5 * depth]) + raw[5 * depth:6 * depth]
        rest = raw[6 * depth:7 * depth + 2]
        fields = jnp.concatenate(
            [offset, slope, rest, jnp.zeros((16 - 3 * depth - 2, extent), F32)], axis=0)
        fields = pltpu.roll(fields, shift, axis=1)
        columns = fields.T
        summed = None
        for level in range(depth):
            offset = columns[0:capacity, level:level + 1]
            slope = columns[0:capacity, depth + level:depth + level + 1]
            middle, weights = row_taps(offset, slope, extent)
            first, pair = column_taps(offset, slope, extent)
            wide = [weight.astype(F32) for weight in weights]
            values = [middle] + wide + [first] + [weight.astype(F32) for weight in pair]
            at = member * group
            if not isinstance(at, int):
                at = pl.multiple_of(at, 8)
            at = pl.ds(at + level * capacity, capacity)
            for ref, value in zip(tables, values):
                ref[at, :] = value
            parts = (wide[0] + wide[1]) + wide[2]
            summed = parts if summed is None else summed + parts
        row = 3 * depth
        tile_of = jnp.broadcast_to(fields[row:row + 1, 0:capacity], (ray_tiles, capacity))
        count = jnp.broadcast_to(fields[row + 1:row + 2, 0:capacity], (ray_tiles, capacity))
        tile = lax.broadcasted_iota(I32, (ray_tiles, capacity), 0).astype(F32)
        within = lax.broadcasted_iota(I32, (ray_tiles, capacity), 1).astype(F32)
        hot = jnp.logical_and(tile_of == tile, within < count).astype(F32)
        total = total + jnp.dot(hot, summed, precision=HIGHEST, preferred_element_type=F32)
        lane = lax.broadcasted_iota(I32, fields.shape, 1)
        own = jnp.where(lane < capacity, fields, 0.0)
        if lanes > extent:
            own = jnp.concatenate(
                [own, jnp.zeros((fields.shape[0], lanes - extent), F32)], axis=1)
        return total, lined + pltpu.roll(own, member * capacity, axis=1)

    carry = jnp.zeros((ray_tiles, extent), F32), jnp.zeros((16, lanes), F32)
    if members <= 16:
        for member in range(members):
            carry = build(member, carry)
    else:
        carry = lax.fori_loop(0, members, build, carry)
    row_ref[...], lined = carry
    for ref in tables:
        ref[dead:, :] = jnp.zeros((group, extent), ref.dtype)

    slot = lax.broadcasted_iota(I32, (1, lanes), 1)
    member = lax.div(slot, capacity)
    within = lax.rem(slot, capacity)
    line = (member * group + within - dead).astype(F32)
    row = 2 * depth
    base = member.astype(F32) * tiles
    voxels = [(lined[row + level:row + level + 1] + base) * frames for level in range(depth)]
    ray = lined[3 * depth:3 * depth + 1] * frames
    table = jnp.concatenate([line, ray] + voxels + [jnp.zeros((6 - depth, lanes), F32)], axis=0)
    alive = jnp.logical_and(
        within.astype(F32) < lined[3 * depth + 1:3 * depth + 2], member < members).astype(F32)
    order = lax.broadcasted_iota(I32, (lanes, lanes), 0)
    earlier = (lax.broadcasted_iota(I32, (lanes, lanes), 1) < order).astype(F32)
    position = contract_lanes(jnp.broadcast_to(alive, (8, lanes)), earlier)[0:1]
    position = jnp.where(alive > 0.0, position, -1.0).astype(I32)
    choose = jnp.broadcast_to(position, (lanes, lanes)) == order
    packed = contract_lanes(table, choose.astype(F32))
    kind = lax.broadcasted_iota(I32, (8, lanes), 0)
    total = jnp.sum(alive, axis=1, keepdims=True)
    extra = jnp.where(kind == 0, float(dead), jnp.where(kind == 7, total, 0.0))
    list_ref[...] = (packed + extra + 0.5).astype(I32)


def column_kernel(sizes, offset_ref, slope_ref, voxel_ref, live_ref, out_ref):
    capacity, depth, frames = sizes
    tiles = out_ref.shape[0] // frames
    slots = offset_ref.shape[1]
    extent = out_ref.shape[1]
    offsets = offset_ref[...].T
    slopes = slope_ref[...].T
    within = lax.rem(lax.broadcasted_iota(I32, (1, slots), 1), capacity).astype(F32)
    alive = jnp.broadcast_to(within, (tiles, slots)) < per_slot(live_ref, slots, capacity)
    total = jnp.zeros((tiles, extent), F32)
    for level in range(depth):
        unused, pair = column_taps(
            offsets[:, level:level + 1], slopes[:, level:level + 1], extent)
        tile_of = jnp.broadcast_to(voxel_ref[level:level + 1, :], (tiles, slots))
        match = tile_of == lax.broadcasted_iota(I32, (tiles, slots), 0)
        hot = jnp.logical_and(match, alive).astype(F32).astype(BF16)
        for weight in pair:
            total += jnp.dot(hot, weight, preferred_element_type=F32)
    out_ref[...] = repeat_rows(1.0 / jnp.maximum(total, 1.0), frames)


def pick(values, index):
    numbers = lax.GatherDimensionNumbers(
        offset_dims=(), collapsed_slice_dims=(1,), start_index_map=(1,),
        operand_batching_dims=(0,), start_indices_batching_dims=(0,))
    return lax.gather(
        values, index[:, :, None], numbers, slice_sizes=(1, 1),
        mode=lax.GatherScatterMode.PROMISE_IN_BOUNDS)


def pack_pair(first, second):
    kind = jnp.int16 if first.dtype == I32 else BF16
    return jnp.concatenate([first, second], axis=0).astype(kind)


def spread(ref, row, frames):
    return jnp.broadcast_to(ref[pl.ds(row, 1), :], (frames, ref.shape[1]))


def tile_at(start, frames):
    return pl.ds(pl.multiple_of(start, frames), frames)


def for_slots(list_ref, body):
    def some(step, carry):
        for place in range(CHUNK):
            body(step * CHUNK + place, place)
        return carry

    lax.fori_loop(0, lax.div(list_ref[7, 0] + (CHUNK - 1), CHUNK), some, 0)


def for_rows(rows, body):
    step = 128

    def some(number, carry):
        body(pl.ds(pl.multiple_of(number * step, step), step))
        return carry

    lax.fori_loop(0, rows // step, some, 0)


def project(sizes, stride, list_ref, values_ref, tables, projections, wide):
    capacity, depth, frames = sizes
    members = values_ref.shape[0] // stride
    rows = wide.shape[0] // members

    def widen(member, carry):
        at = pl.ds(pl.multiple_of(member * rows, rows), rows)
        wide[at, :] = values_ref[pl.ds(pl.multiple_of(member * stride, 16), rows), :].astype(F32)
        return carry

    lax.fori_loop(0, members, widen, 0)

    def one(slot, place):
        line = list_ref[0, slot]
        taps = []
        for start in range(0, depth, 2):
            levels = range(start, start + 2)
            values = [wide[tile_at(list_ref[2 + level, slot], frames), :] for level in levels]
            middles = [spread(tables[0], line + level * capacity, frames) for level in levels]
            lower = [
                pick(pack_pair(value, value), pack_pair(middle - 1, middle)).astype(F32)
                for value, middle in zip(values, middles)]
            upper = pick(
                pack_pair(*values), pack_pair(*[middle + 1 for middle in middles])).astype(F32)
            for which, pair in enumerate(lower):
                taps.append((pair[0:frames], pair[frames:2 * frames],
                             upper[which * frames:(which + 1) * frames]))
        total = None
        for level, three in enumerate(taps):
            for ref, tap in zip(tables[1:], three):
                term = spread(ref, line + level * capacity, frames) * tap
                total = term if total is None else total + term
        projection = projections[place % len(projections)]
        projection[tile_at(list_ref[1, slot], frames), :] += total.astype(BF16).astype(F32)

    for_slots(list_ref, one)


def backproject(sizes, list_ref, residual, tables, banks):
    capacity, depth, frames = sizes

    def clear(at):
        for bank in banks:
            bank[at, :] = jnp.zeros((at.size, bank.shape[1]), F32)

    for_rows(banks[0].shape[0], clear)

    def one(slot, place):
        line = list_ref[0, slot]
        values = residual[tile_at(list_ref[1, slot], frames), :]
        twice = pack_pair(values, values)
        for level in range(depth):
            row = line + level * capacity
            first = spread(tables[0], row, frames)
            taps = pick(twice, pack_pair(first, first + 1)).astype(F32)
            term = (spread(tables[1], row, frames) * taps[0:frames]
                    + spread(tables[2], row, frames) * taps[frames:2 * frames])
            banks[level % len(banks)][tile_at(list_ref[2 + level, slot], frames), :] += term

    for_slots(list_ref, one)


def forward_kernel(sizes, stride, first, list_ref, values_ref, *refs):
    tables, refs = refs[:4], refs[4:]
    if not first:
        start_ref, refs = refs[0], refs[1:]
    out_ref, wide, projection = refs
    projection[...] = jnp.zeros_like(projection) if first else start_ref[...]
    out_ref[...] = jnp.zeros_like(out_ref)
    project(sizes, stride, list_ref, values_ref, tables, (projection, out_ref), wide)
    out_ref[...] += projection[...]


def residual_of(sizes, projection, sinogram_ref, row_refs):
    total = sum([ref[...] for ref in row_refs[1:]], row_refs[0][...])
    weight = repeat_rows(1.0 / jnp.maximum(total, 1.0), sizes[2])
    scaled = (sinogram_ref[...].astype(F32) - projection) * weight
    return scaled.astype(BF16).astype(F32)


def turn_kernel(sizes, stride, n_rows, first, list_ref, values_ref, *refs):
    forward, backward, refs = refs[:4], refs[4:7], refs[7:]
    sinogram_ref, row_refs, refs = refs[0], refs[1:1 + n_rows], refs[1 + n_rows:]
    if not first:
        start_ref, refs = refs[0], refs[1:]
    out_ref, residual, projection, other = refs[:4]
    wide, banks = refs[4], refs[5:]
    projection[...] = jnp.zeros_like(projection) if first else start_ref[...]
    other[...] = jnp.zeros_like(other)
    project(sizes, stride, list_ref, values_ref, forward, (projection, other), wide)
    residual[...] = residual_of(sizes, projection[...] + other[...], sinogram_ref, row_refs)
    backproject(sizes, list_ref, residual, backward, banks)

    def finish(at):
        out_ref[at, :] = sum([bank[at, :] for bank in banks[1:]], banks[0][at, :]).astype(BF16)

    for_rows(out_ref.shape[0], finish)


def backward_kernel(sizes, list_ref, residual, *refs):
    tables, out_ref, banks = refs[:3], refs[3], refs[4:]
    backproject(sizes, list_ref, residual, tables, (out_ref,) + banks)

    def finish(at):
        out_ref[at, :] = sum([bank[at, :] for bank in banks], out_ref[at, :])

    if banks:
        for_rows(out_ref.shape[0], finish)


def combine_y_kernel(sum_ref, core_ref, out_ref):
    rows = sum_ref.shape[0]
    out_ref[...] = (sum_ref[...] + core_ref[rows:2 * rows, :].astype(F32)).astype(BF16)


def combine_z_kernel(sum_ref, core_ref, y_ref, own_ref, *piece_refs):
    rows = own_ref.shape[0]
    for place, ref in enumerate((own_ref,) + piece_refs):
        at = pl.ds(place * rows, rows)
        total = sum_ref[at, :] + core_ref[at, :].astype(F32) + y_ref[at, :].astype(F32)
        ref[...] = total.astype(ref.dtype)


def join_kernel(*refs):
    out_ref, at = refs[-1], 0
    for ref in refs[:-1]:
        if ref.dtype == out_ref.dtype:
            out_ref[at:at + ref.shape[0], :] = ref[...]
            at += ref.shape[0]


def update_kernel(n_pieces, volume_ref, column_ref, *refs):
    back = refs[0][...]
    for ref in refs[1:n_pieces]:
        back = back + ref[...].astype(F32)
    volume = volume_ref[...] + column_ref[...] * back
    for ref in refs[n_pieces:]:
        ref[...] = volume.astype(ref.dtype)


def call(kernel, name, mib, in_specs, out_shape, *operands, scratch=()):
    one = not isinstance(out_shape, list)
    return pl.pallas_call(
        kernel,
        out_shape=out_shape,
        in_specs=in_specs,
        out_specs=VMEM if one else [VMEM] * len(out_shape),
        scratch_shapes=list(scratch),
        compiler_params=pltpu.CompilerParams(vmem_limit_bytes=mib * 1024 * 1024),
        name=name,
    )(*operands)


def exchange(values, n_slab, distance):
    return lax.ppermute(
        values, "slab", [(device, device ^ distance) for device in range(n_slab)])


def shards(sinogram, start_volume, slot_voxel, slot_ray, live_count, block_slope, block_offset):
    n_slab = lax.axis_size("slab")
    n_slots, depth = slot_voxel.shape
    capacity = n_slots // n_slab
    ray_tiles, frames, extent = sinogram.shape
    voxel_tiles = start_volume.shape[0]
    rows = voxel_tiles * frames
    sizes = (capacity, depth, frames)
    paired = n_slab == 16
    n_bank = 4 if paired else 1
    shape = jax.ShapeDtypeStruct
    rays = shape((ray_tiles * frames, extent), F32)
    volume = start_volume.reshape(rows, extent)
    sino = sinogram.reshape(rays.shape)
    me = lax.axis_index("slab").astype(I32).reshape(1)
    slots_by_depth = (block_offset.T, block_slope.T, slot_voxel.T)
    live = live_count.reshape(1, n_slab)
    height = -(-(7 * depth + 2) // 16) * 16 * (n_slots // extent)
    operands = (volume, *slots_by_depth, slot_ray.reshape(1, n_slots), live)
    payload = call(
        functools.partial(pack_kernel, capacity), "pack", 60, [ANY] * 6,
        shape((rows + height, extent), BF16), *operands,
        scratch=[pltpu.VMEM(operand.shape, operand.dtype) for operand in operands]
        + [pltpu.SemaphoreType.DMA((6,))])

    def setup(values, members):
        group = capacity * depth
        lines = (members + 1) * group
        lanes = -(-members * capacity // 128) * 128
        table = [shape((lines, extent), I32)] + [shape((lines, extent), F32)] * 3
        table += [shape((lines, extent), I32)] + [shape((lines, extent), F32)] * 2
        out = [shape((8, lanes), I32), shape((ray_tiles, extent), F32)] + table
        stride = values.shape[0] // members
        found = call(
            functools.partial(setup_kernel, members, stride, sizes, voxel_tiles), "setup", 24,
            [SMEM, VMEM], out, me, values)
        return found[0], found[1], found[2:6], found[6:9]

    def join(*parts, after=None):
        total = sum(part.shape[0] for part in parts)
        waits = [] if after is None else [after]
        return call(
            join_kernel, "join", 16, [VMEM] * len(parts) + [ANY] * len(waits),
            shape((total, extent), BF16), *parts, *waits)

    def wide(members):
        return pltpu.VMEM((members * rows, extent), F32)

    def forward(values, group, start, members):
        operands = [values, *group[2]] + ([] if start is None else [start])
        return call(
            functools.partial(forward_kernel, sizes, values.shape[0] // members, start is None),
            "forward", 16, [SMEM] + [VMEM] * len(operands), rays,
            group[0], *operands, scratch=[wide(members), pltpu.VMEM(rays.shape, F32)])

    def turn(values, group, row_sums, start, members):
        operands = [values, *group[2], *group[3], sino, *row_sums] + ([] if start is None else [start])
        return call(
            functools.partial(turn_kernel, sizes, values.shape[0] // members, len(row_sums),
                              start is None),
            "turn", 24 if paired else 40, [SMEM] + [VMEM] * len(operands),
            [shape((members * rows, extent), BF16), rays],
            group[0], *operands,
            scratch=[pltpu.VMEM(rays.shape, F32)] * 2 + [wide(members)] * (1 + n_bank))

    def backward(residual, group, members):
        return call(
            functools.partial(backward_kernel, sizes), "backward", 16, [SMEM] + [VMEM] * 4,
            shape((members * rows, extent), F32), group[0], residual, *group[3],
            scratch=[wide(members)] * (n_bank - 1))

    def update(volume, pieces, last):
        out = [shape((rows, extent), F32)] + ([] if last else [shape((rows, extent), BF16)])
        return call(
            functools.partial(update_kernel, len(pieces)), "update", 16,
            [VMEM] * (2 + len(pieces)), out, volume, column_weight, *pieces)

    column_weight = call(
        functools.partial(column_kernel, sizes), "column_weight", 16, [VMEM] * 4,
        shape((rows, extent), F32), *slots_by_depth, live)

    groups = None
    for sweep in range(ITERS):
        last = sweep + 1 == ITERS
        if paired:
            along_z = join(
                payload, *[exchange(payload, n_slab, distance) for distance in (8, 12, 4)])
            along_y = exchange(along_z, n_slab, 2)
            if sweep == 0:
                groups = [setup(along_z, 4)]
            projection = forward(along_z, groups[0], None, 4)
            other = exchange(join(along_z, along_y, after=projection), n_slab, 1)
            if sweep == 0:
                groups += [setup(along_y, 4), setup(other, 8)]
                row_sums = [group[1] for group in groups]
            projection = forward(along_y, groups[1], projection, 4)
            other_sum, residual = turn(other, groups[2], row_sums, projection, 8)
            core_part = exchange(other_sum, n_slab, 1)
            y_sum = backward(residual, groups[1], 4)
            y_part = exchange(
                call(combine_y_kernel, "combine_y", 16, [VMEM] * 2,
                     shape((4 * rows, extent), BF16), y_sum, core_part), n_slab, 2)
            z_sum = backward(residual, groups[0], 4)
            own, *pieces = call(
                combine_z_kernel, "combine_z", 16, [VMEM] * 3,
                [shape((rows, extent), F32)] + [shape((rows, extent), BF16)] * 3,
                z_sum, core_part, y_part)
            pieces = [own] + [
                exchange(piece, n_slab, distance) for piece, distance in zip(pieces, (8, 12, 4))]
        else:
            everyone = lax.all_gather(payload, "slab", axis=0, tiled=True)
            if groups is None:
                groups = [setup(everyone, n_slab)]
                row_sums = [groups[0][1]]
            sums, residual = turn(everyone, groups[0], row_sums, None, n_slab)
            parts = lax.all_to_all(
                sums.reshape(n_slab, rows, extent), "slab", split_axis=0, concat_axis=0, tiled=True)
            pieces = [jnp.sum(parts.astype(F32), axis=0)]
        volume, *rounded = update(volume, pieces, last)
        if not last:
            payload = rounded[0]
    return volume.reshape(start_volume.shape)


def solution(mesh):
    in_specs = (
        P(("scan", "slab"), None, None),
        P(("scan", "slab"), None, None),
        P(("scan", "slab"), None),
        P(("scan", "slab")),
        P(("scan", "slab")),
        P(("scan", "slab"), None),
        P(("scan", "slab"), None),
    )
    out_specs = P(("scan", "slab"), None, None)
    return jax.shard_map(shards, mesh=mesh, in_specs=in_specs, out_specs=out_specs, check_vma=False)
```

```python
import functools

import jax
import jax.numpy as jnp
from jax import lax
from jax.experimental import pallas as pl
from jax.experimental.pallas import tpu as pltpu
from jax.sharding import PartitionSpec as P

ITERS = 2
CHUNK = 8
F32 = jnp.float32
BF16 = jnp.bfloat16
I32 = jnp.int32
HIGHEST = lax.Precision.HIGHEST
VMEM = pl.BlockSpec(memory_space=pltpu.VMEM)
ANY = pl.BlockSpec(memory_space=pl.ANY)


def hat(ray, centre):
    return jnp.maximum(0.0, 1.0 - jnp.abs(ray - centre)).astype(BF16)


def row_taps(offset, slope, extent):
    shape = (offset.shape[0], extent)
    ray = lax.broadcasted_iota(I32, shape, 1).astype(F32)
    offset = jnp.broadcast_to(offset, shape)
    slope = jnp.broadcast_to(slope, shape)
    middle = jnp.floor((ray - offset) / slope + 0.5)
    middle = jnp.minimum(jnp.maximum(middle, 1.0), extent - 2.0)
    weights = [hat(ray, offset + slope * (middle + step)) for step in (-1.0, 0.0, 1.0)]
    return middle.astype(I32), weights


def column_taps(offset, slope, extent):
    shape = (offset.shape[0], extent)
    voxel = lax.broadcasted_iota(I32, shape, 1).astype(F32)
    centre = jnp.broadcast_to(offset, shape) + jnp.broadcast_to(slope, shape) * voxel
    first = jnp.minimum(jnp.maximum(jnp.floor(centre), 0.0), extent - 2.0)
    weights = [hat(first + step, centre) for step in (0.0, 1.0)]
    return first.astype(I32), weights


def repeat_rows(values, times):
    return jnp.concatenate(
        [jnp.broadcast_to(values[row:row + 1, :], (times, values.shape[1]))
         for row in range(values.shape[0])], axis=0)


def contract_lanes(left, right):
    return lax.dot_general(
        left.astype(BF16), right.astype(BF16), (((1,), (1,)), ((), ())), preferred_element_type=F32)


def per_slot(live_ref, slots, capacity):
    targets = live_ref.shape[1]
    slot = lax.broadcasted_iota(I32, (targets, slots), 1)
    owner = lax.broadcasted_iota(I32, (targets, slots), 0)
    expand = (lax.div(slot, capacity) == owner).astype(F32)
    return jnp.dot(live_ref[...].astype(F32), expand, precision=HIGHEST, preferred_element_type=F32)


def pack_kernel(capacity, *refs):
    sources, out_ref, loaded, arrived = refs[:6], refs[6], refs[7:13], refs[13]
    copies = [
        pltpu.make_async_copy(source, ref, arrived.at[place])
        for place, (source, ref) in enumerate(zip(sources, loaded))]
    for copy in copies:
        copy.start()
    for copy in copies:
        copy.wait()
    volume_ref, offset_ref, slope_ref, voxel_ref, ray_ref, live_ref = loaded
    rows, extent = volume_ref.shape
    out_ref[0:rows, :] = volume_ref[...].astype(BF16)
    slots = ray_ref.shape[1]
    fields = []
    for ref in (offset_ref, slope_ref):
        left = ref[...]
        for addend in range(3):
            part = left.astype(BF16).astype(F32)
            fields.append(part)
            left = left - part
    fields.append(voxel_ref[...].astype(F32))
    fields.append(ray_ref[...].astype(F32))
    fields.append(per_slot(live_ref, slots, capacity))
    used = sum(field.shape[0] for field in fields)
    fields.append(jnp.zeros((-used % 16, slots), F32))
    fields = jnp.concatenate(fields, axis=0)
    height = fields.shape[0]
    for part in range(slots // extent):
        at = pl.ds(rows + part * height, height)
        out_ref[at, :] = fields[:, part * extent:(part + 1) * extent].astype(BF16)


def setup_kernel(members, stride, span, sizes, tiles, wanted, payload_ref, *refs):
    refs = refs[-(len(wanted) + 8):]
    list_refs, row_ref, tables = refs[:len(wanted)], refs[len(wanted)], refs[len(wanted) + 1:]
    capacity, depth, frames = sizes
    width = span * capacity
    extent = row_ref.shape[1]
    ray_tiles = row_ref.shape[0] // span
    height = -(-(7 * depth + 2) // 16) * 16
    lanes = list_refs[0].shape[1]
    me = lax.axis_index("slab").astype(I32)
    parity = lax.rem(me, span)
    first_slot = (me - parity) * capacity
    part = lax.div(first_slot, extent)
    shift = lax.rem(extent - lax.rem(first_slot, extent), extent)

    def collect(member, lined):
        at = member * stride + tiles * frames + part * height
        raw = payload_ref[pl.ds(pl.multiple_of(at, 16), height), :].astype(F32)
        offset = (raw[0:depth] + raw[depth:2 * depth]) + raw[2 * depth:3 * depth]
        slope = (raw[3 * depth:4 * depth] + raw[4 * depth:5 * depth]) + raw[5 * depth:6 * depth]
        fields = jnp.concatenate(
            [offset, slope, raw[6 * depth:7 * depth + 2],
             jnp.zeros((16 - 3 * depth - 2, extent), F32)], axis=0)
        fields = pltpu.roll(fields, shift, axis=1)
        lane = lax.broadcasted_iota(I32, fields.shape, 1)
        fields = jnp.where(lane < width, fields, 0.0)
        if lanes > extent:
            fields = jnp.concatenate(
                [fields, jnp.zeros((fields.shape[0], lanes - extent), F32)], axis=1)
        return lined + pltpu.roll(fields, member * width, axis=1)

    lined = jnp.zeros((16, lanes), F32)
    if members <= 16:
        for member in range(members):
            lined = collect(member, lined)
    else:
        lined = lax.fori_loop(0, members, collect, lined)

    columns = lined.T
    summed = None
    for level in range(depth):
        offset = columns[:, level:level + 1]
        slope = columns[:, depth + level:depth + level + 1]
        middle, weights = row_taps(offset, slope, extent)
        first, pair = column_taps(offset, slope, extent)
        wide = [weight.astype(F32) for weight in weights]
        values = [middle] + wide + [first] + [weight.astype(F32) for weight in pair]
        at = level * (lanes + 8)
        for ref, value in zip(tables, values):
            ref[at:at + lanes, :] = value
            blank = jnp.ones if ref.dtype == I32 else jnp.zeros
            ref[at + lanes:at + lanes + 8, :] = blank((8, extent), ref.dtype)
        parts = (wide[0] + wide[1]) + wide[2]
        summed = parts if summed is None else summed + parts

    slot = lax.broadcasted_iota(I32, (1, lanes), 1)
    within = lax.rem(slot, width)
    target = lax.bitwise_xor(lax.div(within, capacity), parity)
    ray = lined[3 * depth:3 * depth + 1]
    count = lined[3 * depth + 1:3 * depth + 2]
    alive = jnp.logical_and(lax.rem(within, capacity).astype(F32) < count, slot < members * width)
    tile = lax.broadcasted_iota(I32, (span * ray_tiles, lanes), 0).astype(F32)
    place = ray + (target * ray_tiles).astype(F32)
    place = jnp.where(alive, place, -1.0)
    hot = (jnp.broadcast_to(place, tile.shape) == tile).astype(F32)
    row_ref[...] = jnp.dot(hot, summed, precision=HIGHEST, preferred_element_type=F32)

    table = jnp.concatenate(
        [slot.astype(F32), ray, target.astype(F32), lined[2 * depth:3 * depth],
         jnp.zeros((5 - depth, lanes), F32)], axis=0)
    order = lax.broadcasted_iota(I32, (lanes, lanes), 0)
    earlier = (lax.broadcasted_iota(I32, (lanes, lanes), 1) < order).astype(F32)
    for ref, kind in zip(list_refs, wanted):
        taken = alive if kind is None else jnp.logical_and(alive, target == kind)
        taken = taken.astype(F32)
        position = contract_lanes(jnp.broadcast_to(taken, (8, lanes)), earlier)[0:1]
        position = jnp.where(taken > 0.0, position, -1.0).astype(I32)
        choose = jnp.broadcast_to(position, (lanes, lanes)) == order
        packed = (contract_lanes(table, choose.astype(F32)) + 0.5).astype(I32)
        total = jnp.sum(taken, axis=1, keepdims=True).astype(I32)
        line = jnp.where(slot < total, packed[0:1], lanes)
        base = packed[1:2] if kind is not None else packed[1:2] + packed[2:3] * ray_tiles
        member = lax.div(packed[0:1], width) * tiles
        rows = [line, base * frames]
        rows += [(packed[3 + level:4 + level] + member) * frames for level in range(depth)]
        rows += [jnp.zeros((5 - depth, lanes), I32), jnp.broadcast_to(total, (1, lanes))]
        ref[...] = jnp.concatenate(rows, axis=0)


def column_kernel(sizes, offset_ref, slope_ref, voxel_ref, live_ref, out_ref):
    capacity, depth, frames = sizes
    tiles = out_ref.shape[0] // frames
    slots = offset_ref.shape[1]
    extent = out_ref.shape[1]
    offsets = offset_ref[...].T
    slopes = slope_ref[...].T
    within = lax.rem(lax.broadcasted_iota(I32, (1, slots), 1), capacity).astype(F32)
    alive = jnp.broadcast_to(within, (tiles, slots)) < per_slot(live_ref, slots, capacity)
    total = jnp.zeros((tiles, extent), F32)
    for level in range(depth):
        unused, pair = column_taps(
            offsets[:, level:level + 1], slopes[:, level:level + 1], extent)
        tile_of = jnp.broadcast_to(voxel_ref[level:level + 1, :], (tiles, slots))
        match = tile_of == lax.broadcasted_iota(I32, (tiles, slots), 0)
        hot = jnp.logical_and(match, alive).astype(F32).astype(BF16)
        for weight in pair:
            total += jnp.dot(hot, weight, preferred_element_type=F32)
    out_ref[...] = repeat_rows(1.0 / jnp.maximum(total, 1.0), frames)


def pick(values, index):
    numbers = lax.GatherDimensionNumbers(
        offset_dims=(), collapsed_slice_dims=(1,), start_index_map=(1,),
        operand_batching_dims=(0,), start_indices_batching_dims=(0,))
    return lax.gather(
        values, index[:, :, None], numbers, slice_sizes=(1, 1),
        mode=lax.GatherScatterMode.PROMISE_IN_BOUNDS)


def pack_pair(first, second):
    kind = jnp.int16 if first.dtype == I32 else BF16
    return jnp.concatenate([first, second], axis=0).astype(kind)


def spread(ref, row, frames):
    return jnp.broadcast_to(ref[pl.ds(row, 1), :], (frames, ref.shape[1]))


def tile_at(start, frames):
    return pl.ds(pl.multiple_of(start, frames), frames)


def for_slots(slots, body):
    def some(step, carry):
        for place in range(CHUNK):
            body(step * CHUNK + place, place)
        return carry

    lax.fori_loop(0, lax.div(slots[7, 0] + (CHUNK - 1), CHUNK), some, 0)


def for_rows(rows, body):
    step = 128

    def some(number, carry):
        body(pl.ds(pl.multiple_of(number * step, step), step))
        return carry

    lax.fori_loop(0, rows // step, some, 0)


def forward_kernel(sizes, stride, start_row, n_sums, list_ref, values_ref, *refs):
    capacity, depth, frames = sizes
    tables, refs = refs[:4], refs[4:]
    start_ref = None
    if start_row is not None:
        start_ref, refs = refs[0], refs[1:]
    sum_refs, (out_ref, slots, arrived, wide, second) = refs[:n_sums], refs[n_sums:]
    copy = pltpu.make_async_copy(list_ref, slots, arrived.at[0])
    copy.start()
    members = values_ref.shape[0] // stride
    rows = wide.shape[0] // members
    rays = second.shape[0]
    line_step = tables[0].shape[0] // depth

    def widen(member, carry):
        at = pl.ds(pl.multiple_of(member * rows, rows), rows)
        wide[at, :] = values_ref[pl.ds(pl.multiple_of(member * stride, 16), rows), :].astype(F32)
        return carry

    lax.fori_loop(0, members, widen, 0)
    second[...] = jnp.zeros_like(second)
    if start_ref is None:
        out_ref[...] = jnp.zeros_like(out_ref)
    else:
        out_ref[0:rays, :] = start_ref[start_row:start_row + rays, :]
    if n_sums:
        half = sum_refs[0].shape[0] // 2
        out_ref[rays:, :] = sum([ref[half:, :] for ref in sum_refs[1:]], sum_refs[0][half:, :])
    copy.wait()

    def one(slot, place):
        line = slots[0, slot]
        taps = []
        for start in range(0, depth, 2):
            levels = range(start, start + 2)
            values = [wide[tile_at(slots[2 + level, slot], frames), :] for level in levels]
            middles = [spread(tables[0], line + level * line_step, frames) for level in levels]
            lower = [
                pick(pack_pair(value, value), pack_pair(middle - 1, middle)).astype(F32)
                for value, middle in zip(values, middles)]
            upper = pick(
                pack_pair(*values), pack_pair(*[middle + 1 for middle in middles])).astype(F32)
            for which, pair in enumerate(lower):
                taps.append((pair[0:frames], pair[frames:2 * frames],
                             upper[which * frames:(which + 1) * frames]))
        total = None
        for level, three in enumerate(taps):
            for ref, tap in zip(tables[1:], three):
                term = spread(ref, line + level * line_step, frames) * tap
                total = term if total is None else total + term
        projection = (out_ref, second)[place % 2]
        projection[tile_at(slots[1, slot], frames), :] += total.astype(BF16).astype(F32)

    for_slots(slots, one)
    out_ref[0:rays, :] += second[...]


def residual_kernel(frames, n_own, projection_ref, sinogram_ref, *refs):
    own, refs, out_ref = refs[:n_own], refs[n_own:-1], refs[-1]
    rays = out_ref.shape[0]
    ray_tiles = rays // frames
    total = sum([ref[0:ray_tiles, :] for ref in own[1:]], own[0][0:ray_tiles, :])
    projection = projection_ref[...]
    if refs:
        projection = projection + refs[0][0:rays, :]
        total = total + refs[-1][rays:, :]
    weight = repeat_rows(1.0 / jnp.maximum(total, 1.0), frames)
    out_ref[...] = ((sinogram_ref[...].astype(F32) - projection) * weight).astype(BF16)


def backward_kernel(sizes, n_parts, has_start, list_ref, *refs):
    capacity, depth, frames = sizes
    part_refs, tables, refs = refs[:n_parts], refs[n_parts:n_parts + 3], refs[n_parts + 3:]
    start_ref = None
    if has_start:
        start_ref, refs = refs[0], refs[1:]
    out_ref, slots, arrived, residual, banks = refs[0], refs[1], refs[2], refs[3], refs[4:]
    copy = pltpu.make_async_copy(list_ref, slots, arrived.at[0])
    copy.start()
    rays = part_refs[0].shape[0]
    line_step = tables[0].shape[0] // depth
    for place, ref in enumerate(part_refs):
        residual[place * rays:(place + 1) * rays, :] = ref[...].astype(F32)

    def clear(at):
        for place, bank in enumerate(banks):
            if place == 0 and has_start:
                bank[at, :] = start_ref[at, :]
            else:
                bank[at, :] = jnp.zeros((at.size, bank.shape[1]), F32)

    for_rows(out_ref.shape[0], clear)
    copy.wait()

    def one(slot, place):
        line = slots[0, slot]
        values = residual[tile_at(slots[1, slot], frames), :]
        twice = pack_pair(values, values)
        for level in range(depth):
            row = line + level * line_step
            first = spread(tables[0], row, frames)
            taps = pick(twice, pack_pair(first, first + 1)).astype(F32)
            term = (spread(tables[1], row, frames) * taps[0:frames]
                    + spread(tables[2], row, frames) * taps[frames:2 * frames])
            banks[level % len(banks)][tile_at(slots[2 + level, slot], frames), :] += term

    for_slots(slots, one)

    def finish(at):
        total = sum([bank[at, :] for bank in banks[1:]], banks[0][at, :])
        out_ref[at, :] = total.astype(out_ref.dtype)

    for_rows(out_ref.shape[0], finish)


def join_kernel(*refs):
    out_ref, at = refs[-1], 0
    for ref in refs[:-1]:
        out_ref[at:at + ref.shape[0], :] = ref[...]
        at += ref.shape[0]


def combine_kernel(sum_ref, y_ref, own_ref, *piece_refs):
    rows = own_ref.shape[0]
    for place, ref in enumerate((own_ref,) + piece_refs):
        at = pl.ds(place * rows, rows)
        ref[...] = (sum_ref[at, :] + y_ref[at, :].astype(F32)).astype(ref.dtype)


def update_kernel(n_pieces, volume_ref, column_ref, *refs):
    back = refs[0][...]
    for ref in refs[1:n_pieces]:
        back = back + ref[...].astype(F32)
    volume = volume_ref[...] + column_ref[...] * back
    for ref in refs[n_pieces:]:
        ref[...] = volume.astype(ref.dtype)


def call(kernel, name, mib, in_specs, out_shape, *operands, scratch=()):
    one = not isinstance(out_shape, list)
    return pl.pallas_call(
        kernel,
        out_shape=out_shape,
        in_specs=in_specs,
        out_specs=VMEM if one else [VMEM] * len(out_shape),
        scratch_shapes=list(scratch),
        compiler_params=pltpu.CompilerParams(vmem_limit_bytes=mib * 1024 * 1024),
        name=name,
    )(*operands)


def exchange(values, n_slab, distance):
    return lax.ppermute(
        values, "slab", [(device, device ^ distance) for device in range(n_slab)])


def shards(sinogram, start_volume, slot_voxel, slot_ray, live_count, block_slope, block_offset):
    n_slab = lax.axis_size("slab")
    n_slots, depth = slot_voxel.shape
    capacity = n_slots // n_slab
    ray_tiles, frames, extent = sinogram.shape
    voxel_tiles = start_volume.shape[0]
    rows = voxel_tiles * frames
    sizes = (capacity, depth, frames)
    paired = n_slab == 16
    span = 2 if paired else 1
    n_bank = 2 if paired else 1
    shape = jax.ShapeDtypeStruct
    n_rays = ray_tiles * frames
    volume = start_volume.reshape(rows, extent)
    sino = sinogram.reshape(n_rays, extent)
    slots_by_depth = (block_offset.T, block_slope.T, slot_voxel.T)
    live = live_count.reshape(1, n_slab)
    height = -(-(7 * depth + 2) // 16) * 16 * (n_slots // extent)
    operands = (volume, *slots_by_depth, slot_ray.reshape(1, n_slots), live)
    payload = call(
        functools.partial(pack_kernel, capacity), "pack", 60, [ANY] * 6,
        shape((rows + height, extent), BF16), *operands,
        scratch=[pltpu.VMEM(operand.shape, operand.dtype) for operand in operands]
        + [pltpu.SemaphoreType.DMA((6,))])

    def setup(values, members, wanted, after=None):
        lanes = -(-members * span * capacity // 128) * 128
        lines = depth * (lanes + 8)
        table = [shape((lines, extent), I32)] + [shape((lines, extent), F32)] * 3
        table += [shape((lines, extent), I32)] + [shape((lines, extent), F32)] * 2
        out = [shape((8, lanes), I32)] * len(wanted) + [shape((span * ray_tiles, extent), F32)] + table
        waits = [] if after is None else [after]
        found = call(
            functools.partial(setup_kernel, members, values.shape[0] // members, span, sizes,
                              voxel_tiles, wanted),
            "setup", 24, [VMEM] + [ANY] * len(waits), out, values, *waits)
        n = len(wanted)
        return found[:n], found[n], found[n + 1:n + 5], found[n + 5:]

    def list_scratch(slots):
        return [pltpu.SMEM(slots.shape, I32), pltpu.SemaphoreType.DMA((1,))]

    def forward(slots, values, members, table, n_out, start=None, start_row=None, sums=()):
        operands = [slots, values, *table] + ([] if start is None else [start]) + list(sums)
        extra = ray_tiles if sums else 0
        return call(
            functools.partial(forward_kernel, sizes, values.shape[0] // members, start_row, len(sums)),
            "forward", 16 if paired else 32, [ANY] + [VMEM] * (len(operands) - 1),
            shape((n_out + extra, extent), F32), *operands,
            scratch=list_scratch(slots)
            + [pltpu.VMEM((members * rows, extent), F32), pltpu.VMEM((n_out, extent), F32)])

    def residual_of(projection, row_sums, *sibling):
        operands = [projection, sino, *row_sums, *sibling]
        return call(
            functools.partial(residual_kernel, frames, len(row_sums)), "residual", 16,
            [VMEM] * len(operands), shape((n_rays, extent), BF16), *operands)

    def backward(slots, parts, members, table, kind, start=None):
        operands = [slots, *parts, *table] + ([] if start is None else [start])
        return call(
            functools.partial(backward_kernel, sizes, len(parts), start is not None),
            "backward", 16 if paired else 32, [ANY] + [VMEM] * (len(operands) - 1),
            shape((members * rows, extent), kind), *operands,
            scratch=list_scratch(slots) + [pltpu.VMEM((len(parts) * n_rays, extent), F32)]
            + [pltpu.VMEM((members * rows, extent), F32)] * n_bank)

    def join(*parts):
        total = sum(part.shape[0] for part in parts)
        return call(join_kernel, "join", 16, [VMEM] * len(parts), shape((total, extent), BF16), *parts)

    def update(volume, pieces, last):
        out = [shape((rows, extent), F32)] + ([] if last else [shape((rows, extent), BF16)])
        return call(
            functools.partial(update_kernel, len(pieces)), "update", 16,
            [VMEM] * (2 + len(pieces)), out, volume, column_weight, *pieces)

    column_weight = call(
        functools.partial(column_kernel, sizes), "column_weight", 16, [VMEM] * 4,
        shape((rows, extent), F32), *slots_by_depth, live)

    for sweep in range(ITERS):
        last = sweep + 1 == ITERS
        if paired:
            along_z = join(
                payload, *[exchange(payload, n_slab, distance) for distance in (8, 12, 4)])
            along_y = exchange(along_z, n_slab, 2)
            if sweep == 0:
                (z_list,), z_rows, z_forward, z_backward = setup(along_z, 4, (None,))
            both = forward(z_list, along_z, 4, z_forward, 2 * n_rays)
            if sweep == 0:
                (own_list, other_list), y_rows, y_forward, y_backward = setup(
                    along_y, 4, (0, 1), after=both)
            other = exchange(
                forward(other_list, along_y, 4, y_forward, n_rays, both, n_rays,
                        (z_rows, y_rows) if sweep == 0 else ()), n_slab, 1)
            if sweep == 0:
                first_other = other
            own = forward(own_list, along_y, 4, y_forward, n_rays, both, 0)
            residual = residual_of(own, (z_rows, y_rows), other, first_other)
            other_residual = exchange(residual, n_slab, 1)
            y_sum = backward(own_list, [residual], 4, y_backward, F32)
            y_sum = backward(other_list, [other_residual], 4, y_backward, BF16, y_sum)
            y_part = exchange(y_sum, n_slab, 2)
            z_sum = backward(z_list, [residual, other_residual], 4, z_backward, F32)
            own_piece, *pieces = call(
                combine_kernel, "combine", 16, [VMEM] * 2,
                [shape((rows, extent), F32)] + [shape((rows, extent), BF16)] * 3, z_sum, y_part)
            pieces = [own_piece] + [
                exchange(piece, n_slab, distance) for piece, distance in zip(pieces, (8, 12, 4))]
        else:
            everyone = lax.all_gather(payload, "slab", axis=0, tiled=True)
            if sweep == 0:
                (slots,), row_sums, to_rays, to_voxels = setup(everyone, n_slab, (None,))
            projection = forward(slots, everyone, n_slab, to_rays, n_rays)
            residual = residual_of(projection, (row_sums,))
            sums = backward(slots, [residual], n_slab, to_voxels, BF16)
            parts = lax.all_to_all(
                sums.reshape(n_slab, rows, extent), "slab", split_axis=0, concat_axis=0, tiled=True)
            pieces = [jnp.sum(parts.astype(F32), axis=0)]
        volume, *rounded = update(volume, pieces, last)
        if not last:
            payload = rounded[0]
    return volume.reshape(start_volume.shape)


def solution(mesh):
    in_specs = (
        P(("scan", "slab"), None, None),
        P(("scan", "slab"), None, None),
        P(("scan", "slab"), None),
        P(("scan", "slab")),
        P(("scan", "slab")),
        P(("scan", "slab"), None),
        P(("scan", "slab"), None),
    )
    out_specs = P(("scan", "slab"), None, None)
    return jax.shard_map(shards, mesh=mesh, in_specs=in_specs, out_specs=out_specs, check_vma=False)
```

```python
import functools

import jax
import jax.numpy as jnp
from jax import lax
from jax.experimental import pallas as pl
from jax.experimental.pallas import tpu as pltpu
from jax.sharding import PartitionSpec as P

ITERS = 2
CHUNK = 8
F32 = jnp.float32
BF16 = jnp.bfloat16
I32 = jnp.int32
HIGHEST = lax.Precision.HIGHEST
VMEM = pl.BlockSpec(memory_space=pltpu.VMEM)
ANY = pl.BlockSpec(memory_space=pl.ANY)
SMEM = pl.BlockSpec(memory_space=pltpu.SMEM)
HBM = pl.BlockSpec(memory_space=pltpu.HBM)


def hat(ray, centre):
    return jnp.maximum(0.0, 1.0 - jnp.abs(ray - centre)).astype(BF16)


def row_taps(offset, slope, extent):
    shape = (offset.shape[0], extent)
    ray = lax.broadcasted_iota(I32, shape, 1).astype(F32)
    offset = jnp.broadcast_to(offset, shape)
    slope = jnp.broadcast_to(slope, shape)
    middle = jnp.floor((ray - offset) / slope + 0.5)
    middle = jnp.minimum(jnp.maximum(middle, 1.0), extent - 2.0)
    weights = [hat(ray, offset + slope * (middle + step)) for step in (-1.0, 0.0, 1.0)]
    return middle.astype(I32), weights


def column_taps(offset, slope, extent):
    shape = (offset.shape[0], extent)
    voxel = lax.broadcasted_iota(I32, shape, 1).astype(F32)
    centre = jnp.broadcast_to(offset, shape) + jnp.broadcast_to(slope, shape) * voxel
    first = jnp.minimum(jnp.maximum(jnp.floor(centre), 0.0), extent - 2.0)
    weights = [hat(first + step, centre) for step in (0.0, 1.0)]
    return first.astype(I32), weights


def repeat_rows(values, times):
    return jnp.concatenate(
        [jnp.broadcast_to(values[row:row + 1, :], (times, values.shape[1]))
         for row in range(values.shape[0])], axis=0)


def contract_lanes(left, right):
    return lax.dot_general(
        left.astype(BF16), right.astype(BF16), (((1,), (1,)), ((), ())), preferred_element_type=F32)


def per_slot(live_ref, slots, capacity):
    targets = live_ref.shape[1]
    slot = lax.broadcasted_iota(I32, (targets, slots), 1)
    owner = lax.broadcasted_iota(I32, (targets, slots), 0)
    expand = (lax.div(slot, capacity) == owner).astype(F32)
    return jnp.dot(live_ref[...].astype(F32), expand, precision=HIGHEST, preferred_element_type=F32)


def pack_kernel(capacity, *refs):
    sources, out_ref, loaded, arrived = refs[:6], refs[6], refs[7:13], refs[13]
    copies = [
        pltpu.make_async_copy(source, ref, arrived.at[place])
        for place, (source, ref) in enumerate(zip(sources, loaded))]
    for copy in copies:
        copy.start()
    for copy in copies:
        copy.wait()
    volume_ref, offset_ref, slope_ref, voxel_ref, ray_ref, live_ref = loaded
    rows, extent = volume_ref.shape
    out_ref[0:rows, :] = volume_ref[...].astype(BF16)
    slots = ray_ref.shape[1]
    fields = []
    for ref in (offset_ref, slope_ref):
        left = ref[...]
        for addend in range(3):
            part = left.astype(BF16).astype(F32)
            fields.append(part)
            left = left - part
    fields.append(voxel_ref[...].astype(F32))
    fields.append(ray_ref[...].astype(F32))
    fields.append(per_slot(live_ref, slots, capacity))
    used = sum(field.shape[0] for field in fields)
    fields.append(jnp.zeros((-used % 16, slots), F32))
    fields = jnp.concatenate(fields, axis=0)
    height = fields.shape[0]
    for part in range(slots // extent):
        at = pl.ds(rows + part * height, height)
        out_ref[at, :] = fields[:, part * extent:(part + 1) * extent].astype(BF16)


def setup_kernel(members, stride, span, sizes, tiles, wanted, payload_ref, *refs):
    refs = refs[-(2 * len(wanted) + 9):]
    list_refs, row_ref, tables = refs[:len(wanted)], refs[len(wanted)], refs[len(wanted) + 1:-len(wanted) - 1]
    drafts, arrived = refs[-len(wanted) - 1:-1], refs[-1]
    copies = [
        pltpu.make_async_copy(draft, ref, arrived.at[place])
        for place, (draft, ref) in enumerate(zip(drafts, list_refs))]
    capacity, depth, frames = sizes
    width = span * capacity
    extent = row_ref.shape[1]
    ray_tiles = row_ref.shape[0] // span
    height = -(-(7 * depth + 2) // 16) * 16
    lanes = drafts[0].shape[1]
    me = lax.axis_index("slab").astype(I32)
    parity = lax.rem(me, span)
    first_slot = (me - parity) * capacity
    part = lax.div(first_slot, extent)
    shift = lax.rem(extent - lax.rem(first_slot, extent), extent)

    def collect(member, lined):
        at = member * stride + tiles * frames + part * height
        raw = payload_ref[pl.ds(pl.multiple_of(at, 16), height), :].astype(F32)
        offset = (raw[0:depth] + raw[depth:2 * depth]) + raw[2 * depth:3 * depth]
        slope = (raw[3 * depth:4 * depth] + raw[4 * depth:5 * depth]) + raw[5 * depth:6 * depth]
        fields = jnp.concatenate(
            [offset, slope, raw[6 * depth:7 * depth + 2],
             jnp.zeros((16 - 3 * depth - 2, extent), F32)], axis=0)
        fields = pltpu.roll(fields, shift, axis=1)
        lane = lax.broadcasted_iota(I32, fields.shape, 1)
        fields = jnp.where(lane < width, fields, 0.0)
        if lanes > extent:
            fields = jnp.concatenate(
                [fields, jnp.zeros((fields.shape[0], lanes - extent), F32)], axis=1)
        return lined + pltpu.roll(fields, member * width, axis=1)

    lined = jnp.zeros((16, lanes), F32)
    if members <= 16:
        for member in range(members):
            lined = collect(member, lined)
    else:
        lined = lax.fori_loop(0, members, collect, lined)

    slot = lax.broadcasted_iota(I32, (1, lanes), 1)
    within = lax.rem(slot, width)
    target = lax.bitwise_xor(lax.div(within, capacity), parity)
    ray = lined[3 * depth:3 * depth + 1]
    count = lined[3 * depth + 1:3 * depth + 2]
    alive = jnp.logical_and(lax.rem(within, capacity).astype(F32) < count, slot < members * width)

    table = jnp.concatenate(
        [slot.astype(F32), ray, target.astype(F32), lined[2 * depth:3 * depth],
         jnp.zeros((5 - depth, lanes), F32)], axis=0)
    order = lax.broadcasted_iota(I32, (lanes, lanes), 0)
    earlier = (lax.broadcasted_iota(I32, (lanes, lanes), 1) < order).astype(F32)
    for ref, kind, copy in zip(drafts, wanted, copies):
        taken = alive if kind is None else jnp.logical_and(alive, target == kind)
        taken = taken.astype(F32)
        position = contract_lanes(jnp.broadcast_to(taken, (8, lanes)), earlier)[0:1]
        position = jnp.where(taken > 0.0, position, -1.0).astype(I32)
        choose = jnp.broadcast_to(position, (lanes, lanes)) == order
        packed = (contract_lanes(table, choose.astype(F32)) + 0.5).astype(I32)
        total = jnp.sum(taken, axis=1, keepdims=True).astype(I32)
        line = jnp.where(slot < total, packed[0:1], lanes)
        base = packed[1:2] if kind is not None else packed[1:2] + packed[2:3] * ray_tiles
        member = lax.div(packed[0:1], width) * tiles
        rows = [line, base * frames]
        rows += [(packed[3 + level:4 + level] + member) * frames for level in range(depth)]
        rows += [jnp.zeros((5 - depth, lanes), I32), jnp.broadcast_to(total, (1, lanes))]
        ref[...] = jnp.concatenate(rows, axis=0)
        copy.start()

    columns = lined.T
    summed = None
    for level in range(depth):
        offset = columns[:, level:level + 1]
        slope = columns[:, depth + level:depth + level + 1]
        middle, weights = row_taps(offset, slope, extent)
        first, pair = column_taps(offset, slope, extent)
        wide = [weight.astype(F32) for weight in weights]
        values = [middle] + wide + [first] + [weight.astype(F32) for weight in pair]
        at = level * (lanes + 8)
        for ref, value in zip(tables, values):
            ref[at:at + lanes, :] = value
            blank = jnp.ones if ref.dtype == I32 else jnp.zeros
            ref[at + lanes:at + lanes + 8, :] = blank((8, extent), ref.dtype)
        parts = (wide[0] + wide[1]) + wide[2]
        summed = parts if summed is None else summed + parts

    tile = lax.broadcasted_iota(I32, (span * ray_tiles, lanes), 0).astype(F32)
    place = ray + (target * ray_tiles).astype(F32)
    place = jnp.where(alive, place, -1.0)
    hot = (jnp.broadcast_to(place, tile.shape) == tile).astype(F32)
    row_ref[...] = jnp.dot(hot, summed, precision=HIGHEST, preferred_element_type=F32)
    for copy in copies:
        copy.wait()


def column_kernel(sizes, offset_ref, slope_ref, voxel_ref, live_ref, out_ref):
    capacity, depth, frames = sizes
    tiles = out_ref.shape[0] // frames
    slots = offset_ref.shape[1]
    extent = out_ref.shape[1]
    offsets = offset_ref[...].T
    slopes = slope_ref[...].T
    within = lax.rem(lax.broadcasted_iota(I32, (1, slots), 1), capacity).astype(F32)
    alive = jnp.broadcast_to(within, (tiles, slots)) < per_slot(live_ref, slots, capacity)
    total = jnp.zeros((tiles, extent), F32)
    for level in range(depth):
        unused, pair = column_taps(
            offsets[:, level:level + 1], slopes[:, level:level + 1], extent)
        tile_of = jnp.broadcast_to(voxel_ref[level:level + 1, :], (tiles, slots))
        match = tile_of == lax.broadcasted_iota(I32, (tiles, slots), 0)
        hot = jnp.logical_and(match, alive).astype(F32).astype(BF16)
        for weight in pair:
            total += jnp.dot(hot, weight, preferred_element_type=F32)
    out_ref[...] = repeat_rows(1.0 / jnp.maximum(total, 1.0), frames)


def pick(values, index):
    numbers = lax.GatherDimensionNumbers(
        offset_dims=(), collapsed_slice_dims=(1,), start_index_map=(1,),
        operand_batching_dims=(0,), start_indices_batching_dims=(0,))
    return lax.gather(
        values, index[:, :, None], numbers, slice_sizes=(1, 1),
        mode=lax.GatherScatterMode.PROMISE_IN_BOUNDS)


def pack_pair(first, second):
    kind = jnp.int16 if first.dtype == I32 else BF16
    return jnp.concatenate([first, second], axis=0).astype(kind)


def spread(ref, row, frames):
    return jnp.broadcast_to(ref[pl.ds(row, 1), :], (frames, ref.shape[1]))


def tile_at(start, frames):
    return pl.ds(pl.multiple_of(start, frames), frames)


def for_slots(slots, body):
    def some(step, carry):
        for place in range(CHUNK):
            body(step * CHUNK + place, place)
        return carry

    lax.fori_loop(0, lax.div(slots[7, 0] + (CHUNK - 1), CHUNK), some, 0)


def for_rows(rows, body):
    step = 128

    def some(number, carry):
        body(pl.ds(pl.multiple_of(number * step, step), step))
        return carry

    lax.fori_loop(0, rows // step, some, 0)


def forward_kernel(sizes, stride, start_row, n_sums, slots, values_ref, *refs):
    capacity, depth, frames = sizes
    tables, refs = refs[:4], refs[4:]
    start_ref = None
    if start_row is not None:
        start_ref, refs = refs[0], refs[1:]
    sum_refs, (out_ref, wide, second) = refs[:n_sums], refs[n_sums:]
    members = values_ref.shape[0] // stride
    rows = wide.shape[0] // members
    rays = second.shape[0]
    line_step = tables[0].shape[0] // depth

    def widen(member, carry):
        at = pl.ds(pl.multiple_of(member * rows, rows), rows)
        wide[at, :] = values_ref[pl.ds(pl.multiple_of(member * stride, 16), rows), :].astype(F32)
        return carry

    lax.fori_loop(0, members, widen, 0)
    second[...] = jnp.zeros_like(second)
    if start_ref is None:
        out_ref[...] = jnp.zeros_like(out_ref)
    else:
        out_ref[0:rays, :] = start_ref[start_row:start_row + rays, :]
    if n_sums:
        half = sum_refs[0].shape[0] // 2
        out_ref[rays:, :] = sum([ref[half:, :] for ref in sum_refs[1:]], sum_refs[0][half:, :])

    def one(slot, place):
        line = slots[0, slot]
        taps = []
        for start in range(0, depth, 2):
            levels = range(start, start + 2)
            values = [wide[tile_at(slots[2 + level, slot], frames), :] for level in levels]
            middles = [spread(tables[0], line + level * line_step, frames) for level in levels]
            lower = [
                pick(pack_pair(value, value), pack_pair(middle - 1, middle)).astype(F32)
                for value, middle in zip(values, middles)]
            upper = pick(
                pack_pair(*values), pack_pair(*[middle + 1 for middle in middles])).astype(F32)
            for which, pair in enumerate(lower):
                taps.append((pair[0:frames], pair[frames:2 * frames],
                             upper[which * frames:(which + 1) * frames]))
        total = None
        for level, three in enumerate(taps):
            for ref, tap in zip(tables[1:], three):
                term = spread(ref, line + level * line_step, frames) * tap
                total = term if total is None else total + term
        projection = (out_ref, second)[place % 2]
        projection[tile_at(slots[1, slot], frames), :] += total.astype(BF16).astype(F32)

    for_slots(slots, one)
    out_ref[0:rays, :] += second[...]


def residual_kernel(frames, n_own, projection_ref, sinogram_ref, *refs):
    own, refs, out_ref = refs[:n_own], refs[n_own:-1], refs[-1]
    rays = out_ref.shape[0]
    ray_tiles = rays // frames
    total = sum([ref[0:ray_tiles, :] for ref in own[1:]], own[0][0:ray_tiles, :])
    projection = projection_ref[...]
    if refs:
        projection = projection + refs[0][0:rays, :]
        total = total + refs[-1][rays:, :]
    weight = repeat_rows(1.0 / jnp.maximum(total, 1.0), frames)
    out_ref[...] = ((sinogram_ref[...].astype(F32) - projection) * weight).astype(BF16)


def backward_kernel(sizes, n_parts, has_start, slots, *refs):
    capacity, depth, frames = sizes
    part_refs, tables, refs = refs[:n_parts], refs[n_parts:n_parts + 3], refs[n_parts + 3:]
    start_ref = None
    if has_start:
        start_ref, refs = refs[0], refs[1:]
    out_ref, residual, banks = refs[0], refs[1], refs[2:]
    rays = part_refs[0].shape[0]
    line_step = tables[0].shape[0] // depth
    for place, ref in enumerate(part_refs):
        residual[place * rays:(place + 1) * rays, :] = ref[...].astype(F32)

    def clear(at):
        for place, bank in enumerate(banks):
            if place == 0 and has_start:
                bank[at, :] = start_ref[at, :]
            else:
                bank[at, :] = jnp.zeros((at.size, bank.shape[1]), F32)

    for_rows(out_ref.shape[0], clear)

    def one(slot, place):
        line = slots[0, slot]
        values = residual[tile_at(slots[1, slot], frames), :]
        twice = pack_pair(values, values)
        for level in range(depth):
            row = line + level * line_step
            first = spread(tables[0], row, frames)
            taps = pick(twice, pack_pair(first, first + 1)).astype(F32)
            term = (spread(tables[1], row, frames) * taps[0:frames]
                    + spread(tables[2], row, frames) * taps[frames:2 * frames])
            banks[level % len(banks)][tile_at(slots[2 + level, slot], frames), :] += term

    for_slots(slots, one)

    def finish(at):
        total = sum([bank[at, :] for bank in banks[1:]], banks[0][at, :])
        out_ref[at, :] = total.astype(out_ref.dtype)

    for_rows(out_ref.shape[0], finish)


def join_kernel(*refs):
    out_ref, at = refs[-1], 0
    for ref in refs[:-1]:
        out_ref[at:at + ref.shape[0], :] = ref[...]
        at += ref.shape[0]


def combine_kernel(sum_ref, y_ref, own_ref, *piece_refs):
    rows = own_ref.shape[0]
    for place, ref in enumerate((own_ref,) + piece_refs):
        at = pl.ds(place * rows, rows)
        ref[...] = (sum_ref[at, :] + y_ref[at, :].astype(F32)).astype(ref.dtype)


def update_kernel(n_pieces, volume_ref, column_ref, *refs):
    back = refs[0][...]
    for ref in refs[1:n_pieces]:
        back = back + ref[...].astype(F32)
    volume = volume_ref[...] + column_ref[...] * back
    for ref in refs[n_pieces:]:
        ref[...] = volume.astype(ref.dtype)


def call(kernel, name, mib, in_specs, out_shape, *operands, scratch=()):
    one = not isinstance(out_shape, list)
    return pl.pallas_call(
        kernel,
        out_shape=out_shape,
        in_specs=in_specs,
        out_specs=VMEM if one else [
            SMEM if getattr(out, "memory_space", None) == pltpu.SMEM else VMEM for out in out_shape],
        scratch_shapes=list(scratch),
        compiler_params=pltpu.CompilerParams(vmem_limit_bytes=mib * 1024 * 1024),
        name=name,
    )(*operands)


def exchange(values, n_slab, distance):
    return lax.ppermute(
        values, "slab", [(device, device ^ distance) for device in range(n_slab)])


def shards(sinogram, start_volume, slot_voxel, slot_ray, live_count, block_slope, block_offset):
    n_slab = lax.axis_size("slab")
    n_slots, depth = slot_voxel.shape
    capacity = n_slots // n_slab
    ray_tiles, frames, extent = sinogram.shape
    voxel_tiles = start_volume.shape[0]
    rows = voxel_tiles * frames
    sizes = (capacity, depth, frames)
    paired = n_slab == 16
    span = 2 if paired else 1
    n_bank = 2 if paired else 1
    shape = jax.ShapeDtypeStruct
    n_rays = ray_tiles * frames
    volume = start_volume.reshape(rows, extent)
    sino = sinogram.reshape(n_rays, extent)
    slots_by_depth = (block_offset.T, block_slope.T, slot_voxel.T)
    live = live_count.reshape(1, n_slab)
    height = -(-(7 * depth + 2) // 16) * 16 * (n_slots // extent)
    operands = (volume, *slots_by_depth, slot_ray.reshape(1, n_slots), live)
    payload = call(
        functools.partial(pack_kernel, capacity), "pack", 16, [HBM] * 6,
        shape((rows + height, extent), BF16),
        *[pltpu.with_memory_space_constraint(operand, pltpu.HBM) for operand in operands],
        scratch=[pltpu.VMEM(operand.shape, operand.dtype) for operand in operands]
        + [pltpu.SemaphoreType.DMA((6,))])

    def setup(values, members, wanted, after=None):
        lanes = -(-members * span * capacity // 128) * 128
        lines = depth * (lanes + 8)
        table = [shape((lines, extent), I32)] + [shape((lines, extent), F32)] * 3
        table += [shape((lines, extent), I32)] + [shape((lines, extent), F32)] * 2
        n = len(wanted)
        out = [pltpu.SMEM((8, lanes), I32)] * n + [shape((span * ray_tiles, extent), F32)] + table
        waits = [] if after is None else [after]
        found = call(
            functools.partial(setup_kernel, members, values.shape[0] // members, span, sizes,
                              voxel_tiles, wanted),
            "setup", 24, [VMEM] + [ANY] * len(waits), out, values, *waits,
            scratch=[pltpu.VMEM((8, lanes), I32)] * n + [pltpu.SemaphoreType.DMA((n,))])
        return found[:n], found[n], found[n + 1:n + 5], found[n + 5:]

    def forward(slots, values, members, table, n_out, start=None, start_row=None, sums=()):
        operands = [pltpu.with_memory_space_constraint(slots, pltpu.SMEM), values, *table] + ([] if start is None else [start]) + list(sums)
        extra = ray_tiles if sums else 0
        return call(
            functools.partial(forward_kernel, sizes, values.shape[0] // members, start_row, len(sums)),
            "forward", 16 if paired else 32, [SMEM] + [VMEM] * (len(operands) - 1),
            shape((n_out + extra, extent), F32), *operands,
            scratch=[pltpu.VMEM((members * rows, extent), F32), pltpu.VMEM((n_out, extent), F32)])

    def residual_of(projection, row_sums, *sibling):
        operands = [projection, sino, *row_sums, *sibling]
        return call(
            functools.partial(residual_kernel, frames, len(row_sums)), "residual", 16,
            [VMEM] * len(operands), shape((n_rays, extent), BF16), *operands)

    def backward(slots, parts, members, table, kind, start=None):
        operands = [pltpu.with_memory_space_constraint(slots, pltpu.SMEM), *parts, *table] + ([] if start is None else [start])
        return call(
            functools.partial(backward_kernel, sizes, len(parts), start is not None),
            "backward", 16 if paired else 32, [SMEM] + [VMEM] * (len(operands) - 1),
            shape((members * rows, extent), kind), *operands,
            scratch=[pltpu.VMEM((len(parts) * n_rays, extent), F32)]
            + [pltpu.VMEM((members * rows, extent), F32)] * n_bank)

    def join(*parts):
        total = sum(part.shape[0] for part in parts)
        return call(join_kernel, "join", 16, [VMEM] * len(parts), shape((total, extent), BF16), *parts)

    def update(volume, pieces, last):
        out = [shape((rows, extent), F32)] + ([] if last else [shape((rows, extent), BF16)])
        return call(
            functools.partial(update_kernel, len(pieces)), "update", 16,
            [VMEM] * (2 + len(pieces)), out, volume, column_weight, *pieces)

    column_weight = call(
        functools.partial(column_kernel, sizes), "column_weight", 16, [VMEM] * 4,
        shape((rows, extent), F32), *slots_by_depth, live)

    for sweep in range(ITERS):
        last = sweep + 1 == ITERS
        if paired:
            along_z = join(
                payload, *[exchange(payload, n_slab, distance) for distance in (8, 12, 4)])
            along_y = exchange(along_z, n_slab, 2)
            if sweep == 0:
                (z_list,), z_rows, z_forward, z_backward = setup(along_z, 4, (None,))
            both = forward(z_list, along_z, 4, z_forward, 2 * n_rays)
            if sweep == 0:
                (own_list, other_list), y_rows, y_forward, y_backward = setup(
                    along_y, 4, (0, 1), after=both)
            other = exchange(
                forward(other_list, along_y, 4, y_forward, n_rays, both, n_rays,
                        (z_rows, y_rows) if sweep == 0 else ()), n_slab, 1)
            if sweep == 0:
                first_other = other
            own = forward(own_list, along_y, 4, y_forward, n_rays, both, 0)
            residual = residual_of(own, (z_rows, y_rows), other, first_other)
            other_residual = exchange(residual, n_slab, 1)
            y_sum = backward(own_list, [residual], 4, y_backward, F32)
            y_sum = backward(other_list, [other_residual], 4, y_backward, BF16, y_sum)
            y_part = exchange(y_sum, n_slab, 2)
            z_sum = backward(z_list, [residual, other_residual], 4, z_backward, F32)
            own_piece, *pieces = call(
                combine_kernel, "combine", 16, [VMEM] * 2,
                [shape((rows, extent), F32)] + [shape((rows, extent), BF16)] * 3, z_sum, y_part)
            pieces = [own_piece] + [
                exchange(piece, n_slab, distance) for piece, distance in zip(pieces, (8, 12, 4))]
        else:
            everyone = lax.all_gather(payload, "slab", axis=0, tiled=True)
            if sweep == 0:
                (slots,), row_sums, to_rays, to_voxels = setup(everyone, n_slab, (None,))
            projection = forward(slots, everyone, n_slab, to_rays, n_rays)
            residual = residual_of(projection, (row_sums,))
            sums = backward(slots, [residual], n_slab, to_voxels, BF16)
            parts = lax.all_to_all(
                sums.reshape(n_slab, rows, extent), "slab", split_axis=0, concat_axis=0, tiled=True)
            pieces = [jnp.sum(parts.astype(F32), axis=0)]
        volume, *rounded = update(volume, pieces, last)
        if not last:
            payload = rounded[0]
    return volume.reshape(start_volume.shape)


def solution(mesh):
    in_specs = (
        P(("scan", "slab"), None, None),
        P(("scan", "slab"), None, None),
        P(("scan", "slab"), None),
        P(("scan", "slab")),
        P(("scan", "slab")),
        P(("scan", "slab"), None),
        P(("scan", "slab"), None),
    )
    out_specs = P(("scan", "slab"), None, None)
    return jax.shard_map(shards, mesh=mesh, in_specs=in_specs, out_specs=out_specs, check_vma=False)
```

```python
import functools

import jax
import jax.numpy as jnp
from jax import lax
from jax.experimental import pallas as pl
from jax.experimental.pallas import tpu as pltpu
from jax.sharding import PartitionSpec as P

ITERS = 2
CHUNK = 8
F32 = jnp.float32
BF16 = jnp.bfloat16
I32 = jnp.int32
HIGHEST = lax.Precision.HIGHEST
VMEM = pl.BlockSpec(memory_space=pltpu.VMEM)
ANY = pl.BlockSpec(memory_space=pl.ANY)
SMEM = pl.BlockSpec(memory_space=pltpu.SMEM)
HBM = pl.BlockSpec(memory_space=pltpu.HBM)


def hat(ray, centre):
    return jnp.maximum(0.0, 1.0 - jnp.abs(ray - centre)).astype(BF16)


def row_taps(offset, slope, extent):
    shape = (offset.shape[0], extent)
    ray = lax.broadcasted_iota(I32, shape, 1).astype(F32)
    offset = jnp.broadcast_to(offset, shape)
    slope = jnp.broadcast_to(slope, shape)
    middle = jnp.floor((ray - offset) / slope + 0.5)
    middle = jnp.minimum(jnp.maximum(middle, 1.0), extent - 2.0)
    weights = [hat(ray, offset + slope * (middle + step)) for step in (-1.0, 0.0, 1.0)]
    return middle.astype(I32), weights


def column_taps(offset, slope, extent):
    shape = (offset.shape[0], extent)
    voxel = lax.broadcasted_iota(I32, shape, 1).astype(F32)
    centre = jnp.broadcast_to(offset, shape) + jnp.broadcast_to(slope, shape) * voxel
    first = jnp.minimum(jnp.maximum(jnp.floor(centre), 0.0), extent - 2.0)
    weights = [hat(first + step, centre) for step in (0.0, 1.0)]
    return first.astype(I32), weights


def repeat_rows(values, times):
    return jnp.concatenate(
        [jnp.broadcast_to(values[row:row + 1, :], (times, values.shape[1]))
         for row in range(values.shape[0])], axis=0)


def contract_lanes(left, right):
    return lax.dot_general(
        left.astype(BF16), right.astype(BF16), (((1,), (1,)), ((), ())), preferred_element_type=F32)


def per_slot(live_ref, slots, capacity):
    targets = live_ref.shape[1]
    slot = lax.broadcasted_iota(I32, (targets, slots), 1)
    owner = lax.broadcasted_iota(I32, (targets, slots), 0)
    expand = (lax.div(slot, capacity) == owner).astype(F32)
    return jnp.dot(live_ref[...].astype(F32), expand, precision=HIGHEST, preferred_element_type=F32)


def pack_kernel(capacity, *refs):
    sources, out_ref, loaded, arrived = refs[:6], refs[6], refs[7:13], refs[13]
    copies = [
        pltpu.make_async_copy(source, ref, arrived.at[place])
        for place, (source, ref) in enumerate(zip(sources, loaded))]
    for copy in copies:
        copy.start()
    for copy in copies:
        copy.wait()
    volume_ref, offset_ref, slope_ref, voxel_ref, ray_ref, live_ref = loaded
    rows, extent = volume_ref.shape
    out_ref[0:rows, :] = volume_ref[...].astype(BF16)
    slots = ray_ref.shape[1]
    fields = []
    for ref in (offset_ref, slope_ref):
        left = ref[...]
        for addend in range(3):
            part = left.astype(BF16).astype(F32)
            fields.append(part)
            left = left - part
    fields.append(voxel_ref[...].astype(F32))
    fields.append(ray_ref[...].astype(F32))
    fields.append(per_slot(live_ref, slots, capacity))
    used = sum(field.shape[0] for field in fields)
    fields.append(jnp.zeros((-used % 16, slots), F32))
    fields = jnp.concatenate(fields, axis=0)
    height = fields.shape[0]
    for part in range(slots // extent):
        at = pl.ds(rows + part * height, height)
        out_ref[at, :] = fields[:, part * extent:(part + 1) * extent].astype(BF16)


def setup_kernel(n_payloads, members, stride, span, sizes, tiles, wanted, *refs):
    payload_refs, refs = refs[:n_payloads], refs[-(2 * len(wanted) + 9):]
    each = members // n_payloads
    list_refs, row_ref, tables = refs[:len(wanted)], refs[len(wanted)], refs[len(wanted) + 1:-len(wanted) - 1]
    drafts, arrived = refs[-len(wanted) - 1:-1], refs[-1]
    copies = [
        pltpu.make_async_copy(draft, ref, arrived.at[place])
        for place, (draft, ref) in enumerate(zip(drafts, list_refs))]
    capacity, depth, frames = sizes
    width = span * capacity
    extent = row_ref.shape[1]
    ray_tiles = row_ref.shape[0] // span
    height = -(-(7 * depth + 2) // 16) * 16
    lanes = drafts[0].shape[1]
    me = lax.axis_index("slab").astype(I32)
    parity = lax.rem(me, span)
    first_slot = (me - parity) * capacity
    part = lax.div(first_slot, extent)
    shift = lax.rem(extent - lax.rem(first_slot, extent), extent)

    def collect(member, lined, payload_ref, within):
        at = within * stride + tiles * frames + part * height
        raw = payload_ref[pl.ds(pl.multiple_of(at, 16), height), :].astype(F32)
        offset = (raw[0:depth] + raw[depth:2 * depth]) + raw[2 * depth:3 * depth]
        slope = (raw[3 * depth:4 * depth] + raw[4 * depth:5 * depth]) + raw[5 * depth:6 * depth]
        fields = jnp.concatenate(
            [offset, slope, raw[6 * depth:7 * depth + 2],
             jnp.zeros((16 - 3 * depth - 2, extent), F32)], axis=0)
        fields = pltpu.roll(fields, shift, axis=1)
        lane = lax.broadcasted_iota(I32, fields.shape, 1)
        fields = jnp.where(lane < width, fields, 0.0)
        if lanes > extent:
            fields = jnp.concatenate(
                [fields, jnp.zeros((fields.shape[0], lanes - extent), F32)], axis=1)
        return lined + pltpu.roll(fields, member * width, axis=1)

    lined = jnp.zeros((16, lanes), F32)
    if members <= 16:
        for member in range(members):
            lined = collect(member, lined, payload_refs[member // each], member % each)
    else:
        lined = lax.fori_loop(
            0, members, lambda member, lined: collect(member, lined, payload_refs[0], member), lined)

    slot = lax.broadcasted_iota(I32, (1, lanes), 1)
    within = lax.rem(slot, width)
    target = lax.bitwise_xor(lax.div(within, capacity), parity)
    ray = lined[3 * depth:3 * depth + 1]
    count = lined[3 * depth + 1:3 * depth + 2]
    alive = jnp.logical_and(lax.rem(within, capacity).astype(F32) < count, slot < members * width)

    table = jnp.concatenate(
        [slot.astype(F32), ray, target.astype(F32), lined[2 * depth:3 * depth],
         jnp.zeros((5 - depth, lanes), F32)], axis=0)
    order = lax.broadcasted_iota(I32, (lanes, lanes), 0)
    earlier = (lax.broadcasted_iota(I32, (lanes, lanes), 1) < order).astype(F32)
    for ref, kind, copy in zip(drafts, wanted, copies):
        taken = alive if kind is None else jnp.logical_and(alive, target == kind)
        taken = taken.astype(F32)
        position = contract_lanes(jnp.broadcast_to(taken, (8, lanes)), earlier)[0:1]
        position = jnp.where(taken > 0.0, position, -1.0).astype(I32)
        choose = jnp.broadcast_to(position, (lanes, lanes)) == order
        packed = (contract_lanes(table, choose.astype(F32)) + 0.5).astype(I32)
        total = jnp.sum(taken, axis=1, keepdims=True).astype(I32)
        line = jnp.where(slot < total, packed[0:1], lanes)
        base = packed[1:2] if kind is not None else packed[1:2] + packed[2:3] * ray_tiles
        member = lax.div(packed[0:1], width) * tiles
        rows = [line, base * frames]
        rows += [(packed[3 + level:4 + level] + member) * frames for level in range(depth)]
        rows += [jnp.zeros((5 - depth, lanes), I32), jnp.broadcast_to(total, (1, lanes))]
        ref[...] = jnp.concatenate(rows, axis=0)
        copy.start()

    columns = lined.T
    summed = None
    for level in range(depth):
        offset = columns[:, level:level + 1]
        slope = columns[:, depth + level:depth + level + 1]
        middle, weights = row_taps(offset, slope, extent)
        first, pair = column_taps(offset, slope, extent)
        wide = [weight.astype(F32) for weight in weights]
        values = [middle] + wide + [first] + [weight.astype(F32) for weight in pair]
        at = level * (lanes + 8)
        for ref, value in zip(tables, values):
            ref[at:at + lanes, :] = value
            blank = jnp.ones if ref.dtype == I32 else jnp.zeros
            ref[at + lanes:at + lanes + 8, :] = blank((8, extent), ref.dtype)
        parts = (wide[0] + wide[1]) + wide[2]
        summed = parts if summed is None else summed + parts

    tile = lax.broadcasted_iota(I32, (span * ray_tiles, lanes), 0).astype(F32)
    place = ray + (target * ray_tiles).astype(F32)
    place = jnp.where(alive, place, -1.0)
    hot = (jnp.broadcast_to(place, tile.shape) == tile).astype(F32)
    row_ref[...] = jnp.dot(hot, summed, precision=HIGHEST, preferred_element_type=F32)
    for copy in copies:
        copy.wait()


def column_kernel(sizes, offset_ref, slope_ref, voxel_ref, live_ref, out_ref):
    capacity, depth, frames = sizes
    tiles = out_ref.shape[0] // frames
    slots = offset_ref.shape[1]
    extent = out_ref.shape[1]
    offsets = offset_ref[...].T
    slopes = slope_ref[...].T
    within = lax.rem(lax.broadcasted_iota(I32, (1, slots), 1), capacity).astype(F32)
    alive = jnp.broadcast_to(within, (tiles, slots)) < per_slot(live_ref, slots, capacity)
    total = jnp.zeros((tiles, extent), F32)
    for level in range(depth):
        unused, pair = column_taps(
            offsets[:, level:level + 1], slopes[:, level:level + 1], extent)
        tile_of = jnp.broadcast_to(voxel_ref[level:level + 1, :], (tiles, slots))
        match = tile_of == lax.broadcasted_iota(I32, (tiles, slots), 0)
        hot = jnp.logical_and(match, alive).astype(F32).astype(BF16)
        for weight in pair:
            total += jnp.dot(hot, weight, preferred_element_type=F32)
    out_ref[...] = repeat_rows(1.0 / jnp.maximum(total, 1.0), frames)


def pick(values, index):
    numbers = lax.GatherDimensionNumbers(
        offset_dims=(), collapsed_slice_dims=(1,), start_index_map=(1,),
        operand_batching_dims=(0,), start_indices_batching_dims=(0,))
    return lax.gather(
        values, index[:, :, None], numbers, slice_sizes=(1, 1),
        mode=lax.GatherScatterMode.PROMISE_IN_BOUNDS)


def pack_pair(first, second):
    kind = jnp.int16 if first.dtype == I32 else BF16
    return jnp.concatenate([first, second], axis=0).astype(kind)


def spread(ref, row, frames):
    return jnp.broadcast_to(ref[pl.ds(row, 1), :], (frames, ref.shape[1]))


def tile_at(start, frames):
    return pl.ds(pl.multiple_of(start, frames), frames)


def for_slots(slots, body):
    def some(step, carry):
        for place in range(CHUNK):
            body(step * CHUNK + place, place)
        return carry

    lax.fori_loop(0, lax.div(slots[7, 0] + (CHUNK - 1), CHUNK), some, 0)


def for_rows(rows, body):
    step = 128

    def some(number, carry):
        body(pl.ds(pl.multiple_of(number * step, step), step))
        return carry

    lax.fori_loop(0, rows // step, some, 0)


def forward_kernel(sizes, n_values, members, start_row, n_sums, slots, *refs):
    capacity, depth, frames = sizes
    value_refs, tables, refs = refs[:n_values], refs[n_values:n_values + 4], refs[n_values + 4:]
    start_ref = None
    if start_row is not None:
        start_ref, refs = refs[0], refs[1:]
    sum_refs, (out_ref, wide, second) = refs[:n_sums], refs[n_sums:]
    rows = wide.shape[0] // members
    each = members // n_values
    stride = value_refs[0].shape[0] // each
    rays = second.shape[0]
    line_step = tables[0].shape[0] // depth

    def widen(member, carry):
        for place, ref in enumerate(value_refs):
            at = pl.ds(pl.multiple_of((place * each + member) * rows, rows), rows)
            wide[at, :] = ref[pl.ds(pl.multiple_of(member * stride, 16), rows), :].astype(F32)
        return carry

    lax.fori_loop(0, each, widen, 0)
    second[...] = jnp.zeros_like(second)
    if start_ref is None:
        out_ref[...] = jnp.zeros_like(out_ref)
    else:
        out_ref[0:rays, :] = start_ref[start_row:start_row + rays, :]
    if n_sums:
        half = sum_refs[0].shape[0] // 2
        out_ref[rays:, :] = sum([ref[half:, :] for ref in sum_refs[1:]], sum_refs[0][half:, :])

    def one(slot, place):
        line = slots[0, slot]
        taps = []
        for start in range(0, depth, 2):
            levels = range(start, start + 2)
            values = [wide[tile_at(slots[2 + level, slot], frames), :] for level in levels]
            middles = [spread(tables[0], line + level * line_step, frames) for level in levels]
            lower = [
                pick(pack_pair(value, value), pack_pair(middle - 1, middle)).astype(F32)
                for value, middle in zip(values, middles)]
            upper = pick(
                pack_pair(*values), pack_pair(*[middle + 1 for middle in middles])).astype(F32)
            for which, pair in enumerate(lower):
                taps.append((pair[0:frames], pair[frames:2 * frames],
                             upper[which * frames:(which + 1) * frames]))
        total = None
        for level, three in enumerate(taps):
            for ref, tap in zip(tables[1:], three):
                term = spread(ref, line + level * line_step, frames) * tap
                total = term if total is None else total + term
        projection = (out_ref, second)[place % 2]
        projection[tile_at(slots[1, slot], frames), :] += total.astype(BF16).astype(F32)

    for_slots(slots, one)
    out_ref[0:rays, :] += second[...]


def residual_kernel(frames, n_own, projection_ref, sinogram_ref, *refs):
    own, refs, out_ref = refs[:n_own], refs[n_own:-1], refs[-1]
    rays = out_ref.shape[0]
    ray_tiles = rays // frames
    total = sum([ref[0:ray_tiles, :] for ref in own[1:]], own[0][0:ray_tiles, :])
    projection = projection_ref[...]
    if refs:
        projection = projection + refs[0][0:rays, :]
        total = total + refs[-1][rays:, :]
    weight = repeat_rows(1.0 / jnp.maximum(total, 1.0), frames)
    out_ref[...] = ((sinogram_ref[...].astype(F32) - projection) * weight).astype(BF16)


def backward_kernel(sizes, n_parts, has_start, split, slots, *refs):
    capacity, depth, frames = sizes
    part_refs, tables, refs = refs[:n_parts], refs[n_parts:n_parts + 3], refs[n_parts + 3:]
    start_ref = None
    if has_start:
        start_ref, refs = refs[0], refs[1:]
    outs = refs[:len(split)] if split else refs[:1]
    residual, banks = refs[len(outs)], refs[len(outs) + 1:]
    rays = part_refs[0].shape[0]
    line_step = tables[0].shape[0] // depth
    for place, ref in enumerate(part_refs):
        residual[place * rays:(place + 1) * rays, :] = ref[...].astype(F32)

    def clear(at):
        for place, bank in enumerate(banks):
            if place == 0 and has_start:
                bank[at, :] = start_ref[at, :]
            else:
                bank[at, :] = jnp.zeros((at.size, bank.shape[1]), F32)

    for_rows(banks[0].shape[0], clear)

    def one(slot, place):
        line = slots[0, slot]
        values = residual[tile_at(slots[1, slot], frames), :]
        twice = pack_pair(values, values)
        for level in range(depth):
            row = line + level * line_step
            first = spread(tables[0], row, frames)
            taps = pick(twice, pack_pair(first, first + 1)).astype(F32)
            term = (spread(tables[1], row, frames) * taps[0:frames]
                    + spread(tables[2], row, frames) * taps[frames:2 * frames])
            banks[level % len(banks)][tile_at(slots[2 + level, slot], frames), :] += term

    for_slots(slots, one)

    def total(at):
        return sum([bank[at, :] for bank in banks[1:]], banks[0][at, :]).astype(outs[0].dtype)

    if split:
        for ref, members in zip(outs, split):
            rows = ref.shape[0] // len(members)
            for place, member in enumerate(members):
                ref[place * rows:(place + 1) * rows, :] = total(pl.ds(member * rows, rows))
    else:
        def finish(at):
            outs[0][at, :] = total(at)

        for_rows(outs[0].shape[0], finish)


def join_kernel(*refs):
    out_ref, at = refs[-1], 0
    for ref in refs[:-1]:
        out_ref[at:at + ref.shape[0], :] = ref[...]
        at += ref.shape[0]


def combine_kernel(members, sum_ref, y_ref, *piece_refs):
    rows = piece_refs[0].shape[0]
    for place, (member, ref) in enumerate(zip(members, piece_refs)):
        mine = sum_ref[member * rows:(member + 1) * rows, :]
        ref[...] = (mine + y_ref[place * rows:(place + 1) * rows, :].astype(F32)).astype(ref.dtype)


def update_kernel(n_pieces, volume_ref, column_ref, *refs):
    back = refs[0][...]
    for ref in refs[1:n_pieces]:
        back = back + ref[...].astype(F32)
    volume = volume_ref[...] + column_ref[...] * back
    for ref in refs[n_pieces:]:
        ref[...] = volume.astype(ref.dtype)


def call(kernel, name, mib, in_specs, out_shape, *operands, scratch=()):
    one = not isinstance(out_shape, list)
    return pl.pallas_call(
        kernel,
        out_shape=out_shape,
        in_specs=in_specs,
        out_specs=VMEM if one else [
            SMEM if getattr(out, "memory_space", None) == pltpu.SMEM else VMEM for out in out_shape],
        scratch_shapes=list(scratch),
        compiler_params=pltpu.CompilerParams(vmem_limit_bytes=mib * 1024 * 1024),
        name=name,
    )(*operands)


def exchange(values, n_slab, distance):
    return lax.ppermute(
        values, "slab", [(device, device ^ distance) for device in range(n_slab)])


def shards(sinogram, start_volume, slot_voxel, slot_ray, live_count, block_slope, block_offset):
    n_slab = lax.axis_size("slab")
    n_slots, depth = slot_voxel.shape
    capacity = n_slots // n_slab
    ray_tiles, frames, extent = sinogram.shape
    voxel_tiles = start_volume.shape[0]
    rows = voxel_tiles * frames
    sizes = (capacity, depth, frames)
    paired = n_slab == 16
    span = 2 if paired else 1
    n_bank = 2 if paired else 1
    shape = jax.ShapeDtypeStruct
    n_rays = ray_tiles * frames
    volume = start_volume.reshape(rows, extent)
    sino = sinogram.reshape(n_rays, extent)
    slots_by_depth = (block_offset.T, block_slope.T, slot_voxel.T)
    live = live_count.reshape(1, n_slab)
    height = -(-(7 * depth + 2) // 16) * 16 * (n_slots // extent)
    operands = (volume, *slots_by_depth, slot_ray.reshape(1, n_slots), live)
    payload = call(
        functools.partial(pack_kernel, capacity), "pack", 16, [HBM] * 6,
        shape((rows + height, extent), BF16),
        *[pltpu.with_memory_space_constraint(operand, pltpu.HBM) for operand in operands],
        scratch=[pltpu.VMEM(operand.shape, operand.dtype) for operand in operands]
        + [pltpu.SemaphoreType.DMA((6,))])

    def setup(payloads, members, wanted, after=None):
        lanes = -(-members * span * capacity // 128) * 128
        lines = depth * (lanes + 8)
        table = [shape((lines, extent), I32)] + [shape((lines, extent), F32)] * 3
        table += [shape((lines, extent), I32)] + [shape((lines, extent), F32)] * 2
        n = len(wanted)
        out = [pltpu.SMEM((8, lanes), I32)] * n + [shape((span * ray_tiles, extent), F32)] + table
        waits = [] if after is None else [after]
        found = call(
            functools.partial(setup_kernel, len(payloads), members,
                              payloads[0].shape[0] * len(payloads) // members, span, sizes,
                              voxel_tiles, wanted),
            "setup", 24, [VMEM] * len(payloads) + [ANY] * len(waits), out, *payloads, *waits,
            scratch=[pltpu.VMEM((8, lanes), I32)] * n + [pltpu.SemaphoreType.DMA((n,))])
        return found[:n], found[n], found[n + 1:n + 5], found[n + 5:]

    def forward(slots, values, members, table, n_out, start=None, start_row=None, sums=()):
        operands = [pltpu.with_memory_space_constraint(slots, pltpu.SMEM), *values, *table] + ([] if start is None else [start]) + list(sums)
        extra = ray_tiles if sums else 0
        return call(
            functools.partial(forward_kernel, sizes, len(values), members, start_row, len(sums)),
            "forward", 16 if paired else 32, [SMEM] + [VMEM] * (len(operands) - 1),
            shape((n_out + extra, extent), F32), *operands,
            scratch=[pltpu.VMEM((members * rows, extent), F32), pltpu.VMEM((n_out, extent), F32)])

    def residual_of(projection, row_sums, *sibling):
        operands = [projection, sino, *row_sums, *sibling]
        return call(
            functools.partial(residual_kernel, frames, len(row_sums)), "residual", 16,
            [VMEM] * len(operands), shape((n_rays, extent), BF16), *operands)

    def backward(slots, parts, members, table, kind, start=None, split=()):
        operands = [pltpu.with_memory_space_constraint(slots, pltpu.SMEM), *parts, *table] + ([] if start is None else [start])
        return call(
            functools.partial(backward_kernel, sizes, len(parts), start is not None, split),
            "backward", 16 if paired else 32, [SMEM] + [VMEM] * (len(operands) - 1),
            [shape((len(some) * rows, extent), kind) for some in split]
            if split else shape((members * rows, extent), kind), *operands,
            scratch=[pltpu.VMEM((len(parts) * n_rays, extent), F32)]
            + [pltpu.VMEM((members * rows, extent), F32)] * n_bank)

    def join(*parts):
        total = sum(part.shape[0] for part in parts)
        return call(join_kernel, "join", 16, [VMEM] * len(parts), shape((total, extent), BF16), *parts)

    def update(volume, pieces, last):
        out = [shape((rows, extent), F32)] + ([] if last else [shape((rows, extent), BF16)])
        return call(
            functools.partial(update_kernel, len(pieces)), "update", 16,
            [VMEM] * (2 + len(pieces)), out, volume, column_weight, *pieces)

    column_weight = call(
        functools.partial(column_kernel, sizes), "column_weight", 16, [VMEM] * 4,
        shape((rows, extent), F32), *slots_by_depth, live)

    for sweep in range(ITERS):
        last = sweep + 1 == ITERS
        if paired:
            over_2, over_3, over_1 = [
                exchange(payload, n_slab, distance) for distance in (8, 12, 4)]
            z_half = join(payload, over_2)
            y_half = exchange(z_half, n_slab, 2)
            z_rest = join(over_3, over_1)
            y_rest = exchange(z_rest, n_slab, 2)
            along_z, along_y = (z_half, z_rest), (y_half, y_rest)
            if sweep == 0:
                (z_list,), z_rows, z_forward, z_backward = setup(along_z, 4, (None,))
            both = forward(z_list, along_z, 4, z_forward, 2 * n_rays)
            if sweep == 0:
                (own_list, other_list), y_rows, y_forward, y_backward = setup(
                    along_y, 4, (0, 1), after=both)
            other = exchange(
                forward(other_list, along_y, 4, y_forward, n_rays, both, n_rays,
                        (z_rows, y_rows) if sweep == 0 else ()), n_slab, 1)
            if sweep == 0:
                first_other = other
            own = forward(own_list, along_y, 4, y_forward, n_rays, both, 0)
            residual = residual_of(own, (z_rows, y_rows), other, first_other)
            other_residual = exchange(residual, n_slab, 1)
            y_sum = backward(own_list, [residual], 4, y_backward, F32)
            far_sum, near_sum = backward(
                other_list, [other_residual], 4, y_backward, BF16, y_sum, ((1, 2), (0, 3)))
            far_part, near_part = exchange(far_sum, n_slab, 2), exchange(near_sum, n_slab, 2)
            z_sum = backward(z_list, [residual, other_residual], 4, z_backward, F32)
            piece = shape((rows, extent), BF16)
            piece_2, piece_3 = call(
                functools.partial(combine_kernel, (1, 2)), "combine", 16, [VMEM] * 2,
                [piece, piece], z_sum, far_part)
            got = [exchange(piece_2, n_slab, 8), exchange(piece_3, n_slab, 12)]
            own_piece, piece_1 = call(
                functools.partial(combine_kernel, (0, 3)), "combine", 16, [VMEM] * 2,
                [shape((rows, extent), F32), piece], z_sum, near_part)
            pieces = [own_piece, *got, exchange(piece_1, n_slab, 4)]
        else:
            everyone = lax.all_gather(payload, "slab", axis=0, tiled=True)
            if sweep == 0:
                (slots,), row_sums, to_rays, to_voxels = setup((everyone,), n_slab, (None,))
            projection = forward(slots, (everyone,), n_slab, to_rays, n_rays)
            residual = residual_of(projection, (row_sums,))
            sums = backward(slots, [residual], n_slab, to_voxels, BF16)
            parts = lax.all_to_all(
                sums.reshape(n_slab, rows, extent), "slab", split_axis=0, concat_axis=0, tiled=True)
            pieces = [jnp.sum(parts.astype(F32), axis=0)]
        volume, *rounded = update(volume, pieces, last)
        if not last:
            payload = rounded[0]
    return volume.reshape(start_volume.shape)


def solution(mesh):
    in_specs = (
        P(("scan", "slab"), None, None),
        P(("scan", "slab"), None, None),
        P(("scan", "slab"), None),
        P(("scan", "slab")),
        P(("scan", "slab")),
        P(("scan", "slab"), None),
        P(("scan", "slab"), None),
    )
    out_specs = P(("scan", "slab"), None, None)
    return jax.shard_map(shards, mesh=mesh, in_specs=in_specs, out_specs=out_specs, check_vma=False)
```

```python
import functools

import jax
import jax.numpy as jnp
from jax import lax
from jax.experimental import pallas as pl
from jax.experimental.pallas import tpu as pltpu
from jax.sharding import PartitionSpec as P

ITERS = 2
CHUNK = 8
F32 = jnp.float32
BF16 = jnp.bfloat16
I32 = jnp.int32
HIGHEST = lax.Precision.HIGHEST
VMEM = pl.BlockSpec(memory_space=pltpu.VMEM)
ANY = pl.BlockSpec(memory_space=pl.ANY)
SMEM = pl.BlockSpec(memory_space=pltpu.SMEM)
HBM = pl.BlockSpec(memory_space=pltpu.HBM)


def hat(ray, centre):
    return jnp.maximum(0.0, 1.0 - jnp.abs(ray - centre)).astype(BF16)


def row_taps(offset, slope, extent):
    shape = (offset.shape[0], extent)
    ray = lax.broadcasted_iota(I32, shape, 1).astype(F32)
    offset = jnp.broadcast_to(offset, shape)
    slope = jnp.broadcast_to(slope, shape)
    middle = jnp.floor((ray - offset) / slope + 0.5)
    middle = jnp.minimum(jnp.maximum(middle, 1.0), extent - 2.0)
    weights = [hat(ray, offset + slope * (middle + step)) for step in (-1.0, 0.0, 1.0)]
    return middle.astype(I32), weights


def column_taps(offset, slope, extent):
    shape = (offset.shape[0], extent)
    voxel = lax.broadcasted_iota(I32, shape, 1).astype(F32)
    centre = jnp.broadcast_to(offset, shape) + jnp.broadcast_to(slope, shape) * voxel
    first = jnp.minimum(jnp.maximum(jnp.floor(centre), 0.0), extent - 2.0)
    weights = [hat(first + step, centre) for step in (0.0, 1.0)]
    return first.astype(I32), weights


def repeat_rows(values, times):
    return jnp.concatenate(
        [jnp.broadcast_to(values[row:row + 1, :], (times, values.shape[1]))
         for row in range(values.shape[0])], axis=0)


def contract_lanes(left, right):
    return lax.dot_general(
        left.astype(BF16), right.astype(BF16), (((1,), (1,)), ((), ())), preferred_element_type=F32)


def per_slot(live_ref, slots, capacity):
    targets = live_ref.shape[1]
    slot = lax.broadcasted_iota(I32, (targets, slots), 1)
    owner = lax.broadcasted_iota(I32, (targets, slots), 0)
    expand = (lax.div(slot, capacity) == owner).astype(F32)
    return jnp.dot(live_ref[...].astype(F32), expand, precision=HIGHEST, preferred_element_type=F32)


def pack_kernel(capacity, *refs):
    sources, out_ref, loaded, arrived = refs[:6], refs[6], refs[7:13], refs[13]
    copies = [
        pltpu.make_async_copy(source, ref, arrived.at[place])
        for place, (source, ref) in enumerate(zip(sources, loaded))]
    for copy in copies:
        copy.start()
    for copy in copies:
        copy.wait()
    volume_ref, offset_ref, slope_ref, voxel_ref, ray_ref, live_ref = loaded
    rows, extent = volume_ref.shape
    out_ref[0:rows, :] = volume_ref[...].astype(BF16)
    slots = ray_ref.shape[1]
    fields = []
    for ref in (offset_ref, slope_ref):
        left = ref[...]
        for addend in range(3):
            part = left.astype(BF16).astype(F32)
            fields.append(part)
            left = left - part
    fields.append(voxel_ref[...].astype(F32))
    fields.append(ray_ref[...].astype(F32))
    fields.append(per_slot(live_ref, slots, capacity))
    used = sum(field.shape[0] for field in fields)
    fields.append(jnp.zeros((-used % 16, slots), F32))
    fields = jnp.concatenate(fields, axis=0)
    height = fields.shape[0]
    for part in range(slots // extent):
        at = pl.ds(rows + part * height, height)
        out_ref[at, :] = fields[:, part * extent:(part + 1) * extent].astype(BF16)


def setup_kernel(n_payloads, members, stride, span, sizes, tiles, wanted, *refs):
    payload_refs, refs = refs[:n_payloads], refs[-(2 * len(wanted) + 9):]
    each = members // n_payloads
    list_refs, row_ref, tables = refs[:len(wanted)], refs[len(wanted)], refs[len(wanted) + 1:-len(wanted) - 1]
    drafts, arrived = refs[-len(wanted) - 1:-1], refs[-1]
    copies = [
        pltpu.make_async_copy(draft, ref, arrived.at[place])
        for place, (draft, ref) in enumerate(zip(drafts, list_refs))]
    capacity, depth, frames = sizes
    width = span * capacity
    extent = row_ref.shape[1]
    ray_tiles = row_ref.shape[0] // span
    height = -(-(7 * depth + 2) // 16) * 16
    lanes = drafts[0].shape[1]
    me = lax.axis_index("slab").astype(I32)
    parity = lax.rem(me, span)
    first_slot = (me - parity) * capacity
    part = lax.div(first_slot, extent)
    shift = lax.rem(extent - lax.rem(first_slot, extent), extent)

    def collect(member, lined, payload_ref, within):
        at = within * stride + tiles * frames + part * height
        raw = payload_ref[pl.ds(pl.multiple_of(at, 16), height), :].astype(F32)
        offset = (raw[0:depth] + raw[depth:2 * depth]) + raw[2 * depth:3 * depth]
        slope = (raw[3 * depth:4 * depth] + raw[4 * depth:5 * depth]) + raw[5 * depth:6 * depth]
        fields = jnp.concatenate(
            [offset, slope, raw[6 * depth:7 * depth + 2],
             jnp.zeros((16 - 3 * depth - 2, extent), F32)], axis=0)
        fields = pltpu.roll(fields, shift, axis=1)
        lane = lax.broadcasted_iota(I32, fields.shape, 1)
        fields = jnp.where(lane < width, fields, 0.0)
        if lanes > extent:
            fields = jnp.concatenate(
                [fields, jnp.zeros((fields.shape[0], lanes - extent), F32)], axis=1)
        return lined + pltpu.roll(fields, member * width, axis=1)

    lined = jnp.zeros((16, lanes), F32)
    if members <= 16:
        for member in range(members):
            lined = collect(member, lined, payload_refs[member // each], member % each)
    else:
        lined = lax.fori_loop(
            0, members, lambda member, lined: collect(member, lined, payload_refs[0], member), lined)

    slot = lax.broadcasted_iota(I32, (1, lanes), 1)
    within = lax.rem(slot, width)
    target = lax.bitwise_xor(lax.div(within, capacity), parity)
    ray = lined[3 * depth:3 * depth + 1]
    count = lined[3 * depth + 1:3 * depth + 2]
    alive = jnp.logical_and(lax.rem(within, capacity).astype(F32) < count, slot < members * width)

    table = jnp.concatenate(
        [slot.astype(F32), ray, target.astype(F32), lined[2 * depth:3 * depth],
         jnp.zeros((5 - depth, lanes), F32)], axis=0)
    order = lax.broadcasted_iota(I32, (lanes, lanes), 0)
    earlier = (lax.broadcasted_iota(I32, (lanes, lanes), 1) < order).astype(F32)
    for ref, kind, copy in zip(drafts, wanted, copies):
        taken = alive if kind is None else jnp.logical_and(alive, target == kind)
        taken = taken.astype(F32)
        position = contract_lanes(jnp.broadcast_to(taken, (8, lanes)), earlier)[0:1]
        position = jnp.where(taken > 0.0, position, -1.0).astype(I32)
        choose = jnp.broadcast_to(position, (lanes, lanes)) == order
        packed = (contract_lanes(table, choose.astype(F32)) + 0.5).astype(I32)
        total = jnp.sum(taken, axis=1, keepdims=True).astype(I32)
        line = jnp.where(slot < total, packed[0:1], lanes)
        base = packed[1:2] if kind is not None else packed[1:2] + packed[2:3] * ray_tiles
        member = lax.div(packed[0:1], width) * tiles
        rows = [line, base * frames]
        rows += [(packed[3 + level:4 + level] + member) * frames for level in range(depth)]
        rows += [jnp.zeros((5 - depth, lanes), I32), jnp.broadcast_to(total, (1, lanes))]
        ref[...] = jnp.concatenate(rows, axis=0)
        copy.start()

    columns = lined.T
    summed = None
    for level in range(depth):
        offset = columns[:, level:level + 1]
        slope = columns[:, depth + level:depth + level + 1]
        middle, weights = row_taps(offset, slope, extent)
        first, pair = column_taps(offset, slope, extent)
        wide = [weight.astype(F32) for weight in weights]
        values = [middle] + wide + [first] + [weight.astype(F32) for weight in pair]
        at = level * (lanes + 8)
        for ref, value in zip(tables, values):
            ref[at:at + lanes, :] = value
            blank = jnp.ones if ref.dtype == I32 else jnp.zeros
            ref[at + lanes:at + lanes + 8, :] = blank((8, extent), ref.dtype)
        parts = (wide[0] + wide[1]) + wide[2]
        summed = parts if summed is None else summed + parts

    tile = lax.broadcasted_iota(I32, (span * ray_tiles, lanes), 0).astype(F32)
    place = ray + (target * ray_tiles).astype(F32)
    place = jnp.where(alive, place, -1.0)
    hot = (jnp.broadcast_to(place, tile.shape) == tile).astype(F32)
    row_ref[...] = jnp.dot(hot, summed, precision=HIGHEST, preferred_element_type=F32)
    for copy in copies:
        copy.wait()


def column_kernel(sizes, offset_ref, slope_ref, voxel_ref, live_ref, out_ref):
    capacity, depth, frames = sizes
    tiles = out_ref.shape[0] // frames
    slots = offset_ref.shape[1]
    extent = out_ref.shape[1]
    offsets = offset_ref[...].T
    slopes = slope_ref[...].T
    within = lax.rem(lax.broadcasted_iota(I32, (1, slots), 1), capacity).astype(F32)
    alive = jnp.broadcast_to(within, (tiles, slots)) < per_slot(live_ref, slots, capacity)
    total = jnp.zeros((tiles, extent), F32)
    for level in range(depth):
        unused, pair = column_taps(
            offsets[:, level:level + 1], slopes[:, level:level + 1], extent)
        tile_of = jnp.broadcast_to(voxel_ref[level:level + 1, :], (tiles, slots))
        match = tile_of == lax.broadcasted_iota(I32, (tiles, slots), 0)
        hot = jnp.logical_and(match, alive).astype(F32).astype(BF16)
        for weight in pair:
            total += jnp.dot(hot, weight, preferred_element_type=F32)
    out_ref[...] = repeat_rows(1.0 / jnp.maximum(total, 1.0), frames)


def pick(values, index):
    numbers = lax.GatherDimensionNumbers(
        offset_dims=(), collapsed_slice_dims=(1,), start_index_map=(1,),
        operand_batching_dims=(0,), start_indices_batching_dims=(0,))
    return lax.gather(
        values, index[:, :, None], numbers, slice_sizes=(1, 1),
        mode=lax.GatherScatterMode.PROMISE_IN_BOUNDS)


def pack_pair(first, second):
    kind = jnp.int16 if first.dtype == I32 else BF16
    return jnp.concatenate([first, second], axis=0).astype(kind)


def spread(ref, row, frames):
    return jnp.broadcast_to(ref[pl.ds(row, 1), :], (frames, ref.shape[1]))


def tile_at(start, frames):
    return pl.ds(pl.multiple_of(start, frames), frames)


def for_slots(slots, body):
    def some(step, carry):
        for place in range(CHUNK):
            body(step * CHUNK + place, place)
        return carry

    lax.fori_loop(0, lax.div(slots[7, 0] + (CHUNK - 1), CHUNK), some, 0)


def for_rows(rows, body):
    step = 128

    def some(number, carry):
        body(pl.ds(pl.multiple_of(number * step, step), step))
        return carry

    lax.fori_loop(0, rows // step, some, 0)


def forward_kernel(sizes, n_values, members, start_row, n_sums, slots, *refs):
    capacity, depth, frames = sizes
    value_refs, tables, refs = refs[:n_values], refs[n_values:n_values + 4], refs[n_values + 4:]
    start_ref = None
    if start_row is not None:
        start_ref, refs = refs[0], refs[1:]
    sum_refs, (out_ref, wide, second) = refs[:n_sums], refs[n_sums:]
    rows = wide.shape[0] // members
    each = members // n_values
    stride = value_refs[0].shape[0] // each
    rays = second.shape[0]
    line_step = tables[0].shape[0] // depth

    def widen(member, carry):
        for place, ref in enumerate(value_refs):
            at = pl.ds(pl.multiple_of((place * each + member) * rows, rows), rows)
            wide[at, :] = ref[pl.ds(pl.multiple_of(member * stride, 16), rows), :].astype(F32)
        return carry

    lax.fori_loop(0, each, widen, 0)
    second[...] = jnp.zeros_like(second)
    if start_ref is None:
        out_ref[...] = jnp.zeros_like(out_ref)
    else:
        out_ref[0:rays, :] = start_ref[start_row:start_row + rays, :]
    if n_sums:
        half = sum_refs[0].shape[0] // 2
        out_ref[rays:, :] = sum([ref[half:, :] for ref in sum_refs[1:]], sum_refs[0][half:, :])

    def one(slot, place):
        line = slots[0, slot]
        taps = []
        for start in range(0, depth, 2):
            levels = range(start, start + 2)
            values = [wide[tile_at(slots[2 + level, slot], frames), :] for level in levels]
            middles = [spread(tables[0], line + level * line_step, frames) for level in levels]
            lower = [
                pick(pack_pair(value, value), pack_pair(middle - 1, middle)).astype(F32)
                for value, middle in zip(values, middles)]
            upper = pick(
                pack_pair(*values), pack_pair(*[middle + 1 for middle in middles])).astype(F32)
            for which, pair in enumerate(lower):
                taps.append((pair[0:frames], pair[frames:2 * frames],
                             upper[which * frames:(which + 1) * frames]))
        total = None
        for level, three in enumerate(taps):
            for ref, tap in zip(tables[1:], three):
                term = spread(ref, line + level * line_step, frames) * tap
                total = term if total is None else total + term
        projection = (out_ref, second)[place % 2]
        projection[tile_at(slots[1, slot], frames), :] += total.astype(BF16).astype(F32)

    for_slots(slots, one)
    out_ref[0:rays, :] += second[...]


def residual_kernel(frames, n_own, projection_ref, sinogram_ref, *refs):
    own, refs, out_ref = refs[:n_own], refs[n_own:-1], refs[-1]
    rays = out_ref.shape[0]
    ray_tiles = rays // frames
    total = sum([ref[0:ray_tiles, :] for ref in own[1:]], own[0][0:ray_tiles, :])
    projection = projection_ref[...]
    if refs:
        projection = projection + refs[0][0:rays, :]
        total = total + refs[-1][rays:, :]
    weight = repeat_rows(1.0 / jnp.maximum(total, 1.0), frames)
    out_ref[...] = ((sinogram_ref[...].astype(F32) - projection) * weight).astype(BF16)


def backward_kernel(sizes, n_parts, has_start, split, slots, *refs):
    capacity, depth, frames = sizes
    part_refs, tables, refs = refs[:n_parts], refs[n_parts:n_parts + 3], refs[n_parts + 3:]
    start_ref = None
    if has_start:
        start_ref, refs = refs[0], refs[1:]
    outs = refs[:len(split)] if split else refs[:1]
    residual, banks = refs[len(outs)], refs[len(outs) + 1:]
    rays = part_refs[0].shape[0]
    line_step = tables[0].shape[0] // depth
    for place, ref in enumerate(part_refs):
        residual[place * rays:(place + 1) * rays, :] = ref[...].astype(F32)

    def clear(at):
        for place, bank in enumerate(banks):
            if place == 0 and has_start:
                bank[at, :] = start_ref[at, :]
            else:
                bank[at, :] = jnp.zeros((at.size, bank.shape[1]), F32)

    for_rows(banks[0].shape[0], clear)

    def one(slot, place):
        line = slots[0, slot]
        values = residual[tile_at(slots[1, slot], frames), :]
        twice = pack_pair(values, values)
        for level in range(depth):
            row = line + level * line_step
            first = spread(tables[0], row, frames)
            taps = pick(twice, pack_pair(first, first + 1)).astype(F32)
            term = (spread(tables[1], row, frames) * taps[0:frames]
                    + spread(tables[2], row, frames) * taps[frames:2 * frames])
            banks[level % len(banks)][tile_at(slots[2 + level, slot], frames), :] += term

    for_slots(slots, one)

    def total(at):
        return sum([bank[at, :] for bank in banks[1:]], banks[0][at, :]).astype(outs[0].dtype)

    if split:
        for ref, members in zip(outs, split):
            rows = ref.shape[0] // len(members)
            for place, member in enumerate(members):
                ref[place * rows:(place + 1) * rows, :] = total(pl.ds(member * rows, rows))
    else:
        def finish(at):
            outs[0][at, :] = total(at)

        for_rows(outs[0].shape[0], finish)


def join_kernel(*refs):
    out_ref, at = refs[-1], 0
    for ref in refs[:-1]:
        out_ref[at:at + ref.shape[0], :] = ref[...]
        at += ref.shape[0]


def combine_kernel(members, sum_ref, y_ref, *piece_refs):
    rows = piece_refs[0].shape[0]
    for place, (member, ref) in enumerate(zip(members, piece_refs)):
        mine = sum_ref[member * rows:(member + 1) * rows, :]
        ref[...] = (mine + y_ref[place * rows:(place + 1) * rows, :].astype(F32)).astype(ref.dtype)


def update_kernel(n_pieces, volume_ref, column_ref, *refs):
    back = refs[0][...]
    for ref in refs[1:n_pieces]:
        back = back + ref[...].astype(F32)
    volume = volume_ref[...] + column_ref[...] * back
    for ref in refs[n_pieces:]:
        ref[...] = volume.astype(ref.dtype)


def call(kernel, name, mib, in_specs, out_shape, *operands, scratch=()):
    one = not isinstance(out_shape, list)
    return pl.pallas_call(
        kernel,
        out_shape=out_shape,
        in_specs=in_specs,
        out_specs=VMEM if one else [
            SMEM if getattr(out, "memory_space", None) == pltpu.SMEM else VMEM for out in out_shape],
        scratch_shapes=list(scratch),
        compiler_params=pltpu.CompilerParams(vmem_limit_bytes=mib * 1024 * 1024),
        name=name,
    )(*operands)


def exchange(values, n_slab, distance):
    return lax.ppermute(
        values, "slab", [(device, device ^ distance) for device in range(n_slab)])


def shards(sinogram, start_volume, slot_voxel, slot_ray, live_count, block_slope, block_offset):
    n_slab = lax.axis_size("slab")
    n_slots, depth = slot_voxel.shape
    capacity = n_slots // n_slab
    ray_tiles, frames, extent = sinogram.shape
    voxel_tiles = start_volume.shape[0]
    rows = voxel_tiles * frames
    sizes = (capacity, depth, frames)
    paired = n_slab == 16
    span = 2 if paired else 1
    n_bank = 2 if paired else 1
    shape = jax.ShapeDtypeStruct
    n_rays = ray_tiles * frames
    volume = start_volume.reshape(rows, extent)
    sino = sinogram.reshape(n_rays, extent)
    slots_by_depth = (block_offset.T, block_slope.T, slot_voxel.T)
    live = live_count.reshape(1, n_slab)
    height = -(-(7 * depth + 2) // 16) * 16 * (n_slots // extent)
    operands = (volume, *slots_by_depth, slot_ray.reshape(1, n_slots), live)
    payload = call(
        functools.partial(pack_kernel, capacity), "pack", 16, [HBM] * 6,
        shape((rows + height, extent), BF16),
        *[pltpu.with_memory_space_constraint(operand, pltpu.HBM) for operand in operands],
        scratch=[pltpu.VMEM(operand.shape, operand.dtype) for operand in operands]
        + [pltpu.SemaphoreType.DMA((6,))])

    def setup(payloads, members, wanted, after=None):
        lanes = -(-members * span * capacity // 128) * 128
        lines = depth * (lanes + 8)
        table = [shape((lines, extent), I32)] + [shape((lines, extent), F32)] * 3
        table += [shape((lines, extent), I32)] + [shape((lines, extent), F32)] * 2
        n = len(wanted)
        out = [pltpu.SMEM((8, lanes), I32)] * n + [shape((span * ray_tiles, extent), F32)] + table
        waits = [] if after is None else [after]
        found = call(
            functools.partial(setup_kernel, len(payloads), members,
                              payloads[0].shape[0] * len(payloads) // members, span, sizes,
                              voxel_tiles, wanted),
            "setup", 24, [VMEM] * len(payloads) + [ANY] * len(waits), out, *payloads, *waits,
            scratch=[pltpu.VMEM((8, lanes), I32)] * n + [pltpu.SemaphoreType.DMA((n,))])
        return found[:n], found[n], found[n + 1:n + 5], found[n + 5:]

    def forward(slots, values, members, table, n_out, start=None, start_row=None, sums=()):
        operands = [pltpu.with_memory_space_constraint(slots, pltpu.SMEM), *values, *table] + ([] if start is None else [start]) + list(sums)
        extra = ray_tiles if sums else 0
        return call(
            functools.partial(forward_kernel, sizes, len(values), members, start_row, len(sums)),
            "forward", 16 if paired else 32, [SMEM] + [VMEM] * (len(operands) - 1),
            shape((n_out + extra, extent), F32), *operands,
            scratch=[pltpu.VMEM((members * rows, extent), F32), pltpu.VMEM((n_out, extent), F32)])

    def residual_of(projection, row_sums, *sibling):
        operands = [projection, sino, *row_sums, *sibling]
        return call(
            functools.partial(residual_kernel, frames, len(row_sums)), "residual", 16,
            [VMEM] * len(operands), shape((n_rays, extent), BF16), *operands)

    def backward(slots, parts, members, table, kind, start=None, split=()):
        operands = [pltpu.with_memory_space_constraint(slots, pltpu.SMEM), *parts, *table] + ([] if start is None else [start])
        return call(
            functools.partial(backward_kernel, sizes, len(parts), start is not None, split),
            "backward", 16 if paired else 32, [SMEM] + [VMEM] * (len(operands) - 1),
            [shape((len(some) * rows, extent), kind) for some in split]
            if split else shape((members * rows, extent), kind), *operands,
            scratch=[pltpu.VMEM((len(parts) * n_rays, extent), F32)]
            + [pltpu.VMEM((members * rows, extent), F32)] * n_bank)

    def join(*parts):
        total = sum(part.shape[0] for part in parts)
        return call(join_kernel, "join", 16, [VMEM] * len(parts), shape((total, extent), BF16), *parts)

    def update(volume, pieces, last):
        out = [shape((rows, extent), F32)] + ([] if last else [shape((rows, extent), BF16)])
        return call(
            functools.partial(update_kernel, len(pieces)), "update", 16,
            [VMEM] * (2 + len(pieces)), out, volume, column_weight, *pieces)

    column_weight = call(
        functools.partial(column_kernel, sizes), "column_weight", 16, [VMEM] * 4,
        shape((rows, extent), F32), *slots_by_depth, live)

    for sweep in range(ITERS):
        last = sweep + 1 == ITERS
        if paired:
            over_2 = exchange(payload, n_slab, 8)
            over_1 = exchange(payload, n_slab, 4)
            over_3 = exchange(over_2, n_slab, 4)
            z_half = join(payload, over_1)
            y_half = exchange(z_half, n_slab, 2)
            z_rest = join(over_2, over_3)
            y_rest = exchange(z_rest, n_slab, 2)
            along_z, along_y = (z_half, z_rest), (y_half, y_rest)
            if sweep == 0:
                (z_list,), z_rows, z_forward, z_backward = setup(along_z, 4, (None,))
            both = forward(z_list, along_z, 4, z_forward, 2 * n_rays)
            if sweep == 0:
                (own_list, other_list), y_rows, y_forward, y_backward = setup(
                    along_y, 4, (0, 1), after=both)
            other = exchange(
                forward(other_list, along_y, 4, y_forward, n_rays, both, n_rays,
                        (z_rows, y_rows) if sweep == 0 else ()), n_slab, 1)
            if sweep == 0:
                first_other = other
            own = forward(own_list, along_y, 4, y_forward, n_rays, both, 0)
            residual = residual_of(own, (z_rows, y_rows), other, first_other)
            other_residual = exchange(residual, n_slab, 1)
            y_sum = backward(own_list, [residual], 4, y_backward, F32)
            far_sum, near_sum = backward(
                other_list, [other_residual], 4, y_backward, BF16, y_sum, ((2, 3), (0, 1)))
            far_part, near_part = exchange(far_sum, n_slab, 2), exchange(near_sum, n_slab, 2)
            z_sum = backward(z_list, [residual, other_residual], 4, z_backward, F32)
            whole, piece = shape((rows, extent), F32), shape((rows, extent), BF16)
            sum_2, piece_3 = call(
                functools.partial(combine_kernel, (2, 3)), "combine", 16, [VMEM] * 2,
                [whole, piece], z_sum, far_part)
            piece_2 = call(
                functools.partial(combine_kernel, (0,)), "combine", 16, [VMEM] * 2,
                [piece], sum_2, exchange(piece_3, n_slab, 4))[0]
            own_piece, piece_1 = call(
                functools.partial(combine_kernel, (0, 1)), "combine", 16, [VMEM] * 2,
                [whole, piece], z_sum, near_part)
            pieces = [own_piece, exchange(piece_2, n_slab, 8), exchange(piece_1, n_slab, 4)]
        else:
            everyone = lax.all_gather(payload, "slab", axis=0, tiled=True)
            if sweep == 0:
                (slots,), row_sums, to_rays, to_voxels = setup((everyone,), n_slab, (None,))
            projection = forward(slots, (everyone,), n_slab, to_rays, n_rays)
            residual = residual_of(projection, (row_sums,))
            sums = backward(slots, [residual], n_slab, to_voxels, BF16)
            parts = lax.all_to_all(
                sums.reshape(n_slab, rows, extent), "slab", split_axis=0, concat_axis=0, tiled=True)
            pieces = [jnp.sum(parts.astype(F32), axis=0)]
        volume, *rounded = update(volume, pieces, last)
        if not last:
            payload = rounded[0]
    return volume.reshape(start_volume.shape)


def solution(mesh):
    in_specs = (
        P(("scan", "slab"), None, None),
        P(("scan", "slab"), None, None),
        P(("scan", "slab"), None),
        P(("scan", "slab")),
        P(("scan", "slab")),
        P(("scan", "slab"), None),
        P(("scan", "slab"), None),
    )
    out_specs = P(("scan", "slab"), None, None)
    return jax.shard_map(shards, mesh=mesh, in_specs=in_specs, out_specs=out_specs, check_vma=False)
```

```python
import functools

import jax
import jax.numpy as jnp
from jax import lax
from jax.experimental import pallas as pl
from jax.experimental.pallas import tpu as pltpu
from jax.sharding import PartitionSpec as P

ITERS = 2
CHUNK = 8
F32 = jnp.float32
BF16 = jnp.bfloat16
I32 = jnp.int32
HIGHEST = lax.Precision.HIGHEST
VMEM = pl.BlockSpec(memory_space=pltpu.VMEM)
ANY = pl.BlockSpec(memory_space=pl.ANY)
SMEM = pl.BlockSpec(memory_space=pltpu.SMEM)
HBM = pl.BlockSpec(memory_space=pltpu.HBM)


def hat(ray, centre):
    return jnp.maximum(0.0, 1.0 - jnp.abs(ray - centre)).astype(BF16)


def row_taps(offset, slope, extent):
    shape = (offset.shape[0], extent)
    ray = lax.broadcasted_iota(I32, shape, 1).astype(F32)
    offset = jnp.broadcast_to(offset, shape)
    slope = jnp.broadcast_to(slope, shape)
    middle = jnp.floor((ray - offset) / slope + 0.5)
    middle = jnp.minimum(jnp.maximum(middle, 1.0), extent - 2.0)
    weights = [hat(ray, offset + slope * (middle + step)) for step in (-1.0, 0.0, 1.0)]
    return middle.astype(I32), weights


def column_taps(offset, slope, extent):
    shape = (offset.shape[0], extent)
    voxel = lax.broadcasted_iota(I32, shape, 1).astype(F32)
    centre = jnp.broadcast_to(offset, shape) + jnp.broadcast_to(slope, shape) * voxel
    first = jnp.minimum(jnp.maximum(jnp.floor(centre), 0.0), extent - 2.0)
    weights = [hat(first + step, centre) for step in (0.0, 1.0)]
    return first.astype(I32), weights


def repeat_rows(values, times):
    return jnp.concatenate(
        [jnp.broadcast_to(values[row:row + 1, :], (times, values.shape[1]))
         for row in range(values.shape[0])], axis=0)


def contract_lanes(left, right):
    return lax.dot_general(
        left.astype(BF16), right.astype(BF16), (((1,), (1,)), ((), ())), preferred_element_type=F32)


def per_slot(live_ref, slots, capacity):
    targets = live_ref.shape[1]
    slot = lax.broadcasted_iota(I32, (targets, slots), 1)
    owner = lax.broadcasted_iota(I32, (targets, slots), 0)
    expand = (lax.div(slot, capacity) == owner).astype(F32)
    return jnp.dot(live_ref[...].astype(F32), expand, precision=HIGHEST, preferred_element_type=F32)


def pack_kernel(capacity, *refs):
    sources, out_ref, loaded, arrived = refs[:6], refs[6], refs[7:13], refs[13]
    copies = [
        pltpu.make_async_copy(source, ref, arrived.at[place])
        for place, (source, ref) in enumerate(zip(sources, loaded))]
    for copy in copies:
        copy.start()
    for copy in copies:
        copy.wait()
    volume_ref, offset_ref, slope_ref, voxel_ref, ray_ref, live_ref = loaded
    rows, extent = volume_ref.shape
    out_ref[0:rows, :] = volume_ref[...].astype(BF16)
    slots = ray_ref.shape[1]
    fields = []
    for ref in (offset_ref, slope_ref):
        left = ref[...]
        for addend in range(3):
            part = left.astype(BF16).astype(F32)
            fields.append(part)
            left = left - part
    fields.append(voxel_ref[...].astype(F32))
    fields.append(ray_ref[...].astype(F32))
    fields.append(per_slot(live_ref, slots, capacity))
    used = sum(field.shape[0] for field in fields)
    fields.append(jnp.zeros((-used % 16, slots), F32))
    fields = jnp.concatenate(fields, axis=0)
    height = fields.shape[0]
    for part in range(slots // extent):
        at = pl.ds(rows + part * height, height)
        out_ref[at, :] = fields[:, part * extent:(part + 1) * extent].astype(BF16)


def setup_kernel(n_payloads, members, stride, span, sizes, tiles, wanted, *refs):
    payload_refs, refs = refs[:n_payloads], refs[-(2 * len(wanted) + 9):]
    each = members // n_payloads
    list_refs, row_ref, tables = refs[:len(wanted)], refs[len(wanted)], refs[len(wanted) + 1:-len(wanted) - 1]
    drafts, arrived = refs[-len(wanted) - 1:-1], refs[-1]
    copies = [
        pltpu.make_async_copy(draft, ref, arrived.at[place])
        for place, (draft, ref) in enumerate(zip(drafts, list_refs))]
    capacity, depth, frames = sizes
    width = span * capacity
    extent = row_ref.shape[1]
    ray_tiles = row_ref.shape[0] // span
    height = -(-(7 * depth + 2) // 16) * 16
    lanes = drafts[0].shape[1]
    me = lax.axis_index("slab").astype(I32)
    parity = lax.rem(me, span)
    first_slot = (me - parity) * capacity
    part = lax.div(first_slot, extent)
    shift = lax.rem(extent - lax.rem(first_slot, extent), extent)

    def collect(member, lined, payload_ref, within):
        at = within * stride + tiles * frames + part * height
        raw = payload_ref[pl.ds(pl.multiple_of(at, 16), height), :].astype(F32)
        offset = (raw[0:depth] + raw[depth:2 * depth]) + raw[2 * depth:3 * depth]
        slope = (raw[3 * depth:4 * depth] + raw[4 * depth:5 * depth]) + raw[5 * depth:6 * depth]
        fields = jnp.concatenate(
            [offset, slope, raw[6 * depth:7 * depth + 2],
             jnp.zeros((16 - 3 * depth - 2, extent), F32)], axis=0)
        fields = pltpu.roll(fields, shift, axis=1)
        lane = lax.broadcasted_iota(I32, fields.shape, 1)
        fields = jnp.where(lane < width, fields, 0.0)
        if lanes > extent:
            fields = jnp.concatenate(
                [fields, jnp.zeros((fields.shape[0], lanes - extent), F32)], axis=1)
        return lined + pltpu.roll(fields, member * width, axis=1)

    lined = jnp.zeros((16, lanes), F32)
    if members <= 16:
        for member in range(members):
            lined = collect(member, lined, payload_refs[member // each], member % each)
    else:
        lined = lax.fori_loop(
            0, members, lambda member, lined: collect(member, lined, payload_refs[0], member), lined)

    slot = lax.broadcasted_iota(I32, (1, lanes), 1)
    within = lax.rem(slot, width)
    target = lax.bitwise_xor(lax.div(within, capacity), parity)
    ray = lined[3 * depth:3 * depth + 1]
    count = lined[3 * depth + 1:3 * depth + 2]
    alive = jnp.logical_and(lax.rem(within, capacity).astype(F32) < count, slot < members * width)

    table = jnp.concatenate(
        [slot.astype(F32), ray, target.astype(F32), lined[2 * depth:3 * depth],
         jnp.zeros((5 - depth, lanes), F32)], axis=0)
    order = lax.broadcasted_iota(I32, (lanes, lanes), 0)
    earlier = (lax.broadcasted_iota(I32, (lanes, lanes), 1) < order).astype(F32)
    for ref, kind, copy in zip(drafts, wanted, copies):
        taken = alive if kind is None else jnp.logical_and(alive, target == kind)
        taken = taken.astype(F32)
        position = contract_lanes(jnp.broadcast_to(taken, (8, lanes)), earlier)[0:1]
        position = jnp.where(taken > 0.0, position, -1.0).astype(I32)
        choose = jnp.broadcast_to(position, (lanes, lanes)) == order
        packed = (contract_lanes(table, choose.astype(F32)) + 0.5).astype(I32)
        total = jnp.sum(taken, axis=1, keepdims=True).astype(I32)
        line = jnp.where(slot < total, packed[0:1], lanes)
        base = packed[1:2] if kind is not None else packed[1:2] + packed[2:3] * ray_tiles
        member = lax.div(packed[0:1], width) * tiles
        rows = [line, base * frames]
        rows += [(packed[3 + level:4 + level] + member) * frames for level in range(depth)]
        rows += [jnp.zeros((5 - depth, lanes), I32), jnp.broadcast_to(total, (1, lanes))]
        ref[...] = jnp.concatenate(rows, axis=0)
        copy.start()

    columns = lined.T
    summed = None
    for level in range(depth):
        offset = columns[:, level:level + 1]
        slope = columns[:, depth + level:depth + level + 1]
        middle, weights = row_taps(offset, slope, extent)
        first, pair = column_taps(offset, slope, extent)
        wide = [weight.astype(F32) for weight in weights]
        values = [middle] + wide + [first] + [weight.astype(F32) for weight in pair]
        at = level * (lanes + 8)
        for ref, value in zip(tables, values):
            ref[at:at + lanes, :] = value
            blank = jnp.ones if ref.dtype == I32 else jnp.zeros
            ref[at + lanes:at + lanes + 8, :] = blank((8, extent), ref.dtype)
        parts = (wide[0] + wide[1]) + wide[2]
        summed = parts if summed is None else summed + parts

    tile = lax.broadcasted_iota(I32, (span * ray_tiles, lanes), 0).astype(F32)
    place = ray + (target * ray_tiles).astype(F32)
    place = jnp.where(alive, place, -1.0)
    hot = (jnp.broadcast_to(place, tile.shape) == tile).astype(F32)
    row_ref[...] = jnp.dot(hot, summed, precision=HIGHEST, preferred_element_type=F32)
    for copy in copies:
        copy.wait()


def column_kernel(sizes, offset_ref, slope_ref, voxel_ref, live_ref, out_ref):
    capacity, depth, frames = sizes
    tiles = out_ref.shape[0] // frames
    slots = offset_ref.shape[1]
    extent = out_ref.shape[1]
    offsets = offset_ref[...].T
    slopes = slope_ref[...].T
    within = lax.rem(lax.broadcasted_iota(I32, (1, slots), 1), capacity).astype(F32)
    alive = jnp.broadcast_to(within, (tiles, slots)) < per_slot(live_ref, slots, capacity)
    total = jnp.zeros((tiles, extent), F32)
    for level in range(depth):
        unused, pair = column_taps(
            offsets[:, level:level + 1], slopes[:, level:level + 1], extent)
        tile_of = jnp.broadcast_to(voxel_ref[level:level + 1, :], (tiles, slots))
        match = tile_of == lax.broadcasted_iota(I32, (tiles, slots), 0)
        hot = jnp.logical_and(match, alive).astype(F32).astype(BF16)
        for weight in pair:
            total += jnp.dot(hot, weight, preferred_element_type=F32)
    out_ref[...] = repeat_rows(1.0 / jnp.maximum(total, 1.0), frames)


def pick(values, index):
    numbers = lax.GatherDimensionNumbers(
        offset_dims=(), collapsed_slice_dims=(1,), start_index_map=(1,),
        operand_batching_dims=(0,), start_indices_batching_dims=(0,))
    return lax.gather(
        values, index[:, :, None], numbers, slice_sizes=(1, 1),
        mode=lax.GatherScatterMode.PROMISE_IN_BOUNDS)


def pack_pair(first, second):
    kind = jnp.int16 if first.dtype == I32 else BF16
    return jnp.concatenate([first, second], axis=0).astype(kind)


def spread(ref, row, frames):
    return jnp.broadcast_to(ref[pl.ds(row, 1), :], (frames, ref.shape[1]))


def tile_at(start, frames):
    return pl.ds(pl.multiple_of(start, frames), frames)


def for_slots(slots, body):
    def some(step, carry):
        for place in range(CHUNK):
            body(step * CHUNK + place, place)
        return carry

    lax.fori_loop(0, lax.div(slots[7, 0] + (CHUNK - 1), CHUNK), some, 0)


def for_rows(rows, body):
    step = 128

    def some(number, carry):
        body(pl.ds(pl.multiple_of(number * step, step), step))
        return carry

    lax.fori_loop(0, rows // step, some, 0)


def forward_kernel(sizes, n_values, members, start_row, n_sums, slots, *refs):
    capacity, depth, frames = sizes
    value_refs, tables, refs = refs[:n_values], refs[n_values:n_values + 4], refs[n_values + 4:]
    start_ref = None
    if start_row is not None:
        start_ref, refs = refs[0], refs[1:]
    sum_refs, (out_ref, wide, second) = refs[:n_sums], refs[n_sums:]
    rows = wide.shape[0] // members
    each = members // n_values
    stride = value_refs[0].shape[0] // each
    rays = second.shape[0]
    line_step = tables[0].shape[0] // depth

    def widen(member, carry):
        for place, ref in enumerate(value_refs):
            at = pl.ds(pl.multiple_of((place * each + member) * rows, rows), rows)
            wide[at, :] = ref[pl.ds(pl.multiple_of(member * stride, 16), rows), :].astype(F32)
        return carry

    lax.fori_loop(0, each, widen, 0)
    second[...] = jnp.zeros_like(second)
    if start_ref is None:
        out_ref[...] = jnp.zeros_like(out_ref)
    else:
        out_ref[0:rays, :] = start_ref[start_row:start_row + rays, :]
    if n_sums:
        half = sum_refs[0].shape[0] // 2
        out_ref[rays:, :] = sum([ref[half:, :] for ref in sum_refs[1:]], sum_refs[0][half:, :])

    def one(slot, place):
        line = slots[0, slot]
        taps = []
        for start in range(0, depth, 2):
            levels = range(start, start + 2)
            values = [wide[tile_at(slots[2 + level, slot], frames), :] for level in levels]
            middles = [spread(tables[0], line + level * line_step, frames) for level in levels]
            lower = [
                pick(pack_pair(value, value), pack_pair(middle - 1, middle)).astype(F32)
                for value, middle in zip(values, middles)]
            upper = pick(
                pack_pair(*values), pack_pair(*[middle + 1 for middle in middles])).astype(F32)
            for which, pair in enumerate(lower):
                taps.append((pair[0:frames], pair[frames:2 * frames],
                             upper[which * frames:(which + 1) * frames]))
        total = None
        for level, three in enumerate(taps):
            for ref, tap in zip(tables[1:], three):
                term = spread(ref, line + level * line_step, frames) * tap
                total = term if total is None else total + term
        projection = (out_ref, second)[place % 2]
        projection[tile_at(slots[1, slot], frames), :] += total.astype(BF16).astype(F32)

    for_slots(slots, one)
    out_ref[0:rays, :] += second[...]


def residual_kernel(frames, n_own, projection_ref, sinogram_ref, *refs):
    own, refs, out_ref = refs[:n_own], refs[n_own:-1], refs[-1]
    rays = out_ref.shape[0]
    ray_tiles = rays // frames
    total = sum([ref[0:ray_tiles, :] for ref in own[1:]], own[0][0:ray_tiles, :])
    projection = projection_ref[...]
    if refs:
        projection = projection + refs[0][0:rays, :]
        total = total + refs[-1][rays:, :]
    weight = repeat_rows(1.0 / jnp.maximum(total, 1.0), frames)
    out_ref[...] = ((sinogram_ref[...].astype(F32) - projection) * weight).astype(BF16)


def backward_kernel(sizes, n_parts, has_start, split, slots, *refs):
    capacity, depth, frames = sizes
    part_refs, tables, refs = refs[:n_parts], refs[n_parts:n_parts + 3], refs[n_parts + 3:]
    start_ref = None
    if has_start:
        start_ref, refs = refs[0], refs[1:]
    outs = refs[:len(split)] if split else refs[:1]
    residual, banks = refs[len(outs)], refs[len(outs) + 1:]
    rays = part_refs[0].shape[0]
    line_step = tables[0].shape[0] // depth
    for place, ref in enumerate(part_refs):
        residual[place * rays:(place + 1) * rays, :] = ref[...].astype(F32)

    def clear(at):
        for place, bank in enumerate(banks):
            if place == 0 and has_start:
                bank[at, :] = start_ref[at, :]
            else:
                bank[at, :] = jnp.zeros((at.size, bank.shape[1]), F32)

    for_rows(banks[0].shape[0], clear)

    def one(slot, place):
        line = slots[0, slot]
        values = residual[tile_at(slots[1, slot], frames), :]
        twice = pack_pair(values, values)
        for level in range(depth):
            row = line + level * line_step
            first = spread(tables[0], row, frames)
            taps = pick(twice, pack_pair(first, first + 1)).astype(F32)
            term = (spread(tables[1], row, frames) * taps[0:frames]
                    + spread(tables[2], row, frames) * taps[frames:2 * frames])
            banks[level % len(banks)][tile_at(slots[2 + level, slot], frames), :] += term

    for_slots(slots, one)

    def total(at):
        return sum([bank[at, :] for bank in banks[1:]], banks[0][at, :]).astype(outs[0].dtype)

    if split:
        for ref, members in zip(outs, split):
            rows = ref.shape[0] // len(members)
            for place, member in enumerate(members):
                ref[place * rows:(place + 1) * rows, :] = total(pl.ds(member * rows, rows))
    else:
        def finish(at):
            outs[0][at, :] = total(at)

        for_rows(outs[0].shape[0], finish)


def join_kernel(*refs):
    out_ref, at = refs[-1], 0
    for ref in refs[:-1]:
        out_ref[at:at + ref.shape[0], :] = ref[...]
        at += ref.shape[0]


def combine_kernel(members, sum_ref, y_ref, *piece_refs):
    rows = piece_refs[0].shape[0]
    for place, (member, ref) in enumerate(zip(members, piece_refs)):
        mine = sum_ref[member * rows:(member + 1) * rows, :]
        ref[...] = (mine + y_ref[place * rows:(place + 1) * rows, :].astype(F32)).astype(ref.dtype)


def update_kernel(n_pieces, volume_ref, column_ref, *refs):
    back = refs[0][...]
    for ref in refs[1:n_pieces]:
        back = back + ref[...].astype(F32)
    volume = volume_ref[...] + column_ref[...] * back
    for ref in refs[n_pieces:]:
        ref[...] = volume.astype(ref.dtype)


def call(kernel, name, mib, in_specs, out_shape, *operands, scratch=()):
    one = not isinstance(out_shape, list)
    return pl.pallas_call(
        kernel,
        out_shape=out_shape,
        in_specs=in_specs,
        out_specs=VMEM if one else [
            SMEM if getattr(out, "memory_space", None) == pltpu.SMEM else VMEM for out in out_shape],
        scratch_shapes=list(scratch),
        compiler_params=pltpu.CompilerParams(vmem_limit_bytes=mib * 1024 * 1024),
        name=name,
    )(*operands)


def exchange(values, n_slab, distance, odd_distance=None):
    far = (distance, distance if odd_distance is None else odd_distance)
    return lax.ppermute(
        values, "slab", [(device, device ^ far[device % 2]) for device in range(n_slab)])


def shards(sinogram, start_volume, slot_voxel, slot_ray, live_count, block_slope, block_offset):
    n_slab = lax.axis_size("slab")
    n_slots, depth = slot_voxel.shape
    capacity = n_slots // n_slab
    ray_tiles, frames, extent = sinogram.shape
    voxel_tiles = start_volume.shape[0]
    rows = voxel_tiles * frames
    sizes = (capacity, depth, frames)
    paired = n_slab == 16
    span = 2 if paired else 1
    n_bank = 2 if paired else 1
    shape = jax.ShapeDtypeStruct
    n_rays = ray_tiles * frames
    volume = start_volume.reshape(rows, extent)
    sino = sinogram.reshape(n_rays, extent)
    slots_by_depth = (block_offset.T, block_slope.T, slot_voxel.T)
    live = live_count.reshape(1, n_slab)
    height = -(-(7 * depth + 2) // 16) * 16 * (n_slots // extent)
    operands = (volume, *slots_by_depth, slot_ray.reshape(1, n_slots), live)
    payload = call(
        functools.partial(pack_kernel, capacity), "pack", 16, [HBM] * 6,
        shape((rows + height, extent), BF16),
        *[pltpu.with_memory_space_constraint(operand, pltpu.HBM) for operand in operands],
        scratch=[pltpu.VMEM(operand.shape, operand.dtype) for operand in operands]
        + [pltpu.SemaphoreType.DMA((6,))])

    def setup(payloads, members, wanted, after=None):
        lanes = -(-members * span * capacity // 128) * 128
        lines = depth * (lanes + 8)
        table = [shape((lines, extent), I32)] + [shape((lines, extent), F32)] * 3
        table += [shape((lines, extent), I32)] + [shape((lines, extent), F32)] * 2
        n = len(wanted)
        out = [pltpu.SMEM((8, lanes), I32)] * n + [shape((span * ray_tiles, extent), F32)] + table
        waits = [] if after is None else [after]
        found = call(
            functools.partial(setup_kernel, len(payloads), members,
                              payloads[0].shape[0] * len(payloads) // members, span, sizes,
                              voxel_tiles, wanted),
            "setup", 24, [VMEM] * len(payloads) + [ANY] * len(waits), out, *payloads, *waits,
            scratch=[pltpu.VMEM((8, lanes), I32)] * n + [pltpu.SemaphoreType.DMA((n,))])
        return found[:n], found[n], found[n + 1:n + 5], found[n + 5:]

    def forward(slots, values, members, table, n_out, start=None, start_row=None, sums=()):
        operands = [pltpu.with_memory_space_constraint(slots, pltpu.SMEM), *values, *table] + ([] if start is None else [start]) + list(sums)
        extra = ray_tiles if sums else 0
        return call(
            functools.partial(forward_kernel, sizes, len(values), members, start_row, len(sums)),
            "forward", 16 if paired else 32, [SMEM] + [VMEM] * (len(operands) - 1),
            shape((n_out + extra, extent), F32), *operands,
            scratch=[pltpu.VMEM((members * rows, extent), F32), pltpu.VMEM((n_out, extent), F32)])

    def residual_of(projection, row_sums, *sibling):
        operands = [projection, sino, *row_sums, *sibling]
        return call(
            functools.partial(residual_kernel, frames, len(row_sums)), "residual", 16,
            [VMEM] * len(operands), shape((n_rays, extent), BF16), *operands)

    def backward(slots, parts, members, table, kind, start=None, split=()):
        operands = [pltpu.with_memory_space_constraint(slots, pltpu.SMEM), *parts, *table] + ([] if start is None else [start])
        return call(
            functools.partial(backward_kernel, sizes, len(parts), start is not None, split),
            "backward", 16 if paired else 32, [SMEM] + [VMEM] * (len(operands) - 1),
            [shape((len(some) * rows, extent), kind) for some in split]
            if split else shape((members * rows, extent), kind), *operands,
            scratch=[pltpu.VMEM((len(parts) * n_rays, extent), F32)]
            + [pltpu.VMEM((members * rows, extent), F32)] * n_bank)

    def join(*parts):
        total = sum(part.shape[0] for part in parts)
        return call(join_kernel, "join", 16, [VMEM] * len(parts), shape((total, extent), BF16), *parts)

    def update(volume, pieces, last):
        out = [shape((rows, extent), F32)] + ([] if last else [shape((rows, extent), BF16)])
        return call(
            functools.partial(update_kernel, len(pieces)), "update", 16,
            [VMEM] * (2 + len(pieces)), out, volume, column_weight, *pieces)

    column_weight = call(
        functools.partial(column_kernel, sizes), "column_weight", 16, [VMEM] * 4,
        shape((rows, extent), F32), *slots_by_depth, live)

    for sweep in range(ITERS):
        last = sweep + 1 == ITERS
        if paired:
            place_1, place_2, place_3 = [
                exchange(payload, n_slab, *pair) for pair in ((8, 12), (12, 4), (4, 8))]
            z_half = join(payload, place_1)
            y_half = exchange(z_half, n_slab, 2)
            z_rest = join(place_2, place_3)
            y_rest = exchange(z_rest, n_slab, 2)
            along_z, along_y = (z_half, z_rest), (y_half, y_rest)
            if sweep == 0:
                (z_list,), z_rows, z_forward, z_backward = setup(along_z, 4, (None,))
            both = forward(z_list, along_z, 4, z_forward, 2 * n_rays)
            if sweep == 0:
                (own_list, other_list), y_rows, y_forward, y_backward = setup(
                    along_y, 4, (0, 1), after=both)
            other = exchange(
                forward(other_list, along_y, 4, y_forward, n_rays, both, n_rays,
                        (z_rows, y_rows) if sweep == 0 else ()), n_slab, 1)
            if sweep == 0:
                first_other = other
            own = forward(own_list, along_y, 4, y_forward, n_rays, both, 0)
            residual = residual_of(own, (z_rows, y_rows), other, first_other)
            other_residual = exchange(residual, n_slab, 1)
            y_sum = backward(own_list, [residual], 4, y_backward, F32)
            far_sum, near_sum = backward(
                other_list, [other_residual], 4, y_backward, BF16, y_sum, ((1, 2), (0, 3)))
            far_part, near_part = exchange(far_sum, n_slab, 2), exchange(near_sum, n_slab, 2)
            z_sum = backward(z_list, [residual, other_residual], 4, z_backward, F32)
            piece = shape((rows, extent), BF16)
            piece_1, piece_2 = call(
                functools.partial(combine_kernel, (1, 2)), "combine", 16, [VMEM] * 2,
                [piece, piece], z_sum, far_part)
            got = [exchange(piece_1, n_slab, 8, 12), exchange(piece_2, n_slab, 12, 4)]
            own_piece, piece_3 = call(
                functools.partial(combine_kernel, (0, 3)), "combine", 16, [VMEM] * 2,
                [shape((rows, extent), F32), piece], z_sum, near_part)
            pieces = [own_piece, *got, exchange(piece_3, n_slab, 4, 8)]
        else:
            everyone = lax.all_gather(payload, "slab", axis=0, tiled=True)
            if sweep == 0:
                (slots,), row_sums, to_rays, to_voxels = setup((everyone,), n_slab, (None,))
            projection = forward(slots, (everyone,), n_slab, to_rays, n_rays)
            residual = residual_of(projection, (row_sums,))
            sums = backward(slots, [residual], n_slab, to_voxels, BF16)
            parts = lax.all_to_all(
                sums.reshape(n_slab, rows, extent), "slab", split_axis=0, concat_axis=0, tiled=True)
            pieces = [jnp.sum(parts.astype(F32), axis=0)]
        volume, *rounded = update(volume, pieces, last)
        if not last:
            payload = rounded[0]
    return volume.reshape(start_volume.shape)


def solution(mesh):
    in_specs = (
        P(("scan", "slab"), None, None),
        P(("scan", "slab"), None, None),
        P(("scan", "slab"), None),
        P(("scan", "slab")),
        P(("scan", "slab")),
        P(("scan", "slab"), None),
        P(("scan", "slab"), None),
    )
    out_specs = P(("scan", "slab"), None, None)
    return jax.shard_map(shards, mesh=mesh, in_specs=in_specs, out_specs=out_specs, check_vma=False)
```

```python
import functools

import jax
import jax.numpy as jnp
from jax import lax
from jax.experimental import pallas as pl
from jax.experimental.pallas import tpu as pltpu
from jax.sharding import PartitionSpec as P

ITERS = 2
CHUNK = 8
F32 = jnp.float32
BF16 = jnp.bfloat16
I32 = jnp.int32
HIGHEST = lax.Precision.HIGHEST
VMEM = pl.BlockSpec(memory_space=pltpu.VMEM)
ANY = pl.BlockSpec(memory_space=pl.ANY)
SMEM = pl.BlockSpec(memory_space=pltpu.SMEM)
HBM = pl.BlockSpec(memory_space=pltpu.HBM)


def hat(ray, centre):
    return jnp.maximum(0.0, 1.0 - jnp.abs(ray - centre)).astype(BF16)


def row_taps(offset, slope, extent):
    shape = (offset.shape[0], extent)
    ray = lax.broadcasted_iota(I32, shape, 1).astype(F32)
    offset = jnp.broadcast_to(offset, shape)
    slope = jnp.broadcast_to(slope, shape)
    middle = jnp.floor((ray - offset) / slope + 0.5)
    middle = jnp.minimum(jnp.maximum(middle, 1.0), extent - 2.0)
    weights = [hat(ray, offset + slope * (middle + step)) for step in (-1.0, 0.0, 1.0)]
    return middle.astype(I32), weights


def column_taps(offset, slope, extent):
    shape = (offset.shape[0], extent)
    voxel = lax.broadcasted_iota(I32, shape, 1).astype(F32)
    centre = jnp.broadcast_to(offset, shape) + jnp.broadcast_to(slope, shape) * voxel
    first = jnp.minimum(jnp.maximum(jnp.floor(centre), 0.0), extent - 2.0)
    weights = [hat(first + step, centre) for step in (0.0, 1.0)]
    return first.astype(I32), weights


def repeat_rows(values, times):
    return jnp.concatenate(
        [jnp.broadcast_to(values[row:row + 1, :], (times, values.shape[1]))
         for row in range(values.shape[0])], axis=0)


def contract_lanes(left, right):
    return lax.dot_general(
        left.astype(BF16), right.astype(BF16), (((1,), (1,)), ((), ())), preferred_element_type=F32)


def per_slot(live_ref, slots, capacity):
    targets = live_ref.shape[1]
    slot = lax.broadcasted_iota(I32, (targets, slots), 1)
    owner = lax.broadcasted_iota(I32, (targets, slots), 0)
    expand = (lax.div(slot, capacity) == owner).astype(F32)
    return jnp.dot(live_ref[...].astype(F32), expand, precision=HIGHEST, preferred_element_type=F32)


def pack_kernel(capacity, *refs):
    sources, out_ref, loaded, arrived = refs[:6], refs[6], refs[7:13], refs[13]
    copies = [
        pltpu.make_async_copy(source, ref, arrived.at[place])
        for place, (source, ref) in enumerate(zip(sources, loaded))]
    for copy in copies:
        copy.start()
    for copy in copies:
        copy.wait()
    volume_ref, offset_ref, slope_ref, voxel_ref, ray_ref, live_ref = loaded
    rows, extent = volume_ref.shape
    out_ref[0:rows, :] = volume_ref[...].astype(BF16)
    slots = ray_ref.shape[1]
    fields = []
    for ref in (offset_ref, slope_ref):
        left = ref[...]
        for addend in range(3):
            part = left.astype(BF16).astype(F32)
            fields.append(part)
            left = left - part
    fields.append(voxel_ref[...].astype(F32))
    fields.append(ray_ref[...].astype(F32))
    fields.append(per_slot(live_ref, slots, capacity))
    used = sum(field.shape[0] for field in fields)
    fields.append(jnp.zeros((-used % 16, slots), F32))
    fields = jnp.concatenate(fields, axis=0)
    height = fields.shape[0]
    for part in range(slots // extent):
        at = pl.ds(rows + part * height, height)
        out_ref[at, :] = fields[:, part * extent:(part + 1) * extent].astype(BF16)
    below = rows + height * (slots // extent)
    if below < out_ref.shape[0]:
        left = volume_ref[...] - volume_ref[...].astype(BF16).astype(F32)
        out_ref[below:below + rows, :] = left.astype(BF16)


def read_fields(payload_ref, at, depth):
    height = -(-(7 * depth + 2) // 16) * 16
    raw = payload_ref[pl.ds(at, height), :].astype(F32)
    offset = (raw[0:depth] + raw[depth:2 * depth]) + raw[2 * depth:3 * depth]
    slope = (raw[3 * depth:4 * depth] + raw[4 * depth:5 * depth]) + raw[5 * depth:6 * depth]
    return jnp.concatenate(
        [offset, slope, raw[6 * depth:7 * depth + 2],
         jnp.zeros((16 - 3 * depth - 2, raw.shape[1]), F32)], axis=0)


def setup_kernel(n_payloads, members, stride, span, sizes, tiles, wanted, *refs):
    payload_refs, refs = refs[:n_payloads], refs[-(2 * len(wanted) + 9):]
    each = members // n_payloads
    list_refs, row_ref, tables = refs[:len(wanted)], refs[len(wanted)], refs[len(wanted) + 1:-len(wanted) - 1]
    drafts, arrived = refs[-len(wanted) - 1:-1], refs[-1]
    copies = [
        pltpu.make_async_copy(draft, ref, arrived.at[place])
        for place, (draft, ref) in enumerate(zip(drafts, list_refs))]
    capacity, depth, frames = sizes
    width = span * capacity
    extent = row_ref.shape[1]
    ray_tiles = row_ref.shape[0] // span
    height = -(-(7 * depth + 2) // 16) * 16
    lanes = drafts[0].shape[1]
    me = lax.axis_index("slab").astype(I32)
    parity = lax.rem(me, span)
    first_slot = (me - parity) * capacity
    part = lax.div(first_slot, extent)
    shift = lax.rem(extent - lax.rem(first_slot, extent), extent)

    def collect(member, lined, payload_ref, within):
        at = within * stride + tiles * frames + part * height
        fields = read_fields(payload_ref, pl.multiple_of(at, 16), depth)
        fields = pltpu.roll(fields, shift, axis=1)
        lane = lax.broadcasted_iota(I32, fields.shape, 1)
        fields = jnp.where(lane < width, fields, 0.0)
        if lanes > extent:
            fields = jnp.concatenate(
                [fields, jnp.zeros((fields.shape[0], lanes - extent), F32)], axis=1)
        return lined + pltpu.roll(fields, member * width, axis=1)

    lined = jnp.zeros((16, lanes), F32)
    if members <= 16:
        for member in range(members):
            lined = collect(member, lined, payload_refs[member // each], member % each)
    else:
        lined = lax.fori_loop(
            0, members, lambda member, lined: collect(member, lined, payload_refs[0], member), lined)

    slot = lax.broadcasted_iota(I32, (1, lanes), 1)
    within = lax.rem(slot, width)
    target = lax.bitwise_xor(lax.div(within, capacity), parity)
    ray = lined[3 * depth:3 * depth + 1]
    count = lined[3 * depth + 1:3 * depth + 2]
    alive = jnp.logical_and(lax.rem(within, capacity).astype(F32) < count, slot < members * width)

    table = jnp.concatenate(
        [slot.astype(F32), ray, target.astype(F32), lined[2 * depth:3 * depth],
         jnp.zeros((5 - depth, lanes), F32)], axis=0)
    order = lax.broadcasted_iota(I32, (lanes, lanes), 0)
    earlier = (lax.broadcasted_iota(I32, (lanes, lanes), 1) < order).astype(F32)
    for ref, (low, high, kind), copy in zip(drafts, wanted, copies):
        taken = alive if kind is None else jnp.logical_and(alive, target == kind)
        taken = jnp.logical_and(taken, jnp.logical_and(slot >= low * width, slot < high * width))
        taken = taken.astype(F32)
        position = contract_lanes(jnp.broadcast_to(taken, (8, lanes)), earlier)[0:1]
        position = jnp.where(taken > 0.0, position, -1.0).astype(I32)
        choose = jnp.broadcast_to(position, (lanes, lanes)) == order
        packed = (contract_lanes(table, choose.astype(F32)) + 0.5).astype(I32)
        total = jnp.sum(taken, axis=1, keepdims=True).astype(I32)
        line = jnp.where(slot < total, packed[0:1], lanes)
        base = packed[1:2] if kind is not None else packed[1:2] + packed[2:3] * ray_tiles
        member = jnp.maximum(lax.div(packed[0:1], width) - low, 0) * tiles
        rows = [line, base * frames]
        rows += [(packed[3 + level:4 + level] + member) * frames for level in range(depth)]
        rows += [jnp.zeros((5 - depth, lanes), I32), jnp.broadcast_to(total, (1, lanes))]
        ref[...] = jnp.concatenate(rows, axis=0)
        copy.start()

    columns = lined.T
    summed = None
    for level in range(depth):
        offset = columns[:, level:level + 1]
        slope = columns[:, depth + level:depth + level + 1]
        middle, weights = row_taps(offset, slope, extent)
        first, pair = column_taps(offset, slope, extent)
        wide = [weight.astype(F32) for weight in weights]
        values = [middle] + wide + [first] + [weight.astype(F32) for weight in pair]
        at = level * (lanes + 8)
        for ref, value in zip(tables, values):
            ref[at:at + lanes, :] = value
            blank = jnp.ones if ref.dtype == I32 else jnp.zeros
            ref[at + lanes:at + lanes + 8, :] = blank((8, extent), ref.dtype)
        parts = (wide[0] + wide[1]) + wide[2]
        summed = parts if summed is None else summed + parts

    tile = lax.broadcasted_iota(I32, (span * ray_tiles, lanes), 0).astype(F32)
    place = ray + (target * ray_tiles).astype(F32)
    place = jnp.where(alive, place, -1.0)
    hot = (jnp.broadcast_to(place, tile.shape) == tile).astype(F32)
    row_ref[...] = jnp.dot(hot, summed, precision=HIGHEST, preferred_element_type=F32)
    for copy in copies:
        copy.wait()


def column_kernel(sizes, stride, tiles, slots, payload_ref, out_ref):
    capacity, depth, frames = sizes
    extent = out_ref.shape[1]
    height = -(-(7 * depth + 2) // 16) * 16
    rows = tiles * frames
    within = lax.rem(lax.broadcasted_iota(I32, (1, extent), 1), capacity).astype(F32)
    tile = lax.broadcasted_iota(I32, (tiles, extent), 0).astype(F32)
    for member in range(out_ref.shape[0] // rows):
        total = jnp.zeros((tiles, extent), F32)
        for part in range(slots // extent):
            at = member * stride + rows + part * height
            fields = read_fields(payload_ref, at, depth)
            columns = fields.T
            alive = within < fields[3 * depth + 1:3 * depth + 2]
            for level in range(depth):
                unused, pair = column_taps(
                    columns[:, level:level + 1], columns[:, depth + level:depth + level + 1], extent)
                voxel = jnp.where(alive, fields[2 * depth + level:2 * depth + level + 1], -1.0)
                hot = (jnp.broadcast_to(voxel, tile.shape) == tile).astype(F32).astype(BF16)
                for weight in pair:
                    total += jnp.dot(hot, weight, preferred_element_type=F32)
        out_ref[member * rows:(member + 1) * rows, :] = repeat_rows(
            1.0 / jnp.maximum(total, 1.0), frames)


def pick(values, index):
    numbers = lax.GatherDimensionNumbers(
        offset_dims=(), collapsed_slice_dims=(1,), start_index_map=(1,),
        operand_batching_dims=(0,), start_indices_batching_dims=(0,))
    return lax.gather(
        values, index[:, :, None], numbers, slice_sizes=(1, 1),
        mode=lax.GatherScatterMode.PROMISE_IN_BOUNDS)


def pack_pair(first, second):
    kind = jnp.int16 if first.dtype == I32 else BF16
    return jnp.concatenate([first, second], axis=0).astype(kind)


def spread(ref, row, frames):
    return jnp.broadcast_to(ref[pl.ds(row, 1), :], (frames, ref.shape[1]))


def tile_at(start, frames):
    return pl.ds(pl.multiple_of(start, frames), frames)


def for_slots(slots, body):
    def some(step, carry):
        for place in range(CHUNK):
            body(step * CHUNK + place, place)
        return carry

    lax.fori_loop(0, lax.div(slots[7, 0] + (CHUNK - 1), CHUNK), some, 0)


def for_rows(rows, body):
    step = 128

    def some(number, carry):
        body(pl.ds(pl.multiple_of(number * step, step), step))
        return carry

    lax.fori_loop(0, rows // step, some, 0)


def forward_kernel(sizes, n_values, members, start_row, n_sums, slots, *refs):
    capacity, depth, frames = sizes
    value_refs, tables, refs = refs[:n_values], refs[n_values:n_values + 4], refs[n_values + 4:]
    start_ref = None
    if start_row is not None:
        start_ref, refs = refs[0], refs[1:]
    sum_refs, (out_ref, wide, second) = refs[:n_sums], refs[n_sums:]
    rows = wide.shape[0] // members
    each = members // n_values
    stride = value_refs[0].shape[0] // each
    rays = second.shape[0]
    line_step = tables[0].shape[0] // depth

    def widen(member, carry):
        for place, ref in enumerate(value_refs):
            at = pl.ds(pl.multiple_of((place * each + member) * rows, rows), rows)
            wide[at, :] = ref[pl.ds(pl.multiple_of(member * stride, 16), rows), :].astype(F32)
        return carry

    lax.fori_loop(0, each, widen, 0)
    second[...] = jnp.zeros_like(second)
    if start_ref is None:
        out_ref[...] = jnp.zeros_like(out_ref)
    else:
        out_ref[0:rays, :] = start_ref[start_row:start_row + rays, :]
    if n_sums:
        half = sum_refs[0].shape[0] // 2
        out_ref[rays:, :] = sum([ref[half:, :] for ref in sum_refs[1:]], sum_refs[0][half:, :])

    def one(slot, place):
        line = slots[0, slot]
        taps = []
        for start in range(0, depth, 2):
            levels = range(start, start + 2)
            values = [wide[tile_at(slots[2 + level, slot], frames), :] for level in levels]
            middles = [spread(tables[0], line + level * line_step, frames) for level in levels]
            lower = [
                pick(pack_pair(value, value), pack_pair(middle - 1, middle)).astype(F32)
                for value, middle in zip(values, middles)]
            upper = pick(
                pack_pair(*values), pack_pair(*[middle + 1 for middle in middles])).astype(F32)
            for which, pair in enumerate(lower):
                taps.append((pair[0:frames], pair[frames:2 * frames],
                             upper[which * frames:(which + 1) * frames]))
        total = None
        for level, three in enumerate(taps):
            for ref, tap in zip(tables[1:], three):
                term = spread(ref, line + level * line_step, frames) * tap
                total = term if total is None else total + term
        projection = (out_ref, second)[place % 2]
        projection[tile_at(slots[1, slot], frames), :] += total.astype(BF16).astype(F32)

    for_slots(slots, one)
    out_ref[0:rays, :] += second[...]


def residual_kernel(frames, n_own, projection_ref, sinogram_ref, *refs):
    own, refs, out_ref = refs[:n_own], refs[n_own:-1], refs[-1]
    rays = out_ref.shape[0]
    ray_tiles = rays // frames
    total = sum([ref[0:ray_tiles, :] for ref in own[1:]], own[0][0:ray_tiles, :])
    projection = projection_ref[...]
    if refs:
        projection = projection + refs[0][0:rays, :]
        total = total + refs[-1][rays:, :]
    weight = repeat_rows(1.0 / jnp.maximum(total, 1.0), frames)
    out_ref[...] = ((sinogram_ref[...].astype(F32) - projection) * weight).astype(BF16)


def backward_kernel(sizes, n_parts, has_start, slots, *refs):
    capacity, depth, frames = sizes
    part_refs, tables, refs = refs[:n_parts], refs[n_parts:n_parts + 3], refs[n_parts + 3:]
    start_ref = None
    if has_start:
        start_ref, refs = refs[0], refs[1:]
    out_ref, residual, banks = refs[0], refs[1], refs[2:]
    rays = part_refs[0].shape[0]
    line_step = tables[0].shape[0] // depth
    for place, ref in enumerate(part_refs):
        residual[place * rays:(place + 1) * rays, :] = ref[...].astype(F32)

    def clear(at):
        for place, bank in enumerate(banks):
            if place == 0 and has_start:
                bank[at, :] = start_ref[at, :]
            else:
                bank[at, :] = jnp.zeros((at.size, bank.shape[1]), F32)

    for_rows(banks[0].shape[0], clear)

    def one(slot, place):
        line = slots[0, slot]
        values = residual[tile_at(slots[1, slot], frames), :]
        twice = pack_pair(values, values)
        for level in range(depth):
            row = line + level * line_step
            first = spread(tables[0], row, frames)
            taps = pick(twice, pack_pair(first, first + 1)).astype(F32)
            term = (spread(tables[1], row, frames) * taps[0:frames]
                    + spread(tables[2], row, frames) * taps[frames:2 * frames])
            banks[level % len(banks)][tile_at(slots[2 + level, slot], frames), :] += term

    for_slots(slots, one)

    def finish(at):
        total = sum([bank[at, :] for bank in banks[1:]], banks[0][at, :])
        out_ref[at, :] = total.astype(out_ref.dtype)

    for_rows(out_ref.shape[0], finish)


def join_kernel(rows, *refs):
    for place, ref in enumerate(refs[:-1]):
        refs[-1][place * rows:(place + 1) * rows, :] = ref[0:rows, :]


def combine_kernel(sum_ref, *refs):
    total = sum_ref[...]
    for ref in refs[:-2]:
        total = total + ref[...].astype(F32)
    out_ref, send_ref = refs[-2:]
    out_ref[...] = total
    send_ref[...] = total[total.shape[0] - send_ref.shape[0]:].astype(BF16)


def update_pair_kernel(last, volume_ref, column_ref, sum_ref, got_ref, *refs):
    rows = volume_ref.shape[0]
    if last:
        back = sum_ref[0:rows, :] + got_ref[...].astype(F32)
        refs[0][...] = volume_ref[...] + column_ref[0:rows, :] * back
        return
    other_ref, out_ref, other_out, payload_ref = refs
    if other_ref.dtype == BF16:
        left = other_ref.shape[0] - rows
        other = other_ref[0:rows, :].astype(F32) + other_ref[left:, :].astype(F32)
    else:
        other = other_ref[...]
    mine = sum_ref[...].astype(BF16).astype(F32)
    back = mine[0:rows] + got_ref[rows:, :].astype(F32)
    other_back = mine[rows:] + got_ref[0:rows, :].astype(F32)
    volume = volume_ref[...] + column_ref[0:rows, :] * back
    other = other + column_ref[rows:, :] * other_back
    out_ref[...] = volume
    other_out[...] = other
    payload_ref[0:rows, :] = volume.astype(BF16)
    payload_ref[rows:, :] = other.astype(BF16)


def update_kernel(volume_ref, column_ref, back_ref, *refs):
    volume = volume_ref[...] + column_ref[...] * back_ref[...]
    for ref in refs:
        ref[...] = volume.astype(ref.dtype)


def call(kernel, name, mib, in_specs, out_shape, *operands, scratch=()):
    one = not isinstance(out_shape, list)
    return pl.pallas_call(
        kernel,
        out_shape=out_shape,
        in_specs=in_specs,
        out_specs=VMEM if one else [
            SMEM if getattr(out, "memory_space", None) == pltpu.SMEM else VMEM for out in out_shape],
        scratch_shapes=list(scratch),
        compiler_params=pltpu.CompilerParams(vmem_limit_bytes=mib * 1024 * 1024),
        name=name,
    )(*operands)


def exchange(values, n_slab, distance):
    return lax.ppermute(
        values, "slab", [(device, device ^ distance) for device in range(n_slab)])


def shards(sinogram, start_volume, slot_voxel, slot_ray, live_count, block_slope, block_offset):
    n_slab = lax.axis_size("slab")
    n_slots, depth = slot_voxel.shape
    capacity = n_slots // n_slab
    ray_tiles, frames, extent = sinogram.shape
    voxel_tiles = start_volume.shape[0]
    rows = voxel_tiles * frames
    sizes = (capacity, depth, frames)
    paired = n_slab == 16
    span = 2 if paired else 1
    n_bank = 2 if paired else 1
    shape = jax.ShapeDtypeStruct
    n_rays = ray_tiles * frames
    volume = start_volume.reshape(rows, extent)
    sino = sinogram.reshape(n_rays, extent)
    slots_by_depth = (block_offset.T, block_slope.T, slot_voxel.T)
    live = live_count.reshape(1, n_slab)
    height = -(-(7 * depth + 2) // 16) * 16 * (n_slots // extent)
    operands = (volume, *slots_by_depth, slot_ray.reshape(1, n_slots), live)
    payload = call(
        functools.partial(pack_kernel, capacity), "pack", 16, [HBM] * 6,
        shape((rows + height + (rows if paired else 0), extent), BF16),
        *[pltpu.with_memory_space_constraint(operand, pltpu.HBM) for operand in operands],
        scratch=[pltpu.VMEM(operand.shape, operand.dtype) for operand in operands]
        + [pltpu.SemaphoreType.DMA((6,))])

    def setup(payloads, members, wanted, after=None):
        lanes = -(-members * span * capacity // 128) * 128
        lines = depth * (lanes + 8)
        table = [shape((lines, extent), I32)] + [shape((lines, extent), F32)] * 3
        table += [shape((lines, extent), I32)] + [shape((lines, extent), F32)] * 2
        n = len(wanted)
        out = [pltpu.SMEM((8, lanes), I32)] * n + [shape((span * ray_tiles, extent), F32)] + table
        waits = [] if after is None else [after]
        found = call(
            functools.partial(setup_kernel, len(payloads), members,
                              payloads[0].shape[0] * len(payloads) // members, span, sizes,
                              voxel_tiles, wanted),
            "setup", 24, [VMEM] * len(payloads) + [ANY] * len(waits), out, *payloads, *waits,
            scratch=[pltpu.VMEM((8, lanes), I32)] * n + [pltpu.SemaphoreType.DMA((n,))])
        return found[:n], found[n], found[n + 1:n + 5], found[n + 5:]

    def forward(slots, values, members, table, n_out, start=None, start_row=None, sums=()):
        operands = [pltpu.with_memory_space_constraint(slots, pltpu.SMEM), *values, *table] + ([] if start is None else [start]) + list(sums)
        extra = ray_tiles if sums else 0
        return call(
            functools.partial(forward_kernel, sizes, len(values), members, start_row, len(sums)),
            "forward", 16 if paired else 32, [SMEM] + [VMEM] * (len(operands) - 1),
            shape((n_out + extra, extent), F32), *operands,
            scratch=[pltpu.VMEM((members * rows, extent), F32), pltpu.VMEM((n_out, extent), F32)])

    def residual_of(projection, row_sums, *sibling):
        operands = [projection, sino, *row_sums, *sibling]
        return call(
            functools.partial(residual_kernel, frames, len(row_sums)), "residual", 16,
            [VMEM] * len(operands), shape((n_rays, extent), BF16), *operands)

    def backward(slots, parts, members, table, kind, start=None):
        operands = [pltpu.with_memory_space_constraint(slots, pltpu.SMEM), *parts, *table]
        operands += [] if start is None else [start]
        return call(
            functools.partial(backward_kernel, sizes, len(parts), start is not None),
            "backward", 16 if paired else 32, [SMEM] + [VMEM] * (len(operands) - 1),
            shape((members * rows, extent), kind), *operands,
            scratch=[pltpu.VMEM((len(parts) * n_rays, extent), F32)]
            + [pltpu.VMEM((members * rows, extent), F32)] * n_bank)

    def column_weights(payload, members):
        return call(
            functools.partial(column_kernel, sizes, payload.shape[0] // members, voxel_tiles, n_slots),
            "column_weight", 16, [VMEM], shape((members * rows, extent), F32), payload)

    whole, rounded = shape((rows, extent), F32), shape((rows, extent), BF16)
    if not paired:
        column_weight = column_weights(payload, 1)
    for sweep in range(ITERS):
        last = sweep + 1 == ITERS
        if paired:
            if sweep == 0:
                beside = exchange(payload, n_slab, 2)
                group_0 = call(
                    functools.partial(join_kernel, rows + height), "join", 16, [VMEM] * 2,
                    shape((2 * (rows + height), extent), BF16), payload, beside)
            group_1, group_2, group_3 = [
                exchange(group_0, n_slab, distance) for distance in (8, 12, 4)]
            if sweep == 0:
                (list_0, list_1), rows_a, forward_a, backward_a = setup(
                    (group_0, group_1), 4, ((0, 2, None), (2, 4, None)))
            both = forward(list_0, (group_0,), 2, forward_a, 2 * n_rays)
            both = forward(list_1, (group_1,), 2, forward_a, 2 * n_rays, both, 0)
            if sweep == 0:
                (list_3, list_own, list_other), rows_b, forward_b, backward_b = setup(
                    (group_3, group_2), 4, ((0, 2, None), (2, 4, 0), (2, 4, 1)), after=both)
                row_sums = (rows_a, rows_b)
            both = forward(list_3, (group_3,), 2, forward_b, 2 * n_rays, both, 0)
            other = exchange(
                forward(list_other, (group_2,), 2, forward_b, n_rays, both, n_rays,
                        row_sums if sweep == 0 else ()), n_slab, 1)
            if sweep == 0:
                first_other = other
                column_weight = column_weights(group_0, 2)
            own = forward(list_own, (group_2,), 2, forward_b, n_rays, both, 0)
            residual = residual_of(own, row_sums, other, first_other)
            other_residual = exchange(residual, n_slab, 1)
            residuals = [residual, other_residual]
            sum_2 = backward(list_own, [residual], 2, backward_b, F32)
            sum_2 = backward(list_other, [other_residual], 2, backward_b, BF16, sum_2)
            got_2 = exchange(sum_2, n_slab, 12)
            got_1 = exchange(backward(list_1, residuals, 2, backward_a, BF16), n_slab, 8)
            got_3 = exchange(backward(list_3, residuals, 2, backward_b, BF16), n_slab, 4)
            sum_0 = backward(list_0, residuals, 2, backward_a, F32)
            total, send = call(
                combine_kernel, "combine", 16, [VMEM] * 4,
                [shape((2 * rows, extent), F32), shape(((1 if last else 2) * rows, extent), BF16)],
                sum_0, got_1, got_2, got_3)
            operands = [volume, column_weight, total, exchange(send, n_slab, 2)]
            operands += [] if last else [beside]
            volume, *rest = call(
                functools.partial(update_pair_kernel, last), "update", 16, [VMEM] * len(operands),
                [whole] if last else [whole, whole, shape((2 * rows, extent), BF16)], *operands)
            if not last:
                beside, group_0 = rest
        else:
            everyone = lax.all_gather(payload, "slab", axis=0, tiled=True)
            if sweep == 0:
                (slots,), row_sums, to_rays, to_voxels = setup(
                    (everyone,), n_slab, ((0, n_slab, None),))
            projection = forward(slots, (everyone,), n_slab, to_rays, n_rays)
            residual = residual_of(projection, (row_sums,))
            sums = backward(slots, [residual], n_slab, to_voxels, BF16)
            parts = lax.all_to_all(
                sums.reshape(n_slab, rows, extent), "slab", split_axis=0, concat_axis=0, tiled=True)
            volume, *rest = call(
                update_kernel, "update", 16, [VMEM] * 3, [whole] if last else [whole, rounded],
                volume, column_weight, jnp.sum(parts.astype(F32), axis=0))
            if not last:
                payload = rest[0]
    return volume.reshape(start_volume.shape)


def solution(mesh):
    in_specs = (
        P(("scan", "slab"), None, None),
        P(("scan", "slab"), None, None),
        P(("scan", "slab"), None),
        P(("scan", "slab")),
        P(("scan", "slab")),
        P(("scan", "slab"), None),
        P(("scan", "slab"), None),
    )
    out_specs = P(("scan", "slab"), None, None)
    return jax.shard_map(shards, mesh=mesh, in_specs=in_specs, out_specs=out_specs, check_vma=False)
```

```python
import functools

import jax
import jax.numpy as jnp
from jax import lax
from jax.experimental import pallas as pl
from jax.experimental.pallas import tpu as pltpu
from jax.sharding import PartitionSpec as P

ITERS = 2
CHUNK = 16
F32 = jnp.float32
BF16 = jnp.bfloat16
I32 = jnp.int32
HIGHEST = lax.Precision.HIGHEST
VMEM = pl.BlockSpec(memory_space=pltpu.VMEM)
ANY = pl.BlockSpec(memory_space=pl.ANY)
SMEM = pl.BlockSpec(memory_space=pltpu.SMEM)
HBM = pl.BlockSpec(memory_space=pltpu.HBM)


def hat(ray, centre):
    return jnp.maximum(0.0, 1.0 - jnp.abs(ray - centre)).astype(BF16)


def row_taps(offset, slope, extent):
    shape = (offset.shape[0], extent)
    ray = lax.broadcasted_iota(I32, shape, 1).astype(F32)
    offset = jnp.broadcast_to(offset, shape)
    slope = jnp.broadcast_to(slope, shape)
    middle = jnp.floor((ray - offset) / slope + 0.5)
    middle = jnp.minimum(jnp.maximum(middle, 1.0), extent - 2.0)
    weights = [hat(ray, offset + slope * (middle + step)) for step in (-1.0, 0.0, 1.0)]
    return middle.astype(I32), weights


def column_taps(offset, slope, extent):
    shape = (offset.shape[0], extent)
    voxel = lax.broadcasted_iota(I32, shape, 1).astype(F32)
    centre = jnp.broadcast_to(offset, shape) + jnp.broadcast_to(slope, shape) * voxel
    first = jnp.minimum(jnp.maximum(jnp.floor(centre), 0.0), extent - 2.0)
    weights = [hat(first + step, centre) for step in (0.0, 1.0)]
    return first.astype(I32), weights


def repeat_rows(values, times):
    return jnp.concatenate(
        [jnp.broadcast_to(values[row:row + 1, :], (times, values.shape[1]))
         for row in range(values.shape[0])], axis=0)


def contract_lanes(left, right):
    return lax.dot_general(
        left.astype(BF16), right.astype(BF16), (((1,), (1,)), ((), ())), preferred_element_type=F32)


def per_slot(live_ref, slots, capacity):
    targets = live_ref.shape[1]
    slot = lax.broadcasted_iota(I32, (targets, slots), 1)
    owner = lax.broadcasted_iota(I32, (targets, slots), 0)
    expand = (lax.div(slot, capacity) == owner).astype(F32)
    return jnp.dot(live_ref[...].astype(F32), expand, precision=HIGHEST, preferred_element_type=F32)


def pack_kernel(capacity, *refs):
    sources, out_ref, loaded, arrived = refs[:6], refs[6], refs[7:13], refs[13]
    copies = [
        pltpu.make_async_copy(source, ref, arrived.at[place])
        for place, (source, ref) in enumerate(zip(sources, loaded))]
    for copy in copies:
        copy.start()
    for copy in copies:
        copy.wait()
    volume_ref, offset_ref, slope_ref, voxel_ref, ray_ref, live_ref = loaded
    rows, extent = volume_ref.shape
    out_ref[0:rows, :] = volume_ref[...].astype(BF16)
    slots = ray_ref.shape[1]
    fields = []
    for ref in (offset_ref, slope_ref):
        left = ref[...]
        for addend in range(3):
            part = left.astype(BF16).astype(F32)
            fields.append(part)
            left = left - part
    fields.append(voxel_ref[...].astype(F32))
    fields.append(ray_ref[...].astype(F32))
    fields.append(per_slot(live_ref, slots, capacity))
    used = sum(field.shape[0] for field in fields)
    fields.append(jnp.zeros((-used % 16, slots), F32))
    fields = jnp.concatenate(fields, axis=0)
    height = fields.shape[0]
    for part in range(slots // extent):
        at = pl.ds(rows + part * height, height)
        out_ref[at, :] = fields[:, part * extent:(part + 1) * extent].astype(BF16)


def setup_kernel(n_payloads, members, stride, span, sizes, tiles, wanted, *refs):
    payload_refs, refs = refs[:n_payloads], refs[-(2 * len(wanted) + 9):]
    each = members // n_payloads
    list_refs, row_ref, tables = refs[:len(wanted)], refs[len(wanted)], refs[len(wanted) + 1:-len(wanted) - 1]
    drafts, arrived = refs[-len(wanted) - 1:-1], refs[-1]
    copies = [
        pltpu.make_async_copy(draft, ref, arrived.at[place])
        for place, (draft, ref) in enumerate(zip(drafts, list_refs))]
    capacity, depth, frames = sizes
    width = span * capacity
    extent = row_ref.shape[1]
    ray_tiles = row_ref.shape[0] // span
    height = -(-(7 * depth + 2) // 16) * 16
    lanes = drafts[0].shape[1]
    me = lax.axis_index("slab").astype(I32)
    parity = lax.rem(me, span)
    first_slot = (me - parity) * capacity
    part = lax.div(first_slot, extent)
    shift = lax.rem(extent - lax.rem(first_slot, extent), extent)

    def collect(member, lined, payload_ref, within):
        at = within * stride + tiles * frames + part * height
        raw = payload_ref[pl.ds(pl.multiple_of(at, 16), height), :].astype(F32)
        offset = (raw[0:depth] + raw[depth:2 * depth]) + raw[2 * depth:3 * depth]
        slope = (raw[3 * depth:4 * depth] + raw[4 * depth:5 * depth]) + raw[5 * depth:6 * depth]
        fields = jnp.concatenate(
            [offset, slope, raw[6 * depth:7 * depth + 2],
             jnp.zeros((16 - 3 * depth - 2, extent), F32)], axis=0)
        fields = pltpu.roll(fields, shift, axis=1)
        lane = lax.broadcasted_iota(I32, fields.shape, 1)
        fields = jnp.where(lane < width, fields, 0.0)
        if lanes > extent:
            fields = jnp.concatenate(
                [fields, jnp.zeros((fields.shape[0], lanes - extent), F32)], axis=1)
        return lined + pltpu.roll(fields, member * width, axis=1)

    lined = jnp.zeros((16, lanes), F32)
    if members <= 16:
        for member in range(members):
            lined = collect(member, lined, payload_refs[member // each], member % each)
    else:
        lined = lax.fori_loop(
            0, members, lambda member, lined: collect(member, lined, payload_refs[0], member), lined)

    slot = lax.broadcasted_iota(I32, (1, lanes), 1)
    within = lax.rem(slot, width)
    target = lax.bitwise_xor(lax.div(within, capacity), parity)
    ray = lined[3 * depth:3 * depth + 1]
    count = lined[3 * depth + 1:3 * depth + 2]
    alive = jnp.logical_and(lax.rem(within, capacity).astype(F32) < count, slot < members * width)

    table = jnp.concatenate(
        [slot.astype(F32), ray, target.astype(F32), lined[2 * depth:3 * depth],
         jnp.zeros((5 - depth, lanes), F32)], axis=0)
    order = lax.broadcasted_iota(I32, (lanes, lanes), 0)
    earlier = (lax.broadcasted_iota(I32, (lanes, lanes), 1) < order).astype(F32)
    for ref, kind, copy in zip(drafts, wanted, copies):
        taken = alive if kind is None else jnp.logical_and(alive, target == kind)
        taken = taken.astype(F32)
        position = contract_lanes(jnp.broadcast_to(taken, (8, lanes)), earlier)[0:1]
        position = jnp.where(taken > 0.0, position, -1.0).astype(I32)
        choose = jnp.broadcast_to(position, (lanes, lanes)) == order
        packed = (contract_lanes(table, choose.astype(F32)) + 0.5).astype(I32)
        total = jnp.sum(taken, axis=1, keepdims=True).astype(I32)
        line = jnp.where(slot < total, packed[0:1], lanes)
        base = packed[1:2] if kind is not None else packed[1:2] + packed[2:3] * ray_tiles
        member = lax.div(packed[0:1], width) * tiles
        rows = [line, base * frames]
        rows += [(packed[3 + level:4 + level] + member) * frames for level in range(depth)]
        rows += [jnp.zeros((5 - depth, lanes), I32), jnp.broadcast_to(total, (1, lanes))]
        ref[...] = jnp.concatenate(rows, axis=0)
        copy.start()

    columns = lined.T
    summed = None
    for level in range(depth):
        offset = columns[:, level:level + 1]
        slope = columns[:, depth + level:depth + level + 1]
        middle, weights = row_taps(offset, slope, extent)
        first, pair = column_taps(offset, slope, extent)
        wide = [weight.astype(F32) for weight in weights]
        values = [middle] + wide + [first] + [weight.astype(F32) for weight in pair]
        at = level * (lanes + 8)
        for ref, value in zip(tables, values):
            ref[at:at + lanes, :] = value
            blank = jnp.ones if ref.dtype == I32 else jnp.zeros
            ref[at + lanes:at + lanes + 8, :] = blank((8, extent), ref.dtype)
        parts = (wide[0] + wide[1]) + wide[2]
        summed = parts if summed is None else summed + parts

    tile = lax.broadcasted_iota(I32, (span * ray_tiles, lanes), 0).astype(F32)
    place = ray + (target * ray_tiles).astype(F32)
    place = jnp.where(alive, place, -1.0)
    hot = (jnp.broadcast_to(place, tile.shape) == tile).astype(F32)
    row_ref[...] = jnp.dot(hot, summed, precision=HIGHEST, preferred_element_type=F32)
    for copy in copies:
        copy.wait()


def column_kernel(sizes, offset_ref, slope_ref, voxel_ref, live_ref, out_ref):
    capacity, depth, frames = sizes
    tiles = out_ref.shape[0] // frames
    slots = offset_ref.shape[1]
    extent = out_ref.shape[1]
    offsets = offset_ref[...].T
    slopes = slope_ref[...].T
    within = lax.rem(lax.broadcasted_iota(I32, (1, slots), 1), capacity).astype(F32)
    alive = jnp.broadcast_to(within, (tiles, slots)) < per_slot(live_ref, slots, capacity)
    total = jnp.zeros((tiles, extent), F32)
    for level in range(depth):
        unused, pair = column_taps(
            offsets[:, level:level + 1], slopes[:, level:level + 1], extent)
        tile_of = jnp.broadcast_to(voxel_ref[level:level + 1, :], (tiles, slots))
        match = tile_of == lax.broadcasted_iota(I32, (tiles, slots), 0)
        hot = jnp.logical_and(match, alive).astype(F32).astype(BF16)
        for weight in pair:
            total += jnp.dot(hot, weight, preferred_element_type=F32)
    out_ref[...] = repeat_rows(1.0 / jnp.maximum(total, 1.0), frames)


def pick(values, index):
    numbers = lax.GatherDimensionNumbers(
        offset_dims=(), collapsed_slice_dims=(1,), start_index_map=(1,),
        operand_batching_dims=(0,), start_indices_batching_dims=(0,))
    return lax.gather(
        values, index[:, :, None], numbers, slice_sizes=(1, 1),
        mode=lax.GatherScatterMode.PROMISE_IN_BOUNDS)


def pack_pair(first, second):
    kind = jnp.int16 if first.dtype == I32 else BF16
    return jnp.concatenate([first, second], axis=0).astype(kind)


def spread(ref, row, frames):
    return jnp.broadcast_to(ref[pl.ds(row, 1), :], (frames, ref.shape[1]))


def tile_at(start, frames):
    return pl.ds(pl.multiple_of(start, frames), frames)


def for_slots(slots, body):
    def some(step, carry):
        for place in range(CHUNK):
            body(step * CHUNK + place, place)
        return carry

    lax.fori_loop(0, lax.div(slots[7, 0] + (CHUNK - 1), CHUNK), some, 0)


def for_rows(rows, body):
    step = 128

    def some(number, carry):
        body(pl.ds(pl.multiple_of(number * step, step), step))
        return carry

    lax.fori_loop(0, rows // step, some, 0)


def forward_kernel(sizes, n_values, members, start_row, n_sums, slots, *refs):
    capacity, depth, frames = sizes
    value_refs, tables, refs = refs[:n_values], refs[n_values:n_values + 4], refs[n_values + 4:]
    start_ref = None
    if start_row is not None:
        start_ref, refs = refs[0], refs[1:]
    sum_refs, (out_ref, wide, second) = refs[:n_sums], refs[n_sums:]
    rows = wide.shape[0] // members
    each = members // n_values
    stride = value_refs[0].shape[0] // each
    rays = second.shape[0]
    line_step = tables[0].shape[0] // depth

    def widen(member, carry):
        for place, ref in enumerate(value_refs):
            at = pl.ds(pl.multiple_of((place * each + member) * rows, rows), rows)
            wide[at, :] = ref[pl.ds(pl.multiple_of(member * stride, 16), rows), :].astype(F32)
        return carry

    lax.fori_loop(0, each, widen, 0)
    second[...] = jnp.zeros_like(second)
    if start_ref is None:
        out_ref[...] = jnp.zeros_like(out_ref)
    else:
        out_ref[0:rays, :] = start_ref[start_row:start_row + rays, :]
    if n_sums:
        half = sum_refs[0].shape[0] // 2
        out_ref[rays:, :] = sum([ref[half:, :] for ref in sum_refs[1:]], sum_refs[0][half:, :])

    def one(slot, place):
        line = slots[0, slot]
        taps = []
        for start in range(0, depth, 2):
            levels = range(start, start + 2)
            values = [wide[tile_at(slots[2 + level, slot], frames), :] for level in levels]
            middles = [spread(tables[0], line + level * line_step, frames) for level in levels]
            lower = [
                pick(pack_pair(value, value), pack_pair(middle - 1, middle)).astype(F32)
                for value, middle in zip(values, middles)]
            upper = pick(
                pack_pair(*values), pack_pair(*[middle + 1 for middle in middles])).astype(F32)
            for which, pair in enumerate(lower):
                taps.append((pair[0:frames], pair[frames:2 * frames],
                             upper[which * frames:(which + 1) * frames]))
        total = None
        for level, three in enumerate(taps):
            for ref, tap in zip(tables[1:], three):
                term = spread(ref, line + level * line_step, frames) * tap
                total = term if total is None else total + term
        projection = (out_ref, second)[place % 2]
        projection[tile_at(slots[1, slot], frames), :] += total.astype(BF16).astype(F32)

    for_slots(slots, one)
    out_ref[0:rays, :] += second[...]


def residual_kernel(frames, n_own, projection_ref, sinogram_ref, *refs):
    own, refs, out_ref = refs[:n_own], refs[n_own:-1], refs[-1]
    rays = out_ref.shape[0]
    ray_tiles = rays // frames
    total = sum([ref[0:ray_tiles, :] for ref in own[1:]], own[0][0:ray_tiles, :])
    projection = projection_ref[...]
    if refs:
        projection = projection + refs[0][0:rays, :]
        total = total + refs[-1][rays:, :]
    weight = repeat_rows(1.0 / jnp.maximum(total, 1.0), frames)
    out_ref[...] = ((sinogram_ref[...].astype(F32) - projection) * weight).astype(BF16)


def backward_kernel(sizes, n_parts, has_start, split, slots, *refs):
    capacity, depth, frames = sizes
    part_refs, tables, refs = refs[:n_parts], refs[n_parts:n_parts + 3], refs[n_parts + 3:]
    start_ref = None
    if has_start:
        start_ref, refs = refs[0], refs[1:]
    outs = refs[:len(split)] if split else refs[:1]
    residual, banks = refs[len(outs)], refs[len(outs) + 1:]
    rays = part_refs[0].shape[0]
    line_step = tables[0].shape[0] // depth
    for place, ref in enumerate(part_refs):
        residual[place * rays:(place + 1) * rays, :] = ref[...].astype(F32)

    def clear(at):
        for place, bank in enumerate(banks):
            if place == 0 and has_start:
                bank[at, :] = start_ref[at, :]
            else:
                bank[at, :] = jnp.zeros((at.size, bank.shape[1]), F32)

    for_rows(banks[0].shape[0], clear)

    def one(slot, place):
        line = slots[0, slot]
        values = residual[tile_at(slots[1, slot], frames), :]
        twice = pack_pair(values, values)
        for level in range(depth):
            row = line + level * line_step
            first = spread(tables[0], row, frames)
            taps = pick(twice, pack_pair(first, first + 1)).astype(F32)
            term = (spread(tables[1], row, frames) * taps[0:frames]
                    + spread(tables[2], row, frames) * taps[frames:2 * frames])
            banks[level % len(banks)][tile_at(slots[2 + level, slot], frames), :] += term

    for_slots(slots, one)

    def total(at):
        return sum([bank[at, :] for bank in banks[1:]], banks[0][at, :]).astype(outs[0].dtype)

    if split:
        for ref, members in zip(outs, split):
            rows = ref.shape[0] // len(members)
            for place, member in enumerate(members):
                ref[place * rows:(place + 1) * rows, :] = total(pl.ds(member * rows, rows))
    else:
        def finish(at):
            outs[0][at, :] = total(at)

        for_rows(outs[0].shape[0], finish)


def join_kernel(*refs):
    out_ref, at = refs[-1], 0
    for ref in refs[:-1]:
        out_ref[at:at + ref.shape[0], :] = ref[...]
        at += ref.shape[0]


def combine_kernel(members, sum_ref, y_ref, *piece_refs):
    rows = piece_refs[0].shape[0]
    for place, (member, ref) in enumerate(zip(members, piece_refs)):
        mine = sum_ref[member * rows:(member + 1) * rows, :]
        ref[...] = (mine + y_ref[place * rows:(place + 1) * rows, :].astype(F32)).astype(ref.dtype)


def update_kernel(n_pieces, volume_ref, column_ref, *refs):
    back = refs[0][...]
    for ref in refs[1:n_pieces]:
        back = back + ref[...].astype(F32)
    volume = volume_ref[...] + column_ref[...] * back
    for ref in refs[n_pieces:]:
        ref[...] = volume.astype(ref.dtype)


def call(kernel, name, mib, in_specs, out_shape, *operands, scratch=()):
    one = not isinstance(out_shape, list)
    return pl.pallas_call(
        kernel,
        out_shape=out_shape,
        in_specs=in_specs,
        out_specs=VMEM if one else [
            SMEM if getattr(out, "memory_space", None) == pltpu.SMEM else VMEM for out in out_shape],
        scratch_shapes=list(scratch),
        compiler_params=pltpu.CompilerParams(vmem_limit_bytes=mib * 1024 * 1024),
        name=name,
    )(*operands)


def exchange(values, n_slab, distance, odd_distance=None):
    far = (distance, distance if odd_distance is None else odd_distance)
    return lax.ppermute(
        values, "slab", [(device, device ^ far[device % 2]) for device in range(n_slab)])


def shards(sinogram, start_volume, slot_voxel, slot_ray, live_count, block_slope, block_offset):
    n_slab = lax.axis_size("slab")
    n_slots, depth = slot_voxel.shape
    capacity = n_slots // n_slab
    ray_tiles, frames, extent = sinogram.shape
    voxel_tiles = start_volume.shape[0]
    rows = voxel_tiles * frames
    sizes = (capacity, depth, frames)
    paired = n_slab == 16
    span = 2 if paired else 1
    n_bank = 2 if paired else 1
    shape = jax.ShapeDtypeStruct
    n_rays = ray_tiles * frames
    volume = start_volume.reshape(rows, extent)
    sino = sinogram.reshape(n_rays, extent)
    slots_by_depth = (block_offset.T, block_slope.T, slot_voxel.T)
    live = live_count.reshape(1, n_slab)
    height = -(-(7 * depth + 2) // 16) * 16 * (n_slots // extent)
    operands = (volume, *slots_by_depth, slot_ray.reshape(1, n_slots), live)
    payload = call(
        functools.partial(pack_kernel, capacity), "pack", 16, [HBM] * 6,
        shape((rows + height, extent), BF16),
        *[pltpu.with_memory_space_constraint(operand, pltpu.HBM) for operand in operands],
        scratch=[pltpu.VMEM(operand.shape, operand.dtype) for operand in operands]
        + [pltpu.SemaphoreType.DMA((6,))])

    def setup(payloads, members, wanted, after=None):
        lanes = -(-members * span * capacity // 128) * 128
        lines = depth * (lanes + 8)
        table = [shape((lines, extent), I32)] + [shape((lines, extent), F32)] * 3
        table += [shape((lines, extent), I32)] + [shape((lines, extent), F32)] * 2
        n = len(wanted)
        out = [pltpu.SMEM((8, lanes), I32)] * n + [shape((span * ray_tiles, extent), F32)] + table
        waits = [] if after is None else [after]
        found = call(
            functools.partial(setup_kernel, len(payloads), members,
                              payloads[0].shape[0] * len(payloads) // members, span, sizes,
                              voxel_tiles, wanted),
            "setup", 24, [VMEM] * len(payloads) + [ANY] * len(waits), out, *payloads, *waits,
            scratch=[pltpu.VMEM((8, lanes), I32)] * n + [pltpu.SemaphoreType.DMA((n,))])
        return found[:n], found[n], found[n + 1:n + 5], found[n + 5:]

    def forward(slots, values, members, table, n_out, start=None, start_row=None, sums=()):
        operands = [pltpu.with_memory_space_constraint(slots, pltpu.SMEM), *values, *table] + ([] if start is None else [start]) + list(sums)
        extra = ray_tiles if sums else 0
        return call(
            functools.partial(forward_kernel, sizes, len(values), members, start_row, len(sums)),
            "forward", 16 if paired else 32, [SMEM] + [VMEM] * (len(operands) - 1),
            shape((n_out + extra, extent), F32), *operands,
            scratch=[pltpu.VMEM((members * rows, extent), F32), pltpu.VMEM((n_out, extent), F32)])

    def residual_of(projection, row_sums, *sibling):
        operands = [projection, sino, *row_sums, *sibling]
        return call(
            functools.partial(residual_kernel, frames, len(row_sums)), "residual", 16,
            [VMEM] * len(operands), shape((n_rays, extent), BF16), *operands)

    def backward(slots, parts, members, table, kind, start=None, split=()):
        operands = [pltpu.with_memory_space_constraint(slots, pltpu.SMEM), *parts, *table] + ([] if start is None else [start])
        return call(
            functools.partial(backward_kernel, sizes, len(parts), start is not None, split),
            "backward", 16 if paired else 32, [SMEM] + [VMEM] * (len(operands) - 1),
            [shape((len(some) * rows, extent), kind) for some in split]
            if split else shape((members * rows, extent), kind), *operands,
            scratch=[pltpu.VMEM((len(parts) * n_rays, extent), F32)]
            + [pltpu.VMEM((members * rows, extent), F32)] * n_bank)

    def join(*parts):
        total = sum(part.shape[0] for part in parts)
        return call(join_kernel, "join", 16, [VMEM] * len(parts), shape((total, extent), BF16), *parts)

    def update(volume, pieces, last):
        out = [shape((rows, extent), F32)] + ([] if last else [shape((rows, extent), BF16)])
        return call(
            functools.partial(update_kernel, len(pieces)), "update", 16,
            [VMEM] * (2 + len(pieces)), out, volume, column_weight, *pieces)

    column_weight = call(
        functools.partial(column_kernel, sizes), "column_weight", 16, [VMEM] * 4,
        shape((rows, extent), F32), *slots_by_depth, live)

    for sweep in range(ITERS):
        last = sweep + 1 == ITERS
        if paired:
            place_1, place_2, place_3 = [
                exchange(payload, n_slab, *pair) for pair in ((8, 12), (12, 4), (4, 8))]
            z_half = join(payload, place_1)
            y_half = exchange(z_half, n_slab, 2)
            z_rest = join(place_2, place_3)
            y_rest = exchange(z_rest, n_slab, 2)
            along_z, along_y = (z_half, z_rest), (y_half, y_rest)
            if sweep == 0:
                (z_list,), z_rows, z_forward, z_backward = setup(along_z, 4, (None,))
            both = forward(z_list, along_z, 4, z_forward, 2 * n_rays)
            if sweep == 0:
                (own_list, other_list), y_rows, y_forward, y_backward = setup(
                    along_y, 4, (0, 1), after=both)
            other = exchange(
                forward(other_list, along_y, 4, y_forward, n_rays, both, n_rays,
                        (z_rows, y_rows) if sweep == 0 else ()), n_slab, 1)
            if sweep == 0:
                first_other = other
            own = forward(own_list, along_y, 4, y_forward, n_rays, both, 0)
            residual = residual_of(own, (z_rows, y_rows), other, first_other)
            other_residual = exchange(residual, n_slab, 1)
            y_sum = backward(own_list, [residual], 4, y_backward, F32)
            far_sum, near_sum = backward(
                other_list, [other_residual], 4, y_backward, BF16, y_sum, ((1, 2), (0, 3)))
            far_part, near_part = exchange(far_sum, n_slab, 2), exchange(near_sum, n_slab, 2)
            z_sum = backward(z_list, [residual, other_residual], 4, z_backward, F32)
            piece = shape((rows, extent), BF16)
            piece_1, piece_2 = call(
                functools.partial(combine_kernel, (1, 2)), "combine", 16, [VMEM] * 2,
                [piece, piece], z_sum, far_part)
            got = [exchange(piece_1, n_slab, 8, 12), exchange(piece_2, n_slab, 12, 4)]
            own_piece, piece_3 = call(
                functools.partial(combine_kernel, (0, 3)), "combine", 16, [VMEM] * 2,
                [shape((rows, extent), F32), piece], z_sum, near_part)
            pieces = [own_piece, *got, exchange(piece_3, n_slab, 4, 8)]
        else:
            everyone = lax.all_gather(payload, "slab", axis=0, tiled=True)
            if sweep == 0:
                (slots,), row_sums, to_rays, to_voxels = setup((everyone,), n_slab, (None,))
            projection = forward(slots, (everyone,), n_slab, to_rays, n_rays)
            residual = residual_of(projection, (row_sums,))
            sums = backward(slots, [residual], n_slab, to_voxels, BF16)
            parts = lax.all_to_all(
                sums.reshape(n_slab, rows, extent), "slab", split_axis=0, concat_axis=0, tiled=True)
            pieces = [jnp.sum(parts.astype(F32), axis=0)]
        volume, *rounded = update(volume, pieces, last)
        if not last:
            payload = rounded[0]
    return volume.reshape(start_volume.shape)


def solution(mesh):
    in_specs = (
        P(("scan", "slab"), None, None),
        P(("scan", "slab"), None, None),
        P(("scan", "slab"), None),
        P(("scan", "slab")),
        P(("scan", "slab")),
        P(("scan", "slab"), None),
        P(("scan", "slab"), None),
    )
    out_specs = P(("scan", "slab"), None, None)
    return jax.shard_map(shards, mesh=mesh, in_specs=in_specs, out_specs=out_specs, check_vma=False)
```

```python
import functools

import jax
import jax.numpy as jnp
from jax import lax
from jax.experimental import pallas as pl
from jax.experimental.pallas import tpu as pltpu
from jax.sharding import PartitionSpec as P

ITERS = 2
CHUNK = 16
F32 = jnp.float32
BF16 = jnp.bfloat16
I32 = jnp.int32
HIGHEST = lax.Precision.HIGHEST
VMEM = pl.BlockSpec(memory_space=pltpu.VMEM)
ANY = pl.BlockSpec(memory_space=pl.ANY)
SMEM = pl.BlockSpec(memory_space=pltpu.SMEM)
HBM = pl.BlockSpec(memory_space=pltpu.HBM)


def hat(ray, centre):
    return jnp.maximum(0.0, 1.0 - jnp.abs(ray - centre)).astype(BF16)


def row_taps(offset, slope, extent):
    shape = (offset.shape[0], extent)
    ray = lax.broadcasted_iota(I32, shape, 1).astype(F32)
    offset = jnp.broadcast_to(offset, shape)
    slope = jnp.broadcast_to(slope, shape)
    middle = jnp.floor((ray - offset) / slope + 0.5)
    middle = jnp.minimum(jnp.maximum(middle, 1.0), extent - 2.0)
    weights = [hat(ray, offset + slope * (middle + step)) for step in (-1.0, 0.0, 1.0)]
    return middle.astype(I32), weights


def column_taps(offset, slope, extent):
    shape = (offset.shape[0], extent)
    voxel = lax.broadcasted_iota(I32, shape, 1).astype(F32)
    centre = jnp.broadcast_to(offset, shape) + jnp.broadcast_to(slope, shape) * voxel
    first = jnp.minimum(jnp.maximum(jnp.floor(centre), 0.0), extent - 2.0)
    weights = [hat(first + step, centre) for step in (0.0, 1.0)]
    return first.astype(I32), weights


def repeat_rows(values, times):
    return jnp.concatenate(
        [jnp.broadcast_to(values[row:row + 1, :], (times, values.shape[1]))
         for row in range(values.shape[0])], axis=0)


def contract_lanes(left, right):
    return lax.dot_general(
        left.astype(BF16), right.astype(BF16), (((1,), (1,)), ((), ())), preferred_element_type=F32)


def per_slot(live_ref, slots, capacity):
    targets = live_ref.shape[1]
    slot = lax.broadcasted_iota(I32, (targets, slots), 1)
    owner = lax.broadcasted_iota(I32, (targets, slots), 0)
    expand = (lax.div(slot, capacity) == owner).astype(F32)
    return jnp.dot(live_ref[...].astype(F32), expand, precision=HIGHEST, preferred_element_type=F32)


def pack_kernel(capacity, *refs):
    sources, out_ref, loaded, arrived = refs[:6], refs[6], refs[7:13], refs[13]
    copies = [
        pltpu.make_async_copy(source, ref, arrived.at[place])
        for place, (source, ref) in enumerate(zip(sources, loaded))]
    for copy in copies:
        copy.start()
    for copy in copies:
        copy.wait()
    volume_ref, offset_ref, slope_ref, voxel_ref, ray_ref, live_ref = loaded
    rows, extent = volume_ref.shape
    out_ref[0:rows, :] = volume_ref[...].astype(BF16)
    slots = ray_ref.shape[1]
    fields = []
    for ref in (offset_ref, slope_ref):
        left = ref[...]
        for addend in range(3):
            part = left.astype(BF16).astype(F32)
            fields.append(part)
            left = left - part
    fields.append(voxel_ref[...].astype(F32))
    fields.append(ray_ref[...].astype(F32))
    fields.append(per_slot(live_ref, slots, capacity))
    used = sum(field.shape[0] for field in fields)
    fields.append(jnp.zeros((-used % 16, slots), F32))
    fields = jnp.concatenate(fields, axis=0)
    height = fields.shape[0]
    for part in range(slots // extent):
        at = pl.ds(rows + part * height, height)
        out_ref[at, :] = fields[:, part * extent:(part + 1) * extent].astype(BF16)


def setup_kernel(n_payloads, members, stride, span, sizes, tiles, wanted, *refs):
    payload_refs, refs = refs[:n_payloads], refs[-(2 * len(wanted) + 9):]
    each = members // n_payloads
    list_refs, row_ref, tables = refs[:len(wanted)], refs[len(wanted)], refs[len(wanted) + 1:-len(wanted) - 1]
    drafts, arrived = refs[-len(wanted) - 1:-1], refs[-1]
    copies = [
        pltpu.make_async_copy(draft, ref, arrived.at[place])
        for place, (draft, ref) in enumerate(zip(drafts, list_refs))]
    capacity, depth, frames = sizes
    width = span * capacity
    extent = row_ref.shape[1]
    ray_tiles = row_ref.shape[0] // span
    height = -(-(7 * depth + 2) // 16) * 16
    lanes = drafts[0].shape[1]
    me = lax.axis_index("slab").astype(I32)
    parity = lax.rem(me, span)
    first_slot = (me - parity) * capacity
    part = lax.div(first_slot, extent)
    shift = lax.rem(extent - lax.rem(first_slot, extent), extent)

    def collect(member, lined, payload_ref, within):
        at = within * stride + tiles * frames + part * height
        raw = payload_ref[pl.ds(pl.multiple_of(at, 16), height), :].astype(F32)
        offset = (raw[0:depth] + raw[depth:2 * depth]) + raw[2 * depth:3 * depth]
        slope = (raw[3 * depth:4 * depth] + raw[4 * depth:5 * depth]) + raw[5 * depth:6 * depth]
        fields = jnp.concatenate(
            [offset, slope, raw[6 * depth:7 * depth + 2],
             jnp.zeros((16 - 3 * depth - 2, extent), F32)], axis=0)
        fields = pltpu.roll(fields, shift, axis=1)
        lane = lax.broadcasted_iota(I32, fields.shape, 1)
        fields = jnp.where(lane < width, fields, 0.0)
        if lanes > extent:
            fields = jnp.concatenate(
                [fields, jnp.zeros((fields.shape[0], lanes - extent), F32)], axis=1)
        return lined + pltpu.roll(fields, member * width, axis=1)

    lined = jnp.zeros((16, lanes), F32)
    if members <= 16:
        for member in range(members):
            lined = collect(member, lined, payload_refs[member // each], member % each)
    else:
        lined = lax.fori_loop(
            0, members, lambda member, lined: collect(member, lined, payload_refs[0], member), lined)

    slot = lax.broadcasted_iota(I32, (1, lanes), 1)
    within = lax.rem(slot, width)
    target = lax.bitwise_xor(lax.div(within, capacity), parity)
    ray = lined[3 * depth:3 * depth + 1]
    count = lined[3 * depth + 1:3 * depth + 2]
    alive = jnp.logical_and(lax.rem(within, capacity).astype(F32) < count, slot < members * width)

    table = jnp.concatenate(
        [slot.astype(F32), ray, target.astype(F32), lined[2 * depth:3 * depth],
         jnp.zeros((5 - depth, lanes), F32)], axis=0)
    order = lax.broadcasted_iota(I32, (lanes, lanes), 0)
    earlier = (lax.broadcasted_iota(I32, (lanes, lanes), 1) < order).astype(F32)
    for ref, kind, copy in zip(drafts, wanted, copies):
        taken = alive if kind is None else jnp.logical_and(alive, target == kind)
        taken = taken.astype(F32)
        position = contract_lanes(jnp.broadcast_to(taken, (8, lanes)), earlier)[0:1]
        position = jnp.where(taken > 0.0, position, -1.0).astype(I32)
        choose = jnp.broadcast_to(position, (lanes, lanes)) == order
        packed = (contract_lanes(table, choose.astype(F32)) + 0.5).astype(I32)
        total = jnp.sum(taken, axis=1, keepdims=True).astype(I32)
        line = jnp.where(slot < total, packed[0:1], lanes)
        base = packed[1:2] if kind is not None else packed[1:2] + packed[2:3] * ray_tiles
        member = lax.div(packed[0:1], width) * tiles
        rows = [line, base * frames]
        rows += [(packed[3 + level:4 + level] + member) * frames for level in range(depth)]
        rows += [jnp.zeros((5 - depth, lanes), I32), jnp.broadcast_to(total, (1, lanes))]
        ref[...] = jnp.concatenate(rows, axis=0)
        copy.start()

    columns = lined.T
    summed = None
    for level in range(depth):
        offset = columns[:, level:level + 1]
        slope = columns[:, depth + level:depth + level + 1]
        middle, weights = row_taps(offset, slope, extent)
        first, pair = column_taps(offset, slope, extent)
        wide = [weight.astype(F32) for weight in weights]
        values = [middle] + wide + [first] + [weight.astype(F32) for weight in pair]
        at = level * (lanes + 8)
        for ref, value in zip(tables, values):
            ref[at:at + lanes, :] = value
            blank = jnp.ones if ref.dtype == I32 else jnp.zeros
            ref[at + lanes:at + lanes + 8, :] = blank((8, extent), ref.dtype)
        parts = (wide[0] + wide[1]) + wide[2]
        summed = parts if summed is None else summed + parts

    tile = lax.broadcasted_iota(I32, (span * ray_tiles, lanes), 0).astype(F32)
    place = ray + (target * ray_tiles).astype(F32)
    place = jnp.where(alive, place, -1.0)
    hot = (jnp.broadcast_to(place, tile.shape) == tile).astype(F32)
    row_ref[...] = jnp.dot(hot, summed, precision=HIGHEST, preferred_element_type=F32)
    for copy in copies:
        copy.wait()


def column_kernel(sizes, offset_ref, slope_ref, voxel_ref, live_ref, out_ref):
    capacity, depth, frames = sizes
    tiles = out_ref.shape[0] // frames
    slots = offset_ref.shape[1]
    extent = out_ref.shape[1]
    offsets = offset_ref[...].T
    slopes = slope_ref[...].T
    within = lax.rem(lax.broadcasted_iota(I32, (1, slots), 1), capacity).astype(F32)
    alive = jnp.broadcast_to(within, (tiles, slots)) < per_slot(live_ref, slots, capacity)
    total = jnp.zeros((tiles, extent), F32)
    for level in range(depth):
        unused, pair = column_taps(
            offsets[:, level:level + 1], slopes[:, level:level + 1], extent)
        tile_of = jnp.broadcast_to(voxel_ref[level:level + 1, :], (tiles, slots))
        match = tile_of == lax.broadcasted_iota(I32, (tiles, slots), 0)
        hot = jnp.logical_and(match, alive).astype(F32).astype(BF16)
        for weight in pair:
            total += jnp.dot(hot, weight, preferred_element_type=F32)
    out_ref[...] = repeat_rows(1.0 / jnp.maximum(total, 1.0), frames)


def pick(values, index):
    numbers = lax.GatherDimensionNumbers(
        offset_dims=(), collapsed_slice_dims=(1,), start_index_map=(1,),
        operand_batching_dims=(0,), start_indices_batching_dims=(0,))
    return lax.gather(
        values, index[:, :, None], numbers, slice_sizes=(1, 1),
        mode=lax.GatherScatterMode.PROMISE_IN_BOUNDS)


def pack_pair(first, second):
    kind = jnp.int16 if first.dtype == I32 else BF16
    return jnp.concatenate([first, second], axis=0).astype(kind)


def spread(ref, row, frames):
    return jnp.broadcast_to(ref[pl.ds(row, 1), :], (frames, ref.shape[1]))


def tile_at(start, frames):
    return pl.ds(pl.multiple_of(start, frames), frames)


def for_slots(slots, body):
    def some(step, carry):
        for place in range(CHUNK):
            body(step * CHUNK + place, place)
        return carry

    lax.fori_loop(0, lax.div(slots[7, 0] + (CHUNK - 1), CHUNK), some, 0)


def for_rows(rows, body):
    step = 128

    def some(number, carry):
        body(pl.ds(pl.multiple_of(number * step, step), step))
        return carry

    lax.fori_loop(0, rows // step, some, 0)


def forward_kernel(sizes, n_values, members, start_row, n_sums, slots, *refs):
    capacity, depth, frames = sizes
    value_refs, tables, refs = refs[:n_values], refs[n_values:n_values + 4], refs[n_values + 4:]
    start_ref = None
    if start_row is not None:
        start_ref, refs = refs[0], refs[1:]
    sum_refs, (out_ref, wide, second) = refs[:n_sums], refs[n_sums:]
    rows = wide.shape[0] // members
    each = members // n_values
    stride = value_refs[0].shape[0] // each
    rays = second.shape[0]
    line_step = tables[0].shape[0] // depth

    def widen(member, carry):
        for place, ref in enumerate(value_refs):
            at = pl.ds(pl.multiple_of((place * each + member) * rows, rows), rows)
            wide[at, :] = ref[pl.ds(pl.multiple_of(member * stride, 16), rows), :].astype(F32)
        return carry

    lax.fori_loop(0, each, widen, 0)
    second[...] = jnp.zeros_like(second)
    if start_ref is None:
        out_ref[...] = jnp.zeros_like(out_ref)
    else:
        out_ref[0:rays, :] = start_ref[start_row:start_row + rays, :]
    if n_sums:
        half = sum_refs[0].shape[0] // 2
        out_ref[rays:, :] = sum([ref[half:, :] for ref in sum_refs[1:]], sum_refs[0][half:, :])

    def one(slot, place):
        line = slots[0, slot]
        taps = []
        for start in range(0, depth, 2):
            levels = range(start, start + 2)
            values = [wide[tile_at(slots[2 + level, slot], frames), :] for level in levels]
            middles = [spread(tables[0], line + level * line_step, frames) for level in levels]
            lower = [
                pick(pack_pair(value, value), pack_pair(middle - 1, middle)).astype(F32)
                for value, middle in zip(values, middles)]
            upper = pick(
                pack_pair(*values), pack_pair(*[middle + 1 for middle in middles])).astype(F32)
            for which, pair in enumerate(lower):
                taps.append((pair[0:frames], pair[frames:2 * frames],
                             upper[which * frames:(which + 1) * frames]))
        total = None
        for level, three in enumerate(taps):
            for ref, tap in zip(tables[1:], three):
                term = spread(ref, line + level * line_step, frames) * tap
                total = term if total is None else total + term
        projection = (out_ref, second)[place % 2]
        projection[tile_at(slots[1, slot], frames), :] += total.astype(BF16).astype(F32)

    for_slots(slots, one)
    out_ref[0:rays, :] += second[...]


def residual_kernel(frames, n_own, projection_ref, sinogram_ref, *refs):
    own, refs, out_ref = refs[:n_own], refs[n_own:-1], refs[-1]
    rays = out_ref.shape[0]
    ray_tiles = rays // frames
    total = sum([ref[0:ray_tiles, :] for ref in own[1:]], own[0][0:ray_tiles, :])
    projection = projection_ref[...]
    if refs:
        projection = projection + refs[0][0:rays, :]
        total = total + refs[-1][rays:, :]
    weight = repeat_rows(1.0 / jnp.maximum(total, 1.0), frames)
    out_ref[...] = ((sinogram_ref[...].astype(F32) - projection) * weight).astype(BF16)


def backward_kernel(sizes, n_parts, has_start, split, slots, *refs):
    capacity, depth, frames = sizes
    part_refs, tables, refs = refs[:n_parts], refs[n_parts:n_parts + 3], refs[n_parts + 3:]
    start_ref = None
    if has_start:
        start_ref, refs = refs[0], refs[1:]
    outs = refs[:len(split)] if split else refs[:1]
    residual, banks = refs[len(outs)], refs[len(outs) + 1:]
    rays = part_refs[0].shape[0]
    line_step = tables[0].shape[0] // depth
    for place, ref in enumerate(part_refs):
        residual[place * rays:(place + 1) * rays, :] = ref[...].astype(F32)

    def clear(at):
        for place, bank in enumerate(banks):
            if place == 0 and has_start:
                bank[at, :] = start_ref[at, :]
            else:
                bank[at, :] = jnp.zeros((at.size, bank.shape[1]), F32)

    for_rows(banks[0].shape[0], clear)

    def one(slot, place):
        line = slots[0, slot]
        values = residual[tile_at(slots[1, slot], frames), :]
        twice = pack_pair(values, values)
        for level in range(depth):
            row = line + level * line_step
            first = spread(tables[0], row, frames)
            taps = pick(twice, pack_pair(first, first + 1)).astype(F32)
            term = (spread(tables[1], row, frames) * taps[0:frames]
                    + spread(tables[2], row, frames) * taps[frames:2 * frames])
            banks[level % len(banks)][tile_at(slots[2 + level, slot], frames), :] += term

    for_slots(slots, one)

    def total(at):
        return sum([bank[at, :] for bank in banks[1:]], banks[0][at, :]).astype(outs[0].dtype)

    if split:
        for ref, members in zip(outs, split):
            rows = ref.shape[0] // len(members)
            for place, member in enumerate(members):
                ref[place * rows:(place + 1) * rows, :] = total(pl.ds(member * rows, rows))
    else:
        def finish(at):
            outs[0][at, :] = total(at)

        for_rows(outs[0].shape[0], finish)


def widen_kernel(values_ref, out_ref):
    out_ref[...] = values_ref[...].astype(F32)


def join_kernel(*refs):
    out_ref, at = refs[-1], 0
    for ref in refs[:-1]:
        out_ref[at:at + ref.shape[0], :] = ref[...]
        at += ref.shape[0]


def combine_kernel(members, sum_ref, y_ref, *piece_refs):
    rows = piece_refs[0].shape[0]
    for place, (member, ref) in enumerate(zip(members, piece_refs)):
        mine = sum_ref[member * rows:(member + 1) * rows, :]
        ref[...] = (mine + y_ref[place * rows:(place + 1) * rows, :].astype(F32)).astype(ref.dtype)


def update_kernel(n_pieces, volume_ref, column_ref, *refs):
    back = refs[0][...]
    for ref in refs[1:n_pieces]:
        back = back + ref[...].astype(F32)
    volume = volume_ref[...] + column_ref[...] * back
    for ref in refs[n_pieces:]:
        ref[...] = volume.astype(ref.dtype)


def call(kernel, name, mib, in_specs, out_shape, *operands, scratch=()):
    one = not isinstance(out_shape, list)
    return pl.pallas_call(
        kernel,
        out_shape=out_shape,
        in_specs=in_specs,
        out_specs=VMEM if one else [
            SMEM if getattr(out, "memory_space", None) == pltpu.SMEM else VMEM for out in out_shape],
        scratch_shapes=list(scratch),
        compiler_params=pltpu.CompilerParams(vmem_limit_bytes=mib * 1024 * 1024),
        name=name,
    )(*operands)


def exchange(values, n_slab, distance, odd_distance=None):
    far = (distance, distance if odd_distance is None else odd_distance)
    return lax.ppermute(
        values, "slab", [(device, device ^ far[device % 2]) for device in range(n_slab)])


def shards(sinogram, start_volume, slot_voxel, slot_ray, live_count, block_slope, block_offset):
    n_slab = lax.axis_size("slab")
    n_slots, depth = slot_voxel.shape
    capacity = n_slots // n_slab
    ray_tiles, frames, extent = sinogram.shape
    voxel_tiles = start_volume.shape[0]
    rows = voxel_tiles * frames
    sizes = (capacity, depth, frames)
    paired = n_slab == 16
    span = 2 if paired else 1
    n_bank = 2 if paired else 1
    shape = jax.ShapeDtypeStruct
    n_rays = ray_tiles * frames
    volume = start_volume.reshape(rows, extent)
    sino = sinogram.reshape(n_rays, extent)
    slots_by_depth = (block_offset.T, block_slope.T, slot_voxel.T)
    live = live_count.reshape(1, n_slab)
    height = -(-(7 * depth + 2) // 16) * 16 * (n_slots // extent)
    operands = (volume, *slots_by_depth, slot_ray.reshape(1, n_slots), live)
    payload = call(
        functools.partial(pack_kernel, capacity), "pack", 16, [HBM] * 6,
        shape((rows + height, extent), BF16),
        *[pltpu.with_memory_space_constraint(operand, pltpu.HBM) for operand in operands],
        scratch=[pltpu.VMEM(operand.shape, operand.dtype) for operand in operands]
        + [pltpu.SemaphoreType.DMA((6,))])

    def setup(payloads, members, wanted, after=None):
        lanes = -(-members * span * capacity // 128) * 128
        lines = depth * (lanes + 8)
        table = [shape((lines, extent), I32)] + [shape((lines, extent), F32)] * 3
        table += [shape((lines, extent), I32)] + [shape((lines, extent), F32)] * 2
        n = len(wanted)
        out = [pltpu.SMEM((8, lanes), I32)] * n + [shape((span * ray_tiles, extent), F32)] + table
        waits = [] if after is None else [after]
        found = call(
            functools.partial(setup_kernel, len(payloads), members,
                              payloads[0].shape[0] * len(payloads) // members, span, sizes,
                              voxel_tiles, wanted),
            "setup", 24, [VMEM] * len(payloads) + [ANY] * len(waits), out, *payloads, *waits,
            scratch=[pltpu.VMEM((8, lanes), I32)] * n + [pltpu.SemaphoreType.DMA((n,))])
        return found[:n], found[n], found[n + 1:n + 5], found[n + 5:]

    def forward(slots, values, members, table, n_out, start=None, start_row=None, sums=()):
        operands = [pltpu.with_memory_space_constraint(slots, pltpu.SMEM), *values, *table] + ([] if start is None else [start]) + list(sums)
        extra = ray_tiles if sums else 0
        return call(
            functools.partial(forward_kernel, sizes, len(values), members, start_row, len(sums)),
            "forward", 16 if paired else 32, [SMEM] + [VMEM] * (len(operands) - 1),
            shape((n_out + extra, extent), F32), *operands,
            scratch=[pltpu.VMEM((members * rows, extent), F32), pltpu.VMEM((n_out, extent), F32)])

    def residual_of(projection, row_sums, *sibling):
        operands = [projection, sino, *row_sums, *sibling]
        return call(
            functools.partial(residual_kernel, frames, len(row_sums)), "residual", 16,
            [VMEM] * len(operands), shape((n_rays, extent), BF16), *operands)

    def backward(slots, parts, members, table, kind, start=None, split=()):
        operands = [pltpu.with_memory_space_constraint(slots, pltpu.SMEM), *parts, *table] + ([] if start is None else [start])
        return call(
            functools.partial(backward_kernel, sizes, len(parts), start is not None, split),
            "backward", 16 if paired else 32, [SMEM] + [VMEM] * (len(operands) - 1),
            [shape((len(some) * rows, extent), kind) for some in split]
            if split else shape((members * rows, extent), kind), *operands,
            scratch=[pltpu.VMEM((len(parts) * n_rays, extent), F32)]
            + [pltpu.VMEM((members * rows, extent), F32)] * n_bank)

    def join(*parts):
        total = sum(part.shape[0] for part in parts)
        return call(join_kernel, "join", 16, [VMEM] * len(parts), shape((total, extent), BF16), *parts)

    def update(volume, pieces, last):
        out = [shape((rows, extent), F32)] + ([] if last else [shape((rows, extent), BF16)])
        return call(
            functools.partial(update_kernel, len(pieces)), "update", 16,
            [VMEM] * (2 + len(pieces)), out, volume, column_weight, *pieces)

    column_weight = call(
        functools.partial(column_kernel, sizes), "column_weight", 16, [VMEM] * 4,
        shape((rows, extent), F32), *slots_by_depth, live)

    for sweep in range(ITERS):
        last = sweep + 1 == ITERS
        if paired:
            place_1, place_2, place_3 = [
                exchange(payload, n_slab, *pair) for pair in ((8, 12), (12, 4), (4, 8))]
            z_half = join(payload, place_1)
            y_half = exchange(z_half, n_slab, 2)
            z_rest = join(place_2, place_3)
            y_rest = exchange(z_rest, n_slab, 2)
            along_z = (z_half, z_rest)
            along_y = (call(widen_kernel, "widen", 16, [VMEM], shape(y_half.shape, F32), y_half), y_rest)
            if sweep == 0:
                (z_list,), z_rows, z_forward, z_backward = setup(along_z, 4, (None,))
            both = forward(z_list, along_z, 4, z_forward, 2 * n_rays)
            if sweep == 0:
                (own_list, other_list), y_rows, y_forward, y_backward = setup(
                    (y_half, y_rest), 4, (0, 1), after=both)
            other = exchange(
                forward(other_list, along_y, 4, y_forward, n_rays, both, n_rays,
                        (z_rows, y_rows) if sweep == 0 else ()), n_slab, 1)
            if sweep == 0:
                first_other = other
            own = forward(own_list, along_y, 4, y_forward, n_rays, both, 0)
            residual = residual_of(own, (z_rows, y_rows), other, first_other)
            other_residual = exchange(residual, n_slab, 1)
            y_sum = backward(own_list, [residual], 4, y_backward, F32)
            far_sum, near_sum = backward(
                other_list, [other_residual], 4, y_backward, BF16, y_sum, ((1, 2), (0, 3)))
            far_part, near_part = exchange(far_sum, n_slab, 2), exchange(near_sum, n_slab, 2)
            z_sum = backward(z_list, [residual, other_residual], 4, z_backward, F32)
            piece = shape((rows, extent), BF16)
            piece_1, piece_2 = call(
                functools.partial(combine_kernel, (1, 2)), "combine", 16, [VMEM] * 2,
                [piece, piece], z_sum, far_part)
            got = [exchange(piece_1, n_slab, 8, 12), exchange(piece_2, n_slab, 12, 4)]
            own_piece, piece_3 = call(
                functools.partial(combine_kernel, (0, 3)), "combine", 16, [VMEM] * 2,
                [shape((rows, extent), F32), piece], z_sum, near_part)
            pieces = [own_piece, *got, exchange(piece_3, n_slab, 4, 8)]
        else:
            everyone = lax.all_gather(payload, "slab", axis=0, tiled=True)
            if sweep == 0:
                (slots,), row_sums, to_rays, to_voxels = setup((everyone,), n_slab, (None,))
            projection = forward(slots, (everyone,), n_slab, to_rays, n_rays)
            residual = residual_of(projection, (row_sums,))
            sums = backward(slots, [residual], n_slab, to_voxels, BF16)
            parts = lax.all_to_all(
                sums.reshape(n_slab, rows, extent), "slab", split_axis=0, concat_axis=0, tiled=True)
            pieces = [jnp.sum(parts.astype(F32), axis=0)]
        volume, *rounded = update(volume, pieces, last)
        if not last:
            payload = rounded[0]
    return volume.reshape(start_volume.shape)


def solution(mesh):
    in_specs = (
        P(("scan", "slab"), None, None),
        P(("scan", "slab"), None, None),
        P(("scan", "slab"), None),
        P(("scan", "slab")),
        P(("scan", "slab")),
        P(("scan", "slab"), None),
        P(("scan", "slab"), None),
    )
    out_specs = P(("scan", "slab"), None, None)
    return jax.shard_map(shards, mesh=mesh, in_specs=in_specs, out_specs=out_specs, check_vma=False)
```

```python
import functools

import jax
import jax.numpy as jnp
from jax import lax
from jax.experimental import pallas as pl
from jax.experimental.pallas import tpu as pltpu
from jax.sharding import PartitionSpec as P

ITERS = 2
CHUNK = 16
F32 = jnp.float32
BF16 = jnp.bfloat16
I32 = jnp.int32
HIGHEST = lax.Precision.HIGHEST
VMEM = pl.BlockSpec(memory_space=pltpu.VMEM)
ANY = pl.BlockSpec(memory_space=pl.ANY)
SMEM = pl.BlockSpec(memory_space=pltpu.SMEM)
HBM = pl.BlockSpec(memory_space=pltpu.HBM)


def hat(ray, centre):
    return jnp.maximum(0.0, 1.0 - jnp.abs(ray - centre)).astype(BF16)


def row_taps(offset, slope, extent):
    shape = (offset.shape[0], extent)
    ray = lax.broadcasted_iota(I32, shape, 1).astype(F32)
    offset = jnp.broadcast_to(offset, shape)
    slope = jnp.broadcast_to(slope, shape)
    middle = jnp.floor((ray - offset) / slope + 0.5)
    middle = jnp.minimum(jnp.maximum(middle, 1.0), extent - 2.0)
    weights = [hat(ray, offset + slope * (middle + step)) for step in (-1.0, 0.0, 1.0)]
    return middle.astype(I32), weights


def column_taps(offset, slope, extent):
    shape = (offset.shape[0], extent)
    voxel = lax.broadcasted_iota(I32, shape, 1).astype(F32)
    centre = jnp.broadcast_to(offset, shape) + jnp.broadcast_to(slope, shape) * voxel
    first = jnp.minimum(jnp.maximum(jnp.floor(centre), 0.0), extent - 2.0)
    weights = [hat(first + step, centre) for step in (0.0, 1.0)]
    return first.astype(I32), weights


def repeat_rows(values, times):
    return jnp.concatenate(
        [jnp.broadcast_to(values[row:row + 1, :], (times, values.shape[1]))
         for row in range(values.shape[0])], axis=0)


def contract_lanes(left, right):
    return lax.dot_general(
        left.astype(BF16), right.astype(BF16), (((1,), (1,)), ((), ())), preferred_element_type=F32)


def per_slot(live_ref, slots, capacity):
    targets = live_ref.shape[1]
    slot = lax.broadcasted_iota(I32, (targets, slots), 1)
    owner = lax.broadcasted_iota(I32, (targets, slots), 0)
    expand = (lax.div(slot, capacity) == owner).astype(F32)
    return jnp.dot(live_ref[...].astype(F32), expand, precision=HIGHEST, preferred_element_type=F32)


def pack_kernel(capacity, *refs):
    sources, out_ref, loaded, arrived = refs[:6], refs[6], refs[7:13], refs[13]
    copies = [
        pltpu.make_async_copy(source, ref, arrived.at[place])
        for place, (source, ref) in enumerate(zip(sources, loaded))]
    for copy in copies:
        copy.start()
    for copy in copies:
        copy.wait()
    volume_ref, offset_ref, slope_ref, voxel_ref, ray_ref, live_ref = loaded
    rows, extent = volume_ref.shape
    out_ref[0:rows, :] = volume_ref[...].astype(BF16)
    slots = ray_ref.shape[1]
    fields = []
    for ref in (offset_ref, slope_ref):
        left = ref[...]
        for addend in range(3):
            part = left.astype(BF16).astype(F32)
            fields.append(part)
            left = left - part
    fields.append(voxel_ref[...].astype(F32))
    fields.append(ray_ref[...].astype(F32))
    fields.append(per_slot(live_ref, slots, capacity))
    used = sum(field.shape[0] for field in fields)
    fields.append(jnp.zeros((-used % 16, slots), F32))
    fields = jnp.concatenate(fields, axis=0)
    height = fields.shape[0]
    for part in range(slots // extent):
        at = pl.ds(rows + part * height, height)
        out_ref[at, :] = fields[:, part * extent:(part + 1) * extent].astype(BF16)


def setup_kernel(n_payloads, members, stride, span, sizes, tiles, wanted, *refs):
    payload_refs, refs = refs[:n_payloads], refs[-(2 * len(wanted) + 9):]
    where = [(ref, index) for ref in payload_refs for index in range(ref.shape[0] // stride)]
    list_refs, row_ref, tables = refs[:len(wanted)], refs[len(wanted)], refs[len(wanted) + 1:-len(wanted) - 1]
    drafts, arrived = refs[-len(wanted) - 1:-1], refs[-1]
    copies = [
        pltpu.make_async_copy(draft, ref, arrived.at[place])
        for place, (draft, ref) in enumerate(zip(drafts, list_refs))]
    capacity, depth, frames = sizes
    width = span * capacity
    extent = row_ref.shape[1]
    ray_tiles = row_ref.shape[0] // span
    height = -(-(7 * depth + 2) // 16) * 16
    lanes = drafts[0].shape[1]
    me = lax.axis_index("slab").astype(I32)
    parity = lax.rem(me, span)
    first_slot = (me - parity) * capacity
    part = lax.div(first_slot, extent)
    shift = lax.rem(extent - lax.rem(first_slot, extent), extent)

    def collect(member, lined, payload_ref, within):
        at = within * stride + tiles * frames + part * height
        raw = payload_ref[pl.ds(pl.multiple_of(at, 16), height), :].astype(F32)
        offset = (raw[0:depth] + raw[depth:2 * depth]) + raw[2 * depth:3 * depth]
        slope = (raw[3 * depth:4 * depth] + raw[4 * depth:5 * depth]) + raw[5 * depth:6 * depth]
        fields = jnp.concatenate(
            [offset, slope, raw[6 * depth:7 * depth + 2],
             jnp.zeros((16 - 3 * depth - 2, extent), F32)], axis=0)
        fields = pltpu.roll(fields, shift, axis=1)
        lane = lax.broadcasted_iota(I32, fields.shape, 1)
        fields = jnp.where(lane < width, fields, 0.0)
        if lanes > extent:
            fields = jnp.concatenate(
                [fields, jnp.zeros((fields.shape[0], lanes - extent), F32)], axis=1)
        return lined + pltpu.roll(fields, member * width, axis=1)

    lined = jnp.zeros((16, lanes), F32)
    if members <= 16:
        for member in range(members):
            lined = collect(member, lined, *where[member])
    else:
        lined = lax.fori_loop(
            0, members, lambda member, lined: collect(member, lined, payload_refs[0], member), lined)

    slot = lax.broadcasted_iota(I32, (1, lanes), 1)
    within = lax.rem(slot, width)
    target = lax.bitwise_xor(lax.div(within, capacity), parity)
    ray = lined[3 * depth:3 * depth + 1]
    count = lined[3 * depth + 1:3 * depth + 2]
    alive = jnp.logical_and(lax.rem(within, capacity).astype(F32) < count, slot < members * width)

    table = jnp.concatenate(
        [slot.astype(F32), ray, target.astype(F32), lined[2 * depth:3 * depth],
         jnp.zeros((5 - depth, lanes), F32)], axis=0)
    order = lax.broadcasted_iota(I32, (lanes, lanes), 0)
    earlier = (lax.broadcasted_iota(I32, (lanes, lanes), 1) < order).astype(F32)
    for ref, kind, copy in zip(drafts, wanted, copies):
        taken = alive if kind is None else jnp.logical_and(alive, target == kind)
        taken = taken.astype(F32)
        position = contract_lanes(jnp.broadcast_to(taken, (8, lanes)), earlier)[0:1]
        position = jnp.where(taken > 0.0, position, -1.0).astype(I32)
        choose = jnp.broadcast_to(position, (lanes, lanes)) == order
        packed = (contract_lanes(table, choose.astype(F32)) + 0.5).astype(I32)
        total = jnp.sum(taken, axis=1, keepdims=True).astype(I32)
        line = jnp.where(slot < total, packed[0:1], lanes)
        base = packed[1:2] if kind is not None else packed[1:2] + packed[2:3] * ray_tiles
        member = lax.div(packed[0:1], width) * tiles
        rows = [line, base * frames]
        rows += [(packed[3 + level:4 + level] + member) * frames for level in range(depth)]
        rows += [jnp.zeros((5 - depth, lanes), I32), jnp.broadcast_to(total, (1, lanes))]
        ref[...] = jnp.concatenate(rows, axis=0)
        copy.start()

    columns = lined.T
    summed = None
    for level in range(depth):
        offset = columns[:, level:level + 1]
        slope = columns[:, depth + level:depth + level + 1]
        middle, weights = row_taps(offset, slope, extent)
        first, pair = column_taps(offset, slope, extent)
        wide = [weight.astype(F32) for weight in weights]
        values = [middle] + wide + [first] + [weight.astype(F32) for weight in pair]
        at = level * (lanes + 8)
        for ref, value in zip(tables, values):
            ref[at:at + lanes, :] = value
            blank = jnp.ones if ref.dtype == I32 else jnp.zeros
            ref[at + lanes:at + lanes + 8, :] = blank((8, extent), ref.dtype)
        parts = (wide[0] + wide[1]) + wide[2]
        summed = parts if summed is None else summed + parts

    tile = lax.broadcasted_iota(I32, (span * ray_tiles, lanes), 0).astype(F32)
    place = ray + (target * ray_tiles).astype(F32)
    place = jnp.where(alive, place, -1.0)
    hot = (jnp.broadcast_to(place, tile.shape) == tile).astype(F32)
    row_ref[...] = jnp.dot(hot, summed, precision=HIGHEST, preferred_element_type=F32)
    for copy in copies:
        copy.wait()


def column_kernel(sizes, offset_ref, slope_ref, voxel_ref, live_ref, out_ref):
    capacity, depth, frames = sizes
    tiles = out_ref.shape[0] // frames
    slots = offset_ref.shape[1]
    extent = out_ref.shape[1]
    offsets = offset_ref[...].T
    slopes = slope_ref[...].T
    within = lax.rem(lax.broadcasted_iota(I32, (1, slots), 1), capacity).astype(F32)
    alive = jnp.broadcast_to(within, (tiles, slots)) < per_slot(live_ref, slots, capacity)
    total = jnp.zeros((tiles, extent), F32)
    for level in range(depth):
        unused, pair = column_taps(
            offsets[:, level:level + 1], slopes[:, level:level + 1], extent)
        tile_of = jnp.broadcast_to(voxel_ref[level:level + 1, :], (tiles, slots))
        match = tile_of == lax.broadcasted_iota(I32, (tiles, slots), 0)
        hot = jnp.logical_and(match, alive).astype(F32).astype(BF16)
        for weight in pair:
            total += jnp.dot(hot, weight, preferred_element_type=F32)
    out_ref[...] = repeat_rows(1.0 / jnp.maximum(total, 1.0), frames)


def pick(values, index):
    numbers = lax.GatherDimensionNumbers(
        offset_dims=(), collapsed_slice_dims=(1,), start_index_map=(1,),
        operand_batching_dims=(0,), start_indices_batching_dims=(0,))
    return lax.gather(
        values, index[:, :, None], numbers, slice_sizes=(1, 1),
        mode=lax.GatherScatterMode.PROMISE_IN_BOUNDS)


def pack_pair(first, second):
    kind = jnp.int16 if first.dtype == I32 else BF16
    return jnp.concatenate([first, second], axis=0).astype(kind)


def spread(ref, row, frames):
    return jnp.broadcast_to(ref[pl.ds(row, 1), :], (frames, ref.shape[1]))


def tile_at(start, frames):
    return pl.ds(pl.multiple_of(start, frames), frames)


def for_slots(slots, body):
    def some(step, carry):
        for place in range(CHUNK):
            body(step * CHUNK + place, place)
        return carry

    lax.fori_loop(0, lax.div(slots[7, 0] + (CHUNK - 1), CHUNK), some, 0)


def for_rows(rows, body):
    step = 128

    def some(number, carry):
        body(pl.ds(pl.multiple_of(number * step, step), step))
        return carry

    lax.fori_loop(0, rows // step, some, 0)


def forward_kernel(sizes, n_values, members, start_row, n_sums, slots, *refs):
    capacity, depth, frames = sizes
    value_refs, tables, refs = refs[:n_values], refs[n_values:n_values + 4], refs[n_values + 4:]
    start_ref = None
    if start_row is not None:
        start_ref, refs = refs[0], refs[1:]
    sum_refs, (out_ref, wide, second) = refs[:n_sums], refs[n_sums:]
    rows = wide.shape[0] // members
    stride = sum(ref.shape[0] for ref in value_refs) // members
    rays = second.shape[0]
    line_step = tables[0].shape[0] // depth

    base = 0
    for ref in value_refs:
        def widen(member, carry, ref=ref, base=base):
            at = pl.ds(pl.multiple_of((base + member) * rows, rows), rows)
            wide[at, :] = ref[pl.ds(pl.multiple_of(member * stride, 16), rows), :].astype(F32)
            return carry

        lax.fori_loop(0, ref.shape[0] // stride, widen, 0)
        base += ref.shape[0] // stride
    second[...] = jnp.zeros_like(second)
    if start_ref is None:
        out_ref[...] = jnp.zeros_like(out_ref)
    else:
        out_ref[0:rays, :] = start_ref[start_row:start_row + rays, :]
    if n_sums:
        half = sum_refs[0].shape[0] // 2
        out_ref[rays:, :] = sum([ref[half:, :] for ref in sum_refs[1:]], sum_refs[0][half:, :])

    def one(slot, place):
        line = slots[0, slot]
        taps = []
        for start in range(0, depth, 2):
            levels = range(start, start + 2)
            values = [wide[tile_at(slots[2 + level, slot], frames), :] for level in levels]
            middles = [spread(tables[0], line + level * line_step, frames) for level in levels]
            lower = [
                pick(pack_pair(value, value), pack_pair(middle - 1, middle)).astype(F32)
                for value, middle in zip(values, middles)]
            upper = pick(
                pack_pair(*values), pack_pair(*[middle + 1 for middle in middles])).astype(F32)
            for which, pair in enumerate(lower):
                taps.append((pair[0:frames], pair[frames:2 * frames],
                             upper[which * frames:(which + 1) * frames]))
        total = None
        for level, three in enumerate(taps):
            for ref, tap in zip(tables[1:], three):
                term = spread(ref, line + level * line_step, frames) * tap
                total = term if total is None else total + term
        projection = (out_ref, second)[place % 2]
        projection[tile_at(slots[1, slot], frames), :] += total.astype(BF16).astype(F32)

    for_slots(slots, one)
    out_ref[0:rays, :] += second[...]


def residual_kernel(frames, n_own, projection_ref, sinogram_ref, *refs):
    own, refs, out_ref = refs[:n_own], refs[n_own:-1], refs[-1]
    rays = out_ref.shape[0]
    ray_tiles = rays // frames
    total = sum([ref[0:ray_tiles, :] for ref in own[1:]], own[0][0:ray_tiles, :])
    projection = projection_ref[...]
    if refs:
        projection = projection + refs[0][0:rays, :]
        total = total + refs[-1][rays:, :]
    weight = repeat_rows(1.0 / jnp.maximum(total, 1.0), frames)
    out_ref[...] = ((sinogram_ref[...].astype(F32) - projection) * weight).astype(BF16)


def backward_kernel(sizes, n_parts, has_start, split, slots, *refs):
    capacity, depth, frames = sizes
    part_refs, tables, refs = refs[:n_parts], refs[n_parts:n_parts + 3], refs[n_parts + 3:]
    start_ref = None
    if has_start:
        start_ref, refs = refs[0], refs[1:]
    outs = refs[:len(split)] if split else refs[:1]
    residual, banks = refs[len(outs)], refs[len(outs) + 1:]
    rays = part_refs[0].shape[0]
    line_step = tables[0].shape[0] // depth
    for place, ref in enumerate(part_refs):
        residual[place * rays:(place + 1) * rays, :] = ref[...].astype(F32)

    def clear(at):
        for place, bank in enumerate(banks):
            if place == 0 and has_start:
                bank[at, :] = start_ref[at, :]
            else:
                bank[at, :] = jnp.zeros((at.size, bank.shape[1]), F32)

    for_rows(banks[0].shape[0], clear)

    def one(slot, place):
        line = slots[0, slot]
        values = residual[tile_at(slots[1, slot], frames), :]
        twice = pack_pair(values, values)
        for level in range(depth):
            row = line + level * line_step
            first = spread(tables[0], row, frames)
            taps = pick(twice, pack_pair(first, first + 1)).astype(F32)
            term = (spread(tables[1], row, frames) * taps[0:frames]
                    + spread(tables[2], row, frames) * taps[frames:2 * frames])
            banks[level % len(banks)][tile_at(slots[2 + level, slot], frames), :] += term

    for_slots(slots, one)

    def total(at):
        return sum([bank[at, :] for bank in banks[1:]], banks[0][at, :])

    if split:
        for ref, members in zip(outs, split):
            rows = ref.shape[0] // len(members)
            for place, member in enumerate(members):
                ref[place * rows:(place + 1) * rows, :] = total(pl.ds(member * rows, rows)).astype(ref.dtype)
    else:
        def finish(at):
            outs[0][at, :] = total(at).astype(outs[0].dtype)

        for_rows(outs[0].shape[0], finish)


def join_kernel(*refs):
    out_ref, at = refs[-1], 0
    for ref in refs[:-1]:
        out_ref[at:at + ref.shape[0], :] = ref[...]
        at += ref.shape[0]


def combine_kernel(members, sum_ref, y_ref, *piece_refs):
    rows = piece_refs[0].shape[0]
    for place, (member, ref) in enumerate(zip(members, piece_refs)):
        mine = sum_ref[member * rows:(member + 1) * rows, :]
        ref[...] = (mine + y_ref[place * rows:(place + 1) * rows, :].astype(F32)).astype(ref.dtype)


def update_kernel(n_pieces, volume_ref, column_ref, *refs):
    back = refs[0][...]
    for ref in refs[1:n_pieces]:
        back = back + ref[...].astype(F32)
    volume = volume_ref[...] + column_ref[...] * back
    for ref in refs[n_pieces:]:
        ref[...] = volume.astype(ref.dtype)


def call(kernel, name, mib, in_specs, out_shape, *operands, scratch=()):
    one = not isinstance(out_shape, list)
    return pl.pallas_call(
        kernel,
        out_shape=out_shape,
        in_specs=in_specs,
        out_specs=VMEM if one else [
            SMEM if getattr(out, "memory_space", None) == pltpu.SMEM else VMEM for out in out_shape],
        scratch_shapes=list(scratch),
        compiler_params=pltpu.CompilerParams(vmem_limit_bytes=mib * 1024 * 1024),
        name=name,
        cost_estimate=pl.CostEstimate(flops=4 * 10**9, bytes_accessed=8 * 10**6, transcendentals=0),
    )(*operands)


def exchange(values, n_slab, distance):
    return lax.ppermute(
        values, "slab", [(device, device ^ distance) for device in range(n_slab)])


def shards(sinogram, start_volume, slot_voxel, slot_ray, live_count, block_slope, block_offset):
    n_slab = lax.axis_size("slab")
    n_slots, depth = slot_voxel.shape
    capacity = n_slots // n_slab
    ray_tiles, frames, extent = sinogram.shape
    voxel_tiles = start_volume.shape[0]
    rows = voxel_tiles * frames
    sizes = (capacity, depth, frames)
    paired = n_slab == 16
    span = 2 if paired else 1
    n_bank = 2 if paired else 1
    shape = jax.ShapeDtypeStruct
    n_rays = ray_tiles * frames
    volume = start_volume.reshape(rows, extent)
    sino = sinogram.reshape(n_rays, extent)
    slots_by_depth = (block_offset.T, block_slope.T, slot_voxel.T)
    live = live_count.reshape(1, n_slab)
    height = -(-(7 * depth + 2) // 16) * 16 * (n_slots // extent)
    operands = (volume, *slots_by_depth, slot_ray.reshape(1, n_slots), live)
    payload = call(
        functools.partial(pack_kernel, capacity), "pack", 16, [HBM] * 6,
        shape((rows + height, extent), BF16),
        *[pltpu.with_memory_space_constraint(operand, pltpu.HBM) for operand in operands],
        scratch=[pltpu.VMEM(operand.shape, operand.dtype) for operand in operands]
        + [pltpu.SemaphoreType.DMA((6,))])

    def setup(payloads, members, wanted, after=None):
        lanes = -(-members * span * capacity // 128) * 128
        lines = depth * (lanes + 8)
        table = [shape((lines, extent), I32)] + [shape((lines, extent), F32)] * 3
        table += [shape((lines, extent), I32)] + [shape((lines, extent), F32)] * 2
        n = len(wanted)
        out = [pltpu.SMEM((8, lanes), I32)] * n + [shape((span * ray_tiles, extent), F32)] + table
        waits = [] if after is None else [after]
        found = call(
            functools.partial(setup_kernel, len(payloads), members,
                              sum(one.shape[0] for one in payloads) // members, span, sizes,
                              voxel_tiles, wanted),
            "setup", 24, [VMEM] * len(payloads) + [ANY] * len(waits), out, *payloads, *waits,
            scratch=[pltpu.VMEM((8, lanes), I32)] * n + [pltpu.SemaphoreType.DMA((n,))])
        return found[:n], found[n], found[n + 1:n + 5], found[n + 5:]

    def forward(slots, values, members, table, n_out, start=None, start_row=None, sums=()):
        operands = [pltpu.with_memory_space_constraint(slots, pltpu.SMEM), *values, *table] + ([] if start is None else [start]) + list(sums)
        extra = ray_tiles if sums else 0
        return call(
            functools.partial(forward_kernel, sizes, len(values), members, start_row, len(sums)),
            "forward", 16 if paired else 32, [SMEM] + [VMEM] * (len(operands) - 1),
            shape((n_out + extra, extent), F32), *operands,
            scratch=[pltpu.VMEM((members * rows, extent), F32), pltpu.VMEM((n_out, extent), F32)])

    def residual_of(projection, row_sums, *sibling):
        operands = [projection, sino, *row_sums, *sibling]
        return call(
            functools.partial(residual_kernel, frames, len(row_sums)), "residual", 16,
            [VMEM] * len(operands), shape((n_rays, extent), BF16), *operands)

    def backward(slots, parts, members, table, kind, start=None, split=()):
        operands = [pltpu.with_memory_space_constraint(slots, pltpu.SMEM), *parts, *table] + ([] if start is None else [start])
        return call(
            functools.partial(backward_kernel, sizes, len(parts), start is not None, split),
            "backward", 16 if paired else 32, [SMEM] + [VMEM] * (len(operands) - 1),
            [shape((len(some) * rows, extent), each) for some, each in zip(split, kind)]
            if split else shape((members * rows, extent), kind), *operands,
            scratch=[pltpu.VMEM((len(parts) * n_rays, extent), F32)]
            + [pltpu.VMEM((members * rows, extent), F32)] * n_bank)

    def join(*parts):
        total = sum(part.shape[0] for part in parts)
        return call(join_kernel, "join", 16, [VMEM] * len(parts), shape((total, extent), BF16), *parts)

    def update(volume, pieces, last):
        out = [shape((rows, extent), F32)] + ([] if last else [shape((rows, extent), BF16)])
        return call(
            functools.partial(update_kernel, len(pieces)), "update", 16,
            [VMEM] * (2 + len(pieces)), out, volume, column_weight, *pieces)

    column_weight = call(
        functools.partial(column_kernel, sizes), "column_weight", 16, [VMEM] * 4,
        shape((rows, extent), F32), *slots_by_depth, live)

    for sweep in range(ITERS):
        last = sweep + 1 == ITERS
        if paired:
            over_2, over_1, over_3, across = [
                exchange(payload, n_slab, distance) for distance in (8, 4, 12, 14)]
            z_part = join(payload, over_2, over_1)
            y_part = exchange(z_part, n_slab, 2)
            along_z, along_y = (z_part, over_3), (y_part, across)
            if sweep == 0:
                (z_list,), z_rows, z_forward, z_backward = setup(along_z, 4, (None,))
            both = forward(z_list, along_z, 4, z_forward, 2 * n_rays)
            if sweep == 0:
                (own_list, other_list), y_rows, y_forward, y_backward = setup(
                    along_y, 4, (0, 1), after=both)
            other = exchange(
                forward(other_list, along_y, 4, y_forward, n_rays, both, n_rays,
                        (z_rows, y_rows) if sweep == 0 else ()), n_slab, 1)
            if sweep == 0:
                first_other = other
            own = forward(own_list, along_y, 4, y_forward, n_rays, both, 0)
            residual = residual_of(own, (z_rows, y_rows), other, first_other)
            other_residual = exchange(residual, n_slab, 1)
            y_sum = backward(own_list, [residual], 4, y_backward, F32)
            y_sum, across_sum = backward(
                other_list, [other_residual], 4, y_backward, (BF16, BF16), y_sum, ((0, 1, 2), (3,)))
            y_got, across_got = exchange(y_sum, n_slab, 2), exchange(across_sum, n_slab, 14)
            z_sum, sum_3 = backward(
                z_list, [residual, other_residual], 4, z_backward, (F32, BF16), None, ((0, 1, 2), (3,)))
            got_3 = exchange(sum_3, n_slab, 12)
            piece = shape((rows, extent), BF16)
            own_piece, piece_2, piece_1 = call(
                functools.partial(combine_kernel, (0, 1, 2)), "combine", 16, [VMEM] * 2,
                [shape((rows, extent), F32), piece, piece], z_sum, y_got)
            pieces = [own_piece, exchange(piece_2, n_slab, 8), exchange(piece_1, n_slab, 4),
                      got_3, across_got]
        else:
            everyone = lax.all_gather(payload, "slab", axis=0, tiled=True)
            if sweep == 0:
                (slots,), row_sums, to_rays, to_voxels = setup((everyone,), n_slab, (None,))
            projection = forward(slots, (everyone,), n_slab, to_rays, n_rays)
            residual = residual_of(projection, (row_sums,))
            sums = backward(slots, [residual], n_slab, to_voxels, BF16)
            parts = lax.all_to_all(
                sums.reshape(n_slab, rows, extent), "slab", split_axis=0, concat_axis=0, tiled=True)
            pieces = [jnp.sum(parts.astype(F32), axis=0)]
        volume, *rounded = update(volume, pieces, last)
        if not last:
            payload = rounded[0]
    return volume.reshape(start_volume.shape)


def solution(mesh):
    in_specs = (
        P(("scan", "slab"), None, None),
        P(("scan", "slab"), None, None),
        P(("scan", "slab"), None),
        P(("scan", "slab")),
        P(("scan", "slab")),
        P(("scan", "slab"), None),
        P(("scan", "slab"), None),
    )
    out_specs = P(("scan", "slab"), None, None)
    return jax.shard_map(shards, mesh=mesh, in_specs=in_specs, out_specs=out_specs, check_vma=False)
```

```python
import functools

import jax
import jax.numpy as jnp
from jax import lax
from jax.experimental import pallas as pl
from jax.experimental.pallas import tpu as pltpu
from jax.sharding import PartitionSpec as P

ITERS = 2
CHUNK = 16
F32 = jnp.float32
BF16 = jnp.bfloat16
I32 = jnp.int32
HIGHEST = lax.Precision.HIGHEST
VMEM = pl.BlockSpec(memory_space=pltpu.VMEM)
ANY = pl.BlockSpec(memory_space=pl.ANY)
SMEM = pl.BlockSpec(memory_space=pltpu.SMEM)
HBM = pl.BlockSpec(memory_space=pltpu.HBM)


def hat(ray, centre):
    return jnp.maximum(0.0, 1.0 - jnp.abs(ray - centre)).astype(BF16)


def row_taps(offset, slope, extent):
    shape = (offset.shape[0], extent)
    ray = lax.broadcasted_iota(I32, shape, 1).astype(F32)
    offset = jnp.broadcast_to(offset, shape)
    slope = jnp.broadcast_to(slope, shape)
    middle = jnp.floor((ray - offset) / slope + 0.5)
    middle = jnp.minimum(jnp.maximum(middle, 1.0), extent - 2.0)
    weights = [hat(ray, offset + slope * (middle + step)) for step in (-1.0, 0.0, 1.0)]
    return middle.astype(I32), weights


def column_taps(offset, slope, extent):
    shape = (offset.shape[0], extent)
    voxel = lax.broadcasted_iota(I32, shape, 1).astype(F32)
    centre = jnp.broadcast_to(offset, shape) + jnp.broadcast_to(slope, shape) * voxel
    first = jnp.minimum(jnp.maximum(jnp.floor(centre), 0.0), extent - 2.0)
    weights = [hat(first + step, centre) for step in (0.0, 1.0)]
    return first.astype(I32), weights


def repeat_rows(values, times):
    return jnp.concatenate(
        [jnp.broadcast_to(values[row:row + 1, :], (times, values.shape[1]))
         for row in range(values.shape[0])], axis=0)


def contract_lanes(left, right):
    return lax.dot_general(
        left.astype(BF16), right.astype(BF16), (((1,), (1,)), ((), ())), preferred_element_type=F32)


def per_slot(live_ref, slots, capacity):
    targets = live_ref.shape[1]
    slot = lax.broadcasted_iota(I32, (targets, slots), 1)
    owner = lax.broadcasted_iota(I32, (targets, slots), 0)
    expand = (lax.div(slot, capacity) == owner).astype(F32)
    return jnp.dot(live_ref[...].astype(F32), expand, precision=HIGHEST, preferred_element_type=F32)


def pack_kernel(capacity, *refs):
    sources, out_ref, loaded, arrived = refs[:6], refs[6], refs[7:13], refs[13]
    copies = [
        pltpu.make_async_copy(source, ref, arrived.at[place])
        for place, (source, ref) in enumerate(zip(sources, loaded))]
    for copy in copies:
        copy.start()
    for copy in copies:
        copy.wait()
    volume_ref, offset_ref, slope_ref, voxel_ref, ray_ref, live_ref = loaded
    rows, extent = volume_ref.shape
    out_ref[0:rows, :] = volume_ref[...].astype(BF16)
    slots = ray_ref.shape[1]
    fields = []
    for ref in (offset_ref, slope_ref):
        left = ref[...]
        for addend in range(3):
            part = left.astype(BF16).astype(F32)
            fields.append(part)
            left = left - part
    fields.append(voxel_ref[...].astype(F32))
    fields.append(ray_ref[...].astype(F32))
    fields.append(per_slot(live_ref, slots, capacity))
    used = sum(field.shape[0] for field in fields)
    fields.append(jnp.zeros((-used % 16, slots), F32))
    fields = jnp.concatenate(fields, axis=0)
    height = fields.shape[0]
    for part in range(slots // extent):
        at = pl.ds(rows + part * height, height)
        out_ref[at, :] = fields[:, part * extent:(part + 1) * extent].astype(BF16)


def setup_kernel(n_payloads, members, stride, span, sizes, tiles, wanted, *refs):
    payload_refs, refs = refs[:n_payloads], refs[-(2 * len(wanted) + 9):]
    where = [(ref, index) for ref in payload_refs for index in range(ref.shape[0] // stride)]
    list_refs, row_ref, tables = refs[:len(wanted)], refs[len(wanted)], refs[len(wanted) + 1:-len(wanted) - 1]
    drafts, arrived = refs[-len(wanted) - 1:-1], refs[-1]
    copies = [
        pltpu.make_async_copy(draft, ref, arrived.at[place])
        for place, (draft, ref) in enumerate(zip(drafts, list_refs))]
    capacity, depth, frames = sizes
    width = span * capacity
    extent = row_ref.shape[1]
    ray_tiles = row_ref.shape[0] // span
    height = -(-(7 * depth + 2) // 16) * 16
    lanes = drafts[0].shape[1]
    me = lax.axis_index("slab").astype(I32)
    parity = lax.rem(me, span)
    first_slot = (me - parity) * capacity
    part = lax.div(first_slot, extent)
    shift = lax.rem(extent - lax.rem(first_slot, extent), extent)

    def collect(member, lined, payload_ref, within):
        at = within * stride + tiles * frames + part * height
        raw = payload_ref[pl.ds(pl.multiple_of(at, 16), height), :].astype(F32)
        offset = (raw[0:depth] + raw[depth:2 * depth]) + raw[2 * depth:3 * depth]
        slope = (raw[3 * depth:4 * depth] + raw[4 * depth:5 * depth]) + raw[5 * depth:6 * depth]
        fields = jnp.concatenate(
            [offset, slope, raw[6 * depth:7 * depth + 2],
             jnp.zeros((16 - 3 * depth - 2, extent), F32)], axis=0)
        fields = pltpu.roll(fields, shift, axis=1)
        lane = lax.broadcasted_iota(I32, fields.shape, 1)
        fields = jnp.where(lane < width, fields, 0.0)
        if lanes > extent:
            fields = jnp.concatenate(
                [fields, jnp.zeros((fields.shape[0], lanes - extent), F32)], axis=1)
        return lined + pltpu.roll(fields, member * width, axis=1)

    lined = jnp.zeros((16, lanes), F32)
    if members <= 16:
        for member in range(members):
            lined = collect(member, lined, *where[member])
    else:
        lined = lax.fori_loop(
            0, members, lambda member, lined: collect(member, lined, payload_refs[0], member), lined)

    slot = lax.broadcasted_iota(I32, (1, lanes), 1)
    within = lax.rem(slot, width)
    target = lax.bitwise_xor(lax.div(within, capacity), parity)
    ray = lined[3 * depth:3 * depth + 1]
    count = lined[3 * depth + 1:3 * depth + 2]
    alive = jnp.logical_and(lax.rem(within, capacity).astype(F32) < count, slot < members * width)

    table = jnp.concatenate(
        [slot.astype(F32), ray, target.astype(F32), lined[2 * depth:3 * depth],
         jnp.zeros((5 - depth, lanes), F32)], axis=0)
    order = lax.broadcasted_iota(I32, (lanes, lanes), 0)
    earlier = (lax.broadcasted_iota(I32, (lanes, lanes), 1) < order).astype(F32)
    for ref, kind, copy in zip(drafts, wanted, copies):
        taken = alive if kind is None else jnp.logical_and(alive, target == kind)
        taken = taken.astype(F32)
        position = contract_lanes(jnp.broadcast_to(taken, (8, lanes)), earlier)[0:1]
        position = jnp.where(taken > 0.0, position, -1.0).astype(I32)
        choose = jnp.broadcast_to(position, (lanes, lanes)) == order
        packed = (contract_lanes(table, choose.astype(F32)) + 0.5).astype(I32)
        total = jnp.sum(taken, axis=1, keepdims=True).astype(I32)
        line = jnp.where(slot < total, packed[0:1], lanes)
        base = packed[1:2] if kind is not None else packed[1:2] + packed[2:3] * ray_tiles
        member = lax.div(packed[0:1], width) * tiles
        rows = [line, base * frames]
        rows += [(packed[3 + level:4 + level] + member) * frames for level in range(depth)]
        rows += [jnp.zeros((5 - depth, lanes), I32), jnp.broadcast_to(total, (1, lanes))]
        ref[...] = jnp.concatenate(rows, axis=0)
        copy.start()

    columns = lined.T
    summed = None
    for level in range(depth):
        offset = columns[:, level:level + 1]
        slope = columns[:, depth + level:depth + level + 1]
        middle, weights = row_taps(offset, slope, extent)
        first, pair = column_taps(offset, slope, extent)
        wide = [weight.astype(F32) for weight in weights]
        values = [middle] + wide + [first] + [weight.astype(F32) for weight in pair]
        at = level * (lanes + 8)
        for ref, value in zip(tables, values):
            ref[at:at + lanes, :] = value
            blank = jnp.ones if ref.dtype == I32 else jnp.zeros
            ref[at + lanes:at + lanes + 8, :] = blank((8, extent), ref.dtype)
        parts = (wide[0] + wide[1]) + wide[2]
        summed = parts if summed is None else summed + parts

    tile = lax.broadcasted_iota(I32, (span * ray_tiles, lanes), 0).astype(F32)
    place = ray + (target * ray_tiles).astype(F32)
    place = jnp.where(alive, place, -1.0)
    hot = (jnp.broadcast_to(place, tile.shape) == tile).astype(F32)
    row_ref[...] = jnp.dot(hot, summed, precision=HIGHEST, preferred_element_type=F32)
    for copy in copies:
        copy.wait()


def column_kernel(sizes, offset_ref, slope_ref, voxel_ref, live_ref, out_ref):
    capacity, depth, frames = sizes
    tiles = out_ref.shape[0] // frames
    slots = offset_ref.shape[1]
    extent = out_ref.shape[1]
    offsets = offset_ref[...].T
    slopes = slope_ref[...].T
    within = lax.rem(lax.broadcasted_iota(I32, (1, slots), 1), capacity).astype(F32)
    alive = jnp.broadcast_to(within, (tiles, slots)) < per_slot(live_ref, slots, capacity)
    total = jnp.zeros((tiles, extent), F32)
    for level in range(depth):
        unused, pair = column_taps(
            offsets[:, level:level + 1], slopes[:, level:level + 1], extent)
        tile_of = jnp.broadcast_to(voxel_ref[level:level + 1, :], (tiles, slots))
        match = tile_of == lax.broadcasted_iota(I32, (tiles, slots), 0)
        hot = jnp.logical_and(match, alive).astype(F32).astype(BF16)
        for weight in pair:
            total += jnp.dot(hot, weight, preferred_element_type=F32)
    out_ref[...] = repeat_rows(1.0 / jnp.maximum(total, 1.0), frames)


def pick(values, index):
    numbers = lax.GatherDimensionNumbers(
        offset_dims=(), collapsed_slice_dims=(1,), start_index_map=(1,),
        operand_batching_dims=(0,), start_indices_batching_dims=(0,))
    return lax.gather(
        values, index[:, :, None], numbers, slice_sizes=(1, 1),
        mode=lax.GatherScatterMode.PROMISE_IN_BOUNDS)


def pack_pair(first, second):
    kind = jnp.int16 if first.dtype == I32 else BF16
    return jnp.concatenate([first, second], axis=0).astype(kind)


def spread(ref, row, frames):
    return ref[pl.ds(row, frames, stride=0), :]


def tile_at(start, frames):
    return pl.ds(pl.multiple_of(start, frames), frames)


def for_slots(slots, body):
    def some(step, carry):
        for place in range(CHUNK):
            body(step * CHUNK + place, place)
        return carry

    lax.fori_loop(0, lax.div(slots[7, 0] + (CHUNK - 1), CHUNK), some, 0)


def for_rows(rows, body):
    step = 128

    def some(number, carry):
        body(pl.ds(pl.multiple_of(number * step, step), step))
        return carry

    lax.fori_loop(0, rows // step, some, 0)


def forward_kernel(sizes, n_values, members, start_row, n_sums, slots, *refs):
    capacity, depth, frames = sizes
    value_refs, tables, refs = refs[:n_values], refs[n_values:n_values + 4], refs[n_values + 4:]
    start_ref = None
    if start_row is not None:
        start_ref, refs = refs[0], refs[1:]
    sum_refs, (out_ref, wide, second) = refs[:n_sums], refs[n_sums:]
    rows = wide.shape[0] // members
    stride = sum(ref.shape[0] for ref in value_refs) // members
    rays = second.shape[0]
    line_step = tables[0].shape[0] // depth

    base = 0
    for ref in value_refs:
        def widen(member, carry, ref=ref, base=base):
            at = pl.ds(pl.multiple_of((base + member) * rows, rows), rows)
            wide[at, :] = ref[pl.ds(pl.multiple_of(member * stride, 16), rows), :].astype(F32)
            return carry

        lax.fori_loop(0, ref.shape[0] // stride, widen, 0)
        base += ref.shape[0] // stride
    second[...] = jnp.zeros_like(second)
    if start_ref is None:
        out_ref[...] = jnp.zeros_like(out_ref)
    else:
        out_ref[0:rays, :] = start_ref[start_row:start_row + rays, :]
    if n_sums:
        half = sum_refs[0].shape[0] // 2
        out_ref[rays:, :] = sum([ref[half:, :] for ref in sum_refs[1:]], sum_refs[0][half:, :])

    def one(slot, place):
        line = slots[0, slot]
        taps = []
        for start in range(0, depth, 2):
            levels = range(start, start + 2)
            values = [wide[tile_at(slots[2 + level, slot], frames), :] for level in levels]
            middles = [spread(tables[0], line + level * line_step, frames) for level in levels]
            lower = [
                pick(pack_pair(value, value), pack_pair(middle - 1, middle)).astype(F32)
                for value, middle in zip(values, middles)]
            upper = pick(
                pack_pair(*values), pack_pair(*[middle + 1 for middle in middles])).astype(F32)
            for which, pair in enumerate(lower):
                taps.append((pair[0:frames], pair[frames:2 * frames],
                             upper[which * frames:(which + 1) * frames]))
        total = None
        for level, three in enumerate(taps):
            for ref, tap in zip(tables[1:], three):
                term = spread(ref, line + level * line_step, frames) * tap
                total = term if total is None else total + term
        projection = (out_ref, second)[place % 2]
        projection[tile_at(slots[1, slot], frames), :] += total.astype(BF16).astype(F32)

    for_slots(slots, one)
    out_ref[0:rays, :] += second[...]


def residual_kernel(frames, n_own, projection_ref, sinogram_ref, *refs):
    own, refs, out_ref = refs[:n_own], refs[n_own:-1], refs[-1]
    rays = out_ref.shape[0]
    ray_tiles = rays // frames
    total = sum([ref[0:ray_tiles, :] for ref in own[1:]], own[0][0:ray_tiles, :])
    projection = projection_ref[...]
    if refs:
        projection = projection + refs[0][0:rays, :]
        total = total + refs[-1][rays:, :]
    weight = repeat_rows(1.0 / jnp.maximum(total, 1.0), frames)
    out_ref[...] = ((sinogram_ref[...].astype(F32) - projection) * weight).astype(BF16)


def backward_kernel(sizes, n_parts, has_start, split, slots, *refs):
    capacity, depth, frames = sizes
    part_refs, tables, refs = refs[:n_parts], refs[n_parts:n_parts + 3], refs[n_parts + 3:]
    start_ref = None
    if has_start:
        start_ref, refs = refs[0], refs[1:]
    outs = refs[:len(split)] if split else refs[:1]
    residual, banks = refs[len(outs)], refs[len(outs) + 1:]
    rays = part_refs[0].shape[0]
    line_step = tables[0].shape[0] // depth
    for place, ref in enumerate(part_refs):
        residual[place * rays:(place + 1) * rays, :] = ref[...].astype(F32)

    def clear(at):
        for place, bank in enumerate(banks):
            if place == 0 and has_start:
                bank[at, :] = start_ref[at, :]
            else:
                bank[at, :] = jnp.zeros((at.size, bank.shape[1]), F32)

    for_rows(banks[0].shape[0], clear)

    def one(slot, place):
        line = slots[0, slot]
        values = residual[tile_at(slots[1, slot], frames), :]
        twice = pack_pair(values, values)
        for level in range(depth):
            row = line + level * line_step
            first = spread(tables[0], row, frames)
            taps = pick(twice, pack_pair(first, first + 1)).astype(F32)
            term = (spread(tables[1], row, frames) * taps[0:frames]
                    + spread(tables[2], row, frames) * taps[frames:2 * frames])
            banks[level % len(banks)][tile_at(slots[2 + level, slot], frames), :] += term

    for_slots(slots, one)

    def total(at):
        return sum([bank[at, :] for bank in banks[1:]], banks[0][at, :])

    if split:
        for ref, members in zip(outs, split):
            rows = ref.shape[0] // len(members)
            for place, member in enumerate(members):
                ref[place * rows:(place + 1) * rows, :] = total(pl.ds(member * rows, rows)).astype(ref.dtype)
    else:
        def finish(at):
            outs[0][at, :] = total(at).astype(outs[0].dtype)

        for_rows(outs[0].shape[0], finish)


def join_kernel(*refs):
    out_ref, at = refs[-1], 0
    for ref in refs[:-1]:
        out_ref[at:at + ref.shape[0], :] = ref[...]
        at += ref.shape[0]


def combine_kernel(members, sum_ref, y_ref, *piece_refs):
    rows = piece_refs[0].shape[0]
    for place, (member, ref) in enumerate(zip(members, piece_refs)):
        mine = sum_ref[member * rows:(member + 1) * rows, :]
        ref[...] = (mine + y_ref[place * rows:(place + 1) * rows, :].astype(F32)).astype(ref.dtype)


def update_kernel(n_pieces, volume_ref, column_ref, *refs):
    back = refs[0][...]
    for ref in refs[1:n_pieces]:
        back = back + ref[...].astype(F32)
    volume = volume_ref[...] + column_ref[...] * back
    for ref in refs[n_pieces:]:
        ref[...] = volume.astype(ref.dtype)


def call(kernel, name, mib, in_specs, out_shape, *operands, scratch=()):
    one = not isinstance(out_shape, list)
    return pl.pallas_call(
        kernel,
        out_shape=out_shape,
        in_specs=in_specs,
        out_specs=VMEM if one else [
            SMEM if getattr(out, "memory_space", None) == pltpu.SMEM else VMEM for out in out_shape],
        scratch_shapes=list(scratch),
        compiler_params=pltpu.CompilerParams(vmem_limit_bytes=mib * 1024 * 1024),
        name=name,
        cost_estimate=pl.CostEstimate(flops=4 * 10**9, bytes_accessed=8 * 10**6, transcendentals=0),
    )(*operands)


def exchange(values, n_slab, distance):
    return lax.ppermute(
        values, "slab", [(device, device ^ distance) for device in range(n_slab)])


def shards(sinogram, start_volume, slot_voxel, slot_ray, live_count, block_slope, block_offset):
    n_slab = lax.axis_size("slab")
    n_slots, depth = slot_voxel.shape
    capacity = n_slots // n_slab
    ray_tiles, frames, extent = sinogram.shape
    voxel_tiles = start_volume.shape[0]
    rows = voxel_tiles * frames
    sizes = (capacity, depth, frames)
    paired = n_slab == 16
    span = 2 if paired else 1
    n_bank = 2 if paired else 1
    shape = jax.ShapeDtypeStruct
    n_rays = ray_tiles * frames
    volume = start_volume.reshape(rows, extent)
    sino = sinogram.reshape(n_rays, extent)
    slots_by_depth = (block_offset.T, block_slope.T, slot_voxel.T)
    live = live_count.reshape(1, n_slab)
    height = -(-(7 * depth + 2) // 16) * 16 * (n_slots // extent)
    operands = (volume, *slots_by_depth, slot_ray.reshape(1, n_slots), live)
    payload = call(
        functools.partial(pack_kernel, capacity), "pack", 16, [HBM] * 6,
        shape((rows + height, extent), BF16),
        *[pltpu.with_memory_space_constraint(operand, pltpu.HBM) for operand in operands],
        scratch=[pltpu.VMEM(operand.shape, operand.dtype) for operand in operands]
        + [pltpu.SemaphoreType.DMA((6,))])

    def setup(payloads, members, wanted, after=None):
        lanes = -(-members * span * capacity // 128) * 128
        lines = depth * (lanes + 8)
        table = [shape((lines, extent), I32)] + [shape((lines, extent), F32)] * 3
        table += [shape((lines, extent), I32)] + [shape((lines, extent), F32)] * 2
        n = len(wanted)
        out = [pltpu.SMEM((8, lanes), I32)] * n + [shape((span * ray_tiles, extent), F32)] + table
        waits = [] if after is None else [after]
        found = call(
            functools.partial(setup_kernel, len(payloads), members,
                              sum(one.shape[0] for one in payloads) // members, span, sizes,
                              voxel_tiles, wanted),
            "setup", 24, [VMEM] * len(payloads) + [ANY] * len(waits), out, *payloads, *waits,
            scratch=[pltpu.VMEM((8, lanes), I32)] * n + [pltpu.SemaphoreType.DMA((n,))])
        return found[:n], found[n], found[n + 1:n + 5], found[n + 5:]

    def forward(slots, values, members, table, n_out, start=None, start_row=None, sums=()):
        operands = [pltpu.with_memory_space_constraint(slots, pltpu.SMEM), *values, *table] + ([] if start is None else [start]) + list(sums)
        extra = ray_tiles if sums else 0
        return call(
            functools.partial(forward_kernel, sizes, len(values), members, start_row, len(sums)),
            "forward", 16 if paired else 32, [SMEM] + [VMEM] * (len(operands) - 1),
            shape((n_out + extra, extent), F32), *operands,
            scratch=[pltpu.VMEM((members * rows, extent), F32), pltpu.VMEM((n_out, extent), F32)])

    def residual_of(projection, row_sums, *sibling):
        operands = [projection, sino, *row_sums, *sibling]
        return call(
            functools.partial(residual_kernel, frames, len(row_sums)), "residual", 16,
            [VMEM] * len(operands), shape((n_rays, extent), BF16), *operands)

    def backward(slots, parts, members, table, kind, start=None, split=()):
        operands = [pltpu.with_memory_space_constraint(slots, pltpu.SMEM), *parts, *table] + ([] if start is None else [start])
        return call(
            functools.partial(backward_kernel, sizes, len(parts), start is not None, split),
            "backward", 16 if paired else 32, [SMEM] + [VMEM] * (len(operands) - 1),
            [shape((len(some) * rows, extent), each) for some, each in zip(split, kind)]
            if split else shape((members * rows, extent), kind), *operands,
            scratch=[pltpu.VMEM((len(parts) * n_rays, extent), F32)]
            + [pltpu.VMEM((members * rows, extent), F32)] * n_bank)

    def join(*parts):
        total = sum(part.shape[0] for part in parts)
        return call(join_kernel, "join", 16, [VMEM] * len(parts), shape((total, extent), BF16), *parts)

    def update(volume, pieces, last):
        out = [shape((rows, extent), F32)] + ([] if last else [shape((rows, extent), BF16)])
        return call(
            functools.partial(update_kernel, len(pieces)), "update", 16,
            [VMEM] * (2 + len(pieces)), out, volume, column_weight, *pieces)

    column_weight = call(
        functools.partial(column_kernel, sizes), "column_weight", 16, [VMEM] * 4,
        shape((rows, extent), F32), *slots_by_depth, live)

    for sweep in range(ITERS):
        last = sweep + 1 == ITERS
        if paired:
            over_2, over_1, over_3, across = [
                exchange(payload, n_slab, distance) for distance in (8, 4, 12, 14)]
            z_part = join(payload, over_2, over_1)
            y_part = exchange(z_part, n_slab, 2)
            along_z, along_y = (z_part, over_3), (y_part, across)
            if sweep == 0:
                (z_list,), z_rows, z_forward, z_backward = setup(along_z, 4, (None,))
            both = forward(z_list, along_z, 4, z_forward, 2 * n_rays)
            if sweep == 0:
                (own_list, other_list), y_rows, y_forward, y_backward = setup(
                    along_y, 4, (0, 1), after=both)
            other = exchange(
                forward(other_list, along_y, 4, y_forward, n_rays, both, n_rays,
                        (z_rows, y_rows) if sweep == 0 else ()), n_slab, 1)
            if sweep == 0:
                first_other = other
            own = forward(own_list, along_y, 4, y_forward, n_rays, both, 0)
            residual = residual_of(own, (z_rows, y_rows), other, first_other)
            other_residual = exchange(residual, n_slab, 1)
            y_sum = backward(own_list, [residual], 4, y_backward, F32)
            far_sum, near_sum = backward(
                other_list, [other_residual], 4, y_backward, (BF16, BF16), y_sum, ((1, 3), (0, 2)))
            far_part, near_part = exchange(far_sum, n_slab, 2), exchange(near_sum, n_slab, 2)
            z_sum = backward(z_list, [residual, other_residual], 4, z_backward, F32)
            piece = shape((rows, extent), BF16)
            piece_2, piece_3 = call(
                functools.partial(combine_kernel, (1, 3)), "combine", 16, [VMEM] * 2,
                [piece, piece], z_sum, far_part)
            got = [exchange(piece_2, n_slab, 8), exchange(piece_3, n_slab, 12)]
            own_piece, piece_1 = call(
                functools.partial(combine_kernel, (0, 2)), "combine", 16, [VMEM] * 2,
                [shape((rows, extent), F32), piece], z_sum, near_part)
            pieces = [own_piece, *got, exchange(piece_1, n_slab, 4)]
        else:
            everyone = lax.all_gather(payload, "slab", axis=0, tiled=True)
            if sweep == 0:
                (slots,), row_sums, to_rays, to_voxels = setup((everyone,), n_slab, (None,))
            projection = forward(slots, (everyone,), n_slab, to_rays, n_rays)
            residual = residual_of(projection, (row_sums,))
            sums = backward(slots, [residual], n_slab, to_voxels, BF16)
            parts = lax.all_to_all(
                sums.reshape(n_slab, rows, extent), "slab", split_axis=0, concat_axis=0, tiled=True)
            pieces = [jnp.sum(parts.astype(F32), axis=0)]
        volume, *rounded = update(volume, pieces, last)
        if not last:
            payload = rounded[0]
    return volume.reshape(start_volume.shape)


def solution(mesh):
    in_specs = (
        P(("scan", "slab"), None, None),
        P(("scan", "slab"), None, None),
        P(("scan", "slab"), None),
        P(("scan", "slab")),
        P(("scan", "slab")),
        P(("scan", "slab"), None),
        P(("scan", "slab"), None),
    )
    out_specs = P(("scan", "slab"), None, None)
    return jax.shard_map(shards, mesh=mesh, in_specs=in_specs, out_specs=out_specs, check_vma=False)
```

```python
import functools

import jax
import jax.numpy as jnp
from jax import lax
from jax.experimental import pallas as pl
from jax.experimental.pallas import tpu as pltpu
from jax.sharding import PartitionSpec as P

ITERS = 2
CHUNK = 16
F32 = jnp.float32
BF16 = jnp.bfloat16
I32 = jnp.int32
HIGHEST = lax.Precision.HIGHEST
VMEM = pl.BlockSpec(memory_space=pltpu.VMEM)
ANY = pl.BlockSpec(memory_space=pl.ANY)
SMEM = pl.BlockSpec(memory_space=pltpu.SMEM)
HBM = pl.BlockSpec(memory_space=pltpu.HBM)


def hat(ray, centre):
    return jnp.maximum(0.0, 1.0 - jnp.abs(ray - centre)).astype(BF16)


def row_taps(offset, slope, extent):
    shape = (offset.shape[0], extent)
    ray = lax.broadcasted_iota(I32, shape, 1).astype(F32)
    inverse = jnp.broadcast_to(1.0 / slope, shape)
    offset = jnp.broadcast_to(offset, shape)
    slope = jnp.broadcast_to(slope, shape)
    middle = jnp.floor((ray - offset) * inverse + 0.5)
    middle = jnp.minimum(jnp.maximum(middle, 1.0), extent - 2.0)
    weights = [hat(ray, offset + slope * (middle + step)) for step in (-1.0, 0.0, 1.0)]
    return middle.astype(I32), weights


def column_taps(offset, slope, extent):
    shape = (offset.shape[0], extent)
    voxel = lax.broadcasted_iota(I32, shape, 1).astype(F32)
    centre = jnp.broadcast_to(offset, shape) + jnp.broadcast_to(slope, shape) * voxel
    first = jnp.minimum(jnp.maximum(jnp.floor(centre), 0.0), extent - 2.0)
    weights = [hat(first + step, centre) for step in (0.0, 1.0)]
    return first.astype(I32), weights


def repeat_rows(values, times):
    return jnp.concatenate(
        [jnp.broadcast_to(values[row:row + 1, :], (times, values.shape[1]))
         for row in range(values.shape[0])], axis=0)


def contract_lanes(left, right):
    return lax.dot_general(
        left.astype(BF16), right.astype(BF16), (((1,), (1,)), ((), ())), preferred_element_type=F32)


def per_slot(live_ref, slots, capacity):
    targets = live_ref.shape[1]
    slot = lax.broadcasted_iota(I32, (targets, slots), 1)
    owner = lax.broadcasted_iota(I32, (targets, slots), 0)
    expand = (lax.div(slot, capacity) == owner).astype(F32)
    return jnp.dot(live_ref[...].astype(F32), expand, precision=HIGHEST, preferred_element_type=F32)


def pack_kernel(capacity, *refs):
    sources, out_ref, loaded, arrived = refs[:6], refs[6], refs[7:13], refs[13]
    copies = [
        pltpu.make_async_copy(source, ref, arrived.at[place])
        for place, (source, ref) in enumerate(zip(sources, loaded))]
    for copy in copies:
        copy.start()
    for copy in copies:
        copy.wait()
    volume_ref, offset_ref, slope_ref, voxel_ref, ray_ref, live_ref = loaded
    rows, extent = volume_ref.shape
    out_ref[0:rows, :] = volume_ref[...].astype(BF16)
    slots = ray_ref.shape[1]
    fields = []
    for ref in (offset_ref, slope_ref):
        left = ref[...]
        for addend in range(3):
            part = left.astype(BF16).astype(F32)
            fields.append(part)
            left = left - part
    fields.append(voxel_ref[...].astype(F32))
    fields.append(ray_ref[...].astype(F32))
    fields.append(per_slot(live_ref, slots, capacity))
    used = sum(field.shape[0] for field in fields)
    fields.append(jnp.zeros((-used % 16, slots), F32))
    fields = jnp.concatenate(fields, axis=0)
    height = fields.shape[0]
    for part in range(slots // extent):
        at = pl.ds(rows + part * height, height)
        out_ref[at, :] = fields[:, part * extent:(part + 1) * extent].astype(BF16)


def setup_kernel(n_payloads, members, stride, span, sizes, tiles, wanted, *refs):
    payload_refs, refs = refs[:n_payloads], refs[-(2 * len(wanted) + 10):]
    where = [(ref, index) for ref in payload_refs for index in range(ref.shape[0] // stride)]
    list_refs, row_ref, tables = refs[:len(wanted)], refs[len(wanted)], refs[len(wanted) + 1:-len(wanted) - 2]
    drafts, arrived, summed = refs[-len(wanted) - 2:-2], refs[-2], refs[-1]
    copies = [
        pltpu.make_async_copy(draft, ref, arrived.at[place])
        for place, (draft, ref) in enumerate(zip(drafts, list_refs))]
    capacity, depth, frames = sizes
    width = span * capacity
    extent = row_ref.shape[1]
    ray_tiles = row_ref.shape[0] // span
    height = -(-(7 * depth + 2) // 16) * 16
    lanes = drafts[0].shape[1]
    me = lax.axis_index("slab").astype(I32)
    parity = lax.rem(me, span)
    first_slot = (me - parity) * capacity
    part = lax.div(first_slot, extent)
    shift = lax.rem(extent - lax.rem(first_slot, extent), extent)

    def collect(member, lined, payload_ref, within):
        at = within * stride + tiles * frames + part * height
        raw = payload_ref[pl.ds(pl.multiple_of(at, 16), height), :].astype(F32)
        offset = (raw[0:depth] + raw[depth:2 * depth]) + raw[2 * depth:3 * depth]
        slope = (raw[3 * depth:4 * depth] + raw[4 * depth:5 * depth]) + raw[5 * depth:6 * depth]
        fields = jnp.concatenate(
            [offset, slope, raw[6 * depth:7 * depth + 2],
             jnp.zeros((16 - 3 * depth - 2, extent), F32)], axis=0)
        fields = pltpu.roll(fields, shift, axis=1)
        lane = lax.broadcasted_iota(I32, fields.shape, 1)
        fields = jnp.where(lane < width, fields, 0.0)
        if lanes > extent:
            fields = jnp.concatenate(
                [fields, jnp.zeros((fields.shape[0], lanes - extent), F32)], axis=1)
        return lined + pltpu.roll(fields, member * width, axis=1)

    lined = jnp.zeros((16, lanes), F32)
    if members <= 16:
        for member in range(members):
            lined = collect(member, lined, *where[member])
    else:
        lined = lax.fori_loop(
            0, members, lambda member, lined: collect(member, lined, payload_refs[0], member), lined)

    slot = lax.broadcasted_iota(I32, (1, lanes), 1)
    within = lax.rem(slot, width)
    target = lax.bitwise_xor(lax.div(within, capacity), parity)
    ray = lined[3 * depth:3 * depth + 1]
    count = lined[3 * depth + 1:3 * depth + 2]
    alive = jnp.logical_and(lax.rem(within, capacity).astype(F32) < count, slot < members * width)

    table = jnp.concatenate(
        [slot.astype(F32), ray, target.astype(F32), lined[2 * depth:3 * depth],
         jnp.zeros((5 - depth, lanes), F32)], axis=0)
    order = lax.broadcasted_iota(I32, (lanes, lanes), 0)
    earlier = (lax.broadcasted_iota(I32, (lanes, lanes), 1) < order).astype(F32)
    for ref, kind, copy in zip(drafts, wanted, copies):
        taken = alive if kind is None else jnp.logical_and(alive, target == kind)
        taken = taken.astype(F32)
        position = contract_lanes(jnp.broadcast_to(taken, (8, lanes)), earlier)[0:1]
        position = jnp.where(taken > 0.0, position, -1.0).astype(I32)
        choose = jnp.broadcast_to(position, (lanes, lanes)) == order
        packed = (contract_lanes(table, choose.astype(F32)) + 0.5).astype(I32)
        total = jnp.sum(taken, axis=1, keepdims=True).astype(I32)
        line = jnp.where(slot < total, packed[0:1], lanes)
        base = packed[1:2] if kind is not None else packed[1:2] + packed[2:3] * ray_tiles
        member = lax.div(packed[0:1], width) * tiles
        rows = [line, base * frames]
        rows += [(packed[3 + level:4 + level] + member) * frames for level in range(depth)]
        rows += [jnp.zeros((5 - depth, lanes), I32), jnp.broadcast_to(total, (1, lanes))]
        ref[...] = jnp.concatenate(rows, axis=0)
        copy.start()

    columns = lined.T
    step = 32
    for row in range(0, lanes, step):
        total = None
        for level in range(depth):
            offset = columns[row:row + step, level:level + 1]
            slope = columns[row:row + step, depth + level:depth + level + 1]
            middle, weights = row_taps(offset, slope, extent)
            first, pair = column_taps(offset, slope, extent)
            wide = [weight.astype(F32) for weight in weights]
            values = [middle] + wide + [first] + [weight.astype(F32) for weight in pair]
            at = level * (lanes + 8) + row
            for ref, value in zip(tables, values):
                ref[at:at + step, :] = value
            parts = (wide[0] + wide[1]) + wide[2]
            total = parts if total is None else total + parts
        summed[row:row + step, :] = total
    for ref in tables:
        blank = jnp.ones if ref.dtype == I32 else jnp.zeros
        for level in range(depth):
            at = level * (lanes + 8) + lanes
            ref[at:at + 8, :] = blank((8, extent), ref.dtype)

    tile = lax.broadcasted_iota(I32, (span * ray_tiles, lanes), 0).astype(F32)
    place = ray + (target * ray_tiles).astype(F32)
    place = jnp.where(alive, place, -1.0)
    hot = (jnp.broadcast_to(place, tile.shape) == tile).astype(F32)
    row_ref[...] = jnp.dot(hot, summed[...], precision=HIGHEST, preferred_element_type=F32)
    for copy in copies:
        copy.wait()


def column_kernel(sizes, offset_ref, slope_ref, voxel_ref, live_ref, out_ref):
    capacity, depth, frames = sizes
    tiles = out_ref.shape[0] // frames
    slots = offset_ref.shape[1]
    extent = out_ref.shape[1]
    offsets = offset_ref[...].T
    slopes = slope_ref[...].T
    within = lax.rem(lax.broadcasted_iota(I32, (1, slots), 1), capacity).astype(F32)
    alive = jnp.broadcast_to(within, (tiles, slots)) < per_slot(live_ref, slots, capacity)
    total = jnp.zeros((tiles, extent), F32)
    for level in range(depth):
        unused, pair = column_taps(
            offsets[:, level:level + 1], slopes[:, level:level + 1], extent)
        tile_of = jnp.broadcast_to(voxel_ref[level:level + 1, :], (tiles, slots))
        match = tile_of == lax.broadcasted_iota(I32, (tiles, slots), 0)
        hot = jnp.logical_and(match, alive).astype(F32).astype(BF16)
        for weight in pair:
            total += jnp.dot(hot, weight, preferred_element_type=F32)
    out_ref[...] = repeat_rows(1.0 / jnp.maximum(total, 1.0), frames)


def pick(values, index):
    numbers = lax.GatherDimensionNumbers(
        offset_dims=(), collapsed_slice_dims=(1,), start_index_map=(1,),
        operand_batching_dims=(0,), start_indices_batching_dims=(0,))
    return lax.gather(
        values, index[:, :, None], numbers, slice_sizes=(1, 1),
        mode=lax.GatherScatterMode.PROMISE_IN_BOUNDS)


def pack_pair(first, second):
    kind = jnp.int16 if first.dtype == I32 else BF16
    return jnp.concatenate([first, second], axis=0).astype(kind)


def spread(ref, row, frames):
    return ref[pl.ds(row, frames, stride=0), :]


def tile_at(start, frames):
    return pl.ds(pl.multiple_of(start, frames), frames)


def for_slots(slots, body):
    def some(step, carry):
        for place in range(CHUNK):
            body(step * CHUNK + place, place)
        return carry

    lax.fori_loop(0, lax.div(slots[7, 0] + (CHUNK - 1), CHUNK), some, 0)


def for_rows(rows, body):
    step = 128

    def some(number, carry):
        body(pl.ds(pl.multiple_of(number * step, step), step))
        return carry

    lax.fori_loop(0, rows // step, some, 0)


def forward_kernel(sizes, n_values, members, start_row, n_sums, slots, *refs):
    capacity, depth, frames = sizes
    value_refs, tables, refs = refs[:n_values], refs[n_values:n_values + 4], refs[n_values + 4:]
    start_ref = None
    if start_row is not None:
        start_ref, refs = refs[0], refs[1:]
    sum_refs, (out_ref, wide, second) = refs[:n_sums], refs[n_sums:]
    rows = wide.shape[0] // members
    stride = sum(ref.shape[0] for ref in value_refs) // members
    rays = second.shape[0]
    line_step = tables[0].shape[0] // depth

    base = 0
    for ref in value_refs:
        def widen(member, carry, ref=ref, base=base):
            at = pl.ds(pl.multiple_of((base + member) * rows, rows), rows)
            wide[at, :] = ref[pl.ds(pl.multiple_of(member * stride, 16), rows), :].astype(F32)
            return carry

        lax.fori_loop(0, ref.shape[0] // stride, widen, 0)
        base += ref.shape[0] // stride
    second[...] = jnp.zeros_like(second)
    if start_ref is None:
        out_ref[...] = jnp.zeros_like(out_ref)
    else:
        out_ref[0:rays, :] = start_ref[start_row:start_row + rays, :]
    if n_sums:
        half = sum_refs[0].shape[0] // 2
        out_ref[rays:, :] = sum([ref[half:, :] for ref in sum_refs[1:]], sum_refs[0][half:, :])

    def one(slot, place):
        line = slots[0, slot]
        taps = []
        for start in range(0, depth, 2):
            levels = range(start, start + 2)
            values = [wide[tile_at(slots[2 + level, slot], frames), :] for level in levels]
            middles = [spread(tables[0], line + level * line_step, frames) for level in levels]
            lower = [
                pick(pack_pair(value, value), pack_pair(middle - 1, middle)).astype(F32)
                for value, middle in zip(values, middles)]
            upper = pick(
                pack_pair(*values), pack_pair(*[middle + 1 for middle in middles])).astype(F32)
            for which, pair in enumerate(lower):
                taps.append((pair[0:frames], pair[frames:2 * frames],
                             upper[which * frames:(which + 1) * frames]))
        total = None
        for level, three in enumerate(taps):
            for ref, tap in zip(tables[1:], three):
                term = spread(ref, line + level * line_step, frames) * tap
                total = term if total is None else total + term
        projection = (out_ref, second)[place % 2]
        projection[tile_at(slots[1, slot], frames), :] += total.astype(BF16).astype(F32)

    for_slots(slots, one)
    out_ref[0:rays, :] += second[...]


def residual_kernel(frames, n_own, projection_ref, sinogram_ref, *refs):
    own, refs, out_ref = refs[:n_own], refs[n_own:-1], refs[-1]
    rays = out_ref.shape[0]
    ray_tiles = rays // frames
    total = sum([ref[0:ray_tiles, :] for ref in own[1:]], own[0][0:ray_tiles, :])
    projection = projection_ref[...]
    if refs:
        projection = projection + refs[0][0:rays, :]
        total = total + refs[-1][rays:, :]
    weight = repeat_rows(1.0 / jnp.maximum(total, 1.0), frames)
    out_ref[...] = ((sinogram_ref[...].astype(F32) - projection) * weight).astype(BF16)


def backward_kernel(sizes, n_parts, has_start, split, slots, *refs):
    capacity, depth, frames = sizes
    part_refs, tables, refs = refs[:n_parts], refs[n_parts:n_parts + 3], refs[n_parts + 3:]
    start_ref = None
    if has_start:
        start_ref, refs = refs[0], refs[1:]
    outs = refs[:len(split)] if split else refs[:1]
    residual, banks = refs[len(outs)], refs[len(outs) + 1:]
    rays = part_refs[0].shape[0]
    line_step = tables[0].shape[0] // depth
    for place, ref in enumerate(part_refs):
        residual[place * rays:(place + 1) * rays, :] = ref[...].astype(F32)

    def clear(at):
        for place, bank in enumerate(banks):
            if place == 0 and has_start:
                bank[at, :] = start_ref[at, :]
            else:
                bank[at, :] = jnp.zeros((at.size, bank.shape[1]), F32)

    for_rows(banks[0].shape[0], clear)

    def one(slot, place):
        line = slots[0, slot]
        values = residual[tile_at(slots[1, slot], frames), :]
        twice = pack_pair(values, values)
        for level in range(depth):
            row = line + level * line_step
            first = spread(tables[0], row, frames)
            taps = pick(twice, pack_pair(first, first + 1)).astype(F32)
            term = (spread(tables[1], row, frames) * taps[0:frames]
                    + spread(tables[2], row, frames) * taps[frames:2 * frames])
            banks[level % len(banks)][tile_at(slots[2 + level, slot], frames), :] += term

    for_slots(slots, one)

    def total(at):
        return sum([bank[at, :] for bank in banks[1:]], banks[0][at, :])

    if split:
        for ref, members in zip(outs, split):
            rows = ref.shape[0] // len(members)
            for place, member in enumerate(members):
                ref[place * rows:(place + 1) * rows, :] = total(pl.ds(member * rows, rows)).astype(ref.dtype)
    else:
        def finish(at):
            outs[0][at, :] = total(at).astype(outs[0].dtype)

        for_rows(outs[0].shape[0], finish)


def join_kernel(*refs):
    out_ref, at = refs[-1], 0
    for ref in refs[:-1]:
        out_ref[at:at + ref.shape[0], :] = ref[...]
        at += ref.shape[0]


def combine_kernel(members, sum_ref, y_ref, *piece_refs):
    rows = piece_refs[0].shape[0]
    for place, (member, ref) in enumerate(zip(members, piece_refs)):
        mine = sum_ref[member * rows:(member + 1) * rows, :]
        ref[...] = (mine + y_ref[place * rows:(place + 1) * rows, :].astype(F32)).astype(ref.dtype)


def update_kernel(n_pieces, volume_ref, column_ref, *refs):
    back = refs[0][...]
    for ref in refs[1:n_pieces]:
        back = back + ref[...].astype(F32)
    volume = volume_ref[...] + column_ref[...] * back
    for ref in refs[n_pieces:]:
        ref[...] = volume.astype(ref.dtype)


def call(kernel, name, mib, in_specs, out_shape, *operands, scratch=()):
    one = not isinstance(out_shape, list)
    return pl.pallas_call(
        kernel,
        out_shape=out_shape,
        in_specs=in_specs,
        out_specs=VMEM if one else [
            SMEM if getattr(out, "memory_space", None) == pltpu.SMEM else VMEM for out in out_shape],
        scratch_shapes=list(scratch),
        compiler_params=pltpu.CompilerParams(vmem_limit_bytes=mib * 1024 * 1024),
        name=name,
        cost_estimate=pl.CostEstimate(flops=4 * 10**9, bytes_accessed=8 * 10**6, transcendentals=0),
    )(*operands)


def exchange(values, n_slab, distance):
    return lax.ppermute(
        values, "slab", [(device, device ^ distance) for device in range(n_slab)])


def shards(sinogram, start_volume, slot_voxel, slot_ray, live_count, block_slope, block_offset):
    n_slab = lax.axis_size("slab")
    n_slots, depth = slot_voxel.shape
    capacity = n_slots // n_slab
    ray_tiles, frames, extent = sinogram.shape
    voxel_tiles = start_volume.shape[0]
    rows = voxel_tiles * frames
    sizes = (capacity, depth, frames)
    paired = n_slab == 16
    span = 2 if paired else 1
    n_bank = 2 if paired else 1
    shape = jax.ShapeDtypeStruct
    n_rays = ray_tiles * frames
    volume = start_volume.reshape(rows, extent)
    sino = sinogram.reshape(n_rays, extent)
    slots_by_depth = (block_offset.T, block_slope.T, slot_voxel.T)
    live = live_count.reshape(1, n_slab)
    height = -(-(7 * depth + 2) // 16) * 16 * (n_slots // extent)
    operands = (volume, *slots_by_depth, slot_ray.reshape(1, n_slots), live)
    payload = call(
        functools.partial(pack_kernel, capacity), "pack", 16, [HBM] * 6,
        shape((rows + height, extent), BF16),
        *[pltpu.with_memory_space_constraint(operand, pltpu.HBM) for operand in operands],
        scratch=[pltpu.VMEM(operand.shape, operand.dtype) for operand in operands]
        + [pltpu.SemaphoreType.DMA((6,))])

    def setup(payloads, members, wanted, after=None):
        lanes = -(-members * span * capacity // 128) * 128
        lines = depth * (lanes + 8)
        table = [shape((lines, extent), I32)] + [shape((lines, extent), F32)] * 3
        table += [shape((lines, extent), I32)] + [shape((lines, extent), F32)] * 2
        n = len(wanted)
        out = [pltpu.SMEM((8, lanes), I32)] * n + [shape((span * ray_tiles, extent), F32)] + table
        waits = [] if after is None else [after]
        found = call(
            functools.partial(setup_kernel, len(payloads), members,
                              sum(one.shape[0] for one in payloads) // members, span, sizes,
                              voxel_tiles, wanted),
            "setup", 24, [VMEM] * len(payloads) + [ANY] * len(waits), out, *payloads, *waits,
            scratch=[pltpu.VMEM((8, lanes), I32)] * n
            + [pltpu.SemaphoreType.DMA((n,)), pltpu.VMEM((lanes, extent), F32)])
        return found[:n], found[n], found[n + 1:n + 5], found[n + 5:]

    def forward(slots, values, members, table, n_out, start=None, start_row=None, sums=()):
        operands = [pltpu.with_memory_space_constraint(slots, pltpu.SMEM), *values, *table] + ([] if start is None else [start]) + list(sums)
        extra = ray_tiles if sums else 0
        return call(
            functools.partial(forward_kernel, sizes, len(values), members, start_row, len(sums)),
            "forward", 16 if paired else 32, [SMEM] + [VMEM] * (len(operands) - 1),
            shape((n_out + extra, extent), F32), *operands,
            scratch=[pltpu.VMEM((members * rows, extent), F32), pltpu.VMEM((n_out, extent), F32)])

    def residual_of(projection, row_sums, *sibling):
        operands = [projection, sino, *row_sums, *sibling]
        return call(
            functools.partial(residual_kernel, frames, len(row_sums)), "residual", 16,
            [VMEM] * len(operands), shape((n_rays, extent), BF16), *operands)

    def backward(slots, parts, members, table, kind, start=None, split=()):
        operands = [pltpu.with_memory_space_constraint(slots, pltpu.SMEM), *parts, *table] + ([] if start is None else [start])
        return call(
            functools.partial(backward_kernel, sizes, len(parts), start is not None, split),
            "backward", 16 if paired else 32, [SMEM] + [VMEM] * (len(operands) - 1),
            [shape((len(some) * rows, extent), each) for some, each in zip(split, kind)]
            if split else shape((members * rows, extent), kind), *operands,
            scratch=[pltpu.VMEM((len(parts) * n_rays, extent), F32)]
            + [pltpu.VMEM((members * rows, extent), F32)] * n_bank)

    def join(*parts):
        total = sum(part.shape[0] for part in parts)
        return call(join_kernel, "join", 16, [VMEM] * len(parts), shape((total, extent), BF16), *parts)

    def update(volume, pieces, last):
        out = [shape((rows, extent), F32)] + ([] if last else [shape((rows, extent), BF16)])
        return call(
            functools.partial(update_kernel, len(pieces)), "update", 16,
            [VMEM] * (2 + len(pieces)), out, volume, column_weight, *pieces)

    column_weight = call(
        functools.partial(column_kernel, sizes), "column_weight", 16, [VMEM] * 4,
        shape((rows, extent), F32), *slots_by_depth, live)

    for sweep in range(ITERS):
        last = sweep + 1 == ITERS
        if paired:
            over_2, over_1, over_3, across = [
                exchange(payload, n_slab, distance) for distance in (8, 4, 12, 14)]
            z_part = join(payload, over_2, over_1)
            y_part = exchange(z_part, n_slab, 2)
            along_z, along_y = (z_part, over_3), (y_part, across)
            if sweep == 0:
                (z_list,), z_rows, z_forward, z_backward = setup(along_z, 4, (None,))
            both = forward(z_list, along_z, 4, z_forward, 2 * n_rays)
            if sweep == 0:
                (own_list, other_list), y_rows, y_forward, y_backward = setup(
                    along_y, 4, (0, 1), after=both)
            other = exchange(
                forward(other_list, along_y, 4, y_forward, n_rays, both, n_rays,
                        (z_rows, y_rows) if sweep == 0 else ()), n_slab, 1)
            if sweep == 0:
                first_other = other
            own = forward(own_list, along_y, 4, y_forward, n_rays, both, 0)
            residual = residual_of(own, (z_rows, y_rows), other, first_other)
            other_residual = exchange(residual, n_slab, 1)
            y_sum = backward(own_list, [residual], 4, y_backward, F32)
            far_sum, near_sum = backward(
                other_list, [other_residual], 4, y_backward, (BF16, BF16), y_sum, ((1, 3), (0, 2)))
            far_part, near_part = exchange(far_sum, n_slab, 2), exchange(near_sum, n_slab, 2)
            z_sum = backward(z_list, [residual, other_residual], 4, z_backward, F32)
            piece = shape((rows, extent), BF16)
            piece_2, piece_3 = call(
                functools.partial(combine_kernel, (1, 3)), "combine", 16, [VMEM] * 2,
                [piece, piece], z_sum, far_part)
            got = [exchange(piece_2, n_slab, 8), exchange(piece_3, n_slab, 12)]
            own_piece, piece_1 = call(
                functools.partial(combine_kernel, (0, 2)), "combine", 16, [VMEM] * 2,
                [shape((rows, extent), F32), piece], z_sum, near_part)
            pieces = [own_piece, *got, exchange(piece_1, n_slab, 4)]
        else:
            everyone = lax.all_gather(payload, "slab", axis=0, tiled=True)
            if sweep == 0:
                (slots,), row_sums, to_rays, to_voxels = setup((everyone,), n_slab, (None,))
            projection = forward(slots, (everyone,), n_slab, to_rays, n_rays)
            residual = residual_of(projection, (row_sums,))
            sums = backward(slots, [residual], n_slab, to_voxels, BF16)
            parts = lax.all_to_all(
                sums.reshape(n_slab, rows, extent), "slab", split_axis=0, concat_axis=0, tiled=True)
            pieces = [jnp.sum(parts.astype(F32), axis=0)]
        volume, *rounded = update(volume, pieces, last)
        if not last:
            payload = rounded[0]
    return volume.reshape(start_volume.shape)


def solution(mesh):
    in_specs = (
        P(("scan", "slab"), None, None),
        P(("scan", "slab"), None, None),
        P(("scan", "slab"), None),
        P(("scan", "slab")),
        P(("scan", "slab")),
        P(("scan", "slab"), None),
        P(("scan", "slab"), None),
    )
    out_specs = P(("scan", "slab"), None, None)
    return jax.shard_map(shards, mesh=mesh, in_specs=in_specs, out_specs=out_specs, check_vma=False)
```

```python
import functools

import jax
import jax.numpy as jnp
from jax import lax
from jax.experimental import pallas as pl
from jax.experimental.pallas import tpu as pltpu
from jax.sharding import PartitionSpec as P

ITERS = 2
CHUNK = 16
F32 = jnp.float32
BF16 = jnp.bfloat16
I32 = jnp.int32
HIGHEST = lax.Precision.HIGHEST
VMEM = pl.BlockSpec(memory_space=pltpu.VMEM)
ANY = pl.BlockSpec(memory_space=pl.ANY)
SMEM = pl.BlockSpec(memory_space=pltpu.SMEM)
HBM = pl.BlockSpec(memory_space=pltpu.HBM)


def hat(ray, centre):
    return jnp.maximum(0.0, 1.0 - jnp.abs(ray - centre)).astype(BF16)


def row_taps(offset, slope, extent):
    shape = (offset.shape[0], extent)
    ray = lax.broadcasted_iota(I32, shape, 1).astype(F32)
    inverse = jnp.broadcast_to(1.0 / slope, shape)
    offset = jnp.broadcast_to(offset, shape)
    slope = jnp.broadcast_to(slope, shape)
    middle = jnp.floor((ray - offset) * inverse + 0.5)
    middle = jnp.minimum(jnp.maximum(middle, 1.0), extent - 2.0)
    weights = [hat(ray, offset + slope * (middle + step)) for step in (-1.0, 0.0, 1.0)]
    return middle.astype(I32), weights


def column_taps(offset, slope, extent):
    shape = (offset.shape[0], extent)
    voxel = lax.broadcasted_iota(I32, shape, 1).astype(F32)
    centre = jnp.broadcast_to(offset, shape) + jnp.broadcast_to(slope, shape) * voxel
    first = jnp.minimum(jnp.maximum(jnp.floor(centre), 0.0), extent - 2.0)
    weights = [hat(first + step, centre) for step in (0.0, 1.0)]
    return first.astype(I32), weights


def repeat_rows(values, times):
    return jnp.concatenate(
        [jnp.broadcast_to(values[row:row + 1, :], (times, values.shape[1]))
         for row in range(values.shape[0])], axis=0)


def contract_lanes(left, right):
    return lax.dot_general(
        left.astype(BF16), right.astype(BF16), (((1,), (1,)), ((), ())), preferred_element_type=F32)


def per_slot(live_ref, slots, capacity):
    targets = live_ref.shape[1]
    slot = lax.broadcasted_iota(I32, (targets, slots), 1)
    owner = lax.broadcasted_iota(I32, (targets, slots), 0)
    expand = (lax.div(slot, capacity) == owner).astype(F32)
    return jnp.dot(live_ref[...].astype(F32), expand, precision=HIGHEST, preferred_element_type=F32)


def pack_kernel(capacity, *refs):
    sources, out_ref, loaded, arrived = refs[:6], refs[6], refs[7:13], refs[13]
    copies = [
        pltpu.make_async_copy(source, ref, arrived.at[place])
        for place, (source, ref) in enumerate(zip(sources, loaded))]
    for copy in copies:
        copy.start()
    for copy in copies:
        copy.wait()
    volume_ref, offset_ref, slope_ref, voxel_ref, ray_ref, live_ref = loaded
    rows, extent = volume_ref.shape
    out_ref[0:rows, :] = volume_ref[...].astype(BF16)
    slots = ray_ref.shape[1]
    fields = []
    for ref in (offset_ref, slope_ref):
        left = ref[...]
        for addend in range(3):
            part = left.astype(BF16).astype(F32)
            fields.append(part)
            left = left - part
    fields.append(voxel_ref[...].astype(F32))
    fields.append(ray_ref[...].astype(F32))
    fields.append(per_slot(live_ref, slots, capacity))
    used = sum(field.shape[0] for field in fields)
    fields.append(jnp.zeros((-used % 16, slots), F32))
    fields = jnp.concatenate(fields, axis=0)
    height = fields.shape[0]
    for part in range(slots // extent):
        at = pl.ds(rows + part * height, height)
        out_ref[at, :] = fields[:, part * extent:(part + 1) * extent].astype(BF16)


def setup_kernel(n_payloads, members, stride, span, sizes, tiles, wanted, *refs):
    payload_refs, refs = refs[:n_payloads], refs[-(2 * len(wanted) + 10):]
    where = [(ref, index) for ref in payload_refs for index in range(ref.shape[0] // stride)]
    list_refs, row_ref, tables = refs[:len(wanted)], refs[len(wanted)], refs[len(wanted) + 1:-len(wanted) - 2]
    drafts, arrived, summed = refs[-len(wanted) - 2:-2], refs[-2], refs[-1]
    copies = [
        pltpu.make_async_copy(draft, ref, arrived.at[place])
        for place, (draft, ref) in enumerate(zip(drafts, list_refs))]
    capacity, depth, frames = sizes
    width = span * capacity
    extent = row_ref.shape[1]
    ray_tiles = row_ref.shape[0] // span
    height = -(-(7 * depth + 2) // 16) * 16
    lanes = drafts[0].shape[1]
    me = lax.axis_index("slab").astype(I32)
    parity = lax.rem(me, span)
    first_slot = (me - parity) * capacity
    part = lax.div(first_slot, extent)
    shift = lax.rem(extent - lax.rem(first_slot, extent), extent)

    def collect(member, lined, payload_ref, within):
        at = within * stride + tiles * frames + part * height
        raw = payload_ref[pl.ds(pl.multiple_of(at, 16), height), :].astype(F32)
        offset = (raw[0:depth] + raw[depth:2 * depth]) + raw[2 * depth:3 * depth]
        slope = (raw[3 * depth:4 * depth] + raw[4 * depth:5 * depth]) + raw[5 * depth:6 * depth]
        fields = jnp.concatenate(
            [offset, slope, raw[6 * depth:7 * depth + 2],
             jnp.zeros((16 - 3 * depth - 2, extent), F32)], axis=0)
        fields = pltpu.roll(fields, shift, axis=1)
        lane = lax.broadcasted_iota(I32, fields.shape, 1)
        fields = jnp.where(lane < width, fields, 0.0)
        if lanes > extent:
            fields = jnp.concatenate(
                [fields, jnp.zeros((fields.shape[0], lanes - extent), F32)], axis=1)
        return lined + pltpu.roll(fields, member * width, axis=1)

    lined = jnp.zeros((16, lanes), F32)
    if members <= 16:
        for member in range(members):
            lined = collect(member, lined, *where[member])
    else:
        lined = lax.fori_loop(
            0, members, lambda member, lined: collect(member, lined, payload_refs[0], member), lined)

    slot = lax.broadcasted_iota(I32, (1, lanes), 1)
    within = lax.rem(slot, width)
    target = lax.bitwise_xor(lax.div(within, capacity), parity)
    ray = lined[3 * depth:3 * depth + 1]
    count = lined[3 * depth + 1:3 * depth + 2]
    alive = jnp.logical_and(lax.rem(within, capacity).astype(F32) < count, slot < members * width)

    table = jnp.concatenate(
        [slot.astype(F32), ray, target.astype(F32), lined[2 * depth:3 * depth],
         jnp.zeros((5 - depth, lanes), F32)], axis=0)
    order = lax.broadcasted_iota(I32, (lanes, lanes), 0)
    earlier = (lax.broadcasted_iota(I32, (lanes, lanes), 1) < order).astype(F32)
    for ref, kind, copy in zip(drafts, wanted, copies):
        taken = alive if kind is None else jnp.logical_and(alive, target == kind)
        taken = taken.astype(F32)
        position = contract_lanes(jnp.broadcast_to(taken, (8, lanes)), earlier)[0:1]
        position = jnp.where(taken > 0.0, position, -1.0).astype(I32)
        choose = jnp.broadcast_to(position, (lanes, lanes)) == order
        packed = (contract_lanes(table, choose.astype(F32)) + 0.5).astype(I32)
        total = jnp.sum(taken, axis=1, keepdims=True).astype(I32)
        line = jnp.where(slot < total, packed[0:1], lanes)
        base = packed[1:2] if kind is not None else packed[1:2] + packed[2:3] * ray_tiles
        member = lax.div(packed[0:1], width) * tiles
        rows = [line, base * frames]
        rows += [(packed[3 + level:4 + level] + member) * frames for level in range(depth)]
        rows += [jnp.zeros((5 - depth, lanes), I32), jnp.broadcast_to(total, (1, lanes))]
        ref[...] = jnp.concatenate(rows, axis=0)
        copy.start()

    columns = lined.T
    step = 32
    for row in range(0, lanes, step):
        total = None
        for level in range(depth):
            offset = columns[row:row + step, level:level + 1]
            slope = columns[row:row + step, depth + level:depth + level + 1]
            middle, weights = row_taps(offset, slope, extent)
            first, pair = column_taps(offset, slope, extent)
            wide = [weight.astype(F32) for weight in weights]
            values = [middle] + wide + [first] + [weight.astype(F32) for weight in pair]
            at = level * (lanes + 8) + row
            for ref, value in zip(tables, values):
                ref[at:at + step, :] = value
            parts = (wide[0] + wide[1]) + wide[2]
            total = parts if total is None else total + parts
        summed[row:row + step, :] = total
    for ref in tables:
        blank = jnp.ones if ref.dtype == I32 else jnp.zeros
        for level in range(depth):
            at = level * (lanes + 8) + lanes
            ref[at:at + 8, :] = blank((8, extent), ref.dtype)

    tile = lax.broadcasted_iota(I32, (span * ray_tiles, lanes), 0).astype(F32)
    place = ray + (target * ray_tiles).astype(F32)
    place = jnp.where(alive, place, -1.0)
    hot = (jnp.broadcast_to(place, tile.shape) == tile).astype(F32)
    row_ref[...] = jnp.dot(hot, summed[...], precision=HIGHEST, preferred_element_type=F32)
    for copy in copies:
        copy.wait()


def column_kernel(sizes, offset_ref, slope_ref, voxel_ref, live_ref, out_ref):
    capacity, depth, frames = sizes
    tiles = out_ref.shape[0] // frames
    slots = offset_ref.shape[1]
    extent = out_ref.shape[1]
    offsets = offset_ref[...].T
    slopes = slope_ref[...].T
    within = lax.rem(lax.broadcasted_iota(I32, (1, slots), 1), capacity).astype(F32)
    alive = jnp.broadcast_to(within, (tiles, slots)) < per_slot(live_ref, slots, capacity)
    total = jnp.zeros((tiles, extent), F32)
    for level in range(depth):
        unused, pair = column_taps(
            offsets[:, level:level + 1], slopes[:, level:level + 1], extent)
        tile_of = jnp.broadcast_to(voxel_ref[level:level + 1, :], (tiles, slots))
        match = tile_of == lax.broadcasted_iota(I32, (tiles, slots), 0)
        hot = jnp.logical_and(match, alive).astype(F32).astype(BF16)
        for weight in pair:
            total += jnp.dot(hot, weight, preferred_element_type=F32)
    out_ref[...] = repeat_rows(1.0 / jnp.maximum(total, 1.0), frames)


def pick(values, index):
    numbers = lax.GatherDimensionNumbers(
        offset_dims=(), collapsed_slice_dims=(1,), start_index_map=(1,),
        operand_batching_dims=(0,), start_indices_batching_dims=(0,))
    return lax.gather(
        values, index[:, :, None], numbers, slice_sizes=(1, 1),
        mode=lax.GatherScatterMode.PROMISE_IN_BOUNDS)


def pack_pair(first, second):
    kind = jnp.int16 if first.dtype == I32 else BF16
    return jnp.concatenate([first, second], axis=0).astype(kind)


def spread(ref, row, frames):
    return ref[pl.ds(row, frames, stride=0), :]


def tile_at(start, frames):
    return pl.ds(pl.multiple_of(start, frames), frames)


def for_slots(slots, body):
    def some(step, carry):
        for place in range(CHUNK):
            body(step * CHUNK + place, place)
        return carry

    lax.fori_loop(0, lax.div(slots[7, 0] + (CHUNK - 1), CHUNK), some, 0)


def for_rows(rows, body):
    step = 128

    def some(number, carry):
        body(pl.ds(pl.multiple_of(number * step, step), step))
        return carry

    lax.fori_loop(0, rows // step, some, 0)


def forward_kernel(sizes, n_values, members, start_row, n_sums, slots, *refs):
    capacity, depth, frames = sizes
    value_refs, tables, refs = refs[:n_values], refs[n_values:n_values + 4], refs[n_values + 4:]
    start_ref = None
    if start_row is not None:
        start_ref, refs = refs[0], refs[1:]
    sum_refs, (out_ref, wide, second) = refs[:n_sums], refs[n_sums:]
    rows = wide.shape[0] // members
    stride = sum(ref.shape[0] for ref in value_refs) // members
    rays = second.shape[0]
    line_step = tables[0].shape[0] // depth

    base = 0
    for ref in value_refs:
        def widen(member, carry, ref=ref, base=base):
            at = pl.ds(pl.multiple_of((base + member) * rows, rows), rows)
            wide[at, :] = ref[pl.ds(pl.multiple_of(member * stride, 16), rows), :].astype(F32)
            return carry

        lax.fori_loop(0, ref.shape[0] // stride, widen, 0)
        base += ref.shape[0] // stride
    second[...] = jnp.zeros_like(second)
    if start_ref is None:
        out_ref[...] = jnp.zeros_like(out_ref)
    else:
        out_ref[0:rays, :] = start_ref[start_row:start_row + rays, :]
    if n_sums:
        half = sum_refs[0].shape[0] // 2
        out_ref[rays:, :] = sum([ref[half:, :] for ref in sum_refs[1:]], sum_refs[0][half:, :])

    def one(slot, place):
        line = slots[0, slot]
        taps = []
        for start in range(0, depth, 2):
            levels = range(start, start + 2)
            values = [wide[tile_at(slots[2 + level, slot], frames), :] for level in levels]
            middles = [spread(tables[0], line + level * line_step, frames) for level in levels]
            lower = [
                pick(pack_pair(value, value), pack_pair(middle - 1, middle)).astype(F32)
                for value, middle in zip(values, middles)]
            upper = pick(
                pack_pair(*values), pack_pair(*[middle + 1 for middle in middles])).astype(F32)
            for which, pair in enumerate(lower):
                taps.append((pair[0:frames], pair[frames:2 * frames],
                             upper[which * frames:(which + 1) * frames]))
        total = None
        for level, three in enumerate(taps):
            for ref, tap in zip(tables[1:], three):
                term = spread(ref, line + level * line_step, frames) * tap
                total = term if total is None else total + term
        projection = (out_ref, second)[place % 2]
        projection[tile_at(slots[1, slot], frames), :] += total.astype(BF16).astype(F32)

    for_slots(slots, one)
    out_ref[0:rays, :] += second[...]


def residual_kernel(frames, n_own, projection_ref, sinogram_ref, *refs):
    own, refs, out_ref = refs[:n_own], refs[n_own:-1], refs[-1]
    rays = out_ref.shape[0]
    ray_tiles = rays // frames
    total = sum([ref[0:ray_tiles, :] for ref in own[1:]], own[0][0:ray_tiles, :])
    projection = projection_ref[...]
    if refs:
        projection = projection + refs[0][0:rays, :]
        total = total + refs[-1][rays:, :]
    weight = repeat_rows(1.0 / jnp.maximum(total, 1.0), frames)
    out_ref[...] = ((sinogram_ref[...].astype(F32) - projection) * weight).astype(BF16)


def backward_kernel(sizes, n_parts, has_start, split, slots, *refs):
    capacity, depth, frames = sizes
    part_refs, tables, refs = refs[:n_parts], refs[n_parts:n_parts + 3], refs[n_parts + 3:]
    start_ref = None
    if has_start:
        start_ref, refs = refs[0], refs[1:]
    outs = refs[:len(split)] if split else refs[:1]
    residual, banks = refs[len(outs)], refs[len(outs) + 1:]
    rays = part_refs[0].shape[0]
    line_step = tables[0].shape[0] // depth
    for place, ref in enumerate(part_refs):
        residual[place * rays:(place + 1) * rays, :] = ref[...].astype(F32)

    def clear(at):
        for place, bank in enumerate(banks):
            if place == 0 and has_start:
                bank[at, :] = start_ref[at, :]
            else:
                bank[at, :] = jnp.zeros((at.size, bank.shape[1]), F32)

    for_rows(banks[0].shape[0], clear)

    def one(slot, place):
        line = slots[0, slot]
        values = residual[tile_at(slots[1, slot], frames), :]
        twice = pack_pair(values, values)
        for level in range(depth):
            row = line + level * line_step
            first = spread(tables[0], row, frames)
            taps = pick(twice, pack_pair(first, first + 1)).astype(F32)
            term = (spread(tables[1], row, frames) * taps[0:frames]
                    + spread(tables[2], row, frames) * taps[frames:2 * frames])
            banks[level % len(banks)][tile_at(slots[2 + level, slot], frames), :] += term

    for_slots(slots, one)

    def total(at):
        return sum([bank[at, :] for bank in banks[1:]], banks[0][at, :])

    if split:
        for ref, members in zip(outs, split):
            rows = ref.shape[0] // len(members)
            for place, member in enumerate(members):
                ref[place * rows:(place + 1) * rows, :] = total(pl.ds(member * rows, rows)).astype(ref.dtype)
    else:
        def finish(at):
            outs[0][at, :] = total(at).astype(outs[0].dtype)

        for_rows(outs[0].shape[0], finish)


def join_kernel(*refs):
    out_ref, at = refs[-1], 0
    for ref in refs[:-1]:
        out_ref[at:at + ref.shape[0], :] = ref[...]
        at += ref.shape[0]


def combine_kernel(members, sum_ref, y_ref, *piece_refs):
    rows = piece_refs[0].shape[0]
    for place, (member, ref) in enumerate(zip(members, piece_refs)):
        mine = sum_ref[member * rows:(member + 1) * rows, :]
        ref[...] = (mine + y_ref[place * rows:(place + 1) * rows, :].astype(F32)).astype(ref.dtype)


def update_kernel(n_pieces, volume_ref, column_ref, *refs):
    back = refs[0][...]
    for ref in refs[1:n_pieces]:
        back = back + ref[...].astype(F32)
    volume = volume_ref[...] + column_ref[...] * back
    for ref in refs[n_pieces:]:
        ref[...] = volume.astype(ref.dtype)


def call(kernel, name, mib, in_specs, out_shape, *operands, scratch=()):
    one = not isinstance(out_shape, list)
    return pl.pallas_call(
        kernel,
        out_shape=out_shape,
        in_specs=in_specs,
        out_specs=VMEM if one else [
            SMEM if getattr(out, "memory_space", None) == pltpu.SMEM else VMEM for out in out_shape],
        scratch_shapes=list(scratch),
        compiler_params=pltpu.CompilerParams(vmem_limit_bytes=mib * 1024 * 1024),
        name=name,
        cost_estimate=pl.CostEstimate(flops=4 * 10**9, bytes_accessed=8 * 10**6, transcendentals=0),
    )(*operands)


def exchange(values, n_slab, distance, odd_distance=None):
    far = (distance, distance if odd_distance is None else odd_distance)
    return lax.ppermute(
        values, "slab", [(device, device ^ far[device % 2]) for device in range(n_slab)])


def shards(sinogram, start_volume, slot_voxel, slot_ray, live_count, block_slope, block_offset):
    n_slab = lax.axis_size("slab")
    n_slots, depth = slot_voxel.shape
    capacity = n_slots // n_slab
    ray_tiles, frames, extent = sinogram.shape
    voxel_tiles = start_volume.shape[0]
    rows = voxel_tiles * frames
    sizes = (capacity, depth, frames)
    paired = n_slab == 16
    span = 2 if paired else 1
    n_bank = 2 if paired else 1
    shape = jax.ShapeDtypeStruct
    n_rays = ray_tiles * frames
    volume = start_volume.reshape(rows, extent)
    sino = sinogram.reshape(n_rays, extent)
    slots_by_depth = (block_offset.T, block_slope.T, slot_voxel.T)
    live = live_count.reshape(1, n_slab)
    height = -(-(7 * depth + 2) // 16) * 16 * (n_slots // extent)
    operands = (volume, *slots_by_depth, slot_ray.reshape(1, n_slots), live)
    payload = call(
        functools.partial(pack_kernel, capacity), "pack", 16, [HBM] * 6,
        shape((rows + height, extent), BF16),
        *[pltpu.with_memory_space_constraint(operand, pltpu.HBM) for operand in operands],
        scratch=[pltpu.VMEM(operand.shape, operand.dtype) for operand in operands]
        + [pltpu.SemaphoreType.DMA((6,))])

    def setup(payloads, members, wanted, after=None):
        lanes = -(-members * span * capacity // 128) * 128
        lines = depth * (lanes + 8)
        table = [shape((lines, extent), I32)] + [shape((lines, extent), F32)] * 3
        table += [shape((lines, extent), I32)] + [shape((lines, extent), F32)] * 2
        n = len(wanted)
        out = [pltpu.SMEM((8, lanes), I32)] * n + [shape((span * ray_tiles, extent), F32)] + table
        waits = [] if after is None else [after]
        found = call(
            functools.partial(setup_kernel, len(payloads), members,
                              sum(one.shape[0] for one in payloads) // members, span, sizes,
                              voxel_tiles, wanted),
            "setup", 24, [VMEM] * len(payloads) + [ANY] * len(waits), out, *payloads, *waits,
            scratch=[pltpu.VMEM((8, lanes), I32)] * n
            + [pltpu.SemaphoreType.DMA((n,)), pltpu.VMEM((lanes, extent), F32)])
        return found[:n], found[n], found[n + 1:n + 5], found[n + 5:]

    def forward(slots, values, members, table, n_out, start=None, start_row=None, sums=()):
        operands = [pltpu.with_memory_space_constraint(slots, pltpu.SMEM), *values, *table] + ([] if start is None else [start]) + list(sums)
        extra = ray_tiles if sums else 0
        return call(
            functools.partial(forward_kernel, sizes, len(values), members, start_row, len(sums)),
            "forward", 16 if paired else 32, [SMEM] + [VMEM] * (len(operands) - 1),
            shape((n_out + extra, extent), F32), *operands,
            scratch=[pltpu.VMEM((members * rows, extent), F32), pltpu.VMEM((n_out, extent), F32)])

    def residual_of(projection, row_sums, *sibling):
        operands = [projection, sino, *row_sums, *sibling]
        return call(
            functools.partial(residual_kernel, frames, len(row_sums)), "residual", 16,
            [VMEM] * len(operands), shape((n_rays, extent), BF16), *operands)

    def backward(slots, parts, members, table, kind, start=None, split=()):
        operands = [pltpu.with_memory_space_constraint(slots, pltpu.SMEM), *parts, *table] + ([] if start is None else [start])
        return call(
            functools.partial(backward_kernel, sizes, len(parts), start is not None, split),
            "backward", 16 if paired else 32, [SMEM] + [VMEM] * (len(operands) - 1),
            [shape((len(some) * rows, extent), each) for some, each in zip(split, kind)]
            if split else shape((members * rows, extent), kind), *operands,
            scratch=[pltpu.VMEM((len(parts) * n_rays, extent), F32)]
            + [pltpu.VMEM((members * rows, extent), F32)] * n_bank)

    def join(*parts):
        total = sum(part.shape[0] for part in parts)
        return call(join_kernel, "join", 16, [VMEM] * len(parts), shape((total, extent), BF16), *parts)

    def update(volume, pieces, last):
        out = [shape((rows, extent), F32)] + ([] if last else [shape((rows, extent), BF16)])
        return call(
            functools.partial(update_kernel, len(pieces)), "update", 16,
            [VMEM] * (2 + len(pieces)), out, volume, column_weight, *pieces)

    column_weight = call(
        functools.partial(column_kernel, sizes), "column_weight", 16, [VMEM] * 4,
        shape((rows, extent), F32), *slots_by_depth, live)

    for sweep in range(ITERS):
        last = sweep + 1 == ITERS
        if paired:
            place_1, place_2, place_3, across = [
                exchange(payload, n_slab, *pair) for pair in ((8, 12), (4, 8), (12, 4), (14, 6))]
            z_part = join(payload, place_1, place_2)
            y_part = exchange(z_part, n_slab, 2)
            along_z, along_y = (z_part, place_3), (y_part, across)
            if sweep == 0:
                (z_list,), z_rows, z_forward, z_backward = setup(along_z, 4, (None,))
            both = forward(z_list, along_z, 4, z_forward, 2 * n_rays)
            if sweep == 0:
                (own_list, other_list), y_rows, y_forward, y_backward = setup(
                    along_y, 4, (0, 1), after=both)
            other = exchange(
                forward(other_list, along_y, 4, y_forward, n_rays, both, n_rays,
                        (z_rows, y_rows) if sweep == 0 else ()), n_slab, 1)
            if sweep == 0:
                first_other = other
            own = forward(own_list, along_y, 4, y_forward, n_rays, both, 0)
            residual = residual_of(own, (z_rows, y_rows), other, first_other)
            other_residual = exchange(residual, n_slab, 1)
            y_sum = backward(own_list, [residual], 4, y_backward, F32)
            far_sum, near_sum = backward(
                other_list, [other_residual], 4, y_backward, (BF16, BF16), y_sum, ((1, 3), (0, 2)))
            far_part, near_part = exchange(far_sum, n_slab, 2), exchange(near_sum, n_slab, 2)
            z_sum = backward(z_list, [residual, other_residual], 4, z_backward, F32)
            piece = shape((rows, extent), BF16)
            piece_1, piece_3 = call(
                functools.partial(combine_kernel, (1, 3)), "combine", 16, [VMEM] * 2,
                [piece, piece], z_sum, far_part)
            got = [exchange(piece_1, n_slab, 8, 12), exchange(piece_3, n_slab, 12, 4)]
            own_piece, piece_2 = call(
                functools.partial(combine_kernel, (0, 2)), "combine", 16, [VMEM] * 2,
                [shape((rows, extent), F32), piece], z_sum, near_part)
            pieces = [own_piece, *got, exchange(piece_2, n_slab, 4, 8)]
        else:
            everyone = lax.all_gather(payload, "slab", axis=0, tiled=True)
            if sweep == 0:
                (slots,), row_sums, to_rays, to_voxels = setup((everyone,), n_slab, (None,))
            projection = forward(slots, (everyone,), n_slab, to_rays, n_rays)
            residual = residual_of(projection, (row_sums,))
            sums = backward(slots, [residual], n_slab, to_voxels, BF16)
            parts = lax.all_to_all(
                sums.reshape(n_slab, rows, extent), "slab", split_axis=0, concat_axis=0, tiled=True)
            pieces = [jnp.sum(parts.astype(F32), axis=0)]
        volume, *rounded = update(volume, pieces, last)
        if not last:
            payload = rounded[0]
    return volume.reshape(start_volume.shape)


def solution(mesh):
    in_specs = (
        P(("scan", "slab"), None, None),
        P(("scan", "slab"), None, None),
        P(("scan", "slab"), None),
        P(("scan", "slab")),
        P(("scan", "slab")),
        P(("scan", "slab"), None),
        P(("scan", "slab"), None),
    )
    out_specs = P(("scan", "slab"), None, None)
    return jax.shard_map(shards, mesh=mesh, in_specs=in_specs, out_specs=out_specs, check_vma=False)
```

```python
import functools

import jax
import jax.numpy as jnp
from jax import lax
from jax.experimental import pallas as pl
from jax.experimental.pallas import tpu as pltpu
from jax.sharding import PartitionSpec as P

ITERS = 2
CHUNK = 16
F32 = jnp.float32
BF16 = jnp.bfloat16
I32 = jnp.int32
HIGHEST = lax.Precision.HIGHEST
VMEM = pl.BlockSpec(memory_space=pltpu.VMEM)
ANY = pl.BlockSpec(memory_space=pl.ANY)
SMEM = pl.BlockSpec(memory_space=pltpu.SMEM)
HBM = pl.BlockSpec(memory_space=pltpu.HBM)


def hat(ray, centre):
    return jnp.maximum(0.0, 1.0 - jnp.abs(ray - centre)).astype(BF16)


def row_taps(offset, slope, extent):
    shape = (offset.shape[0], extent)
    ray = lax.broadcasted_iota(I32, shape, 1).astype(F32)
    inverse = jnp.broadcast_to(1.0 / slope, shape)
    offset = jnp.broadcast_to(offset, shape)
    slope = jnp.broadcast_to(slope, shape)
    middle = jnp.floor((ray - offset) * inverse + 0.5)
    middle = jnp.minimum(jnp.maximum(middle, 1.0), extent - 2.0)
    weights = [hat(ray, offset + slope * (middle + step)) for step in (-1.0, 0.0, 1.0)]
    return middle.astype(I32), weights


def column_taps(offset, slope, extent):
    shape = (offset.shape[0], extent)
    voxel = lax.broadcasted_iota(I32, shape, 1).astype(F32)
    centre = jnp.broadcast_to(offset, shape) + jnp.broadcast_to(slope, shape) * voxel
    first = jnp.minimum(jnp.maximum(jnp.floor(centre), 0.0), extent - 2.0)
    weights = [hat(first + step, centre) for step in (0.0, 1.0)]
    return first.astype(I32), weights


def repeat_rows(values, times):
    return jnp.concatenate(
        [jnp.broadcast_to(values[row:row + 1, :], (times, values.shape[1]))
         for row in range(values.shape[0])], axis=0)


def contract_lanes(left, right):
    return lax.dot_general(
        left.astype(BF16), right.astype(BF16), (((1,), (1,)), ((), ())), preferred_element_type=F32)


def per_slot(live_ref, slots, capacity):
    targets = live_ref.shape[1]
    slot = lax.broadcasted_iota(I32, (targets, slots), 1)
    owner = lax.broadcasted_iota(I32, (targets, slots), 0)
    expand = (lax.div(slot, capacity) == owner).astype(F32)
    return jnp.dot(live_ref[...].astype(F32), expand, precision=HIGHEST, preferred_element_type=F32)


def pack_kernel(capacity, *refs):
    sources, out_ref, loaded, arrived = refs[:6], refs[6], refs[7:13], refs[13]
    copies = [
        pltpu.make_async_copy(source, ref, arrived.at[place])
        for place, (source, ref) in enumerate(zip(sources, loaded))]
    for copy in copies:
        copy.start()
    for copy in copies:
        copy.wait()
    volume_ref, offset_ref, slope_ref, voxel_ref, ray_ref, live_ref = loaded
    rows, extent = volume_ref.shape
    out_ref[0:rows, :] = volume_ref[...].astype(BF16)
    slots = ray_ref.shape[1]
    fields = []
    for ref in (offset_ref, slope_ref):
        left = ref[...]
        for addend in range(3):
            part = left.astype(BF16).astype(F32)
            fields.append(part)
            left = left - part
    fields.append(voxel_ref[...].astype(F32))
    fields.append(ray_ref[...].astype(F32))
    fields.append(per_slot(live_ref, slots, capacity))
    used = sum(field.shape[0] for field in fields)
    fields.append(jnp.zeros((-used % 16, slots), F32))
    fields = jnp.concatenate(fields, axis=0)
    height = fields.shape[0]
    for part in range(slots // extent):
        at = pl.ds(rows + part * height, height)
        out_ref[at, :] = fields[:, part * extent:(part + 1) * extent].astype(BF16)


def setup_kernel(n_payloads, members, stride, span, sizes, tiles, wanted, *refs):
    payload_refs, refs = refs[:n_payloads], refs[-(2 * len(wanted) + 10):]
    where = [(ref, index) for ref in payload_refs for index in range(ref.shape[0] // stride)]
    list_refs, row_ref, tables = refs[:len(wanted)], refs[len(wanted)], refs[len(wanted) + 1:-len(wanted) - 2]
    drafts, arrived, summed = refs[-len(wanted) - 2:-2], refs[-2], refs[-1]
    copies = [
        pltpu.make_async_copy(draft, ref, arrived.at[place])
        for place, (draft, ref) in enumerate(zip(drafts, list_refs))]
    capacity, depth, frames = sizes
    width = span * capacity
    extent = row_ref.shape[1]
    ray_tiles = row_ref.shape[0] // span
    height = -(-(7 * depth + 2) // 16) * 16
    lanes = drafts[0].shape[1]
    me = lax.axis_index("slab").astype(I32)
    parity = lax.rem(me, span)
    first_slot = (me - parity) * capacity
    part = lax.div(first_slot, extent)
    shift = lax.rem(extent - lax.rem(first_slot, extent), extent)

    def collect(member, lined, payload_ref, within):
        at = within * stride + tiles * frames + part * height
        raw = payload_ref[pl.ds(pl.multiple_of(at, 16), height), :].astype(F32)
        offset = (raw[0:depth] + raw[depth:2 * depth]) + raw[2 * depth:3 * depth]
        slope = (raw[3 * depth:4 * depth] + raw[4 * depth:5 * depth]) + raw[5 * depth:6 * depth]
        fields = jnp.concatenate(
            [offset, slope, raw[6 * depth:7 * depth + 2],
             jnp.zeros((16 - 3 * depth - 2, extent), F32)], axis=0)
        fields = pltpu.roll(fields, shift, axis=1)
        lane = lax.broadcasted_iota(I32, fields.shape, 1)
        fields = jnp.where(lane < width, fields, 0.0)
        if lanes > extent:
            fields = jnp.concatenate(
                [fields, jnp.zeros((fields.shape[0], lanes - extent), F32)], axis=1)
        return lined + pltpu.roll(fields, member * width, axis=1)

    lined = jnp.zeros((16, lanes), F32)
    if members <= 16:
        for member in range(members):
            lined = collect(member, lined, *where[member])
    else:
        lined = lax.fori_loop(
            0, members, lambda member, lined: collect(member, lined, payload_refs[0], member), lined)

    slot = lax.broadcasted_iota(I32, (1, lanes), 1)
    within = lax.rem(slot, width)
    target = lax.bitwise_xor(lax.div(within, capacity), parity)
    ray = lined[3 * depth:3 * depth + 1]
    count = lined[3 * depth + 1:3 * depth + 2]
    alive = jnp.logical_and(lax.rem(within, capacity).astype(F32) < count, slot < members * width)

    table = jnp.concatenate(
        [slot.astype(F32), ray, target.astype(F32), lined[2 * depth:3 * depth],
         jnp.zeros((5 - depth, lanes), F32)], axis=0)
    order = lax.broadcasted_iota(I32, (lanes, lanes), 0)
    earlier = (lax.broadcasted_iota(I32, (lanes, lanes), 1) < order).astype(F32)
    for ref, kind, copy in zip(drafts, wanted, copies):
        taken = alive if kind is None else jnp.logical_and(alive, target == kind)
        taken = taken.astype(F32)
        position = contract_lanes(jnp.broadcast_to(taken, (8, lanes)), earlier)[0:1]
        position = jnp.where(taken > 0.0, position, -1.0).astype(I32)
        choose = jnp.broadcast_to(position, (lanes, lanes)) == order
        packed = (contract_lanes(table, choose.astype(F32)) + 0.5).astype(I32)
        total = jnp.sum(taken, axis=1, keepdims=True).astype(I32)
        line = jnp.where(slot < total, packed[0:1], lanes)
        base = packed[1:2] if kind is not None else packed[1:2] + packed[2:3] * ray_tiles
        member = lax.div(packed[0:1], width) * tiles
        rows = [line, base * frames]
        rows += [(packed[3 + level:4 + level] + member) * frames for level in range(depth)]
        rows += [jnp.zeros((5 - depth, lanes), I32), jnp.broadcast_to(total, (1, lanes))]
        ref[...] = jnp.concatenate(rows, axis=0)
        copy.start()

    columns = lined.T
    step = 32
    for row in range(0, lanes, step):
        total = None
        for level in range(depth):
            offset = columns[row:row + step, level:level + 1]
            slope = columns[row:row + step, depth + level:depth + level + 1]
            middle, weights = row_taps(offset, slope, extent)
            first, pair = column_taps(offset, slope, extent)
            wide = [weight.astype(F32) for weight in weights]
            values = [middle] + wide + [first] + [weight.astype(F32) for weight in pair]
            at = level * (lanes + 8) + row
            for ref, value in zip(tables, values):
                ref[at:at + step, :] = value
            parts = (wide[0] + wide[1]) + wide[2]
            total = parts if total is None else total + parts
        summed[row:row + step, :] = total
    for ref in tables:
        blank = jnp.ones if ref.dtype == I32 else jnp.zeros
        for level in range(depth):
            at = level * (lanes + 8) + lanes
            ref[at:at + 8, :] = blank((8, extent), ref.dtype)

    tile = lax.broadcasted_iota(I32, (span * ray_tiles, lanes), 0).astype(F32)
    place = ray + (target * ray_tiles).astype(F32)
    place = jnp.where(alive, place, -1.0)
    hot = (jnp.broadcast_to(place, tile.shape) == tile).astype(F32)
    row_ref[...] = jnp.dot(hot, summed[...], precision=HIGHEST, preferred_element_type=F32)
    for copy in copies:
        copy.wait()


def column_kernel(sizes, offset_ref, slope_ref, voxel_ref, live_ref, out_ref):
    capacity, depth, frames = sizes
    tiles = out_ref.shape[0] // frames
    slots = offset_ref.shape[1]
    extent = out_ref.shape[1]
    offsets = offset_ref[...].T
    slopes = slope_ref[...].T
    within = lax.rem(lax.broadcasted_iota(I32, (1, slots), 1), capacity).astype(F32)
    alive = jnp.broadcast_to(within, (tiles, slots)) < per_slot(live_ref, slots, capacity)
    total = jnp.zeros((tiles, extent), F32)
    for level in range(depth):
        unused, pair = column_taps(
            offsets[:, level:level + 1], slopes[:, level:level + 1], extent)
        tile_of = jnp.broadcast_to(voxel_ref[level:level + 1, :], (tiles, slots))
        match = tile_of == lax.broadcasted_iota(I32, (tiles, slots), 0)
        hot = jnp.logical_and(match, alive).astype(F32).astype(BF16)
        for weight in pair:
            total += jnp.dot(hot, weight, preferred_element_type=F32)
    out_ref[...] = repeat_rows(1.0 / jnp.maximum(total, 1.0), frames)


def pick(values, index):
    numbers = lax.GatherDimensionNumbers(
        offset_dims=(), collapsed_slice_dims=(1,), start_index_map=(1,),
        operand_batching_dims=(0,), start_indices_batching_dims=(0,))
    return lax.gather(
        values, index[:, :, None], numbers, slice_sizes=(1, 1),
        mode=lax.GatherScatterMode.PROMISE_IN_BOUNDS)


def pack_pair(first, second):
    kind = jnp.int16 if first.dtype == I32 else BF16
    return jnp.concatenate([first, second], axis=0).astype(kind)


def spread(ref, row, frames):
    return ref[pl.ds(row, frames, stride=0), :]


def tile_at(start, frames):
    return pl.ds(pl.multiple_of(start, frames), frames)


def for_slots(slots, body):
    def some(step, carry):
        for place in range(CHUNK):
            body(step * CHUNK + place, place)
        return carry

    lax.fori_loop(0, lax.div(slots[7, 0] + (CHUNK - 1), CHUNK), some, 0)


def for_rows(rows, body):
    step = 128

    def some(number, carry):
        body(pl.ds(pl.multiple_of(number * step, step), step))
        return carry

    lax.fori_loop(0, rows // step, some, 0)


def forward_kernel(sizes, n_values, members, start_row, n_sums, slots, *refs):
    capacity, depth, frames = sizes
    value_refs, tables, refs = refs[:n_values], refs[n_values:n_values + 4], refs[n_values + 4:]
    start_ref = None
    if start_row is not None:
        start_ref, refs = refs[0], refs[1:]
    sum_refs, (out_ref, wide, second) = refs[:n_sums], refs[n_sums:]
    rows = wide.shape[0] // members
    stride = sum(ref.shape[0] for ref in value_refs) // members
    rays = second.shape[0]
    line_step = tables[0].shape[0] // depth

    base = 0
    for ref in value_refs:
        def widen(member, carry, ref=ref, base=base):
            at = pl.ds(pl.multiple_of((base + member) * rows, rows), rows)
            wide[at, :] = ref[pl.ds(pl.multiple_of(member * stride, 16), rows), :].astype(F32)
            return carry

        lax.fori_loop(0, ref.shape[0] // stride, widen, 0)
        base += ref.shape[0] // stride
    second[...] = jnp.zeros_like(second)
    if start_ref is None:
        out_ref[...] = jnp.zeros_like(out_ref)
    else:
        out_ref[0:rays, :] = start_ref[start_row:start_row + rays, :]
    if n_sums:
        half = sum_refs[0].shape[0] // 2
        out_ref[rays:, :] = sum([ref[half:, :] for ref in sum_refs[1:]], sum_refs[0][half:, :])

    def one(slot, place):
        line = slots[0, slot]
        taps = []
        for start in range(0, depth, 2):
            levels = range(start, start + 2)
            values = [wide[tile_at(slots[2 + level, slot], frames), :] for level in levels]
            middles = [spread(tables[0], line + level * line_step, frames) for level in levels]
            lower = [
                pick(pack_pair(value, value), pack_pair(middle - 1, middle)).astype(F32)
                for value, middle in zip(values, middles)]
            upper = pick(
                pack_pair(*values), pack_pair(*[middle + 1 for middle in middles])).astype(F32)
            for which, pair in enumerate(lower):
                taps.append((pair[0:frames], pair[frames:2 * frames],
                             upper[which * frames:(which + 1) * frames]))
        total = None
        for level, three in enumerate(taps):
            for ref, tap in zip(tables[1:], three):
                term = spread(ref, line + level * line_step, frames) * tap
                total = term if total is None else total + term
        projection = (out_ref, second)[place % 2]
        projection[tile_at(slots[1, slot], frames), :] += total.astype(BF16).astype(F32)

    for_slots(slots, one)
    out_ref[0:rays, :] += second[...]


def residual_kernel(frames, n_own, projection_ref, sinogram_ref, *refs):
    own, refs, out_ref = refs[:n_own], refs[n_own:-1], refs[-1]
    rays = out_ref.shape[0]
    ray_tiles = rays // frames
    total = sum([ref[0:ray_tiles, :] for ref in own[1:]], own[0][0:ray_tiles, :])
    projection = projection_ref[...]
    if refs:
        projection = projection + refs[0][0:rays, :]
        total = total + refs[-1][rays:, :]
    weight = repeat_rows(1.0 / jnp.maximum(total, 1.0), frames)
    out_ref[...] = ((sinogram_ref[...].astype(F32) - projection) * weight).astype(BF16)


def backward_kernel(sizes, n_parts, has_start, split, slots, *refs):
    capacity, depth, frames = sizes
    part_refs, tables, refs = refs[:n_parts], refs[n_parts:n_parts + 3], refs[n_parts + 3:]
    start_ref = None
    if has_start:
        start_ref, refs = refs[0], refs[1:]
    outs = refs[:len(split)] if split else refs[:1]
    residual, banks = refs[len(outs)], refs[len(outs) + 1:]
    rays = part_refs[0].shape[0]
    line_step = tables[0].shape[0] // depth
    for place, ref in enumerate(part_refs):
        residual[place * rays:(place + 1) * rays, :] = ref[...].astype(F32)

    def clear(at):
        for place, bank in enumerate(banks):
            if place == 0 and has_start:
                bank[at, :] = start_ref[at, :]
            else:
                bank[at, :] = jnp.zeros((at.size, bank.shape[1]), F32)

    for_rows(banks[0].shape[0], clear)

    def one(slot, place):
        line = slots[0, slot]
        values = residual[tile_at(slots[1, slot], frames), :]
        twice = pack_pair(values, values)
        for level in range(depth):
            row = line + level * line_step
            first = spread(tables[0], row, frames)
            taps = pick(twice, pack_pair(first, first + 1)).astype(F32)
            term = (spread(tables[1], row, frames) * taps[0:frames]
                    + spread(tables[2], row, frames) * taps[frames:2 * frames])
            banks[level % len(banks)][tile_at(slots[2 + level, slot], frames), :] += term

    for_slots(slots, one)

    def total(at):
        return sum([bank[at, :] for bank in banks[1:]], banks[0][at, :])

    if split:
        for ref, members in zip(outs, split):
            rows = ref.shape[0] // len(members)
            for place, member in enumerate(members):
                ref[place * rows:(place + 1) * rows, :] = total(pl.ds(member * rows, rows)).astype(ref.dtype)
    else:
        def finish(at):
            outs[0][at, :] = total(at).astype(outs[0].dtype)

        for_rows(outs[0].shape[0], finish)


def join_kernel(*refs):
    out_ref, at = refs[-1], 0
    for ref in refs[:-1]:
        out_ref[at:at + ref.shape[0], :] = ref[...]
        at += ref.shape[0]


def combine_kernel(members, sum_ref, y_ref, *piece_refs):
    rows = piece_refs[0].shape[0]
    for place, (member, ref) in enumerate(zip(members, piece_refs)):
        mine = sum_ref[member * rows:(member + 1) * rows, :]
        ref[...] = (mine + y_ref[place * rows:(place + 1) * rows, :].astype(F32)).astype(ref.dtype)


def update_kernel(n_pieces, volume_ref, column_ref, *refs):
    back = refs[0][...]
    for ref in refs[1:n_pieces]:
        back = back + ref[...].astype(F32)
    volume = volume_ref[...] + column_ref[...] * back
    for ref in refs[n_pieces:]:
        ref[...] = volume.astype(ref.dtype)


def call(kernel, name, mib, in_specs, out_shape, *operands, scratch=()):
    one = not isinstance(out_shape, list)
    return pl.pallas_call(
        kernel,
        out_shape=out_shape,
        in_specs=in_specs,
        out_specs=VMEM if one else [
            SMEM if getattr(out, "memory_space", None) == pltpu.SMEM else VMEM for out in out_shape],
        scratch_shapes=list(scratch),
        compiler_params=pltpu.CompilerParams(vmem_limit_bytes=mib * 1024 * 1024),
        name=name,
        cost_estimate=pl.CostEstimate(flops=4 * 10**9, bytes_accessed=8 * 10**6, transcendentals=0),
    )(*operands)


def exchange(values, n_slab, distance):
    return lax.ppermute(
        values, "slab", [(device, device ^ distance) for device in range(n_slab)])


def shards(sinogram, start_volume, slot_voxel, slot_ray, live_count, block_slope, block_offset):
    n_slab = lax.axis_size("slab")
    n_slots, depth = slot_voxel.shape
    capacity = n_slots // n_slab
    ray_tiles, frames, extent = sinogram.shape
    voxel_tiles = start_volume.shape[0]
    rows = voxel_tiles * frames
    sizes = (capacity, depth, frames)
    paired = n_slab == 16
    span = 2 if paired else 1
    n_bank = 2 if paired else 1
    shape = jax.ShapeDtypeStruct
    n_rays = ray_tiles * frames
    volume = start_volume.reshape(rows, extent)
    sino = sinogram.reshape(n_rays, extent)
    slots_by_depth = (block_offset.T, block_slope.T, slot_voxel.T)
    live = live_count.reshape(1, n_slab)
    height = -(-(7 * depth + 2) // 16) * 16 * (n_slots // extent)
    operands = (volume, *slots_by_depth, slot_ray.reshape(1, n_slots), live)
    payload = call(
        functools.partial(pack_kernel, capacity), "pack", 16, [HBM] * 6,
        shape((rows + height, extent), BF16),
        *[pltpu.with_memory_space_constraint(operand, pltpu.HBM) for operand in operands],
        scratch=[pltpu.VMEM(operand.shape, operand.dtype) for operand in operands]
        + [pltpu.SemaphoreType.DMA((6,))])

    def setup(payloads, members, wanted, after=None):
        lanes = -(-members * span * capacity // 128) * 128
        lines = depth * (lanes + 8)
        table = [shape((lines, extent), I32)] + [shape((lines, extent), F32)] * 3
        table += [shape((lines, extent), I32)] + [shape((lines, extent), F32)] * 2
        n = len(wanted)
        out = [pltpu.SMEM((8, lanes), I32)] * n + [shape((span * ray_tiles, extent), F32)] + table
        waits = [] if after is None else [after]
        found = call(
            functools.partial(setup_kernel, len(payloads), members,
                              sum(one.shape[0] for one in payloads) // members, span, sizes,
                              voxel_tiles, wanted),
            "setup", 24, [VMEM] * len(payloads) + [ANY] * len(waits), out, *payloads, *waits,
            scratch=[pltpu.VMEM((8, lanes), I32)] * n
            + [pltpu.SemaphoreType.DMA((n,)), pltpu.VMEM((lanes, extent), F32)])
        return found[:n], found[n], found[n + 1:n + 5], found[n + 5:]

    def forward(slots, values, members, table, n_out, start=None, start_row=None, sums=()):
        operands = [pltpu.with_memory_space_constraint(slots, pltpu.SMEM), *values, *table] + ([] if start is None else [start]) + list(sums)
        extra = ray_tiles if sums else 0
        return call(
            functools.partial(forward_kernel, sizes, len(values), members, start_row, len(sums)),
            "forward", 16 if paired else 32, [SMEM] + [VMEM] * (len(operands) - 1),
            shape((n_out + extra, extent), F32), *operands,
            scratch=[pltpu.VMEM((members * rows, extent), F32), pltpu.VMEM((n_out, extent), F32)])

    def residual_of(projection, row_sums, *sibling):
        operands = [projection, sino, *row_sums, *sibling]
        return call(
            functools.partial(residual_kernel, frames, len(row_sums)), "residual", 16,
            [VMEM] * len(operands), shape((n_rays, extent), BF16), *operands)

    def backward(slots, parts, members, table, kind, start=None, split=()):
        operands = [pltpu.with_memory_space_constraint(slots, pltpu.SMEM), *parts, *table] + ([] if start is None else [start])
        return call(
            functools.partial(backward_kernel, sizes, len(parts), start is not None, split),
            "backward", 16 if paired else 32, [SMEM] + [VMEM] * (len(operands) - 1),
            [shape((len(some) * rows, extent), each) for some, each in zip(split, kind)]
            if split else shape((members * rows, extent), kind), *operands,
            scratch=[pltpu.VMEM((len(parts) * n_rays, extent), F32)]
            + [pltpu.VMEM((members * rows, extent), F32)] * n_bank)

    def join(*parts):
        total = sum(part.shape[0] for part in parts)
        return call(join_kernel, "join", 16, [VMEM] * len(parts), shape((total, extent), BF16), *parts)

    def update(volume, pieces, last):
        out = [shape((rows, extent), F32)] + ([] if last else [shape((rows, extent), BF16)])
        return call(
            functools.partial(update_kernel, len(pieces)), "update", 16,
            [VMEM] * (2 + len(pieces)), out, volume, column_weight, *pieces)

    column_weight = call(
        functools.partial(column_kernel, sizes), "column_weight", 16, [VMEM] * 4,
        shape((rows, extent), F32), *slots_by_depth, live)

    for sweep in range(ITERS):
        last = sweep + 1 == ITERS
        if paired:
            over_2, over_1, over_3, across = [
                exchange(payload, n_slab, distance) for distance in (9, 5, 12, 15)]
            z_part = join(payload, over_2, over_1)
            y_part = exchange(z_part, n_slab, 3)
            along_z, along_y = (z_part, over_3), (y_part, across)
            if sweep == 0:
                (z_list,), z_rows, z_forward, z_backward = setup(along_z, 4, (None,))
            both = forward(z_list, along_z, 4, z_forward, 2 * n_rays)
            if sweep == 0:
                (own_list, other_list), y_rows, y_forward, y_backward = setup(
                    along_y, 4, (0, 1), after=both)
            other = exchange(
                forward(other_list, along_y, 4, y_forward, n_rays, both, n_rays,
                        (z_rows, y_rows) if sweep == 0 else ()), n_slab, 1)
            if sweep == 0:
                first_other = other
            own = forward(own_list, along_y, 4, y_forward, n_rays, both, 0)
            residual = residual_of(own, (z_rows, y_rows), other, first_other)
            other_residual = exchange(residual, n_slab, 1)
            y_sum = backward(own_list, [residual], 4, y_backward, F32)
            far_sum, near_sum = backward(
                other_list, [other_residual], 4, y_backward, (BF16, BF16), y_sum, ((1, 3), (0, 2)))
            far_part, near_part = exchange(far_sum, n_slab, 3), exchange(near_sum, n_slab, 3)
            z_sum = backward(z_list, [residual, other_residual], 4, z_backward, F32)
            piece = shape((rows, extent), BF16)
            piece_2, piece_3 = call(
                functools.partial(combine_kernel, (1, 3)), "combine", 16, [VMEM] * 2,
                [piece, piece], z_sum, far_part)
            got = [exchange(piece_2, n_slab, 9), exchange(piece_3, n_slab, 12)]
            own_piece, piece_1 = call(
                functools.partial(combine_kernel, (0, 2)), "combine", 16, [VMEM] * 2,
                [shape((rows, extent), F32), piece], z_sum, near_part)
            pieces = [own_piece, *got, exchange(piece_1, n_slab, 5)]
        else:
            everyone = lax.all_gather(payload, "slab", axis=0, tiled=True)
            if sweep == 0:
                (slots,), row_sums, to_rays, to_voxels = setup((everyone,), n_slab, (None,))
            projection = forward(slots, (everyone,), n_slab, to_rays, n_rays)
            residual = residual_of(projection, (row_sums,))
            sums = backward(slots, [residual], n_slab, to_voxels, BF16)
            parts = lax.all_to_all(
                sums.reshape(n_slab, rows, extent), "slab", split_axis=0, concat_axis=0, tiled=True)
            pieces = [jnp.sum(parts.astype(F32), axis=0)]
        volume, *rounded = update(volume, pieces, last)
        if not last:
            payload = rounded[0]
    return volume.reshape(start_volume.shape)


def solution(mesh):
    in_specs = (
        P(("scan", "slab"), None, None),
        P(("scan", "slab"), None, None),
        P(("scan", "slab"), None),
        P(("scan", "slab")),
        P(("scan", "slab")),
        P(("scan", "slab"), None),
        P(("scan", "slab"), None),
    )
    out_specs = P(("scan", "slab"), None, None)
    return jax.shard_map(shards, mesh=mesh, in_specs=in_specs, out_specs=out_specs, check_vma=False)
```

```python
import functools

import jax
import jax.numpy as jnp
from jax import lax
from jax.experimental import pallas as pl
from jax.experimental.pallas import tpu as pltpu
from jax.sharding import PartitionSpec as P

ITERS = 2
CHUNK = 16
F32 = jnp.float32
BF16 = jnp.bfloat16
I32 = jnp.int32
HIGHEST = lax.Precision.HIGHEST
VMEM = pl.BlockSpec(memory_space=pltpu.VMEM)
ANY = pl.BlockSpec(memory_space=pl.ANY)
SMEM = pl.BlockSpec(memory_space=pltpu.SMEM)
HBM = pl.BlockSpec(memory_space=pltpu.HBM)


def hat(ray, centre):
    return jnp.maximum(0.0, 1.0 - jnp.abs(ray - centre)).astype(BF16)


def row_taps(offset, slope, extent):
    shape = (offset.shape[0], extent)
    ray = lax.broadcasted_iota(I32, shape, 1).astype(F32)
    inverse = jnp.broadcast_to(1.0 / slope, shape)
    offset = jnp.broadcast_to(offset, shape)
    slope = jnp.broadcast_to(slope, shape)
    middle = jnp.floor((ray - offset) * inverse + 0.5)
    middle = jnp.minimum(jnp.maximum(middle, 1.0), extent - 2.0)
    weights = [hat(ray, offset + slope * (middle + step)) for step in (-1.0, 0.0, 1.0)]
    return middle.astype(I32), weights


def column_taps(offset, slope, extent):
    shape = (offset.shape[0], extent)
    voxel = lax.broadcasted_iota(I32, shape, 1).astype(F32)
    centre = jnp.broadcast_to(offset, shape) + jnp.broadcast_to(slope, shape) * voxel
    first = jnp.minimum(jnp.maximum(jnp.floor(centre), 0.0), extent - 2.0)
    weights = [hat(first + step, centre) for step in (0.0, 1.0)]
    return first.astype(I32), weights


def repeat_rows(values, times):
    return jnp.concatenate(
        [jnp.broadcast_to(values[row:row + 1, :], (times, values.shape[1]))
         for row in range(values.shape[0])], axis=0)


def contract_lanes(left, right):
    return lax.dot_general(
        left.astype(BF16), right.astype(BF16), (((1,), (1,)), ((), ())), preferred_element_type=F32)


def per_slot(live_ref, slots, capacity):
    targets = live_ref.shape[1]
    slot = lax.broadcasted_iota(I32, (targets, slots), 1)
    owner = lax.broadcasted_iota(I32, (targets, slots), 0)
    expand = (lax.div(slot, capacity) == owner).astype(F32)
    return jnp.dot(live_ref[...].astype(F32), expand, precision=HIGHEST, preferred_element_type=F32)


def pack_kernel(capacity, *refs):
    sources, out_ref, loaded, arrived = refs[:6], refs[6], refs[7:13], refs[13]
    copies = [
        pltpu.make_async_copy(source, ref, arrived.at[place])
        for place, (source, ref) in enumerate(zip(sources, loaded))]
    for copy in copies:
        copy.start()
    for copy in copies:
        copy.wait()
    volume_ref, offset_ref, slope_ref, voxel_ref, ray_ref, live_ref = loaded
    rows, extent = volume_ref.shape
    out_ref[0:rows, :] = volume_ref[...].astype(BF16)
    slots = ray_ref.shape[1]
    fields = []
    for ref in (offset_ref, slope_ref):
        left = ref[...]
        for addend in range(3):
            part = left.astype(BF16).astype(F32)
            fields.append(part)
            left = left - part
    fields.append(voxel_ref[...].astype(F32))
    fields.append(ray_ref[...].astype(F32))
    fields.append(per_slot(live_ref, slots, capacity))
    used = sum(field.shape[0] for field in fields)
    fields.append(jnp.zeros((-used % 16, slots), F32))
    fields = jnp.concatenate(fields, axis=0)
    height = fields.shape[0]
    for part in range(slots // extent):
        at = pl.ds(rows + part * height, height)
        out_ref[at, :] = fields[:, part * extent:(part + 1) * extent].astype(BF16)


def setup_kernel(n_payloads, members, stride, span, sizes, tiles, wanted, *refs):
    payload_refs, refs = refs[:n_payloads], refs[-(2 * len(wanted) + 10):]
    where = [(ref, index) for ref in payload_refs for index in range(ref.shape[0] // stride)]
    list_refs, row_ref, tables = refs[:len(wanted)], refs[len(wanted)], refs[len(wanted) + 1:-len(wanted) - 2]
    drafts, arrived, summed = refs[-len(wanted) - 2:-2], refs[-2], refs[-1]
    copies = [
        pltpu.make_async_copy(draft, ref, arrived.at[place])
        for place, (draft, ref) in enumerate(zip(drafts, list_refs))]
    capacity, depth, frames = sizes
    width = span * capacity
    extent = row_ref.shape[1]
    ray_tiles = row_ref.shape[0] // span
    height = -(-(7 * depth + 2) // 16) * 16
    lanes = drafts[0].shape[1]
    me = lax.axis_index("slab").astype(I32)
    parity = lax.rem(me, span)
    first_slot = (me - parity) * capacity
    part = lax.div(first_slot, extent)
    shift = lax.rem(extent - lax.rem(first_slot, extent), extent)

    def collect(member, lined, payload_ref, within):
        at = within * stride + tiles * frames + part * height
        raw = payload_ref[pl.ds(pl.multiple_of(at, 16), height), :].astype(F32)
        offset = (raw[0:depth] + raw[depth:2 * depth]) + raw[2 * depth:3 * depth]
        slope = (raw[3 * depth:4 * depth] + raw[4 * depth:5 * depth]) + raw[5 * depth:6 * depth]
        fields = jnp.concatenate(
            [offset, slope, raw[6 * depth:7 * depth + 2],
             jnp.zeros((16 - 3 * depth - 2, extent), F32)], axis=0)
        fields = pltpu.roll(fields, shift, axis=1)
        lane = lax.broadcasted_iota(I32, fields.shape, 1)
        fields = jnp.where(lane < width, fields, 0.0)
        if lanes > extent:
            fields = jnp.concatenate(
                [fields, jnp.zeros((fields.shape[0], lanes - extent), F32)], axis=1)
        return lined + pltpu.roll(fields, member * width, axis=1)

    lined = jnp.zeros((16, lanes), F32)
    if members <= 16:
        for member in range(members):
            lined = collect(member, lined, *where[member])
    else:
        lined = lax.fori_loop(
            0, members, lambda member, lined: collect(member, lined, payload_refs[0], member), lined)

    slot = lax.broadcasted_iota(I32, (1, lanes), 1)
    within = lax.rem(slot, width)
    target = lax.bitwise_xor(lax.div(within, capacity), parity)
    ray = lined[3 * depth:3 * depth + 1]
    count = lined[3 * depth + 1:3 * depth + 2]
    alive = jnp.logical_and(lax.rem(within, capacity).astype(F32) < count, slot < members * width)

    table = jnp.concatenate(
        [slot.astype(F32), ray, target.astype(F32), lined[2 * depth:3 * depth],
         jnp.zeros((5 - depth, lanes), F32)], axis=0)
    order = lax.broadcasted_iota(I32, (lanes, lanes), 0)
    earlier = (lax.broadcasted_iota(I32, (lanes, lanes), 1) < order).astype(F32)
    for ref, kind, copy in zip(drafts, wanted, copies):
        taken = alive if kind is None else jnp.logical_and(alive, target == kind)
        taken = taken.astype(F32)
        position = contract_lanes(jnp.broadcast_to(taken, (8, lanes)), earlier)[0:1]
        position = jnp.where(taken > 0.0, position, -1.0).astype(I32)
        choose = jnp.broadcast_to(position, (lanes, lanes)) == order
        packed = (contract_lanes(table, choose.astype(F32)) + 0.5).astype(I32)
        total = jnp.sum(taken, axis=1, keepdims=True).astype(I32)
        line = jnp.where(slot < total, packed[0:1], lanes)
        base = packed[1:2] if kind is not None else packed[1:2] + packed[2:3] * ray_tiles
        member = lax.div(packed[0:1], width) * tiles
        rows = [line, base * frames]
        rows += [(packed[3 + level:4 + level] + member) * frames for level in range(depth)]
        rows += [jnp.zeros((5 - depth, lanes), I32), jnp.broadcast_to(total, (1, lanes))]
        ref[...] = jnp.concatenate(rows, axis=0)
        copy.start()

    columns = lined.T
    step = 32
    for row in range(0, lanes, step):
        total = None
        for level in range(depth):
            offset = columns[row:row + step, level:level + 1]
            slope = columns[row:row + step, depth + level:depth + level + 1]
            middle, weights = row_taps(offset, slope, extent)
            first, pair = column_taps(offset, slope, extent)
            wide = [weight.astype(F32) for weight in weights]
            values = [middle] + wide + [first] + [weight.astype(F32) for weight in pair]
            at = level * (lanes + 8) + row
            for ref, value in zip(tables, values):
                ref[at:at + step, :] = value
            parts = (wide[0] + wide[1]) + wide[2]
            total = parts if total is None else total + parts
        summed[row:row + step, :] = total
    for ref in tables:
        blank = jnp.ones if ref.dtype == I32 else jnp.zeros
        for level in range(depth):
            at = level * (lanes + 8) + lanes
            ref[at:at + 8, :] = blank((8, extent), ref.dtype)

    tile = lax.broadcasted_iota(I32, (span * ray_tiles, lanes), 0).astype(F32)
    place = ray + (target * ray_tiles).astype(F32)
    place = jnp.where(alive, place, -1.0)
    hot = (jnp.broadcast_to(place, tile.shape) == tile).astype(F32)
    row_ref[...] = jnp.dot(hot, summed[...], precision=HIGHEST, preferred_element_type=F32)
    for copy in copies:
        copy.wait()


def column_kernel(sizes, offset_ref, slope_ref, voxel_ref, live_ref, out_ref):
    capacity, depth, frames = sizes
    tiles = out_ref.shape[0] // frames
    slots = offset_ref.shape[1]
    extent = out_ref.shape[1]
    offsets = offset_ref[...].T
    slopes = slope_ref[...].T
    within = lax.rem(lax.broadcasted_iota(I32, (1, slots), 1), capacity).astype(F32)
    alive = jnp.broadcast_to(within, (tiles, slots)) < per_slot(live_ref, slots, capacity)
    total = jnp.zeros((tiles, extent), F32)
    for level in range(depth):
        unused, pair = column_taps(
            offsets[:, level:level + 1], slopes[:, level:level + 1], extent)
        tile_of = jnp.broadcast_to(voxel_ref[level:level + 1, :], (tiles, slots))
        match = tile_of == lax.broadcasted_iota(I32, (tiles, slots), 0)
        hot = jnp.logical_and(match, alive).astype(F32).astype(BF16)
        for weight in pair:
            total += jnp.dot(hot, weight, preferred_element_type=F32)
    out_ref[...] = repeat_rows(1.0 / jnp.maximum(total, 1.0), frames)


def pick(values, index):
    numbers = lax.GatherDimensionNumbers(
        offset_dims=(), collapsed_slice_dims=(1,), start_index_map=(1,),
        operand_batching_dims=(0,), start_indices_batching_dims=(0,))
    return lax.gather(
        values, index[:, :, None], numbers, slice_sizes=(1, 1),
        mode=lax.GatherScatterMode.PROMISE_IN_BOUNDS)


def pack_pair(first, second):
    kind = jnp.int16 if first.dtype == I32 else BF16
    return jnp.concatenate([first, second], axis=0).astype(kind)


def spread(ref, row, frames):
    return ref[pl.ds(row, frames, stride=0), :]


def tile_at(start, frames):
    return pl.ds(pl.multiple_of(start, frames), frames)


def for_slots(slots, body):
    def some(step, carry):
        for place in range(CHUNK):
            body(step * CHUNK + place, place)
        return carry

    lax.fori_loop(0, lax.div(slots[7, 0] + (CHUNK - 1), CHUNK), some, 0)


def for_rows(rows, body):
    step = 128

    def some(number, carry):
        body(pl.ds(pl.multiple_of(number * step, step), step))
        return carry

    lax.fori_loop(0, rows // step, some, 0)


def forward_kernel(sizes, n_values, members, start_row, n_sums, slots, *refs):
    capacity, depth, frames = sizes
    value_refs, tables, refs = refs[:n_values], refs[n_values:n_values + 4], refs[n_values + 4:]
    start_ref = None
    if start_row is not None:
        start_ref, refs = refs[0], refs[1:]
    sum_refs, (out_ref, wide, second) = refs[:n_sums], refs[n_sums:]
    rows = wide.shape[0] // members
    stride = sum(ref.shape[0] for ref in value_refs) // members
    rays = second.shape[0]
    line_step = tables[0].shape[0] // depth

    base = 0
    for ref in value_refs:
        def widen(member, carry, ref=ref, base=base):
            at = pl.ds(pl.multiple_of((base + member) * rows, rows), rows)
            wide[at, :] = ref[pl.ds(pl.multiple_of(member * stride, 16), rows), :].astype(F32)
            return carry

        lax.fori_loop(0, ref.shape[0] // stride, widen, 0)
        base += ref.shape[0] // stride
    second[...] = jnp.zeros_like(second)
    if start_ref is None:
        out_ref[...] = jnp.zeros_like(out_ref)
    else:
        out_ref[0:rays, :] = start_ref[start_row:start_row + rays, :]
    if n_sums:
        half = sum_refs[0].shape[0] // 2
        out_ref[rays:, :] = sum([ref[half:, :] for ref in sum_refs[1:]], sum_refs[0][half:, :])

    def one(slot, place):
        line = slots[0, slot]
        taps = []
        for start in range(0, depth, 2):
            levels = range(start, start + 2)
            values = [wide[tile_at(slots[2 + level, slot], frames), :] for level in levels]
            middles = [spread(tables[0], line + level * line_step, frames) for level in levels]
            lower = [
                pick(pack_pair(value, value), pack_pair(middle - 1, middle)).astype(F32)
                for value, middle in zip(values, middles)]
            upper = pick(
                pack_pair(*values), pack_pair(*[middle + 1 for middle in middles])).astype(F32)
            for which, pair in enumerate(lower):
                taps.append((pair[0:frames], pair[frames:2 * frames],
                             upper[which * frames:(which + 1) * frames]))
        total = None
        for level, three in enumerate(taps):
            for ref, tap in zip(tables[1:], three):
                term = spread(ref, line + level * line_step, frames) * tap
                total = term if total is None else total + term
        projection = (out_ref, second)[place % 2]
        projection[tile_at(slots[1, slot], frames), :] += total.astype(BF16).astype(F32)

    for_slots(slots, one)
    out_ref[0:rays, :] += second[...]


def residual_kernel(frames, n_own, projection_ref, sinogram_ref, *refs):
    own, refs, out_ref = refs[:n_own], refs[n_own:-1], refs[-1]
    rays = out_ref.shape[0]
    ray_tiles = rays // frames
    total = sum([ref[0:ray_tiles, :] for ref in own[1:]], own[0][0:ray_tiles, :])
    projection = projection_ref[...]
    if refs:
        projection = projection + refs[0][0:rays, :]
        total = total + refs[-1][rays:, :]
    weight = repeat_rows(1.0 / jnp.maximum(total, 1.0), frames)
    out_ref[...] = ((sinogram_ref[...].astype(F32) - projection) * weight).astype(BF16)


def backward_kernel(sizes, n_parts, has_start, split, slots, *refs):
    capacity, depth, frames = sizes
    part_refs, tables, refs = refs[:n_parts], refs[n_parts:n_parts + 3], refs[n_parts + 3:]
    start_ref = None
    if has_start:
        start_ref, refs = refs[0], refs[1:]
    outs = refs[:len(split)] if split else refs[:1]
    residual, banks = refs[len(outs)], refs[len(outs) + 1:]
    rays = part_refs[0].shape[0]
    line_step = tables[0].shape[0] // depth
    for place, ref in enumerate(part_refs):
        residual[place * rays:(place + 1) * rays, :] = ref[...].astype(F32)

    def clear(at):
        for place, bank in enumerate(banks):
            if place == 0 and has_start:
                bank[at, :] = start_ref[at, :]
            else:
                bank[at, :] = jnp.zeros((at.size, bank.shape[1]), F32)

    for_rows(banks[0].shape[0], clear)

    def one(slot, place):
        line = slots[0, slot]
        values = residual[tile_at(slots[1, slot], frames), :]
        twice = pack_pair(values, values)
        for level in range(depth):
            row = line + level * line_step
            first = spread(tables[0], row, frames)
            taps = pick(twice, pack_pair(first, first + 1)).astype(F32)
            term = (spread(tables[1], row, frames) * taps[0:frames]
                    + spread(tables[2], row, frames) * taps[frames:2 * frames])
            banks[level % len(banks)][tile_at(slots[2 + level, slot], frames), :] += term

    for_slots(slots, one)

    def total(at):
        return sum([bank[at, :] for bank in banks[1:]], banks[0][at, :])

    if split:
        for ref, members in zip(outs, split):
            rows = ref.shape[0] // len(members)
            for place, member in enumerate(members):
                ref[place * rows:(place + 1) * rows, :] = total(pl.ds(member * rows, rows)).astype(ref.dtype)
    else:
        def finish(at):
            outs[0][at, :] = total(at).astype(outs[0].dtype)

        for_rows(outs[0].shape[0], finish)


def join_kernel(*refs):
    out_ref, at = refs[-1], 0
    for ref in refs[:-1]:
        out_ref[at:at + ref.shape[0], :] = ref[...]
        at += ref.shape[0]


def combine_kernel(members, sum_ref, y_ref, *piece_refs):
    rows = piece_refs[0].shape[0]
    for place, (member, ref) in enumerate(zip(members, piece_refs)):
        mine = sum_ref[member * rows:(member + 1) * rows, :]
        ref[...] = (mine + y_ref[place * rows:(place + 1) * rows, :].astype(F32)).astype(ref.dtype)


def update_kernel(n_pieces, volume_ref, column_ref, *refs):
    back = refs[0][...]
    for ref in refs[1:n_pieces]:
        back = back + ref[...].astype(F32)
    volume = volume_ref[...] + column_ref[...] * back
    for ref in refs[n_pieces:]:
        ref[...] = volume.astype(ref.dtype)


def call(kernel, name, mib, in_specs, out_shape, *operands, scratch=()):
    one = not isinstance(out_shape, list)
    return pl.pallas_call(
        kernel,
        out_shape=out_shape,
        in_specs=in_specs,
        out_specs=VMEM if one else [
            SMEM if getattr(out, "memory_space", None) == pltpu.SMEM else VMEM for out in out_shape],
        scratch_shapes=list(scratch),
        compiler_params=pltpu.CompilerParams(vmem_limit_bytes=mib * 1024 * 1024),
        name=name,
        cost_estimate=pl.CostEstimate(flops=4 * 10**9, bytes_accessed=8 * 10**6, transcendentals=0),
    )(*operands)


def exchange(values, n_slab, distance, other_distance=None):
    far = (distance, distance if other_distance is None else other_distance)
    return lax.ppermute(
        values, "slab",
        [(device, device ^ far[device.bit_count() % 2]) for device in range(n_slab)])


def shards(sinogram, start_volume, slot_voxel, slot_ray, live_count, block_slope, block_offset):
    n_slab = lax.axis_size("slab")
    n_slots, depth = slot_voxel.shape
    capacity = n_slots // n_slab
    ray_tiles, frames, extent = sinogram.shape
    voxel_tiles = start_volume.shape[0]
    rows = voxel_tiles * frames
    sizes = (capacity, depth, frames)
    paired = n_slab == 16
    span = 2 if paired else 1
    n_bank = 2 if paired else 1
    shape = jax.ShapeDtypeStruct
    n_rays = ray_tiles * frames
    volume = start_volume.reshape(rows, extent)
    sino = sinogram.reshape(n_rays, extent)
    slots_by_depth = (block_offset.T, block_slope.T, slot_voxel.T)
    live = live_count.reshape(1, n_slab)
    height = -(-(7 * depth + 2) // 16) * 16 * (n_slots // extent)
    operands = (volume, *slots_by_depth, slot_ray.reshape(1, n_slots), live)
    payload = call(
        functools.partial(pack_kernel, capacity), "pack", 16, [HBM] * 6,
        shape((rows + height, extent), BF16),
        *[pltpu.with_memory_space_constraint(operand, pltpu.HBM) for operand in operands],
        scratch=[pltpu.VMEM(operand.shape, operand.dtype) for operand in operands]
        + [pltpu.SemaphoreType.DMA((6,))])

    def setup(payloads, members, wanted, after=None):
        lanes = -(-members * span * capacity // 128) * 128
        lines = depth * (lanes + 8)
        table = [shape((lines, extent), I32)] + [shape((lines, extent), F32)] * 3
        table += [shape((lines, extent), I32)] + [shape((lines, extent), F32)] * 2
        n = len(wanted)
        out = [pltpu.SMEM((8, lanes), I32)] * n + [shape((span * ray_tiles, extent), F32)] + table
        waits = [] if after is None else [after]
        found = call(
            functools.partial(setup_kernel, len(payloads), members,
                              sum(one.shape[0] for one in payloads) // members, span, sizes,
                              voxel_tiles, wanted),
            "setup", 24, [VMEM] * len(payloads) + [ANY] * len(waits), out, *payloads, *waits,
            scratch=[pltpu.VMEM((8, lanes), I32)] * n
            + [pltpu.SemaphoreType.DMA((n,)), pltpu.VMEM((lanes, extent), F32)])
        return found[:n], found[n], found[n + 1:n + 5], found[n + 5:]

    def forward(slots, values, members, table, n_out, start=None, start_row=None, sums=()):
        operands = [pltpu.with_memory_space_constraint(slots, pltpu.SMEM), *values, *table] + ([] if start is None else [start]) + list(sums)
        extra = ray_tiles if sums else 0
        return call(
            functools.partial(forward_kernel, sizes, len(values), members, start_row, len(sums)),
            "forward", 16 if paired else 32, [SMEM] + [VMEM] * (len(operands) - 1),
            shape((n_out + extra, extent), F32), *operands,
            scratch=[pltpu.VMEM((members * rows, extent), F32), pltpu.VMEM((n_out, extent), F32)])

    def residual_of(projection, row_sums, *sibling):
        operands = [projection, sino, *row_sums, *sibling]
        return call(
            functools.partial(residual_kernel, frames, len(row_sums)), "residual", 16,
            [VMEM] * len(operands), shape((n_rays, extent), BF16), *operands)

    def backward(slots, parts, members, table, kind, start=None, split=()):
        operands = [pltpu.with_memory_space_constraint(slots, pltpu.SMEM), *parts, *table] + ([] if start is None else [start])
        return call(
            functools.partial(backward_kernel, sizes, len(parts), start is not None, split),
            "backward", 16 if paired else 32, [SMEM] + [VMEM] * (len(operands) - 1),
            [shape((len(some) * rows, extent), each) for some, each in zip(split, kind)]
            if split else shape((members * rows, extent), kind), *operands,
            scratch=[pltpu.VMEM((len(parts) * n_rays, extent), F32)]
            + [pltpu.VMEM((members * rows, extent), F32)] * n_bank)

    def join(*parts):
        total = sum(part.shape[0] for part in parts)
        return call(join_kernel, "join", 16, [VMEM] * len(parts), shape((total, extent), BF16), *parts)

    def update(volume, pieces, last):
        out = [shape((rows, extent), F32)] + ([] if last else [shape((rows, extent), BF16)])
        return call(
            functools.partial(update_kernel, len(pieces)), "update", 16,
            [VMEM] * (2 + len(pieces)), out, volume, column_weight, *pieces)

    column_weight = call(
        functools.partial(column_kernel, sizes), "column_weight", 16, [VMEM] * 4,
        shape((rows, extent), F32), *slots_by_depth, live)

    for sweep in range(ITERS):
        last = sweep + 1 == ITERS
        if paired:
            place_1, place_2, place_3, across = [
                exchange(payload, n_slab, *pair) for pair in ((9, 5), (5, 9), (12, 12), (15, 15))]
            z_part = join(payload, place_1, place_2)
            y_part = exchange(z_part, n_slab, 3)
            along_z, along_y = (z_part, place_3), (y_part, across)
            if sweep == 0:
                (z_list,), z_rows, z_forward, z_backward = setup(along_z, 4, (None,))
            both = forward(z_list, along_z, 4, z_forward, 2 * n_rays)
            if sweep == 0:
                (own_list, other_list), y_rows, y_forward, y_backward = setup(
                    along_y, 4, (0, 1), after=both)
            other = exchange(
                forward(other_list, along_y, 4, y_forward, n_rays, both, n_rays,
                        (z_rows, y_rows) if sweep == 0 else ()), n_slab, 1)
            if sweep == 0:
                first_other = other
            own = forward(own_list, along_y, 4, y_forward, n_rays, both, 0)
            residual = residual_of(own, (z_rows, y_rows), other, first_other)
            other_residual = exchange(residual, n_slab, 1)
            y_sum = backward(own_list, [residual], 4, y_backward, F32)
            far_sum, near_sum = backward(
                other_list, [other_residual], 4, y_backward, (BF16, BF16), y_sum, ((1, 3), (0, 2)))
            far_part, near_part = exchange(far_sum, n_slab, 3), exchange(near_sum, n_slab, 3)
            z_sum = backward(z_list, [residual, other_residual], 4, z_backward, F32)
            piece = shape((rows, extent), BF16)
            piece_1, piece_3 = call(
                functools.partial(combine_kernel, (1, 3)), "combine", 16, [VMEM] * 2,
                [piece, piece], z_sum, far_part)
            got = [exchange(piece_1, n_slab, 9, 5), exchange(piece_3, n_slab, 12)]
            own_piece, piece_2 = call(
                functools.partial(combine_kernel, (0, 2)), "combine", 16, [VMEM] * 2,
                [shape((rows, extent), F32), piece], z_sum, near_part)
            pieces = [own_piece, *got, exchange(piece_2, n_slab, 5, 9)]
        else:
            everyone = lax.all_gather(payload, "slab", axis=0, tiled=True)
            if sweep == 0:
                (slots,), row_sums, to_rays, to_voxels = setup((everyone,), n_slab, (None,))
            projection = forward(slots, (everyone,), n_slab, to_rays, n_rays)
            residual = residual_of(projection, (row_sums,))
            sums = backward(slots, [residual], n_slab, to_voxels, BF16)
            parts = lax.all_to_all(
                sums.reshape(n_slab, rows, extent), "slab", split_axis=0, concat_axis=0, tiled=True)
            pieces = [jnp.sum(parts.astype(F32), axis=0)]
        volume, *rounded = update(volume, pieces, last)
        if not last:
            payload = rounded[0]
    return volume.reshape(start_volume.shape)


def solution(mesh):
    in_specs = (
        P(("scan", "slab"), None, None),
        P(("scan", "slab"), None, None),
        P(("scan", "slab"), None),
        P(("scan", "slab")),
        P(("scan", "slab")),
        P(("scan", "slab"), None),
        P(("scan", "slab"), None),
    )
    out_specs = P(("scan", "slab"), None, None)
    return jax.shard_map(shards, mesh=mesh, in_specs=in_specs, out_specs=out_specs, check_vma=False)
```

```python
import functools

import jax
import jax.numpy as jnp
from jax import lax
from jax.experimental import pallas as pl
from jax.experimental.pallas import tpu as pltpu
from jax.sharding import PartitionSpec as P

ITERS = 2
CHUNK = 16
F32 = jnp.float32
BF16 = jnp.bfloat16
I32 = jnp.int32
HIGHEST = lax.Precision.HIGHEST
VMEM = pl.BlockSpec(memory_space=pltpu.VMEM)
ANY = pl.BlockSpec(memory_space=pl.ANY)
SMEM = pl.BlockSpec(memory_space=pltpu.SMEM)
HBM = pl.BlockSpec(memory_space=pltpu.HBM)


def hat(ray, centre):
    return jnp.maximum(0.0, 1.0 - jnp.abs(ray - centre)).astype(BF16)


def row_taps(offset, slope, extent):
    shape = (offset.shape[0], extent)
    ray = lax.broadcasted_iota(I32, shape, 1).astype(F32)
    inverse = jnp.broadcast_to(1.0 / slope, shape)
    offset = jnp.broadcast_to(offset, shape)
    slope = jnp.broadcast_to(slope, shape)
    middle = jnp.floor((ray - offset) * inverse + 0.5)
    middle = jnp.minimum(jnp.maximum(middle, 1.0), extent - 2.0)
    weights = [hat(ray, offset + slope * (middle + step)) for step in (-1.0, 0.0, 1.0)]
    return middle.astype(I32), weights


def column_taps(offset, slope, extent):
    shape = (offset.shape[0], extent)
    voxel = lax.broadcasted_iota(I32, shape, 1).astype(F32)
    centre = jnp.broadcast_to(offset, shape) + jnp.broadcast_to(slope, shape) * voxel
    first = jnp.minimum(jnp.maximum(jnp.floor(centre), 0.0), extent - 2.0)
    weights = [hat(first + step, centre) for step in (0.0, 1.0)]
    return first.astype(I32), weights


def repeat_rows(values, times):
    return jnp.concatenate(
        [jnp.broadcast_to(values[row:row + 1, :], (times, values.shape[1]))
         for row in range(values.shape[0])], axis=0)


def contract_lanes(left, right):
    return lax.dot_general(
        left.astype(BF16), right.astype(BF16), (((1,), (1,)), ((), ())), preferred_element_type=F32)


def per_slot(live_ref, slots, capacity):
    targets = live_ref.shape[1]
    slot = lax.broadcasted_iota(I32, (targets, slots), 1)
    owner = lax.broadcasted_iota(I32, (targets, slots), 0)
    expand = (lax.div(slot, capacity) == owner).astype(F32)
    return jnp.dot(live_ref[...].astype(F32), expand, precision=HIGHEST, preferred_element_type=F32)


def pack_kernel(capacity, *refs):
    sources, out_ref, loaded, arrived = refs[:6], refs[6], refs[7:13], refs[13]
    copies = [
        pltpu.make_async_copy(source, ref, arrived.at[place])
        for place, (source, ref) in enumerate(zip(sources, loaded))]
    for copy in copies:
        copy.start()
    for copy in copies:
        copy.wait()
    volume_ref, offset_ref, slope_ref, voxel_ref, ray_ref, live_ref = loaded
    rows, extent = volume_ref.shape
    out_ref[0:rows, :] = volume_ref[...].astype(BF16)
    slots = ray_ref.shape[1]
    fields = []
    for ref in (offset_ref, slope_ref):
        left = ref[...]
        for addend in range(3):
            part = left.astype(BF16).astype(F32)
            fields.append(part)
            left = left - part
    fields.append(voxel_ref[...].astype(F32))
    fields.append(ray_ref[...].astype(F32))
    fields.append(per_slot(live_ref, slots, capacity))
    used = sum(field.shape[0] for field in fields)
    fields.append(jnp.zeros((-used % 16, slots), F32))
    fields = jnp.concatenate(fields, axis=0)
    height = fields.shape[0]
    for part in range(slots // extent):
        at = pl.ds(rows + part * height, height)
        out_ref[at, :] = fields[:, part * extent:(part + 1) * extent].astype(BF16)


def setup_kernel(n_payloads, members, stride, span, sizes, tiles, wanted, *refs):
    payload_refs, refs = refs[:n_payloads], refs[-(2 * len(wanted) + 10):]
    where = [(ref, index) for ref in payload_refs for index in range(ref.shape[0] // stride)]
    list_refs, row_ref, tables = refs[:len(wanted)], refs[len(wanted)], refs[len(wanted) + 1:-len(wanted) - 2]
    drafts, arrived, summed = refs[-len(wanted) - 2:-2], refs[-2], refs[-1]
    copies = [
        pltpu.make_async_copy(draft, ref, arrived.at[place])
        for place, (draft, ref) in enumerate(zip(drafts, list_refs))]
    capacity, depth, frames = sizes
    width = span * capacity
    extent = row_ref.shape[1]
    ray_tiles = row_ref.shape[0] // span
    height = -(-(7 * depth + 2) // 16) * 16
    lanes = drafts[0].shape[1]
    me = lax.axis_index("slab").astype(I32)
    parity = lax.rem(me, span)
    first_slot = (me - parity) * capacity
    part = lax.div(first_slot, extent)
    shift = lax.rem(extent - lax.rem(first_slot, extent), extent)

    def collect(member, lined, payload_ref, within):
        at = within * stride + tiles * frames + part * height
        raw = payload_ref[pl.ds(pl.multiple_of(at, 16), height), :].astype(F32)
        offset = (raw[0:depth] + raw[depth:2 * depth]) + raw[2 * depth:3 * depth]
        slope = (raw[3 * depth:4 * depth] + raw[4 * depth:5 * depth]) + raw[5 * depth:6 * depth]
        fields = jnp.concatenate(
            [offset, slope, raw[6 * depth:7 * depth + 2],
             jnp.zeros((16 - 3 * depth - 2, extent), F32)], axis=0)
        fields = pltpu.roll(fields, shift, axis=1)
        lane = lax.broadcasted_iota(I32, fields.shape, 1)
        fields = jnp.where(lane < width, fields, 0.0)
        if lanes > extent:
            fields = jnp.concatenate(
                [fields, jnp.zeros((fields.shape[0], lanes - extent), F32)], axis=1)
        return lined + pltpu.roll(fields, member * width, axis=1)

    lined = jnp.zeros((16, lanes), F32)
    if members <= 16:
        for member in range(members):
            lined = collect(member, lined, *where[member])
    else:
        lined = lax.fori_loop(
            0, members, lambda member, lined: collect(member, lined, payload_refs[0], member), lined)

    slot = lax.broadcasted_iota(I32, (1, lanes), 1)
    within = lax.rem(slot, width)
    target = lax.bitwise_xor(lax.div(within, capacity), parity)
    ray = lined[3 * depth:3 * depth + 1]
    count = lined[3 * depth + 1:3 * depth + 2]
    alive = jnp.logical_and(lax.rem(within, capacity).astype(F32) < count, slot < members * width)

    table = jnp.concatenate(
        [slot.astype(F32), ray, target.astype(F32), lined[2 * depth:3 * depth],
         jnp.zeros((5 - depth, lanes), F32)], axis=0)
    order = lax.broadcasted_iota(I32, (lanes, lanes), 0)
    earlier = (lax.broadcasted_iota(I32, (lanes, lanes), 1) < order).astype(F32)
    for ref, kind, copy in zip(drafts, wanted, copies):
        taken = alive if kind is None else jnp.logical_and(alive, target == kind)
        taken = taken.astype(F32)
        position = contract_lanes(jnp.broadcast_to(taken, (8, lanes)), earlier)[0:1]
        position = jnp.where(taken > 0.0, position, -1.0).astype(I32)
        choose = jnp.broadcast_to(position, (lanes, lanes)) == order
        packed = (contract_lanes(table, choose.astype(F32)) + 0.5).astype(I32)
        total = jnp.sum(taken, axis=1, keepdims=True).astype(I32)
        line = jnp.where(slot < total, packed[0:1], lanes)
        base = packed[1:2] if kind is not None else packed[1:2] + packed[2:3] * ray_tiles
        member = lax.div(packed[0:1], width) * tiles
        rows = [line, base * frames]
        rows += [(packed[3 + level:4 + level] + member) * frames for level in range(depth)]
        rows += [jnp.zeros((5 - depth, lanes), I32), jnp.broadcast_to(total, (1, lanes))]
        ref[...] = jnp.concatenate(rows, axis=0)
        copy.start()

    columns = lined.T
    step = 32
    for row in range(0, lanes, step):
        total = None
        for level in range(depth):
            offset = columns[row:row + step, level:level + 1]
            slope = columns[row:row + step, depth + level:depth + level + 1]
            middle, weights = row_taps(offset, slope, extent)
            first, pair = column_taps(offset, slope, extent)
            wide = [weight.astype(F32) for weight in weights]
            values = [middle] + wide + [first] + [weight.astype(F32) for weight in pair]
            at = level * (lanes + 8) + row
            for ref, value in zip(tables, values):
                ref[at:at + step, :] = value
            parts = (wide[0] + wide[1]) + wide[2]
            total = parts if total is None else total + parts
        summed[row:row + step, :] = total
    for ref in tables:
        blank = jnp.ones if ref.dtype == I32 else jnp.zeros
        for level in range(depth):
            at = level * (lanes + 8) + lanes
            ref[at:at + 8, :] = blank((8, extent), ref.dtype)

    tile = lax.broadcasted_iota(I32, (span * ray_tiles, lanes), 0).astype(F32)
    place = ray + (target * ray_tiles).astype(F32)
    place = jnp.where(alive, place, -1.0)
    hot = (jnp.broadcast_to(place, tile.shape) == tile).astype(F32)
    row_ref[...] = jnp.dot(hot, summed[...], precision=HIGHEST, preferred_element_type=F32)
    for copy in copies:
        copy.wait()


def column_kernel(sizes, offset_ref, slope_ref, voxel_ref, live_ref, out_ref):
    capacity, depth, frames = sizes
    tiles = out_ref.shape[0] // frames
    slots = offset_ref.shape[1]
    extent = out_ref.shape[1]
    offsets = offset_ref[...].T
    slopes = slope_ref[...].T
    within = lax.rem(lax.broadcasted_iota(I32, (1, slots), 1), capacity).astype(F32)
    alive = jnp.broadcast_to(within, (tiles, slots)) < per_slot(live_ref, slots, capacity)
    total = jnp.zeros((tiles, extent), F32)
    for level in range(depth):
        unused, pair = column_taps(
            offsets[:, level:level + 1], slopes[:, level:level + 1], extent)
        tile_of = jnp.broadcast_to(voxel_ref[level:level + 1, :], (tiles, slots))
        match = tile_of == lax.broadcasted_iota(I32, (tiles, slots), 0)
        hot = jnp.logical_and(match, alive).astype(F32).astype(BF16)
        for weight in pair:
            total += jnp.dot(hot, weight, preferred_element_type=F32)
    out_ref[...] = repeat_rows(1.0 / jnp.maximum(total, 1.0), frames)


def pick(values, index):
    numbers = lax.GatherDimensionNumbers(
        offset_dims=(), collapsed_slice_dims=(1,), start_index_map=(1,),
        operand_batching_dims=(0,), start_indices_batching_dims=(0,))
    return lax.gather(
        values, index[:, :, None], numbers, slice_sizes=(1, 1),
        mode=lax.GatherScatterMode.PROMISE_IN_BOUNDS)


def pack_pair(first, second):
    kind = jnp.int16 if first.dtype == I32 else BF16
    return jnp.concatenate([first, second], axis=0).astype(kind)


def spread(ref, row, frames):
    return ref[pl.ds(row, frames, stride=0), :]


def tile_at(start, frames):
    return pl.ds(pl.multiple_of(start, frames), frames)


def for_slots(slots, body):
    def some(step, carry):
        for place in range(CHUNK):
            body(step * CHUNK + place, place)
        return carry

    lax.fori_loop(0, lax.div(slots[7, 0] + (CHUNK - 1), CHUNK), some, 0)


def for_rows(rows, body):
    step = 128

    def some(number, carry):
        body(pl.ds(pl.multiple_of(number * step, step), step))
        return carry

    lax.fori_loop(0, rows // step, some, 0)


def forward_kernel(sizes, n_values, members, start_row, n_sums, slots, *refs):
    capacity, depth, frames = sizes
    value_refs, tables, refs = refs[:n_values], refs[n_values:n_values + 4], refs[n_values + 4:]
    start_ref = None
    if start_row is not None:
        start_ref, refs = refs[0], refs[1:]
    sum_refs, (out_ref, wide, second) = refs[:n_sums], refs[n_sums:]
    rows = wide.shape[0] // members
    stride = sum(ref.shape[0] for ref in value_refs) // members
    rays = second.shape[0]
    line_step = tables[0].shape[0] // depth

    base = 0
    for ref in value_refs:
        def widen(member, carry, ref=ref, base=base):
            at = pl.ds(pl.multiple_of((base + member) * rows, rows), rows)
            wide[at, :] = ref[pl.ds(pl.multiple_of(member * stride, 16), rows), :].astype(F32)
            return carry

        lax.fori_loop(0, ref.shape[0] // stride, widen, 0)
        base += ref.shape[0] // stride
    second[...] = jnp.zeros_like(second)
    if start_ref is None:
        out_ref[...] = jnp.zeros_like(out_ref)
    else:
        out_ref[0:rays, :] = start_ref[start_row:start_row + rays, :]
    if n_sums:
        half = sum_refs[0].shape[0] // 2
        out_ref[rays:, :] = sum([ref[half:, :] for ref in sum_refs[1:]], sum_refs[0][half:, :])

    def one(slot, place):
        line = slots[0, slot]
        taps = []
        for start in range(0, depth, 2):
            levels = range(start, start + 2)
            values = [wide[tile_at(slots[2 + level, slot], frames), :] for level in levels]
            middles = [spread(tables[0], line + level * line_step, frames) for level in levels]
            lower = [
                pick(pack_pair(value, value), pack_pair(middle - 1, middle)).astype(F32)
                for value, middle in zip(values, middles)]
            upper = pick(
                pack_pair(*values), pack_pair(*[middle + 1 for middle in middles])).astype(F32)
            for which, pair in enumerate(lower):
                taps.append((pair[0:frames], pair[frames:2 * frames],
                             upper[which * frames:(which + 1) * frames]))
        total = None
        for level, three in enumerate(taps):
            for ref, tap in zip(tables[1:], three):
                term = spread(ref, line + level * line_step, frames) * tap
                total = term if total is None else total + term
        projection = (out_ref, second)[place % 2]
        projection[tile_at(slots[1, slot], frames), :] += total.astype(BF16).astype(F32)

    for_slots(slots, one)
    out_ref[0:rays, :] += second[...]


def residual_kernel(frames, n_own, projection_ref, sinogram_ref, *refs):
    own, refs, out_ref = refs[:n_own], refs[n_own:-1], refs[-1]
    rays = out_ref.shape[0]
    ray_tiles = rays // frames
    total = sum([ref[0:ray_tiles, :] for ref in own[1:]], own[0][0:ray_tiles, :])
    projection = projection_ref[...]
    if refs:
        projection = projection + refs[0][0:rays, :]
        total = total + refs[-1][rays:, :]
    weight = repeat_rows(1.0 / jnp.maximum(total, 1.0), frames)
    out_ref[...] = ((sinogram_ref[...].astype(F32) - projection) * weight).astype(BF16)


def backward_kernel(sizes, n_parts, has_start, split, slots, *refs):
    capacity, depth, frames = sizes
    part_refs, tables, refs = refs[:n_parts], refs[n_parts:n_parts + 3], refs[n_parts + 3:]
    start_ref = None
    if has_start:
        start_ref, refs = refs[0], refs[1:]
    outs = refs[:len(split)] if split else refs[:1]
    residual, banks = refs[len(outs)], refs[len(outs) + 1:]
    rays = part_refs[0].shape[0]
    line_step = tables[0].shape[0] // depth
    for place, ref in enumerate(part_refs):
        residual[place * rays:(place + 1) * rays, :] = ref[...].astype(F32)

    def clear(at):
        for place, bank in enumerate(banks):
            if place == 0 and has_start:
                bank[at, :] = start_ref[at, :]
            else:
                bank[at, :] = jnp.zeros((at.size, bank.shape[1]), F32)

    for_rows(banks[0].shape[0], clear)

    def one(slot, place):
        line = slots[0, slot]
        values = residual[tile_at(slots[1, slot], frames), :]
        twice = pack_pair(values, values)
        for level in range(depth):
            row = line + level * line_step
            first = spread(tables[0], row, frames)
            taps = pick(twice, pack_pair(first, first + 1)).astype(F32)
            term = (spread(tables[1], row, frames) * taps[0:frames]
                    + spread(tables[2], row, frames) * taps[frames:2 * frames])
            banks[level % len(banks)][tile_at(slots[2 + level, slot], frames), :] += term

    for_slots(slots, one)

    def total(at):
        return sum([bank[at, :] for bank in banks[1:]], banks[0][at, :])

    if split:
        for ref, members in zip(outs, split):
            rows = ref.shape[0] // len(members)
            for place, member in enumerate(members):
                ref[place * rows:(place + 1) * rows, :] = total(pl.ds(member * rows, rows)).astype(ref.dtype)
    else:
        def finish(at):
            outs[0][at, :] = total(at).astype(outs[0].dtype)

        for_rows(outs[0].shape[0], finish)


def join_kernel(*refs):
    out_ref, at = refs[-1], 0
    for ref in refs[:-1]:
        out_ref[at:at + ref.shape[0], :] = ref[...]
        at += ref.shape[0]


def combine_kernel(members, sum_ref, y_ref, *piece_refs):
    rows = piece_refs[0].shape[0]
    for place, (member, ref) in enumerate(zip(members, piece_refs)):
        mine = sum_ref[member * rows:(member + 1) * rows, :]
        ref[...] = (mine + y_ref[place * rows:(place + 1) * rows, :].astype(F32)).astype(ref.dtype)


def update_kernel(n_pieces, volume_ref, column_ref, *refs):
    back = refs[0][...]
    for ref in refs[1:n_pieces]:
        back = back + ref[...].astype(F32)
    volume = volume_ref[...] + column_ref[...] * back
    for ref in refs[n_pieces:]:
        ref[...] = volume.astype(ref.dtype)


def call(kernel, name, mib, in_specs, out_shape, *operands, scratch=()):
    one = not isinstance(out_shape, list)
    return pl.pallas_call(
        kernel,
        out_shape=out_shape,
        in_specs=in_specs,
        out_specs=VMEM if one else [
            SMEM if getattr(out, "memory_space", None) == pltpu.SMEM else VMEM for out in out_shape],
        scratch_shapes=list(scratch),
        compiler_params=pltpu.CompilerParams(vmem_limit_bytes=mib * 1024 * 1024),
        name=name,
        cost_estimate=pl.CostEstimate(flops=4 * 10**9, bytes_accessed=8 * 10**6, transcendentals=0),
    )(*operands)


def exchange(values, n_slab, distance, other_distance=None):
    far = (distance, distance if other_distance is None else other_distance)
    return lax.ppermute(
        values, "slab",
        [(device, device ^ far[device.bit_count() % 2]) for device in range(n_slab)])


def shards(sinogram, start_volume, slot_voxel, slot_ray, live_count, block_slope, block_offset):
    n_slab = lax.axis_size("slab")
    n_slots, depth = slot_voxel.shape
    capacity = n_slots // n_slab
    ray_tiles, frames, extent = sinogram.shape
    voxel_tiles = start_volume.shape[0]
    rows = voxel_tiles * frames
    sizes = (capacity, depth, frames)
    paired = n_slab == 16
    span = 2 if paired else 1
    n_bank = 2 if paired else 1
    shape = jax.ShapeDtypeStruct
    n_rays = ray_tiles * frames
    volume = start_volume.reshape(rows, extent)
    sino = sinogram.reshape(n_rays, extent)
    slots_by_depth = (block_offset.T, block_slope.T, slot_voxel.T)
    live = live_count.reshape(1, n_slab)
    height = -(-(7 * depth + 2) // 16) * 16 * (n_slots // extent)
    operands = (volume, *slots_by_depth, slot_ray.reshape(1, n_slots), live)
    payload = call(
        functools.partial(pack_kernel, capacity), "pack", 16, [HBM] * 6,
        shape((rows + height, extent), BF16),
        *[pltpu.with_memory_space_constraint(operand, pltpu.HBM) for operand in operands],
        scratch=[pltpu.VMEM(operand.shape, operand.dtype) for operand in operands]
        + [pltpu.SemaphoreType.DMA((6,))])

    def setup(payloads, members, wanted, after=None):
        lanes = -(-members * span * capacity // 128) * 128
        lines = depth * (lanes + 8)
        table = [shape((lines, extent), I32)] + [shape((lines, extent), F32)] * 3
        table += [shape((lines, extent), I32)] + [shape((lines, extent), F32)] * 2
        n = len(wanted)
        out = [pltpu.SMEM((8, lanes), I32)] * n + [shape((span * ray_tiles, extent), F32)] + table
        waits = [] if after is None else [after]
        found = call(
            functools.partial(setup_kernel, len(payloads), members,
                              sum(one.shape[0] for one in payloads) // members, span, sizes,
                              voxel_tiles, wanted),
            "setup", 24, [VMEM] * len(payloads) + [ANY] * len(waits), out, *payloads, *waits,
            scratch=[pltpu.VMEM((8, lanes), I32)] * n
            + [pltpu.SemaphoreType.DMA((n,)), pltpu.VMEM((lanes, extent), F32)])
        return found[:n], found[n], found[n + 1:n + 5], found[n + 5:]

    def forward(slots, values, members, table, n_out, start=None, start_row=None, sums=()):
        operands = [pltpu.with_memory_space_constraint(slots, pltpu.SMEM), *values, *table] + ([] if start is None else [start]) + list(sums)
        extra = ray_tiles if sums else 0
        return call(
            functools.partial(forward_kernel, sizes, len(values), members, start_row, len(sums)),
            "forward", 16 if paired else 32, [SMEM] + [VMEM] * (len(operands) - 1),
            shape((n_out + extra, extent), F32), *operands,
            scratch=[pltpu.VMEM((members * rows, extent), F32), pltpu.VMEM((n_out, extent), F32)])

    def residual_of(projection, row_sums, *sibling):
        operands = [projection, sino, *row_sums, *sibling]
        return call(
            functools.partial(residual_kernel, frames, len(row_sums)), "residual", 16,
            [VMEM] * len(operands), shape((n_rays, extent), BF16), *operands)

    def backward(slots, parts, members, table, kind, start=None, split=()):
        operands = [pltpu.with_memory_space_constraint(slots, pltpu.SMEM), *parts, *table] + ([] if start is None else [start])
        return call(
            functools.partial(backward_kernel, sizes, len(parts), start is not None, split),
            "backward", 16 if paired else 32, [SMEM] + [VMEM] * (len(operands) - 1),
            [shape((len(some) * rows, extent), each) for some, each in zip(split, kind)]
            if split else shape((members * rows, extent), kind), *operands,
            scratch=[pltpu.VMEM((len(parts) * n_rays, extent), F32)]
            + [pltpu.VMEM((members * rows, extent), F32)] * n_bank)

    def join(*parts):
        total = sum(part.shape[0] for part in parts)
        return call(join_kernel, "join", 16, [VMEM] * len(parts), shape((total, extent), BF16), *parts)

    def update(volume, pieces, last):
        out = [shape((rows, extent), F32)] + ([] if last else [shape((rows, extent), BF16)])
        return call(
            functools.partial(update_kernel, len(pieces)), "update", 16,
            [VMEM] * (2 + len(pieces)), out, volume, column_weight, *pieces)

    column_weight = call(
        functools.partial(column_kernel, sizes), "column_weight", 16, [VMEM] * 4,
        shape((rows, extent), F32), *slots_by_depth, live)

    for sweep in range(ITERS):
        last = sweep + 1 == ITERS
        if paired:
            place_1, place_2, place_3, across = [
                exchange(payload, n_slab, *pair) for pair in ((9, 3), (5, 9), (12, 10), (15, 15))]
            z_part = join(payload, place_1, place_2)
            y_part = exchange(z_part, n_slab, 3, 5)
            along_z, along_y = (z_part, place_3), (y_part, across)
            if sweep == 0:
                (z_list,), z_rows, z_forward, z_backward = setup(along_z, 4, (None,))
            both = forward(z_list, along_z, 4, z_forward, 2 * n_rays)
            if sweep == 0:
                (own_list, other_list), y_rows, y_forward, y_backward = setup(
                    along_y, 4, (0, 1), after=both)
            other = exchange(
                forward(other_list, along_y, 4, y_forward, n_rays, both, n_rays,
                        (z_rows, y_rows) if sweep == 0 else ()), n_slab, 1)
            if sweep == 0:
                first_other = other
            own = forward(own_list, along_y, 4, y_forward, n_rays, both, 0)
            residual = residual_of(own, (z_rows, y_rows), other, first_other)
            other_residual = exchange(residual, n_slab, 1)
            y_sum = backward(own_list, [residual], 4, y_backward, F32)
            far_sum, near_sum = backward(
                other_list, [other_residual], 4, y_backward, (BF16, BF16), y_sum, ((1, 3), (0, 2)))
            far_part, near_part = exchange(far_sum, n_slab, 3, 5), exchange(near_sum, n_slab, 3, 5)
            z_sum = backward(z_list, [residual, other_residual], 4, z_backward, F32)
            piece = shape((rows, extent), BF16)
            piece_1, piece_3 = call(
                functools.partial(combine_kernel, (1, 3)), "combine", 16, [VMEM] * 2,
                [piece, piece], z_sum, far_part)
            got = [exchange(piece_1, n_slab, 9, 3), exchange(piece_3, n_slab, 12, 10)]
            own_piece, piece_2 = call(
                functools.partial(combine_kernel, (0, 2)), "combine", 16, [VMEM] * 2,
                [shape((rows, extent), F32), piece], z_sum, near_part)
            pieces = [own_piece, *got, exchange(piece_2, n_slab, 5, 9)]
        else:
            everyone = lax.all_gather(payload, "slab", axis=0, tiled=True)
            if sweep == 0:
                (slots,), row_sums, to_rays, to_voxels = setup((everyone,), n_slab, (None,))
            projection = forward(slots, (everyone,), n_slab, to_rays, n_rays)
            residual = residual_of(projection, (row_sums,))
            sums = backward(slots, [residual], n_slab, to_voxels, BF16)
            parts = lax.all_to_all(
                sums.reshape(n_slab, rows, extent), "slab", split_axis=0, concat_axis=0, tiled=True)
            pieces = [jnp.sum(parts.astype(F32), axis=0)]
        volume, *rounded = update(volume, pieces, last)
        if not last:
            payload = rounded[0]
    return volume.reshape(start_volume.shape)


def solution(mesh):
    in_specs = (
        P(("scan", "slab"), None, None),
        P(("scan", "slab"), None, None),
        P(("scan", "slab"), None),
        P(("scan", "slab")),
        P(("scan", "slab")),
        P(("scan", "slab"), None),
        P(("scan", "slab"), None),
    )
    out_specs = P(("scan", "slab"), None, None)
    return jax.shard_map(shards, mesh=mesh, in_specs=in_specs, out_specs=out_specs, check_vma=False)
```

```python
import functools

import jax
import jax.numpy as jnp
from jax import lax
from jax.experimental import pallas as pl
from jax.experimental.pallas import tpu as pltpu
from jax.sharding import PartitionSpec as P

ITERS = 2
CHUNK = 16
F32 = jnp.float32
BF16 = jnp.bfloat16
I32 = jnp.int32
HIGHEST = lax.Precision.HIGHEST
VMEM = pl.BlockSpec(memory_space=pltpu.VMEM)
ANY = pl.BlockSpec(memory_space=pl.ANY)
SMEM = pl.BlockSpec(memory_space=pltpu.SMEM)
HBM = pl.BlockSpec(memory_space=pltpu.HBM)


def hat(ray, centre):
    return jnp.maximum(0.0, 1.0 - jnp.abs(ray - centre)).astype(BF16)


def row_taps(offset, slope, extent):
    shape = (offset.shape[0], extent)
    ray = lax.broadcasted_iota(I32, shape, 1).astype(F32)
    inverse = jnp.broadcast_to(1.0 / slope, shape)
    offset = jnp.broadcast_to(offset, shape)
    slope = jnp.broadcast_to(slope, shape)
    middle = jnp.floor((ray - offset) * inverse + 0.5)
    middle = jnp.minimum(jnp.maximum(middle, 1.0), extent - 2.0)
    weights = [hat(ray, offset + slope * (middle + step)) for step in (-1.0, 0.0, 1.0)]
    return middle.astype(I32), weights


def column_taps(offset, slope, extent):
    shape = (offset.shape[0], extent)
    voxel = lax.broadcasted_iota(I32, shape, 1).astype(F32)
    centre = jnp.broadcast_to(offset, shape) + jnp.broadcast_to(slope, shape) * voxel
    first = jnp.minimum(jnp.maximum(jnp.floor(centre), 0.0), extent - 2.0)
    weights = [hat(first + step, centre) for step in (0.0, 1.0)]
    return first.astype(I32), weights


def repeat_rows(values, times):
    return jnp.concatenate(
        [jnp.broadcast_to(values[row:row + 1, :], (times, values.shape[1]))
         for row in range(values.shape[0])], axis=0)


def contract_lanes(left, right):
    return lax.dot_general(
        left.astype(BF16), right.astype(BF16), (((1,), (1,)), ((), ())), preferred_element_type=F32)


def per_slot(live_ref, slots, capacity):
    targets = live_ref.shape[1]
    slot = lax.broadcasted_iota(I32, (targets, slots), 1)
    owner = lax.broadcasted_iota(I32, (targets, slots), 0)
    expand = (lax.div(slot, capacity) == owner).astype(F32)
    return jnp.dot(live_ref[...].astype(F32), expand, precision=HIGHEST, preferred_element_type=F32)


def pack_kernel(capacity, *refs):
    sources, out_ref, loaded, arrived = refs[:6], refs[6], refs[7:13], refs[13]
    copies = [
        pltpu.make_async_copy(source, ref, arrived.at[place])
        for place, (source, ref) in enumerate(zip(sources, loaded))]
    for copy in copies:
        copy.start()
    for copy in copies:
        copy.wait()
    volume_ref, offset_ref, slope_ref, voxel_ref, ray_ref, live_ref = loaded
    rows, extent = volume_ref.shape
    out_ref[0:rows, :] = volume_ref[...].astype(BF16)
    slots = ray_ref.shape[1]
    fields = []
    for ref in (offset_ref, slope_ref):
        left = ref[...]
        for addend in range(3):
            part = left.astype(BF16).astype(F32)
            fields.append(part)
            left = left - part
    fields.append(voxel_ref[...].astype(F32))
    fields.append(ray_ref[...].astype(F32))
    fields.append(per_slot(live_ref, slots, capacity))
    used = sum(field.shape[0] for field in fields)
    fields.append(jnp.zeros((-used % 16, slots), F32))
    fields = jnp.concatenate(fields, axis=0)
    height = fields.shape[0]
    for part in range(slots // extent):
        at = pl.ds(rows + part * height, height)
        out_ref[at, :] = fields[:, part * extent:(part + 1) * extent].astype(BF16)


def setup_kernel(n_payloads, members, stride, span, sizes, tiles, wanted, *refs):
    payload_refs, refs = refs[:n_payloads], refs[-(2 * len(wanted) + 10):]
    where = [(ref, index) for ref in payload_refs for index in range(ref.shape[0] // stride)]
    list_refs, row_ref, tables = refs[:len(wanted)], refs[len(wanted)], refs[len(wanted) + 1:-len(wanted) - 2]
    drafts, arrived, summed = refs[-len(wanted) - 2:-2], refs[-2], refs[-1]
    copies = [
        pltpu.make_async_copy(draft, ref, arrived.at[place])
        for place, (draft, ref) in enumerate(zip(drafts, list_refs))]
    capacity, depth, frames = sizes
    width = span * capacity
    extent = row_ref.shape[1]
    ray_tiles = row_ref.shape[0] // span
    height = -(-(7 * depth + 2) // 16) * 16
    lanes = drafts[0].shape[1]
    me = lax.axis_index("slab").astype(I32)
    parity = lax.rem(me, span)
    first_slot = (me - parity) * capacity
    part = lax.div(first_slot, extent)
    shift = lax.rem(extent - lax.rem(first_slot, extent), extent)

    def collect(member, lined, payload_ref, within):
        at = within * stride + tiles * frames + part * height
        raw = payload_ref[pl.ds(pl.multiple_of(at, 16), height), :].astype(F32)
        offset = (raw[0:depth] + raw[depth:2 * depth]) + raw[2 * depth:3 * depth]
        slope = (raw[3 * depth:4 * depth] + raw[4 * depth:5 * depth]) + raw[5 * depth:6 * depth]
        fields = jnp.concatenate(
            [offset, slope, raw[6 * depth:7 * depth + 2],
             jnp.zeros((16 - 3 * depth - 2, extent), F32)], axis=0)
        fields = pltpu.roll(fields, shift, axis=1)
        lane = lax.broadcasted_iota(I32, fields.shape, 1)
        fields = jnp.where(lane < width, fields, 0.0)
        if lanes > extent:
            fields = jnp.concatenate(
                [fields, jnp.zeros((fields.shape[0], lanes - extent), F32)], axis=1)
        return lined + pltpu.roll(fields, member * width, axis=1)

    lined = jnp.zeros((16, lanes), F32)
    if members <= 16:
        for member in range(members):
            lined = collect(member, lined, *where[member])
    else:
        lined = lax.fori_loop(
            0, members, lambda member, lined: collect(member, lined, payload_refs[0], member), lined)

    slot = lax.broadcasted_iota(I32, (1, lanes), 1)
    within = lax.rem(slot, width)
    target = lax.bitwise_xor(lax.div(within, capacity), parity)
    ray = lined[3 * depth:3 * depth + 1]
    count = lined[3 * depth + 1:3 * depth + 2]
    alive = jnp.logical_and(lax.rem(within, capacity).astype(F32) < count, slot < members * width)

    table = jnp.concatenate(
        [slot.astype(F32), ray, target.astype(F32), lined[2 * depth:3 * depth],
         jnp.zeros((5 - depth, lanes), F32)], axis=0)
    order = lax.broadcasted_iota(I32, (lanes, lanes), 0)
    earlier = (lax.broadcasted_iota(I32, (lanes, lanes), 1) < order).astype(F32)
    for ref, kind, copy in zip(drafts, wanted, copies):
        taken = alive if kind is None else jnp.logical_and(alive, target == kind)
        taken = taken.astype(F32)
        position = contract_lanes(jnp.broadcast_to(taken, (8, lanes)), earlier)[0:1]
        position = jnp.where(taken > 0.0, position, -1.0).astype(I32)
        choose = jnp.broadcast_to(position, (lanes, lanes)) == order
        packed = (contract_lanes(table, choose.astype(F32)) + 0.5).astype(I32)
        total = jnp.sum(taken, axis=1, keepdims=True).astype(I32)
        line = jnp.where(slot < total, packed[0:1], lanes)
        base = packed[1:2] if kind is not None else packed[1:2] + packed[2:3] * ray_tiles
        member = lax.div(packed[0:1], width) * tiles
        rows = [line, base * frames]
        rows += [(packed[3 + level:4 + level] + member) * frames for level in range(depth)]
        rows += [jnp.zeros((5 - depth, lanes), I32), jnp.broadcast_to(total, (1, lanes))]
        ref[...] = jnp.concatenate(rows, axis=0)
        copy.start()

    columns = lined.T
    step = 32
    for row in range(0, lanes, step):
        total = None
        for level in range(depth):
            offset = columns[row:row + step, level:level + 1]
            slope = columns[row:row + step, depth + level:depth + level + 1]
            middle, weights = row_taps(offset, slope, extent)
            first, pair = column_taps(offset, slope, extent)
            wide = [weight.astype(F32) for weight in weights]
            values = [middle] + wide + [first] + [weight.astype(F32) for weight in pair]
            at = level * (lanes + 8) + row
            for ref, value in zip(tables, values):
                ref[at:at + step, :] = value
            parts = (wide[0] + wide[1]) + wide[2]
            total = parts if total is None else total + parts
        summed[row:row + step, :] = total
    for ref in tables:
        blank = jnp.ones if ref.dtype == I32 else jnp.zeros
        for level in range(depth):
            at = level * (lanes + 8) + lanes
            ref[at:at + 8, :] = blank((8, extent), ref.dtype)

    tile = lax.broadcasted_iota(I32, (span * ray_tiles, lanes), 0).astype(F32)
    place = ray + (target * ray_tiles).astype(F32)
    place = jnp.where(alive, place, -1.0)
    hot = (jnp.broadcast_to(place, tile.shape) == tile).astype(F32)
    row_ref[...] = jnp.dot(hot, summed[...], precision=HIGHEST, preferred_element_type=F32)
    for copy in copies:
        copy.wait()


def column_kernel(sizes, offset_ref, slope_ref, voxel_ref, live_ref, out_ref):
    capacity, depth, frames = sizes
    tiles = out_ref.shape[0] // frames
    slots = offset_ref.shape[1]
    extent = out_ref.shape[1]
    offsets = offset_ref[...].T
    slopes = slope_ref[...].T
    within = lax.rem(lax.broadcasted_iota(I32, (1, slots), 1), capacity).astype(F32)
    alive = jnp.broadcast_to(within, (tiles, slots)) < per_slot(live_ref, slots, capacity)
    total = jnp.zeros((tiles, extent), F32)
    for level in range(depth):
        unused, pair = column_taps(
            offsets[:, level:level + 1], slopes[:, level:level + 1], extent)
        tile_of = jnp.broadcast_to(voxel_ref[level:level + 1, :], (tiles, slots))
        match = tile_of == lax.broadcasted_iota(I32, (tiles, slots), 0)
        hot = jnp.logical_and(match, alive).astype(F32).astype(BF16)
        for weight in pair:
            total += jnp.dot(hot, weight, preferred_element_type=F32)
    out_ref[...] = repeat_rows(1.0 / jnp.maximum(total, 1.0), frames)


def pick(values, index):
    numbers = lax.GatherDimensionNumbers(
        offset_dims=(), collapsed_slice_dims=(1,), start_index_map=(1,),
        operand_batching_dims=(0,), start_indices_batching_dims=(0,))
    return lax.gather(
        values, index[:, :, None], numbers, slice_sizes=(1, 1),
        mode=lax.GatherScatterMode.PROMISE_IN_BOUNDS)


def pack_pair(first, second):
    kind = jnp.int16 if first.dtype == I32 else BF16
    return jnp.concatenate([first, second], axis=0).astype(kind)


def spread(ref, row, frames):
    return ref[pl.ds(row, frames, stride=0), :]


def tile_at(start, frames):
    return pl.ds(pl.multiple_of(start, frames), frames)


def for_slots(slots, body):
    def some(step, carry):
        for place in range(CHUNK):
            body(step * CHUNK + place, place)
        return carry

    lax.fori_loop(0, lax.div(slots[7, 0] + (CHUNK - 1), CHUNK), some, 0)


def for_rows(rows, body):
    step = 128
    if rows <= 8 * step:
        for start in range(0, rows, step):
            body(pl.ds(start, step))
        return

    def some(number, carry):
        body(pl.ds(pl.multiple_of(number * step, step), step))
        return carry

    lax.fori_loop(0, rows // step, some, 0)


def forward_kernel(sizes, n_values, members, start_row, n_sums, slots, *refs):
    capacity, depth, frames = sizes
    value_refs, tables, refs = refs[:n_values], refs[n_values:n_values + 4], refs[n_values + 4:]
    start_ref = None
    if start_row is not None:
        start_ref, refs = refs[0], refs[1:]
    sum_refs, (out_ref, wide, second) = refs[:n_sums], refs[n_sums:]
    rows = wide.shape[0] // members
    stride = sum(ref.shape[0] for ref in value_refs) // members
    rays = second.shape[0]
    line_step = tables[0].shape[0] // depth

    base = 0
    for ref in value_refs:
        def widen(member, carry, ref=ref, base=base):
            at = (base + member) * rows
            start = member * stride
            if not isinstance(member, int):
                at, start = pl.multiple_of(at, rows), pl.multiple_of(start, 16)
            wide[pl.ds(at, rows), :] = ref[pl.ds(start, rows), :].astype(F32)
            return carry

        here = ref.shape[0] // stride
        if here <= 8:
            for member in range(here):
                widen(member, 0)
        else:
            lax.fori_loop(0, here, widen, 0)
        base += here
    second[...] = jnp.zeros_like(second)
    if start_ref is None:
        out_ref[...] = jnp.zeros_like(out_ref)
    else:
        out_ref[0:rays, :] = start_ref[start_row:start_row + rays, :]
    if n_sums:
        half = sum_refs[0].shape[0] // 2
        out_ref[rays:, :] = sum([ref[half:, :] for ref in sum_refs[1:]], sum_refs[0][half:, :])

    def one(slot, place):
        line = slots[0, slot]
        taps = []
        for start in range(0, depth, 2):
            levels = range(start, start + 2)
            values = [wide[tile_at(slots[2 + level, slot], frames), :] for level in levels]
            middles = [spread(tables[0], line + level * line_step, frames) for level in levels]
            lower = [
                pick(pack_pair(value, value), pack_pair(middle - 1, middle)).astype(F32)
                for value, middle in zip(values, middles)]
            upper = pick(
                pack_pair(*values), pack_pair(*[middle + 1 for middle in middles])).astype(F32)
            for which, pair in enumerate(lower):
                taps.append((pair[0:frames], pair[frames:2 * frames],
                             upper[which * frames:(which + 1) * frames]))
        total = None
        for level, three in enumerate(taps):
            for ref, tap in zip(tables[1:], three):
                term = spread(ref, line + level * line_step, frames) * tap
                total = term if total is None else total + term
        projection = (out_ref, second)[place % 2]
        projection[tile_at(slots[1, slot], frames), :] += total.astype(BF16).astype(F32)

    for_slots(slots, one)
    out_ref[0:rays, :] += second[...]


def residual_kernel(frames, n_own, projection_ref, sinogram_ref, *refs):
    own, refs, out_ref = refs[:n_own], refs[n_own:-1], refs[-1]
    rays = out_ref.shape[0]
    ray_tiles = rays // frames
    total = sum([ref[0:ray_tiles, :] for ref in own[1:]], own[0][0:ray_tiles, :])
    projection = projection_ref[...]
    if refs:
        projection = projection + refs[0][0:rays, :]
        total = total + refs[-1][rays:, :]
    weight = repeat_rows(1.0 / jnp.maximum(total, 1.0), frames)
    out_ref[...] = ((sinogram_ref[...].astype(F32) - projection) * weight).astype(BF16)


def backward_kernel(sizes, n_parts, has_start, split, slots, *refs):
    capacity, depth, frames = sizes
    part_refs, tables, refs = refs[:n_parts], refs[n_parts:n_parts + 3], refs[n_parts + 3:]
    start_ref = None
    if has_start:
        start_ref, refs = refs[0], refs[1:]
    outs = refs[:len(split)] if split else refs[:1]
    residual, banks = refs[len(outs)], refs[len(outs) + 1:]
    rays = part_refs[0].shape[0]
    line_step = tables[0].shape[0] // depth
    for place, ref in enumerate(part_refs):
        residual[place * rays:(place + 1) * rays, :] = ref[...].astype(F32)

    def clear(at):
        for place, bank in enumerate(banks):
            if place == 0 and has_start:
                bank[at, :] = start_ref[at, :]
            else:
                bank[at, :] = jnp.zeros((at.size, bank.shape[1]), F32)

    for_rows(banks[0].shape[0], clear)

    def one(slot, place):
        line = slots[0, slot]
        values = residual[tile_at(slots[1, slot], frames), :]
        twice = pack_pair(values, values)
        for level in range(depth):
            row = line + level * line_step
            first = spread(tables[0], row, frames)
            taps = pick(twice, pack_pair(first, first + 1)).astype(F32)
            term = (spread(tables[1], row, frames) * taps[0:frames]
                    + spread(tables[2], row, frames) * taps[frames:2 * frames])
            banks[level % len(banks)][tile_at(slots[2 + level, slot], frames), :] += term

    for_slots(slots, one)

    def total(at):
        return sum([bank[at, :] for bank in banks[1:]], banks[0][at, :])

    if split:
        for ref, members in zip(outs, split):
            rows = ref.shape[0] // len(members)
            for place, member in enumerate(members):
                ref[place * rows:(place + 1) * rows, :] = total(pl.ds(member * rows, rows)).astype(ref.dtype)
    else:
        def finish(at):
            outs[0][at, :] = total(at).astype(outs[0].dtype)

        for_rows(outs[0].shape[0], finish)


def join_kernel(*refs):
    out_ref, at = refs[-1], 0
    for ref in refs[:-1]:
        out_ref[at:at + ref.shape[0], :] = ref[...]
        at += ref.shape[0]


def combine_kernel(members, sum_ref, y_ref, *piece_refs):
    rows = piece_refs[0].shape[0]
    for place, (member, ref) in enumerate(zip(members, piece_refs)):
        mine = sum_ref[member * rows:(member + 1) * rows, :]
        ref[...] = (mine + y_ref[place * rows:(place + 1) * rows, :].astype(F32)).astype(ref.dtype)


def update_kernel(n_pieces, volume_ref, column_ref, *refs):
    back = refs[0][...]
    for ref in refs[1:n_pieces]:
        back = back + ref[...].astype(F32)
    volume = volume_ref[...] + column_ref[...] * back
    for ref in refs[n_pieces:]:
        ref[...] = volume.astype(ref.dtype)


def call(kernel, name, mib, in_specs, out_shape, *operands, scratch=()):
    one = not isinstance(out_shape, list)
    return pl.pallas_call(
        kernel,
        out_shape=out_shape,
        in_specs=in_specs,
        out_specs=VMEM if one else [
            SMEM if getattr(out, "memory_space", None) == pltpu.SMEM else VMEM for out in out_shape],
        scratch_shapes=list(scratch),
        compiler_params=pltpu.CompilerParams(vmem_limit_bytes=mib * 1024 * 1024),
        name=name,
        cost_estimate=pl.CostEstimate(flops=4 * 10**9, bytes_accessed=8 * 10**6, transcendentals=0),
    )(*operands)


def exchange(values, n_slab, distance, other_distance=None):
    far = (distance, distance if other_distance is None else other_distance)
    return lax.ppermute(
        values, "slab",
        [(device, device ^ far[device.bit_count() % 2]) for device in range(n_slab)])


def shards(sinogram, start_volume, slot_voxel, slot_ray, live_count, block_slope, block_offset):
    n_slab = lax.axis_size("slab")
    n_slots, depth = slot_voxel.shape
    capacity = n_slots // n_slab
    ray_tiles, frames, extent = sinogram.shape
    voxel_tiles = start_volume.shape[0]
    rows = voxel_tiles * frames
    sizes = (capacity, depth, frames)
    paired = n_slab == 16
    span = 2 if paired else 1
    n_bank = 2 if paired else 1
    shape = jax.ShapeDtypeStruct
    n_rays = ray_tiles * frames
    volume = start_volume.reshape(rows, extent)
    sino = sinogram.reshape(n_rays, extent)
    slots_by_depth = (block_offset.T, block_slope.T, slot_voxel.T)
    live = live_count.reshape(1, n_slab)
    height = -(-(7 * depth + 2) // 16) * 16 * (n_slots // extent)
    operands = (volume, *slots_by_depth, slot_ray.reshape(1, n_slots), live)
    payload = call(
        functools.partial(pack_kernel, capacity), "pack", 16, [HBM] * 6,
        shape((rows + height, extent), BF16),
        *[pltpu.with_memory_space_constraint(operand, pltpu.HBM) for operand in operands],
        scratch=[pltpu.VMEM(operand.shape, operand.dtype) for operand in operands]
        + [pltpu.SemaphoreType.DMA((6,))])

    def setup(payloads, members, wanted, after=None):
        lanes = -(-members * span * capacity // 128) * 128
        lines = depth * (lanes + 8)
        table = [shape((lines, extent), I32)] + [shape((lines, extent), F32)] * 3
        table += [shape((lines, extent), I32)] + [shape((lines, extent), F32)] * 2
        n = len(wanted)
        out = [pltpu.SMEM((8, lanes), I32)] * n + [shape((span * ray_tiles, extent), F32)] + table
        waits = [] if after is None else [after]
        found = call(
            functools.partial(setup_kernel, len(payloads), members,
                              sum(one.shape[0] for one in payloads) // members, span, sizes,
                              voxel_tiles, wanted),
            "setup", 24, [VMEM] * len(payloads) + [ANY] * len(waits), out, *payloads, *waits,
            scratch=[pltpu.VMEM((8, lanes), I32)] * n
            + [pltpu.SemaphoreType.DMA((n,)), pltpu.VMEM((lanes, extent), F32)])
        return found[:n], found[n], found[n + 1:n + 5], found[n + 5:]

    def forward(slots, values, members, table, n_out, start=None, start_row=None, sums=()):
        operands = [pltpu.with_memory_space_constraint(slots, pltpu.SMEM), *values, *table] + ([] if start is None else [start]) + list(sums)
        extra = ray_tiles if sums else 0
        return call(
            functools.partial(forward_kernel, sizes, len(values), members, start_row, len(sums)),
            "forward", 16 if paired else 32, [SMEM] + [VMEM] * (len(operands) - 1),
            shape((n_out + extra, extent), F32), *operands,
            scratch=[pltpu.VMEM((members * rows, extent), F32), pltpu.VMEM((n_out, extent), F32)])

    def residual_of(projection, row_sums, *sibling):
        operands = [projection, sino, *row_sums, *sibling]
        return call(
            functools.partial(residual_kernel, frames, len(row_sums)), "residual", 16,
            [VMEM] * len(operands), shape((n_rays, extent), BF16), *operands)

    def backward(slots, parts, members, table, kind, start=None, split=()):
        operands = [pltpu.with_memory_space_constraint(slots, pltpu.SMEM), *parts, *table] + ([] if start is None else [start])
        return call(
            functools.partial(backward_kernel, sizes, len(parts), start is not None, split),
            "backward", 16 if paired else 32, [SMEM] + [VMEM] * (len(operands) - 1),
            [shape((len(some) * rows, extent), each) for some, each in zip(split, kind)]
            if split else shape((members * rows, extent), kind), *operands,
            scratch=[pltpu.VMEM((len(parts) * n_rays, extent), F32)]
            + [pltpu.VMEM((members * rows, extent), F32)] * n_bank)

    def join(*parts):
        total = sum(part.shape[0] for part in parts)
        return call(join_kernel, "join", 16, [VMEM] * len(parts), shape((total, extent), BF16), *parts)

    def update(volume, pieces, last):
        out = [shape((rows, extent), F32)] + ([] if last else [shape((rows, extent), BF16)])
        return call(
            functools.partial(update_kernel, len(pieces)), "update", 16,
            [VMEM] * (2 + len(pieces)), out, volume, column_weight, *pieces)

    column_weight = call(
        functools.partial(column_kernel, sizes), "column_weight", 16, [VMEM] * 4,
        shape((rows, extent), F32), *slots_by_depth, live)

    for sweep in range(ITERS):
        last = sweep + 1 == ITERS
        if paired:
            place_1, place_2, place_3, across = [
                exchange(payload, n_slab, *pair) for pair in ((9, 3), (5, 9), (12, 10), (15, 15))]
            z_part = join(payload, place_1, place_2)
            y_part = exchange(z_part, n_slab, 3, 5)
            along_z, along_y = (z_part, place_3), (y_part, across)
            if sweep == 0:
                (z_list,), z_rows, z_forward, z_backward = setup(along_z, 4, (None,))
            both = forward(z_list, along_z, 4, z_forward, 2 * n_rays)
            if sweep == 0:
                (own_list, other_list), y_rows, y_forward, y_backward = setup(
                    along_y, 4, (0, 1), after=both)
            other = exchange(
                forward(other_list, along_y, 4, y_forward, n_rays, both, n_rays,
                        (z_rows, y_rows) if sweep == 0 else ()), n_slab, 1)
            if sweep == 0:
                first_other = other
            own = forward(own_list, along_y, 4, y_forward, n_rays, both, 0)
            residual = residual_of(own, (z_rows, y_rows), other, first_other)
            other_residual = exchange(residual, n_slab, 1)
            y_sum = backward(own_list, [residual], 4, y_backward, F32)
            far_sum, near_sum = backward(
                other_list, [other_residual], 4, y_backward, (BF16, BF16), y_sum, ((1, 3), (0, 2)))
            far_part, near_part = exchange(far_sum, n_slab, 3, 5), exchange(near_sum, n_slab, 3, 5)
            z_sum = backward(z_list, [residual, other_residual], 4, z_backward, F32)
            piece = shape((rows, extent), BF16)
            piece_1, piece_3 = call(
                functools.partial(combine_kernel, (1, 3)), "combine", 16, [VMEM] * 2,
                [piece, piece], z_sum, far_part)
            got = [exchange(piece_1, n_slab, 9, 3), exchange(piece_3, n_slab, 12, 10)]
            own_piece, piece_2 = call(
                functools.partial(combine_kernel, (0, 2)), "combine", 16, [VMEM] * 2,
                [shape((rows, extent), F32), piece], z_sum, near_part)
            pieces = [own_piece, *got, exchange(piece_2, n_slab, 5, 9)]
        else:
            everyone = lax.all_gather(payload, "slab", axis=0, tiled=True)
            if sweep == 0:
                (slots,), row_sums, to_rays, to_voxels = setup((everyone,), n_slab, (None,))
            projection = forward(slots, (everyone,), n_slab, to_rays, n_rays)
            residual = residual_of(projection, (row_sums,))
            sums = backward(slots, [residual], n_slab, to_voxels, BF16)
            parts = lax.all_to_all(
                sums.reshape(n_slab, rows, extent), "slab", split_axis=0, concat_axis=0, tiled=True)
            pieces = [jnp.sum(parts.astype(F32), axis=0)]
        volume, *rounded = update(volume, pieces, last)
        if not last:
            payload = rounded[0]
    return volume.reshape(start_volume.shape)


def solution(mesh):
    in_specs = (
        P(("scan", "slab"), None, None),
        P(("scan", "slab"), None, None),
        P(("scan", "slab"), None),
        P(("scan", "slab")),
        P(("scan", "slab")),
        P(("scan", "slab"), None),
        P(("scan", "slab"), None),
    )
    out_specs = P(("scan", "slab"), None, None)
    return jax.shard_map(shards, mesh=mesh, in_specs=in_specs, out_specs=out_specs, check_vma=False)
```

```python
import functools

import jax
import jax.numpy as jnp
from jax import lax
from jax.experimental import pallas as pl
from jax.experimental.pallas import tpu as pltpu
from jax.sharding import PartitionSpec as P

ITERS = 2
CHUNK = 16
F32 = jnp.float32
BF16 = jnp.bfloat16
I32 = jnp.int32
HIGHEST = lax.Precision.HIGHEST
VMEM = pl.BlockSpec(memory_space=pltpu.VMEM)
ANY = pl.BlockSpec(memory_space=pl.ANY)
SMEM = pl.BlockSpec(memory_space=pltpu.SMEM)
HBM = pl.BlockSpec(memory_space=pltpu.HBM)


def hat(ray, centre):
    return jnp.maximum(0.0, 1.0 - jnp.abs(ray - centre)).astype(BF16)


def row_taps(offset, slope, extent):
    shape = (offset.shape[0], extent)
    ray = lax.broadcasted_iota(I32, shape, 1).astype(F32)
    inverse = jnp.broadcast_to(1.0 / slope, shape)
    offset = jnp.broadcast_to(offset, shape)
    slope = jnp.broadcast_to(slope, shape)
    middle = jnp.floor((ray - offset) * inverse + 0.5)
    middle = jnp.minimum(jnp.maximum(middle, 1.0), extent - 2.0)
    weights = [hat(ray, offset + slope * (middle + step)) for step in (-1.0, 0.0, 1.0)]
    return middle.astype(I32), weights


def column_taps(offset, slope, extent):
    shape = (offset.shape[0], extent)
    voxel = lax.broadcasted_iota(I32, shape, 1).astype(F32)
    centre = jnp.broadcast_to(offset, shape) + jnp.broadcast_to(slope, shape) * voxel
    first = jnp.minimum(jnp.maximum(jnp.floor(centre), 0.0), extent - 2.0)
    weights = [hat(first + step, centre) for step in (0.0, 1.0)]
    return first.astype(I32), weights


def repeat_rows(values, times):
    return jnp.concatenate(
        [jnp.broadcast_to(values[row:row + 1, :], (times, values.shape[1]))
         for row in range(values.shape[0])], axis=0)


def contract_lanes(left, right):
    return lax.dot_general(
        left.astype(BF16), right.astype(BF16), (((1,), (1,)), ((), ())), preferred_element_type=F32)


def per_slot(live_ref, slots, capacity):
    targets = live_ref.shape[1]
    slot = lax.broadcasted_iota(I32, (targets, slots), 1)
    owner = lax.broadcasted_iota(I32, (targets, slots), 0)
    expand = (lax.div(slot, capacity) == owner).astype(F32)
    return jnp.dot(live_ref[...].astype(F32), expand, precision=HIGHEST, preferred_element_type=F32)


def pack_kernel(capacity, *refs):
    sources, out_ref, loaded, arrived = refs[:6], refs[6], refs[7:13], refs[13]
    copies = [
        pltpu.make_async_copy(source, ref, arrived.at[place])
        for place, (source, ref) in enumerate(zip(sources, loaded))]
    for copy in copies:
        copy.start()
    for copy in copies:
        copy.wait()
    volume_ref, offset_ref, slope_ref, voxel_ref, ray_ref, live_ref = loaded
    rows, extent = volume_ref.shape
    out_ref[0:rows, :] = volume_ref[...].astype(BF16)
    slots = ray_ref.shape[1]
    fields = []
    for ref in (offset_ref, slope_ref):
        left = ref[...]
        for addend in range(3):
            part = left.astype(BF16).astype(F32)
            fields.append(part)
            left = left - part
    fields.append(voxel_ref[...].astype(F32))
    fields.append(ray_ref[...].astype(F32))
    fields.append(per_slot(live_ref, slots, capacity))
    used = sum(field.shape[0] for field in fields)
    fields.append(jnp.zeros((-used % 16, slots), F32))
    fields = jnp.concatenate(fields, axis=0)
    height = fields.shape[0]
    for part in range(slots // extent):
        at = pl.ds(rows + part * height, height)
        out_ref[at, :] = fields[:, part * extent:(part + 1) * extent].astype(BF16)


def setup_kernel(n_payloads, members, stride, span, sizes, tiles, wanted, *refs):
    payload_refs, refs = refs[:n_payloads], refs[-(2 * len(wanted) + 10):]
    where = [(ref, index) for ref in payload_refs for index in range(ref.shape[0] // stride)]
    list_refs, row_ref, tables = refs[:len(wanted)], refs[len(wanted)], refs[len(wanted) + 1:-len(wanted) - 2]
    drafts, arrived, summed = refs[-len(wanted) - 2:-2], refs[-2], refs[-1]
    copies = [
        pltpu.make_async_copy(draft, ref, arrived.at[place])
        for place, (draft, ref) in enumerate(zip(drafts, list_refs))]
    capacity, depth, frames = sizes
    width = span * capacity
    extent = row_ref.shape[1]
    ray_tiles = row_ref.shape[0] // span
    height = -(-(7 * depth + 2) // 16) * 16
    lanes = drafts[0].shape[1]
    me = lax.axis_index("slab").astype(I32)
    parity = lax.rem(me, span)
    first_slot = (me - parity) * capacity
    part = lax.div(first_slot, extent)
    shift = lax.rem(extent - lax.rem(first_slot, extent), extent)

    def collect(member, lined, payload_ref, within):
        at = within * stride + tiles * frames + part * height
        raw = payload_ref[pl.ds(pl.multiple_of(at, 16), height), :].astype(F32)
        offset = (raw[0:depth] + raw[depth:2 * depth]) + raw[2 * depth:3 * depth]
        slope = (raw[3 * depth:4 * depth] + raw[4 * depth:5 * depth]) + raw[5 * depth:6 * depth]
        fields = jnp.concatenate(
            [offset, slope, raw[6 * depth:7 * depth + 2],
             jnp.zeros((16 - 3 * depth - 2, extent), F32)], axis=0)
        fields = pltpu.roll(fields, shift, axis=1)
        lane = lax.broadcasted_iota(I32, fields.shape, 1)
        fields = jnp.where(lane < width, fields, 0.0)
        if lanes > extent:
            fields = jnp.concatenate(
                [fields, jnp.zeros((fields.shape[0], lanes - extent), F32)], axis=1)
        return lined + pltpu.roll(fields, member * width, axis=1)

    lined = jnp.zeros((16, lanes), F32)
    if members <= 16:
        for member in range(members):
            lined = collect(member, lined, *where[member])
    else:
        lined = lax.fori_loop(
            0, members, lambda member, lined: collect(member, lined, payload_refs[0], member), lined)

    slot = lax.broadcasted_iota(I32, (1, lanes), 1)
    within = lax.rem(slot, width)
    target = lax.bitwise_xor(lax.div(within, capacity), parity)
    ray = lined[3 * depth:3 * depth + 1]
    count = lined[3 * depth + 1:3 * depth + 2]
    alive = jnp.logical_and(lax.rem(within, capacity).astype(F32) < count, slot < members * width)

    table = jnp.concatenate(
        [slot.astype(F32), ray, target.astype(F32), lined[2 * depth:3 * depth],
         jnp.zeros((5 - depth, lanes), F32)], axis=0)
    order = lax.broadcasted_iota(I32, (lanes, lanes), 0)
    earlier = (lax.broadcasted_iota(I32, (lanes, lanes), 1) < order).astype(F32)
    for ref, kind, copy in zip(drafts, wanted, copies):
        taken = alive if kind is None else jnp.logical_and(alive, target == kind)
        taken = taken.astype(F32)
        position = contract_lanes(jnp.broadcast_to(taken, (8, lanes)), earlier)[0:1]
        position = jnp.where(taken > 0.0, position, -1.0).astype(I32)
        choose = jnp.broadcast_to(position, (lanes, lanes)) == order
        packed = (contract_lanes(table, choose.astype(F32)) + 0.5).astype(I32)
        total = jnp.sum(taken, axis=1, keepdims=True).astype(I32)
        line = jnp.where(slot < total, packed[0:1], lanes)
        base = packed[1:2] if kind is not None else packed[1:2] + packed[2:3] * ray_tiles
        member = lax.div(packed[0:1], width) * tiles
        rows = [line, base * frames]
        rows += [(packed[3 + level:4 + level] + member) * frames for level in range(depth)]
        rows += [jnp.zeros((5 - depth, lanes), I32), jnp.broadcast_to(total, (1, lanes))]
        ref[...] = jnp.concatenate(rows, axis=0)
        copy.start()

    columns = lined.T
    step = 32
    for row in range(0, lanes, step):
        total = None
        for level in range(depth):
            offset = columns[row:row + step, level:level + 1]
            slope = columns[row:row + step, depth + level:depth + level + 1]
            middle, weights = row_taps(offset, slope, extent)
            first, pair = column_taps(offset, slope, extent)
            wide = [weight.astype(F32) for weight in weights]
            values = [middle] + wide + [first] + [weight.astype(F32) for weight in pair]
            at = level * (lanes + 8) + row
            for ref, value in zip(tables, values):
                ref[at:at + step, :] = value
            parts = (wide[0] + wide[1]) + wide[2]
            total = parts if total is None else total + parts
        summed[row:row + step, :] = total
    for ref in tables:
        blank = jnp.ones if ref.dtype == I32 else jnp.zeros
        for level in range(depth):
            at = level * (lanes + 8) + lanes
            ref[at:at + 8, :] = blank((8, extent), ref.dtype)

    tile = lax.broadcasted_iota(I32, (span * ray_tiles, lanes), 0).astype(F32)
    place = ray + (target * ray_tiles).astype(F32)
    place = jnp.where(alive, place, -1.0)
    hot = (jnp.broadcast_to(place, tile.shape) == tile).astype(F32)
    row_ref[...] = jnp.dot(hot, summed[...], precision=HIGHEST, preferred_element_type=F32)
    for copy in copies:
        copy.wait()


def column_kernel(sizes, offset_ref, slope_ref, voxel_ref, live_ref, out_ref):
    capacity, depth, frames = sizes
    tiles = out_ref.shape[0] // frames
    slots = offset_ref.shape[1]
    extent = out_ref.shape[1]
    offsets = offset_ref[...].T
    slopes = slope_ref[...].T
    within = lax.rem(lax.broadcasted_iota(I32, (1, slots), 1), capacity).astype(F32)
    alive = jnp.broadcast_to(within, (tiles, slots)) < per_slot(live_ref, slots, capacity)
    total = jnp.zeros((tiles, extent), F32)
    for level in range(depth):
        unused, pair = column_taps(
            offsets[:, level:level + 1], slopes[:, level:level + 1], extent)
        tile_of = jnp.broadcast_to(voxel_ref[level:level + 1, :], (tiles, slots))
        match = tile_of == lax.broadcasted_iota(I32, (tiles, slots), 0)
        hot = jnp.logical_and(match, alive).astype(F32).astype(BF16)
        for weight in pair:
            total += jnp.dot(hot, weight, preferred_element_type=F32)
    out_ref[...] = repeat_rows(1.0 / jnp.maximum(total, 1.0), frames)


def pick(values, index):
    numbers = lax.GatherDimensionNumbers(
        offset_dims=(), collapsed_slice_dims=(1,), start_index_map=(1,),
        operand_batching_dims=(0,), start_indices_batching_dims=(0,))
    return lax.gather(
        values, index[:, :, None], numbers, slice_sizes=(1, 1),
        mode=lax.GatherScatterMode.PROMISE_IN_BOUNDS)


def pack_pair(first, second):
    kind = jnp.int16 if first.dtype == I32 else BF16
    return jnp.concatenate([first, second], axis=0).astype(kind)


def spread(ref, row, frames):
    return ref[pl.ds(row, frames, stride=0), :]


def tile_at(start, frames):
    return pl.ds(pl.multiple_of(start, frames), frames)


def for_slots(slots, body):
    def some(step, carry):
        for place in range(CHUNK):
            body(step * CHUNK + place, place)
        return carry

    lax.fori_loop(0, lax.div(slots[7, 0] + (CHUNK - 1), CHUNK), some, 0)


def for_rows(rows, body):
    step = 128
    if rows <= 8 * step:
        for start in range(0, rows, step):
            body(pl.ds(start, step))
        return

    def some(number, carry):
        body(pl.ds(pl.multiple_of(number * step, step), step))
        return carry

    lax.fori_loop(0, rows // step, some, 0)


def forward_kernel(sizes, n_values, members, start_row, n_sums, slots, *refs):
    capacity, depth, frames = sizes
    value_refs, tables, refs = refs[:n_values], refs[n_values:n_values + 4], refs[n_values + 4:]
    start_ref = None
    if start_row is not None:
        start_ref, refs = refs[0], refs[1:]
    sum_refs, (out_ref, wide, second) = refs[:n_sums], refs[n_sums:]
    rows = wide.shape[0] // members
    stride = sum(ref.shape[0] for ref in value_refs) // members
    rays = second.shape[0]
    line_step = tables[0].shape[0] // depth

    base = 0
    for ref in value_refs:
        def widen(member, carry, ref=ref, base=base):
            at = (base + member) * rows
            start = member * stride
            if not isinstance(member, int):
                at, start = pl.multiple_of(at, rows), pl.multiple_of(start, 16)
            wide[pl.ds(at, rows), :] = ref[pl.ds(start, rows), :].astype(F32)
            return carry

        here = ref.shape[0] // stride
        if here <= 8:
            for member in range(here):
                widen(member, 0)
        else:
            lax.fori_loop(0, here, widen, 0)
        base += here
    second[...] = jnp.zeros_like(second)
    if start_ref is None:
        out_ref[...] = jnp.zeros_like(out_ref)
    else:
        out_ref[0:rays, :] = start_ref[start_row:start_row + rays, :]
    if n_sums:
        half = sum_refs[0].shape[0] // 2
        out_ref[rays:, :] = sum([ref[half:, :] for ref in sum_refs[1:]], sum_refs[0][half:, :])

    def one(slot, place):
        line = slots[0, slot]
        taps = []
        for start in range(0, depth, 2):
            levels = range(start, start + 2)
            values = [wide[tile_at(slots[2 + level, slot], frames), :] for level in levels]
            middles = [spread(tables[0], line + level * line_step, frames) for level in levels]
            lower = [
                pick(pack_pair(value, value), pack_pair(middle - 1, middle)).astype(F32)
                for value, middle in zip(values, middles)]
            upper = pick(
                pack_pair(*values), pack_pair(*[middle + 1 for middle in middles])).astype(F32)
            for which, pair in enumerate(lower):
                taps.append((pair[0:frames], pair[frames:2 * frames],
                             upper[which * frames:(which + 1) * frames]))
        total = None
        for level, three in enumerate(taps):
            for ref, tap in zip(tables[1:], three):
                term = spread(ref, line + level * line_step, frames) * tap
                total = term if total is None else total + term
        projection = (out_ref, second)[place % 2]
        projection[tile_at(slots[1, slot], frames), :] += total.astype(BF16).astype(F32)

    for_slots(slots, one)
    out_ref[0:rays, :] += second[...]


def residual_kernel(frames, n_own, projection_ref, sinogram_ref, *refs):
    own, refs, out_ref = refs[:n_own], refs[n_own:-1], refs[-1]
    rays = out_ref.shape[0]
    ray_tiles = rays // frames
    total = sum([ref[0:ray_tiles, :] for ref in own[1:]], own[0][0:ray_tiles, :])
    projection = projection_ref[...]
    if refs:
        projection = projection + refs[0][0:rays, :]
        total = total + refs[-1][rays:, :]
    weight = repeat_rows(1.0 / jnp.maximum(total, 1.0), frames)
    out_ref[...] = ((sinogram_ref[...].astype(F32) - projection) * weight).astype(BF16)


def backward_kernel(sizes, n_parts, has_start, split, slots, *refs):
    capacity, depth, frames = sizes
    part_refs, tables, refs = refs[:n_parts], refs[n_parts:n_parts + 3], refs[n_parts + 3:]
    start_ref = None
    if has_start:
        start_ref, refs = refs[0], refs[1:]
    outs = refs[:len(split)] if split else refs[:1]
    residual, banks = refs[len(outs)], refs[len(outs) + 1:]
    rays = part_refs[0].shape[0]
    line_step = tables[0].shape[0] // depth
    for place, ref in enumerate(part_refs):
        residual[place * rays:(place + 1) * rays, :] = ref[...].astype(F32)

    def clear(at):
        for place, bank in enumerate(banks):
            if place == 0 and has_start:
                bank[at, :] = start_ref[at, :]
            else:
                bank[at, :] = jnp.zeros((at.size, bank.shape[1]), F32)

    for_rows(banks[0].shape[0], clear)

    def one(slot, place):
        line = slots[0, slot]
        values = residual[tile_at(slots[1, slot], frames), :]
        twice = pack_pair(values, values)
        for level in range(depth):
            row = line + level * line_step
            first = spread(tables[0], row, frames)
            taps = pick(twice, pack_pair(first, first + 1)).astype(F32)
            term = (spread(tables[1], row, frames) * taps[0:frames]
                    + spread(tables[2], row, frames) * taps[frames:2 * frames])
            banks[level % len(banks)][tile_at(slots[2 + level, slot], frames), :] += term

    for_slots(slots, one)

    def total(at):
        return sum([bank[at, :] for bank in banks[1:]], banks[0][at, :])

    if split:
        for ref, members in zip(outs, split):
            rows = ref.shape[0] // len(members)
            for place, member in enumerate(members):
                ref[place * rows:(place + 1) * rows, :] = total(pl.ds(member * rows, rows)).astype(ref.dtype)
    else:
        def finish(at):
            outs[0][at, :] = total(at).astype(outs[0].dtype)

        for_rows(outs[0].shape[0], finish)


def join_kernel(*refs):
    out_ref, at = refs[-1], 0
    for ref in refs[:-1]:
        out_ref[at:at + ref.shape[0], :] = ref[...]
        at += ref.shape[0]


def combine_kernel(members, sum_ref, y_ref, *piece_refs):
    rows = piece_refs[0].shape[0]
    for place, (member, ref) in enumerate(zip(members, piece_refs)):
        mine = sum_ref[member * rows:(member + 1) * rows, :]
        ref[...] = (mine + y_ref[place * rows:(place + 1) * rows, :].astype(F32)).astype(ref.dtype)


def update_kernel(n_pieces, volume_ref, column_ref, *refs):
    back = refs[0][...]
    for ref in refs[1:n_pieces]:
        back = back + ref[...].astype(F32)
    volume = volume_ref[...] + column_ref[...] * back
    for ref in refs[n_pieces:]:
        ref[...] = volume.astype(ref.dtype)


def call(kernel, name, mib, in_specs, out_shape, *operands, scratch=()):
    one = not isinstance(out_shape, list)
    return pl.pallas_call(
        kernel,
        out_shape=out_shape,
        in_specs=in_specs,
        out_specs=VMEM if one else [
            SMEM if getattr(out, "memory_space", None) == pltpu.SMEM else VMEM for out in out_shape],
        scratch_shapes=list(scratch),
        compiler_params=pltpu.CompilerParams(vmem_limit_bytes=mib * 1024 * 1024),
        name=name,
        cost_estimate=pl.CostEstimate(flops=4 * 10**9, bytes_accessed=8 * 10**6, transcendentals=0),
    )(*operands)


def exchange(values, n_slab, distance, other_distance=None):
    far = (distance, distance if other_distance is None else other_distance)
    return lax.ppermute(
        values, "slab",
        [(device, device ^ far[device.bit_count() % 2]) for device in range(n_slab)])


def shards(sinogram, start_volume, slot_voxel, slot_ray, live_count, block_slope, block_offset):
    n_slab = lax.axis_size("slab")
    n_slots, depth = slot_voxel.shape
    capacity = n_slots // n_slab
    ray_tiles, frames, extent = sinogram.shape
    voxel_tiles = start_volume.shape[0]
    rows = voxel_tiles * frames
    sizes = (capacity, depth, frames)
    paired = n_slab == 16
    span = 2 if paired else 1
    n_bank = 2 if paired else 1
    shape = jax.ShapeDtypeStruct
    n_rays = ray_tiles * frames
    volume = start_volume.reshape(rows, extent)
    sino = sinogram.reshape(n_rays, extent)
    slots_by_depth = (block_offset.T, block_slope.T, slot_voxel.T)
    live = live_count.reshape(1, n_slab)
    height = -(-(7 * depth + 2) // 16) * 16 * (n_slots // extent)
    operands = (volume, *slots_by_depth, slot_ray.reshape(1, n_slots), live)
    payload = call(
        functools.partial(pack_kernel, capacity), "pack", 16, [HBM] * 6,
        shape((rows + height, extent), BF16),
        *[pltpu.with_memory_space_constraint(operand, pltpu.HBM) for operand in operands],
        scratch=[pltpu.VMEM(operand.shape, operand.dtype) for operand in operands]
        + [pltpu.SemaphoreType.DMA((6,))])

    def setup(payloads, members, wanted, after=None):
        lanes = -(-members * span * capacity // 128) * 128
        lines = depth * (lanes + 8)
        table = [shape((lines, extent), I32)] + [shape((lines, extent), F32)] * 3
        table += [shape((lines, extent), I32)] + [shape((lines, extent), F32)] * 2
        n = len(wanted)
        out = [pltpu.SMEM((8, lanes), I32)] * n + [shape((span * ray_tiles, extent), F32)] + table
        waits = [] if after is None else [after]
        found = call(
            functools.partial(setup_kernel, len(payloads), members,
                              sum(one.shape[0] for one in payloads) // members, span, sizes,
                              voxel_tiles, wanted),
            "setup", 24, [VMEM] * len(payloads) + [ANY] * len(waits), out, *payloads, *waits,
            scratch=[pltpu.VMEM((8, lanes), I32)] * n
            + [pltpu.SemaphoreType.DMA((n,)), pltpu.VMEM((lanes, extent), F32)])
        return found[:n], found[n], found[n + 1:n + 5], found[n + 5:]

    def forward(slots, values, members, table, n_out, start=None, start_row=None, sums=()):
        operands = [pltpu.with_memory_space_constraint(slots, pltpu.SMEM), *values, *table] + ([] if start is None else [start]) + list(sums)
        extra = ray_tiles if sums else 0
        return call(
            functools.partial(forward_kernel, sizes, len(values), members, start_row, len(sums)),
            "forward", 16 if paired else 32, [SMEM] + [VMEM] * (len(operands) - 1),
            shape((n_out + extra, extent), F32), *operands,
            scratch=[pltpu.VMEM((members * rows, extent), F32), pltpu.VMEM((n_out, extent), F32)])

    def residual_of(projection, row_sums, *sibling):
        operands = [projection, sino, *row_sums, *sibling]
        return call(
            functools.partial(residual_kernel, frames, len(row_sums)), "residual", 16,
            [VMEM] * len(operands), shape((n_rays, extent), BF16), *operands)

    def backward(slots, parts, members, table, kind, start=None, split=()):
        operands = [pltpu.with_memory_space_constraint(slots, pltpu.SMEM), *parts, *table] + ([] if start is None else [start])
        return call(
            functools.partial(backward_kernel, sizes, len(parts), start is not None, split),
            "backward", 16 if paired else 32, [SMEM] + [VMEM] * (len(operands) - 1),
            [shape((len(some) * rows, extent), each) for some, each in zip(split, kind)]
            if split else shape((members * rows, extent), kind), *operands,
            scratch=[pltpu.VMEM((len(parts) * n_rays, extent), F32)]
            + [pltpu.VMEM((members * rows, extent), F32)] * n_bank)

    def join(*parts):
        total = sum(part.shape[0] for part in parts)
        return call(join_kernel, "join", 16, [VMEM] * len(parts), shape((total, extent), BF16), *parts)

    def update(volume, pieces, last):
        out = [shape((rows, extent), F32)] + ([] if last else [shape((rows, extent), BF16)])
        return call(
            functools.partial(update_kernel, len(pieces)), "update", 16,
            [VMEM] * (2 + len(pieces)), out, volume, column_weight, *pieces)

    column_weight = call(
        functools.partial(column_kernel, sizes), "column_weight", 16, [VMEM] * 4,
        shape((rows, extent), F32), *slots_by_depth, live)

    for sweep in range(ITERS):
        last = sweep + 1 == ITERS
        if paired:
            place_1, place_2, place_3, across = [
                exchange(payload, n_slab, *pair) for pair in ((9, 3), (5, 9), (12, 10), (15, 15))]
            z_part = join(payload, place_1, place_2)
            y_part = exchange(z_part, n_slab, 3, 5)
            along_z, along_y = (z_part, place_3), (y_part, across)
            if sweep == 0:
                (z_list,), z_rows, z_forward, z_backward = setup(along_z, 4, (None,))
            both = forward(z_list, along_z, 4, z_forward, 2 * n_rays)
            if sweep == 0:
                (own_list, other_list), y_rows, y_forward, y_backward = setup(
                    along_y, 4, (0, 1), after=both)
            other = exchange(
                forward(other_list, along_y, 4, y_forward, n_rays, both, n_rays,
                        (z_rows, y_rows) if sweep == 0 else ()), n_slab, 1)
            if sweep == 0:
                first_other = other
            own = forward(own_list, along_y, 4, y_forward, n_rays, both, 0)
            residual = residual_of(own, (z_rows, y_rows), other, first_other)
            other_residual = exchange(residual, n_slab, 1)
            y_sum = backward(own_list, [residual], 4, y_backward, F32)
            far_sum, near_sum = backward(
                other_list, [other_residual], 4, y_backward, (BF16, BF16), y_sum, ((1, 3), (0, 2)))
            far_part, near_part = exchange(far_sum, n_slab, 3, 5), exchange(near_sum, n_slab, 3, 5)
            z_sum = backward(z_list, [residual, other_residual], 4, z_backward, F32)
            piece = shape((rows, extent), BF16)
            piece_1, piece_3 = call(
                functools.partial(combine_kernel, (1, 3)), "combine", 16, [VMEM] * 2,
                [piece, piece], z_sum, far_part)
            got = [exchange(piece_1, n_slab, 9, 3), exchange(piece_3, n_slab, 12, 10)]
            own_piece, piece_2 = call(
                functools.partial(combine_kernel, (0, 2)), "combine", 16, [VMEM] * 2,
                [shape((rows, extent), F32), piece], z_sum, near_part)
            pieces = [own_piece, exchange(piece_2, n_slab, 5, 9), *got]
        else:
            everyone = lax.all_gather(payload, "slab", axis=0, tiled=True)
            if sweep == 0:
                (slots,), row_sums, to_rays, to_voxels = setup((everyone,), n_slab, (None,))
            projection = forward(slots, (everyone,), n_slab, to_rays, n_rays)
            residual = residual_of(projection, (row_sums,))
            sums = backward(slots, [residual], n_slab, to_voxels, BF16)
            parts = lax.all_to_all(
                sums.reshape(n_slab, rows, extent), "slab", split_axis=0, concat_axis=0, tiled=True)
            pieces = [jnp.sum(parts.astype(F32), axis=0)]
        volume, *rounded = update(volume, pieces, last)
        if not last:
            payload = rounded[0]
    return volume.reshape(start_volume.shape)


def solution(mesh):
    in_specs = (
        P(("scan", "slab"), None, None),
        P(("scan", "slab"), None, None),
        P(("scan", "slab"), None),
        P(("scan", "slab")),
        P(("scan", "slab")),
        P(("scan", "slab"), None),
        P(("scan", "slab"), None),
    )
    out_specs = P(("scan", "slab"), None, None)
    return jax.shard_map(shards, mesh=mesh, in_specs=in_specs, out_specs=out_specs, check_vma=False)
```

```python
import functools

import jax
import jax.numpy as jnp
from jax import lax
from jax.experimental import pallas as pl
from jax.experimental.pallas import tpu as pltpu
from jax.sharding import PartitionSpec as P

ITERS = 2
CHUNK = 16
F32 = jnp.float32
BF16 = jnp.bfloat16
I32 = jnp.int32
HIGHEST = lax.Precision.HIGHEST
VMEM = pl.BlockSpec(memory_space=pltpu.VMEM)
ANY = pl.BlockSpec(memory_space=pl.ANY)
SMEM = pl.BlockSpec(memory_space=pltpu.SMEM)
HBM = pl.BlockSpec(memory_space=pltpu.HBM)


def hat(ray, centre):
    return jnp.maximum(0.0, 1.0 - jnp.abs(ray - centre)).astype(BF16)


def row_taps(offset, slope, extent):
    shape = (offset.shape[0], extent)
    ray = lax.broadcasted_iota(I32, shape, 1).astype(F32)
    inverse = jnp.broadcast_to(1.0 / slope, shape)
    offset = jnp.broadcast_to(offset, shape)
    slope = jnp.broadcast_to(slope, shape)
    middle = jnp.floor((ray - offset) * inverse + 0.5)
    middle = jnp.minimum(jnp.maximum(middle, 1.0), extent - 2.0)
    weights = [hat(ray, offset + slope * (middle + step)) for step in (-1.0, 0.0, 1.0)]
    return middle.astype(I32), weights


def column_taps(offset, slope, extent):
    shape = (offset.shape[0], extent)
    voxel = lax.broadcasted_iota(I32, shape, 1).astype(F32)
    centre = jnp.broadcast_to(offset, shape) + jnp.broadcast_to(slope, shape) * voxel
    first = jnp.minimum(jnp.maximum(jnp.floor(centre), 0.0), extent - 2.0)
    weights = [hat(first + step, centre) for step in (0.0, 1.0)]
    return first.astype(I32), weights


def repeat_rows(values, times):
    return jnp.concatenate(
        [jnp.broadcast_to(values[row:row + 1, :], (times, values.shape[1]))
         for row in range(values.shape[0])], axis=0)


def contract_lanes(left, right):
    return lax.dot_general(
        left.astype(BF16), right.astype(BF16), (((1,), (1,)), ((), ())), preferred_element_type=F32)


def per_slot(live_ref, slots, capacity):
    targets = live_ref.shape[1]
    slot = lax.broadcasted_iota(I32, (targets, slots), 1)
    owner = lax.broadcasted_iota(I32, (targets, slots), 0)
    expand = (lax.div(slot, capacity) == owner).astype(F32)
    return jnp.dot(live_ref[...].astype(F32), expand, precision=HIGHEST, preferred_element_type=F32)


def pack_kernel(capacity, partners, *refs):
    sources, outs, loaded, arrived, packed = refs[:6], refs[6:-8], refs[-8:-2], refs[-2], refs[-1]
    copies = [
        pltpu.make_async_copy(source, ref, arrived.at[place])
        for place, (source, ref) in enumerate(zip(sources, loaded))]
    for copy in copies:
        copy.start()
    for copy in copies:
        copy.wait()
    volume_ref, offset_ref, slope_ref, voxel_ref, ray_ref, live_ref = loaded
    rows, extent = volume_ref.shape
    slots = ray_ref.shape[1]
    fields = []
    for ref in (offset_ref, slope_ref):
        left = ref[...]
        for addend in range(3):
            part = left.astype(BF16).astype(F32)
            fields.append(part)
            left = left - part
    fields.append(voxel_ref[...].astype(F32))
    fields.append(ray_ref[...].astype(F32))
    fields.append(per_slot(live_ref, slots, capacity))
    used = sum(field.shape[0] for field in fields)
    fields.append(jnp.zeros((-used % 16, slots), F32))
    fields = jnp.concatenate(fields, axis=0)
    height = fields.shape[0]
    for part in range(slots // extent):
        at = pl.ds(part * height, height)
        packed[at, :] = fields[:, part * extent:(part + 1) * extent].astype(BF16)
    me = lax.axis_index("slab").astype(I32)
    odd = sum(lax.bitwise_and(lax.shift_right_logical(me, bit), 1) for bit in range(4)) % 2
    for place, out_ref in enumerate(outs):
        out_ref[0:rows, :] = volume_ref[...].astype(BF16)
        if not partners:
            out_ref[rows:, :] = packed[...]
            continue
        distance = jnp.where(odd == 0, partners[place][0], partners[place][1])
        part = lax.div(lax.bitwise_xor(me, distance) * capacity, extent)
        out_ref[rows:, :] = packed[pl.ds(pl.multiple_of(part * height, 16), height), :]


def setup_kernel(n_payloads, members, stride, span, sizes, tiles, wanted, *refs):
    payload_refs, refs = refs[:n_payloads], refs[-(2 * len(wanted) + 10):]
    where = [(ref, index) for ref in payload_refs for index in range(ref.shape[0] // stride)]
    list_refs, row_ref, tables = refs[:len(wanted)], refs[len(wanted)], refs[len(wanted) + 1:-len(wanted) - 2]
    drafts, arrived, summed = refs[-len(wanted) - 2:-2], refs[-2], refs[-1]
    copies = [
        pltpu.make_async_copy(draft, ref, arrived.at[place])
        for place, (draft, ref) in enumerate(zip(drafts, list_refs))]
    capacity, depth, frames = sizes
    width = span * capacity
    extent = row_ref.shape[1]
    ray_tiles = row_ref.shape[0] // span
    height = -(-(7 * depth + 2) // 16) * 16
    lanes = drafts[0].shape[1]
    me = lax.axis_index("slab").astype(I32)
    parity = lax.rem(me, span)
    first_slot = (me - parity) * capacity
    part = 0 if n_payloads > 1 else lax.div(first_slot, extent)
    shift = lax.rem(extent - lax.rem(first_slot, extent), extent)

    def collect(member, lined, payload_ref, within):
        at = within * stride + tiles * frames + part * height
        raw = payload_ref[pl.ds(pl.multiple_of(at, 16), height), :].astype(F32)
        offset = (raw[0:depth] + raw[depth:2 * depth]) + raw[2 * depth:3 * depth]
        slope = (raw[3 * depth:4 * depth] + raw[4 * depth:5 * depth]) + raw[5 * depth:6 * depth]
        fields = jnp.concatenate(
            [offset, slope, raw[6 * depth:7 * depth + 2],
             jnp.zeros((16 - 3 * depth - 2, extent), F32)], axis=0)
        fields = pltpu.roll(fields, shift, axis=1)
        lane = lax.broadcasted_iota(I32, fields.shape, 1)
        fields = jnp.where(lane < width, fields, 0.0)
        if lanes > extent:
            fields = jnp.concatenate(
                [fields, jnp.zeros((fields.shape[0], lanes - extent), F32)], axis=1)
        return lined + pltpu.roll(fields, member * width, axis=1)

    lined = jnp.zeros((16, lanes), F32)
    if members <= 16:
        for member in range(members):
            lined = collect(member, lined, *where[member])
    else:
        lined = lax.fori_loop(
            0, members, lambda member, lined: collect(member, lined, payload_refs[0], member), lined)

    slot = lax.broadcasted_iota(I32, (1, lanes), 1)
    within = lax.rem(slot, width)
    target = lax.bitwise_xor(lax.div(within, capacity), parity)
    ray = lined[3 * depth:3 * depth + 1]
    count = lined[3 * depth + 1:3 * depth + 2]
    alive = jnp.logical_and(lax.rem(within, capacity).astype(F32) < count, slot < members * width)

    table = jnp.concatenate(
        [slot.astype(F32), ray, target.astype(F32), lined[2 * depth:3 * depth],
         jnp.zeros((5 - depth, lanes), F32)], axis=0)
    order = lax.broadcasted_iota(I32, (lanes, lanes), 0)
    earlier = (lax.broadcasted_iota(I32, (lanes, lanes), 1) < order).astype(F32)
    for ref, kind, copy in zip(drafts, wanted, copies):
        taken = alive if kind is None else jnp.logical_and(alive, target == kind)
        taken = taken.astype(F32)
        position = contract_lanes(jnp.broadcast_to(taken, (8, lanes)), earlier)[0:1]
        position = jnp.where(taken > 0.0, position, -1.0).astype(I32)
        choose = jnp.broadcast_to(position, (lanes, lanes)) == order
        packed = (contract_lanes(table, choose.astype(F32)) + 0.5).astype(I32)
        total = jnp.sum(taken, axis=1, keepdims=True).astype(I32)
        line = jnp.where(slot < total, packed[0:1], lanes)
        base = packed[1:2] if kind is not None else packed[1:2] + packed[2:3] * ray_tiles
        member = lax.div(packed[0:1], width) * tiles
        rows = [line, base * frames]
        rows += [(packed[3 + level:4 + level] + member) * frames for level in range(depth)]
        rows += [jnp.zeros((5 - depth, lanes), I32), jnp.broadcast_to(total, (1, lanes))]
        ref[...] = jnp.concatenate(rows, axis=0)
        copy.start()

    columns = lined.T
    step = 32
    for row in range(0, lanes, step):
        total = None
        for level in range(depth):
            offset = columns[row:row + step, level:level + 1]
            slope = columns[row:row + step, depth + level:depth + level + 1]
            middle, weights = row_taps(offset, slope, extent)
            first, pair = column_taps(offset, slope, extent)
            wide = [weight.astype(F32) for weight in weights]
            values = [middle] + wide + [first] + [weight.astype(F32) for weight in pair]
            at = level * (lanes + 8) + row
            for ref, value in zip(tables, values):
                ref[at:at + step, :] = value
            parts = (wide[0] + wide[1]) + wide[2]
            total = parts if total is None else total + parts
        summed[row:row + step, :] = total
    for ref in tables:
        blank = jnp.ones if ref.dtype == I32 else jnp.zeros
        for level in range(depth):
            at = level * (lanes + 8) + lanes
            ref[at:at + 8, :] = blank((8, extent), ref.dtype)

    tile = lax.broadcasted_iota(I32, (span * ray_tiles, lanes), 0).astype(F32)
    place = ray + (target * ray_tiles).astype(F32)
    place = jnp.where(alive, place, -1.0)
    hot = (jnp.broadcast_to(place, tile.shape) == tile).astype(F32)
    row_ref[...] = jnp.dot(hot, summed[...], precision=HIGHEST, preferred_element_type=F32)
    for copy in copies:
        copy.wait()


def column_kernel(sizes, offset_ref, slope_ref, voxel_ref, live_ref, out_ref):
    capacity, depth, frames = sizes
    tiles = out_ref.shape[0] // frames
    slots = offset_ref.shape[1]
    extent = out_ref.shape[1]
    offsets = offset_ref[...].T
    slopes = slope_ref[...].T
    within = lax.rem(lax.broadcasted_iota(I32, (1, slots), 1), capacity).astype(F32)
    alive = jnp.broadcast_to(within, (tiles, slots)) < per_slot(live_ref, slots, capacity)
    total = jnp.zeros((tiles, extent), F32)
    for level in range(depth):
        unused, pair = column_taps(
            offsets[:, level:level + 1], slopes[:, level:level + 1], extent)
        tile_of = jnp.broadcast_to(voxel_ref[level:level + 1, :], (tiles, slots))
        match = tile_of == lax.broadcasted_iota(I32, (tiles, slots), 0)
        hot = jnp.logical_and(match, alive).astype(F32).astype(BF16)
        for weight in pair:
            total += jnp.dot(hot, weight, preferred_element_type=F32)
    out_ref[...] = repeat_rows(1.0 / jnp.maximum(total, 1.0), frames)


def pick(values, index):
    numbers = lax.GatherDimensionNumbers(
        offset_dims=(), collapsed_slice_dims=(1,), start_index_map=(1,),
        operand_batching_dims=(0,), start_indices_batching_dims=(0,))
    return lax.gather(
        values, index[:, :, None], numbers, slice_sizes=(1, 1),
        mode=lax.GatherScatterMode.PROMISE_IN_BOUNDS)


def pack_pair(first, second):
    kind = jnp.int16 if first.dtype == I32 else BF16
    return jnp.concatenate([first, second], axis=0).astype(kind)


def spread(ref, row, frames):
    return ref[pl.ds(row, frames, stride=0), :]


def tile_at(start, frames):
    return pl.ds(pl.multiple_of(start, frames), frames)


def for_slots(slots, body):
    def some(step, carry):
        for place in range(CHUNK):
            body(step * CHUNK + place, place)
        return carry

    lax.fori_loop(0, lax.div(slots[7, 0] + (CHUNK - 1), CHUNK), some, 0)


def for_rows(rows, body):
    step = 128
    if rows <= 8 * step:
        for start in range(0, rows, step):
            body(pl.ds(start, step))
        return

    def some(number, carry):
        body(pl.ds(pl.multiple_of(number * step, step), step))
        return carry

    lax.fori_loop(0, rows // step, some, 0)


def forward_kernel(sizes, n_values, members, start_row, n_sums, slots, *refs):
    capacity, depth, frames = sizes
    value_refs, tables, refs = refs[:n_values], refs[n_values:n_values + 4], refs[n_values + 4:]
    start_ref = None
    if start_row is not None:
        start_ref, refs = refs[0], refs[1:]
    sum_refs, (out_ref, wide, second) = refs[:n_sums], refs[n_sums:]
    rows = wide.shape[0] // members
    stride = sum(ref.shape[0] for ref in value_refs) // members
    rays = second.shape[0]
    line_step = tables[0].shape[0] // depth

    base = 0
    for ref in value_refs:
        def widen(member, carry, ref=ref, base=base):
            at = (base + member) * rows
            start = member * stride
            if not isinstance(member, int):
                at, start = pl.multiple_of(at, rows), pl.multiple_of(start, 16)
            wide[pl.ds(at, rows), :] = ref[pl.ds(start, rows), :].astype(F32)
            return carry

        here = ref.shape[0] // stride
        if here <= 8:
            for member in range(here):
                widen(member, 0)
        else:
            lax.fori_loop(0, here, widen, 0)
        base += here
    second[...] = jnp.zeros_like(second)
    if start_ref is None:
        out_ref[...] = jnp.zeros_like(out_ref)
    else:
        out_ref[0:rays, :] = start_ref[start_row:start_row + rays, :]
    if n_sums:
        half = sum_refs[0].shape[0] // 2
        out_ref[rays:, :] = sum([ref[half:, :] for ref in sum_refs[1:]], sum_refs[0][half:, :])

    def one(slot, place):
        line = slots[0, slot]
        taps = []
        for start in range(0, depth, 2):
            levels = range(start, start + 2)
            values = [wide[tile_at(slots[2 + level, slot], frames), :] for level in levels]
            middles = [spread(tables[0], line + level * line_step, frames) for level in levels]
            lower = [
                pick(pack_pair(value, value), pack_pair(middle - 1, middle)).astype(F32)
                for value, middle in zip(values, middles)]
            upper = pick(
                pack_pair(*values), pack_pair(*[middle + 1 for middle in middles])).astype(F32)
            for which, pair in enumerate(lower):
                taps.append((pair[0:frames], pair[frames:2 * frames],
                             upper[which * frames:(which + 1) * frames]))
        total = None
        for level, three in enumerate(taps):
            for ref, tap in zip(tables[1:], three):
                term = spread(ref, line + level * line_step, frames) * tap
                total = term if total is None else total + term
        projection = (out_ref, second)[place % 2]
        projection[tile_at(slots[1, slot], frames), :] += total.astype(BF16).astype(F32)

    for_slots(slots, one)
    out_ref[0:rays, :] += second[...]


def residual_kernel(frames, n_own, projection_ref, sinogram_ref, *refs):
    own, refs, out_ref = refs[:n_own], refs[n_own:-1], refs[-1]
    rays = out_ref.shape[0]
    ray_tiles = rays // frames
    total = sum([ref[0:ray_tiles, :] for ref in own[1:]], own[0][0:ray_tiles, :])
    projection = projection_ref[...]
    if refs:
        projection = projection + refs[0][0:rays, :]
        total = total + refs[-1][rays:, :]
    weight = repeat_rows(1.0 / jnp.maximum(total, 1.0), frames)
    out_ref[...] = ((sinogram_ref[...].astype(F32) - projection) * weight).astype(BF16)


def backward_kernel(sizes, n_parts, has_start, split, slots, *refs):
    capacity, depth, frames = sizes
    part_refs, tables, refs = refs[:n_parts], refs[n_parts:n_parts + 3], refs[n_parts + 3:]
    start_ref = None
    if has_start:
        start_ref, refs = refs[0], refs[1:]
    outs = refs[:len(split)] if split else refs[:1]
    residual, banks = refs[len(outs)], refs[len(outs) + 1:]
    rays = part_refs[0].shape[0]
    line_step = tables[0].shape[0] // depth
    for place, ref in enumerate(part_refs):
        residual[place * rays:(place + 1) * rays, :] = ref[...].astype(F32)

    def clear(at):
        for place, bank in enumerate(banks):
            if place == 0 and has_start:
                bank[at, :] = start_ref[at, :]
            else:
                bank[at, :] = jnp.zeros((at.size, bank.shape[1]), F32)

    for_rows(banks[0].shape[0], clear)

    def one(slot, place):
        line = slots[0, slot]
        values = residual[tile_at(slots[1, slot], frames), :]
        twice = pack_pair(values, values)
        for level in range(depth):
            row = line + level * line_step
            first = spread(tables[0], row, frames)
            taps = pick(twice, pack_pair(first, first + 1)).astype(F32)
            term = (spread(tables[1], row, frames) * taps[0:frames]
                    + spread(tables[2], row, frames) * taps[frames:2 * frames])
            banks[level % len(banks)][tile_at(slots[2 + level, slot], frames), :] += term

    for_slots(slots, one)

    def total(at):
        return sum([bank[at, :] for bank in banks[1:]], banks[0][at, :])

    if split:
        for ref, members in zip(outs, split):
            rows = ref.shape[0] // len(members)
            for place, member in enumerate(members):
                ref[place * rows:(place + 1) * rows, :] = total(pl.ds(member * rows, rows)).astype(ref.dtype)
    else:
        def finish(at):
            outs[0][at, :] = total(at).astype(outs[0].dtype)

        for_rows(outs[0].shape[0], finish)


def join_kernel(*refs):
    out_ref, at = refs[-1], 0
    for ref in refs[:-1]:
        out_ref[at:at + ref.shape[0], :] = ref[...]
        at += ref.shape[0]


def combine_kernel(members, sum_ref, y_ref, *piece_refs):
    rows = piece_refs[0].shape[0]
    for place, (member, ref) in enumerate(zip(members, piece_refs)):
        mine = sum_ref[member * rows:(member + 1) * rows, :]
        ref[...] = (mine + y_ref[place * rows:(place + 1) * rows, :].astype(F32)).astype(ref.dtype)


def update_kernel(n_pieces, volume_ref, column_ref, *refs):
    back = refs[0][...]
    for ref in refs[1:n_pieces]:
        back = back + ref[...].astype(F32)
    volume = volume_ref[...] + column_ref[...] * back
    for ref in refs[n_pieces:]:
        ref[...] = volume.astype(ref.dtype)


def call(kernel, name, mib, in_specs, out_shape, *operands, scratch=()):
    one = not isinstance(out_shape, list)
    return pl.pallas_call(
        kernel,
        out_shape=out_shape,
        in_specs=in_specs,
        out_specs=VMEM if one else [
            SMEM if getattr(out, "memory_space", None) == pltpu.SMEM else VMEM for out in out_shape],
        scratch_shapes=list(scratch),
        compiler_params=pltpu.CompilerParams(vmem_limit_bytes=mib * 1024 * 1024),
        name=name,
        cost_estimate=pl.CostEstimate(flops=4 * 10**9, bytes_accessed=8 * 10**6, transcendentals=0),
    )(*operands)


def exchange(values, n_slab, distance, other_distance=None):
    far = (distance, distance if other_distance is None else other_distance)
    return lax.ppermute(
        values, "slab",
        [(device, device ^ far[device.bit_count() % 2]) for device in range(n_slab)])


def shards(sinogram, start_volume, slot_voxel, slot_ray, live_count, block_slope, block_offset):
    n_slab = lax.axis_size("slab")
    n_slots, depth = slot_voxel.shape
    capacity = n_slots // n_slab
    ray_tiles, frames, extent = sinogram.shape
    voxel_tiles = start_volume.shape[0]
    rows = voxel_tiles * frames
    sizes = (capacity, depth, frames)
    paired = n_slab == 16
    span = 2 if paired else 1
    n_bank = 2 if paired else 1
    shape = jax.ShapeDtypeStruct
    n_rays = ray_tiles * frames
    volume = start_volume.reshape(rows, extent)
    sino = sinogram.reshape(n_rays, extent)
    slots_by_depth = (block_offset.T, block_slope.T, slot_voxel.T)
    live = live_count.reshape(1, n_slab)
    height = -(-(7 * depth + 2) // 16) * 16 * (n_slots // extent)
    operands = (volume, *slots_by_depth, slot_ray.reshape(1, n_slots), live)
    partners = ((0, 0), (9, 3), (5, 9), (12, 10), (15, 15)) if paired else ()
    size = rows + height // (n_slots // extent if paired else 1)
    payloads = call(
        functools.partial(pack_kernel, capacity, partners), "pack", 16, [HBM] * 6,
        [shape((size, extent), BF16)] * max(1, len(partners)),
        *[pltpu.with_memory_space_constraint(operand, pltpu.HBM) for operand in operands],
        scratch=[pltpu.VMEM(operand.shape, operand.dtype) for operand in operands]
        + [pltpu.SemaphoreType.DMA((6,)), pltpu.VMEM((height, extent), BF16)])
    payload = payloads[0]

    def setup(payloads, members, wanted, after=None):
        lanes = -(-members * span * capacity // 128) * 128
        lines = depth * (lanes + 8)
        table = [shape((lines, extent), I32)] + [shape((lines, extent), F32)] * 3
        table += [shape((lines, extent), I32)] + [shape((lines, extent), F32)] * 2
        n = len(wanted)
        out = [pltpu.SMEM((8, lanes), I32)] * n + [shape((span * ray_tiles, extent), F32)] + table
        waits = [] if after is None else [after]
        found = call(
            functools.partial(setup_kernel, len(payloads), members,
                              sum(one.shape[0] for one in payloads) // members, span, sizes,
                              voxel_tiles, wanted),
            "setup", 24, [VMEM] * len(payloads) + [ANY] * len(waits), out, *payloads, *waits,
            scratch=[pltpu.VMEM((8, lanes), I32)] * n
            + [pltpu.SemaphoreType.DMA((n,)), pltpu.VMEM((lanes, extent), F32)])
        return found[:n], found[n], found[n + 1:n + 5], found[n + 5:]

    def forward(slots, values, members, table, n_out, start=None, start_row=None, sums=()):
        operands = [pltpu.with_memory_space_constraint(slots, pltpu.SMEM), *values, *table] + ([] if start is None else [start]) + list(sums)
        extra = ray_tiles if sums else 0
        return call(
            functools.partial(forward_kernel, sizes, len(values), members, start_row, len(sums)),
            "forward", 16 if paired else 32, [SMEM] + [VMEM] * (len(operands) - 1),
            shape((n_out + extra, extent), F32), *operands,
            scratch=[pltpu.VMEM((members * rows, extent), F32), pltpu.VMEM((n_out, extent), F32)])

    def residual_of(projection, row_sums, *sibling):
        operands = [projection, sino, *row_sums, *sibling]
        return call(
            functools.partial(residual_kernel, frames, len(row_sums)), "residual", 16,
            [VMEM] * len(operands), shape((n_rays, extent), BF16), *operands)

    def backward(slots, parts, members, table, kind, start=None, split=()):
        operands = [pltpu.with_memory_space_constraint(slots, pltpu.SMEM), *parts, *table] + ([] if start is None else [start])
        return call(
            functools.partial(backward_kernel, sizes, len(parts), start is not None, split),
            "backward", 16 if paired else 32, [SMEM] + [VMEM] * (len(operands) - 1),
            [shape((len(some) * rows, extent), each) for some, each in zip(split, kind)]
            if split else shape((members * rows, extent), kind), *operands,
            scratch=[pltpu.VMEM((len(parts) * n_rays, extent), F32)]
            + [pltpu.VMEM((members * rows, extent), F32)] * n_bank)

    def join(*parts):
        total = sum(part.shape[0] for part in parts)
        return call(join_kernel, "join", 16, [VMEM] * len(parts), shape((total, extent), BF16), *parts)

    def update(volume, pieces, last):
        out = [shape((rows, extent), F32)] + ([] if last else [shape((rows, extent), BF16)])
        return call(
            functools.partial(update_kernel, len(pieces)), "update", 16,
            [VMEM] * (2 + len(pieces)), out, volume, column_weight, *pieces)

    column_weight = call(
        functools.partial(column_kernel, sizes), "column_weight", 16, [VMEM] * 4,
        shape((rows, extent), F32), *slots_by_depth, live)

    for sweep in range(ITERS):
        last = sweep + 1 == ITERS
        if paired:
            place_1, place_2, place_3, across = [
                exchange(one, n_slab, *pair) for one, pair in zip(payloads[1:], partners[1:])]
            z_part = join(payload, place_1, place_2)
            y_part = exchange(z_part, n_slab, 3, 5)
            along_z, along_y = (z_part, place_3), (y_part, across)
            if sweep == 0:
                (z_list,), z_rows, z_forward, z_backward = setup(along_z, 4, (None,))
            both = forward(z_list, along_z, 4, z_forward, 2 * n_rays)
            if sweep == 0:
                (own_list, other_list), y_rows, y_forward, y_backward = setup(
                    along_y, 4, (0, 1), after=both)
            other = exchange(
                forward(other_list, along_y, 4, y_forward, n_rays, both, n_rays,
                        (z_rows, y_rows) if sweep == 0 else ()), n_slab, 1)
            if sweep == 0:
                first_other = other
            own = forward(own_list, along_y, 4, y_forward, n_rays, both, 0)
            residual = residual_of(own, (z_rows, y_rows), other, first_other)
            other_residual = exchange(residual, n_slab, 1)
            y_sum = backward(own_list, [residual], 4, y_backward, F32)
            far_sum, near_sum = backward(
                other_list, [other_residual], 4, y_backward, (BF16, BF16), y_sum, ((1, 3), (0, 2)))
            far_part, near_part = exchange(far_sum, n_slab, 3, 5), exchange(near_sum, n_slab, 3, 5)
            z_sum = backward(z_list, [residual, other_residual], 4, z_backward, F32)
            piece = shape((rows, extent), BF16)
            piece_1, piece_3 = call(
                functools.partial(combine_kernel, (1, 3)), "combine", 16, [VMEM] * 2,
                [piece, piece], z_sum, far_part)
            got = [exchange(piece_1, n_slab, 9, 3), exchange(piece_3, n_slab, 12, 10)]
            own_piece, piece_2 = call(
                functools.partial(combine_kernel, (0, 2)), "combine", 16, [VMEM] * 2,
                [shape((rows, extent), F32), piece], z_sum, near_part)
            pieces = [own_piece, exchange(piece_2, n_slab, 5, 9), *got]
        else:
            everyone = lax.all_gather(payload, "slab", axis=0, tiled=True)
            if sweep == 0:
                (slots,), row_sums, to_rays, to_voxels = setup((everyone,), n_slab, (None,))
            projection = forward(slots, (everyone,), n_slab, to_rays, n_rays)
            residual = residual_of(projection, (row_sums,))
            sums = backward(slots, [residual], n_slab, to_voxels, BF16)
            parts = lax.all_to_all(
                sums.reshape(n_slab, rows, extent), "slab", split_axis=0, concat_axis=0, tiled=True)
            pieces = [jnp.sum(parts.astype(F32), axis=0)]
        volume, *rounded = update(volume, pieces, last)
        if not last:
            payload = rounded[0]
            payloads = [payload] * (1 + len(partners))
    return volume.reshape(start_volume.shape)


def solution(mesh):
    in_specs = (
        P(("scan", "slab"), None, None),
        P(("scan", "slab"), None, None),
        P(("scan", "slab"), None),
        P(("scan", "slab")),
        P(("scan", "slab")),
        P(("scan", "slab"), None),
        P(("scan", "slab"), None),
    )
    out_specs = P(("scan", "slab"), None, None)
    return jax.shard_map(shards, mesh=mesh, in_specs=in_specs, out_specs=out_specs, check_vma=False)
```

```python
import functools

import jax
import jax.numpy as jnp
from jax import lax
from jax.experimental import pallas as pl
from jax.experimental.pallas import tpu as pltpu
from jax.sharding import PartitionSpec as P

ITERS = 2
CHUNK = 16
F32 = jnp.float32
BF16 = jnp.bfloat16
I32 = jnp.int32
HIGHEST = lax.Precision.HIGHEST
VMEM = pl.BlockSpec(memory_space=pltpu.VMEM)
ANY = pl.BlockSpec(memory_space=pl.ANY)
SMEM = pl.BlockSpec(memory_space=pltpu.SMEM)
HBM = pl.BlockSpec(memory_space=pltpu.HBM)


def hat(ray, centre):
    return jnp.maximum(0.0, 1.0 - jnp.abs(ray - centre)).astype(BF16)


def row_taps(offset, slope, extent):
    shape = (offset.shape[0], extent)
    ray = lax.broadcasted_iota(I32, shape, 1).astype(F32)
    inverse = jnp.broadcast_to(1.0 / slope, shape)
    offset = jnp.broadcast_to(offset, shape)
    slope = jnp.broadcast_to(slope, shape)
    middle = jnp.floor((ray - offset) * inverse + 0.5)
    middle = jnp.minimum(jnp.maximum(middle, 1.0), extent - 2.0)
    weights = [hat(ray, offset + slope * (middle + step)) for step in (-1.0, 0.0, 1.0)]
    return middle.astype(I32), weights


def column_taps(offset, slope, extent):
    shape = (offset.shape[0], extent)
    voxel = lax.broadcasted_iota(I32, shape, 1).astype(F32)
    centre = jnp.broadcast_to(offset, shape) + jnp.broadcast_to(slope, shape) * voxel
    first = jnp.minimum(jnp.maximum(jnp.floor(centre), 0.0), extent - 2.0)
    weights = [hat(first + step, centre) for step in (0.0, 1.0)]
    return first.astype(I32), weights


def repeat_rows(values, times):
    return jnp.concatenate(
        [jnp.broadcast_to(values[row:row + 1, :], (times, values.shape[1]))
         for row in range(values.shape[0])], axis=0)


def contract_lanes(left, right):
    return lax.dot_general(
        left.astype(BF16), right.astype(BF16), (((1,), (1,)), ((), ())), preferred_element_type=F32)


def per_slot(live_ref, slots, capacity):
    targets = live_ref.shape[1]
    slot = lax.broadcasted_iota(I32, (targets, slots), 1)
    owner = lax.broadcasted_iota(I32, (targets, slots), 0)
    expand = (lax.div(slot, capacity) == owner).astype(F32)
    return jnp.dot(live_ref[...].astype(F32), expand, precision=HIGHEST, preferred_element_type=F32)


def pack_kernel(capacity, partners, *refs):
    sources, outs, loaded, arrived, packed = refs[:6], refs[6:-8], refs[-8:-2], refs[-2], refs[-1]
    copies = [
        pltpu.make_async_copy(source, ref, arrived.at[place])
        for place, (source, ref) in enumerate(zip(sources, loaded))]
    for copy in copies:
        copy.start()
    for copy in copies:
        copy.wait()
    volume_ref, offset_ref, slope_ref, voxel_ref, ray_ref, live_ref = loaded
    rows, extent = volume_ref.shape
    slots = ray_ref.shape[1]
    fields = []
    for ref in (offset_ref, slope_ref):
        left = ref[...]
        for addend in range(3):
            part = left.astype(BF16).astype(F32)
            fields.append(part)
            left = left - part
    fields.append(voxel_ref[...].astype(F32))
    fields.append(ray_ref[...].astype(F32))
    fields.append(per_slot(live_ref, slots, capacity))
    used = sum(field.shape[0] for field in fields)
    fields.append(jnp.zeros((-used % 16, slots), F32))
    fields = jnp.concatenate(fields, axis=0)
    height = fields.shape[0]
    for part in range(slots // extent):
        at = pl.ds(part * height, height)
        packed[at, :] = fields[:, part * extent:(part + 1) * extent].astype(BF16)
    me = lax.axis_index("slab").astype(I32)
    odd = sum(lax.bitwise_and(lax.shift_right_logical(me, bit), 1) for bit in range(4)) % 2
    for place, out_ref in enumerate(outs):
        out_ref[0:rows, :] = volume_ref[...].astype(BF16)
        if not partners:
            out_ref[rows:, :] = packed[...]
            continue
        distance = jnp.where(odd == 0, partners[place][0], partners[place][1])
        part = lax.div(lax.bitwise_xor(me, distance) * capacity, extent)
        out_ref[rows:, :] = packed[pl.ds(pl.multiple_of(part * height, 16), height), :]


def setup_kernel(n_payloads, members, stride, span, sizes, tiles, wanted, *refs):
    payload_refs, refs = refs[:n_payloads], refs[-(2 * len(wanted) + 10):]
    where = [(ref, index) for ref in payload_refs for index in range(ref.shape[0] // stride)]
    list_refs, row_ref, tables = refs[:len(wanted)], refs[len(wanted)], refs[len(wanted) + 1:-len(wanted) - 2]
    drafts, arrived, summed = refs[-len(wanted) - 2:-2], refs[-2], refs[-1]
    copies = [
        pltpu.make_async_copy(draft, ref, arrived.at[place])
        for place, (draft, ref) in enumerate(zip(drafts, list_refs))]
    capacity, depth, frames = sizes
    width = span * capacity
    extent = row_ref.shape[1]
    ray_tiles = row_ref.shape[0] // span
    height = -(-(7 * depth + 2) // 16) * 16
    lanes = drafts[0].shape[1]
    me = lax.axis_index("slab").astype(I32)
    parity = lax.rem(me, span)
    first_slot = (me - parity) * capacity
    part = 0 if n_payloads > 1 else lax.div(first_slot, extent)
    shift = lax.rem(extent - lax.rem(first_slot, extent), extent)

    def collect(member, lined, payload_ref, within):
        at = within * stride + tiles * frames + part * height
        raw = payload_ref[pl.ds(pl.multiple_of(at, 16), height), :].astype(F32)
        offset = (raw[0:depth] + raw[depth:2 * depth]) + raw[2 * depth:3 * depth]
        slope = (raw[3 * depth:4 * depth] + raw[4 * depth:5 * depth]) + raw[5 * depth:6 * depth]
        fields = jnp.concatenate(
            [offset, slope, raw[6 * depth:7 * depth + 2],
             jnp.zeros((16 - 3 * depth - 2, extent), F32)], axis=0)
        fields = pltpu.roll(fields, shift, axis=1)
        lane = lax.broadcasted_iota(I32, fields.shape, 1)
        fields = jnp.where(lane < width, fields, 0.0)
        if lanes > extent:
            fields = jnp.concatenate(
                [fields, jnp.zeros((fields.shape[0], lanes - extent), F32)], axis=1)
        return lined + pltpu.roll(fields, member * width, axis=1)

    lined = jnp.zeros((16, lanes), F32)
    if members <= 16:
        for member in range(members):
            lined = collect(member, lined, *where[member])
    else:
        lined = lax.fori_loop(
            0, members, lambda member, lined: collect(member, lined, payload_refs[0], member), lined)

    slot = lax.broadcasted_iota(I32, (1, lanes), 1)
    within = lax.rem(slot, width)
    target = lax.bitwise_xor(lax.div(within, capacity), parity)
    ray = lined[3 * depth:3 * depth + 1]
    count = lined[3 * depth + 1:3 * depth + 2]
    alive = jnp.logical_and(lax.rem(within, capacity).astype(F32) < count, slot < members * width)

    table = jnp.concatenate(
        [slot.astype(F32), ray, target.astype(F32), lined[2 * depth:3 * depth],
         jnp.zeros((5 - depth, lanes), F32)], axis=0)
    order = lax.broadcasted_iota(I32, (lanes, lanes), 0)
    earlier = (lax.broadcasted_iota(I32, (lanes, lanes), 1) < order).astype(F32)
    for ref, kind, copy in zip(drafts, wanted, copies):
        taken = alive if kind is None else jnp.logical_and(alive, target == kind)
        taken = taken.astype(F32)
        position = contract_lanes(jnp.broadcast_to(taken, (8, lanes)), earlier)[0:1]
        position = jnp.where(taken > 0.0, position, -1.0).astype(I32)
        choose = jnp.broadcast_to(position, (lanes, lanes)) == order
        packed = (contract_lanes(table, choose.astype(F32)) + 0.5).astype(I32)
        total = jnp.sum(taken, axis=1, keepdims=True).astype(I32)
        line = jnp.where(slot < total, packed[0:1], lanes)
        base = packed[1:2] if kind is not None else packed[1:2] + packed[2:3] * ray_tiles
        member = lax.div(packed[0:1], width) * tiles
        rows = [line, base * frames]
        rows += [(packed[3 + level:4 + level] + member) * frames for level in range(depth)]
        rows += [jnp.zeros((5 - depth, lanes), I32), jnp.broadcast_to(total, (1, lanes))]
        ref[...] = jnp.concatenate(rows, axis=0)
        copy.start()

    columns = lined.T
    step = 32
    for row in range(0, lanes, step):
        total = None
        for level in range(depth):
            offset = columns[row:row + step, level:level + 1]
            slope = columns[row:row + step, depth + level:depth + level + 1]
            middle, weights = row_taps(offset, slope, extent)
            first, pair = column_taps(offset, slope, extent)
            wide = [weight.astype(F32) for weight in weights]
            values = [middle] + wide + [first] + [weight.astype(F32) for weight in pair]
            at = level * (lanes + 8) + row
            for ref, value in zip(tables, values):
                ref[at:at + step, :] = value
            parts = (wide[0] + wide[1]) + wide[2]
            total = parts if total is None else total + parts
        summed[row:row + step, :] = total
    for ref in tables:
        blank = jnp.ones if ref.dtype == I32 else jnp.zeros
        for level in range(depth):
            at = level * (lanes + 8) + lanes
            ref[at:at + 8, :] = blank((8, extent), ref.dtype)

    tile = lax.broadcasted_iota(I32, (span * ray_tiles, lanes), 0).astype(F32)
    place = ray + (target * ray_tiles).astype(F32)
    place = jnp.where(alive, place, -1.0)
    hot = (jnp.broadcast_to(place, tile.shape) == tile).astype(F32)
    row_ref[...] = jnp.dot(hot, summed[...], precision=HIGHEST, preferred_element_type=F32)
    for copy in copies:
        copy.wait()


def column_kernel(sizes, offset_ref, slope_ref, voxel_ref, live_ref, out_ref):
    capacity, depth, frames = sizes
    tiles = out_ref.shape[0] // frames
    slots = offset_ref.shape[1]
    extent = out_ref.shape[1]
    offsets = offset_ref[...].T
    slopes = slope_ref[...].T
    within = lax.rem(lax.broadcasted_iota(I32, (1, slots), 1), capacity).astype(F32)
    alive = jnp.broadcast_to(within, (tiles, slots)) < per_slot(live_ref, slots, capacity)
    total = jnp.zeros((tiles, extent), F32)
    for level in range(depth):
        unused, pair = column_taps(
            offsets[:, level:level + 1], slopes[:, level:level + 1], extent)
        tile_of = jnp.broadcast_to(voxel_ref[level:level + 1, :], (tiles, slots))
        match = tile_of == lax.broadcasted_iota(I32, (tiles, slots), 0)
        hot = jnp.logical_and(match, alive).astype(F32).astype(BF16)
        for weight in pair:
            total += jnp.dot(hot, weight, preferred_element_type=F32)
    out_ref[...] = repeat_rows(1.0 / jnp.maximum(total, 1.0), frames)


def pick(values, index):
    numbers = lax.GatherDimensionNumbers(
        offset_dims=(), collapsed_slice_dims=(1,), start_index_map=(1,),
        operand_batching_dims=(0,), start_indices_batching_dims=(0,))
    return lax.gather(
        values, index[:, :, None], numbers, slice_sizes=(1, 1),
        mode=lax.GatherScatterMode.PROMISE_IN_BOUNDS)


def pack_pair(first, second):
    kind = jnp.int16 if first.dtype == I32 else BF16
    return jnp.concatenate([first, second], axis=0).astype(kind)


def spread(ref, row, frames):
    return ref[pl.ds(row, frames, stride=0), :]


def tile_at(start, frames):
    return pl.ds(pl.multiple_of(start, frames), frames)


def for_slots(slots, body):
    def some(step, carry):
        for place in range(CHUNK):
            body(step * CHUNK + place, place)
        return carry

    lax.fori_loop(0, lax.div(slots[7, 0] + (CHUNK - 1), CHUNK), some, 0)


def for_rows(rows, body):
    step = 128
    if rows <= 8 * step:
        for start in range(0, rows, step):
            body(pl.ds(start, step))
        return

    def some(number, carry):
        body(pl.ds(pl.multiple_of(number * step, step), step))
        return carry

    lax.fori_loop(0, rows // step, some, 0)


def forward_kernel(sizes, n_values, members, start_row, n_sums, slots, *refs):
    capacity, depth, frames = sizes
    value_refs, tables, refs = refs[:n_values], refs[n_values:n_values + 4], refs[n_values + 4:]
    start_ref = None
    if start_row is not None:
        start_ref, refs = refs[0], refs[1:]
    sum_refs, (out_ref, wide, second) = refs[:n_sums], refs[n_sums:]
    rows = wide.shape[0] // members
    stride = sum(ref.shape[0] for ref in value_refs) // members
    rays = second.shape[0]
    line_step = tables[0].shape[0] // depth

    base = 0
    for ref in value_refs:
        def widen(member, carry, ref=ref, base=base):
            at = (base + member) * rows
            start = member * stride
            if not isinstance(member, int):
                at, start = pl.multiple_of(at, rows), pl.multiple_of(start, 16)
            wide[pl.ds(at, rows), :] = ref[pl.ds(start, rows), :].astype(F32)
            return carry

        here = ref.shape[0] // stride
        if here <= 8:
            for member in range(here):
                widen(member, 0)
        else:
            lax.fori_loop(0, here, widen, 0)
        base += here
    second[...] = jnp.zeros_like(second)
    if start_ref is None:
        out_ref[...] = jnp.zeros_like(out_ref)
    else:
        out_ref[0:rays, :] = start_ref[start_row:start_row + rays, :]
    if n_sums:
        half = sum_refs[0].shape[0] // 2
        out_ref[rays:, :] = sum([ref[half:, :] for ref in sum_refs[1:]], sum_refs[0][half:, :])

    def one(slot, place):
        line = slots[0, slot]
        taps = []
        for start in range(0, depth, 2):
            levels = range(start, start + 2)
            values = [wide[tile_at(slots[2 + level, slot], frames), :] for level in levels]
            middles = [spread(tables[0], line + level * line_step, frames) for level in levels]
            lower = [
                pick(pack_pair(value, value), pack_pair(middle - 1, middle)).astype(F32)
                for value, middle in zip(values, middles)]
            upper = pick(
                pack_pair(*values), pack_pair(*[middle + 1 for middle in middles])).astype(F32)
            for which, pair in enumerate(lower):
                taps.append((pair[0:frames], pair[frames:2 * frames],
                             upper[which * frames:(which + 1) * frames]))
        total = None
        for level, three in enumerate(taps):
            for ref, tap in zip(tables[1:], three):
                term = spread(ref, line + level * line_step, frames) * tap
                total = term if total is None else total + term
        projection = (out_ref, second)[place % 2]
        projection[tile_at(slots[1, slot], frames), :] += total.astype(BF16).astype(F32)

    for_slots(slots, one)
    out_ref[0:rays, :] += second[...]


def residual_kernel(frames, n_own, projection_ref, sinogram_ref, *refs):
    own, refs, out_ref = refs[:n_own], refs[n_own:-1], refs[-1]
    rays = out_ref.shape[0]
    ray_tiles = rays // frames
    total = sum([ref[0:ray_tiles, :] for ref in own[1:]], own[0][0:ray_tiles, :])
    projection = projection_ref[...]
    if refs:
        projection = projection + refs[0][0:rays, :]
        total = total + refs[-1][rays:, :]
    weight = repeat_rows(1.0 / jnp.maximum(total, 1.0), frames)
    out_ref[...] = ((sinogram_ref[...].astype(F32) - projection) * weight).astype(BF16)


def backward_kernel(sizes, n_parts, has_start, split, slots, *refs):
    capacity, depth, frames = sizes
    part_refs, tables, refs = refs[:n_parts], refs[n_parts:n_parts + 3], refs[n_parts + 3:]
    start_ref = None
    if has_start:
        start_ref, refs = refs[0], refs[1:]
    outs = refs[:len(split)] if split else refs[:1]
    residual, banks = refs[len(outs)], refs[len(outs) + 1:]
    rays = part_refs[0].shape[0]
    line_step = tables[0].shape[0] // depth
    for place, ref in enumerate(part_refs):
        residual[place * rays:(place + 1) * rays, :] = ref[...].astype(F32)

    def clear(at):
        for place, bank in enumerate(banks):
            if place == 0 and has_start:
                bank[at, :] = start_ref[at, :]
            else:
                bank[at, :] = jnp.zeros((at.size, bank.shape[1]), F32)

    for_rows(banks[0].shape[0], clear)

    def one(slot, place):
        line = slots[0, slot]
        values = residual[tile_at(slots[1, slot], frames), :]
        twice = pack_pair(values, values)
        for level in range(depth):
            row = line + level * line_step
            first = spread(tables[0], row, frames)
            taps = pick(twice, pack_pair(first, first + 1)).astype(F32)
            term = (spread(tables[1], row, frames) * taps[0:frames]
                    + spread(tables[2], row, frames) * taps[frames:2 * frames])
            banks[level % len(banks)][tile_at(slots[2 + level, slot], frames), :] += term

    for_slots(slots, one)

    def total(at):
        return sum([bank[at, :] for bank in banks[1:]], banks[0][at, :])

    if split:
        for ref, members in zip(outs, split):
            rows = ref.shape[0] // len(members)
            for place, member in enumerate(members):
                ref[place * rows:(place + 1) * rows, :] = total(pl.ds(member * rows, rows)).astype(ref.dtype)
    else:
        def finish(at):
            outs[0][at, :] = total(at).astype(outs[0].dtype)

        for_rows(outs[0].shape[0], finish)


def join_kernel(*refs):
    out_ref, at = refs[-1], 0
    for ref in refs[:-1]:
        out_ref[at:at + ref.shape[0], :] = ref[...]
        at += ref.shape[0]


def combine_kernel(members, sum_ref, y_ref, *piece_refs):
    rows = piece_refs[0].shape[0]
    for place, (member, ref) in enumerate(zip(members, piece_refs)):
        mine = sum_ref[member * rows:(member + 1) * rows, :]
        ref[...] = (mine + y_ref[place * rows:(place + 1) * rows, :].astype(F32)).astype(ref.dtype)


def update_kernel(n_pieces, volume_ref, column_ref, *refs):
    back = refs[0][...]
    for ref in refs[1:n_pieces]:
        back = back + ref[...].astype(F32)
    volume = volume_ref[...] + column_ref[...] * back
    for ref in refs[n_pieces:]:
        ref[...] = volume.astype(ref.dtype)


def call(kernel, name, mib, in_specs, out_shape, *operands, scratch=()):
    one = not isinstance(out_shape, list)
    return pl.pallas_call(
        kernel,
        out_shape=out_shape,
        in_specs=in_specs,
        out_specs=VMEM if one else [
            SMEM if getattr(out, "memory_space", None) == pltpu.SMEM else VMEM for out in out_shape],
        scratch_shapes=list(scratch),
        compiler_params=pltpu.CompilerParams(vmem_limit_bytes=mib * 1024 * 1024),
        name=name,
        cost_estimate=pl.CostEstimate(flops=4 * 10**9, bytes_accessed=8 * 10**6, transcendentals=0),
    )(*operands)


def exchange(values, n_slab, distance, other_distance=None):
    far = (distance, distance if other_distance is None else other_distance)
    return lax.ppermute(
        values, "slab",
        [(device, device ^ far[device.bit_count() % 2]) for device in range(n_slab)])


def shards(sinogram, start_volume, slot_voxel, slot_ray, live_count, block_slope, block_offset):
    n_slab = lax.axis_size("slab")
    n_slots, depth = slot_voxel.shape
    capacity = n_slots // n_slab
    ray_tiles, frames, extent = sinogram.shape
    voxel_tiles = start_volume.shape[0]
    rows = voxel_tiles * frames
    sizes = (capacity, depth, frames)
    paired = n_slab == 16
    span = 2 if paired else 1
    n_bank = 2 if paired else 1
    shape = jax.ShapeDtypeStruct
    n_rays = ray_tiles * frames
    volume = start_volume.reshape(rows, extent)
    sino = sinogram.reshape(n_rays, extent)
    slots_by_depth = (block_offset.T, block_slope.T, slot_voxel.T)
    live = live_count.reshape(1, n_slab)
    height = -(-(7 * depth + 2) // 16) * 16 * (n_slots // extent)
    operands = (volume, *slots_by_depth, slot_ray.reshape(1, n_slots), live)
    partners = ((0, 0), (12, 3), (5, 10), (9, 9), (10, 12)) if paired else ()
    size = rows + height // (n_slots // extent if paired else 1)
    payloads = call(
        functools.partial(pack_kernel, capacity, partners), "pack", 16, [HBM] * 6,
        [shape((size, extent), BF16)] * max(1, len(partners)),
        *[pltpu.with_memory_space_constraint(operand, pltpu.HBM) for operand in operands],
        scratch=[pltpu.VMEM(operand.shape, operand.dtype) for operand in operands]
        + [pltpu.SemaphoreType.DMA((6,)), pltpu.VMEM((height, extent), BF16)])
    payload = payloads[0]

    def setup(payloads, members, wanted, after=None):
        lanes = -(-members * span * capacity // 128) * 128
        lines = depth * (lanes + 8)
        table = [shape((lines, extent), I32)] + [shape((lines, extent), F32)] * 3
        table += [shape((lines, extent), I32)] + [shape((lines, extent), F32)] * 2
        n = len(wanted)
        out = [pltpu.SMEM((8, lanes), I32)] * n + [shape((span * ray_tiles, extent), F32)] + table
        waits = [] if after is None else [after]
        found = call(
            functools.partial(setup_kernel, len(payloads), members,
                              sum(one.shape[0] for one in payloads) // members, span, sizes,
                              voxel_tiles, wanted),
            "setup", 24, [VMEM] * len(payloads) + [ANY] * len(waits), out, *payloads, *waits,
            scratch=[pltpu.VMEM((8, lanes), I32)] * n
            + [pltpu.SemaphoreType.DMA((n,)), pltpu.VMEM((lanes, extent), F32)])
        return found[:n], found[n], found[n + 1:n + 5], found[n + 5:]

    def forward(slots, values, members, table, n_out, start=None, start_row=None, sums=()):
        operands = [pltpu.with_memory_space_constraint(slots, pltpu.SMEM), *values, *table] + ([] if start is None else [start]) + list(sums)
        extra = ray_tiles if sums else 0
        return call(
            functools.partial(forward_kernel, sizes, len(values), members, start_row, len(sums)),
            "forward", 16 if paired else 32, [SMEM] + [VMEM] * (len(operands) - 1),
            shape((n_out + extra, extent), F32), *operands,
            scratch=[pltpu.VMEM((members * rows, extent), F32), pltpu.VMEM((n_out, extent), F32)])

    def residual_of(projection, row_sums, *sibling):
        operands = [projection, sino, *row_sums, *sibling]
        return call(
            functools.partial(residual_kernel, frames, len(row_sums)), "residual", 16,
            [VMEM] * len(operands), shape((n_rays, extent), BF16), *operands)

    def backward(slots, parts, members, table, kind, start=None, split=()):
        operands = [pltpu.with_memory_space_constraint(slots, pltpu.SMEM), *parts, *table] + ([] if start is None else [start])
        return call(
            functools.partial(backward_kernel, sizes, len(parts), start is not None, split),
            "backward", 16 if paired else 32, [SMEM] + [VMEM] * (len(operands) - 1),
            [shape((len(some) * rows, extent), each) for some, each in zip(split, kind)]
            if split else shape((members * rows, extent), kind), *operands,
            scratch=[pltpu.VMEM((len(parts) * n_rays, extent), F32)]
            + [pltpu.VMEM((members * rows, extent), F32)] * n_bank)

    def join(*parts):
        total = sum(part.shape[0] for part in parts)
        return call(join_kernel, "join", 16, [VMEM] * len(parts), shape((total, extent), BF16), *parts)

    def update(volume, pieces, last):
        out = [shape((rows, extent), F32)] + ([] if last else [shape((rows, extent), BF16)])
        return call(
            functools.partial(update_kernel, len(pieces)), "update", 16,
            [VMEM] * (2 + len(pieces)), out, volume, column_weight, *pieces)

    column_weight = call(
        functools.partial(column_kernel, sizes), "column_weight", 16, [VMEM] * 4,
        shape((rows, extent), F32), *slots_by_depth, live)

    for sweep in range(ITERS):
        last = sweep + 1 == ITERS
        if paired:
            place_1, place_2, place_3, across = [
                exchange(one, n_slab, *pair) for one, pair in zip(payloads[1:], partners[1:])]
            z_part = join(payload, place_1, place_2)
            y_part = exchange(z_part, n_slab, 3, 5)
            along_z, along_y = (z_part, place_3), (y_part, across)
            if sweep == 0:
                (z_list,), z_rows, z_forward, z_backward = setup(along_z, 4, (None,))
            both = forward(z_list, along_z, 4, z_forward, 2 * n_rays)
            if sweep == 0:
                (own_list, other_list), y_rows, y_forward, y_backward = setup(
                    along_y, 4, (0, 1), after=both)
            other = exchange(
                forward(other_list, along_y, 4, y_forward, n_rays, both, n_rays,
                        (z_rows, y_rows) if sweep == 0 else ()), n_slab, 1)
            if sweep == 0:
                first_other = other
            own = forward(own_list, along_y, 4, y_forward, n_rays, both, 0)
            residual = residual_of(own, (z_rows, y_rows), other, first_other)
            other_residual = exchange(residual, n_slab, 1)
            y_sum = backward(own_list, [residual], 4, y_backward, F32)
            far_sum, near_sum = backward(
                other_list, [other_residual], 4, y_backward, (BF16, BF16), y_sum, ((1, 3), (0, 2)))
            far_part, near_part = exchange(far_sum, n_slab, 3, 5), exchange(near_sum, n_slab, 3, 5)
            z_sum = backward(z_list, [residual, other_residual], 4, z_backward, F32)
            piece = shape((rows, extent), BF16)
            piece_1, piece_3 = call(
                functools.partial(combine_kernel, (1, 3)), "combine", 16, [VMEM] * 2,
                [piece, piece], z_sum, far_part)
            got = [exchange(piece_1, n_slab, 12, 3), exchange(piece_3, n_slab, 9)]
            own_piece, piece_2 = call(
                functools.partial(combine_kernel, (0, 2)), "combine", 16, [VMEM] * 2,
                [shape((rows, extent), F32), piece], z_sum, near_part)
            pieces = [own_piece, exchange(piece_2, n_slab, 5, 10), *got]
        else:
            everyone = lax.all_gather(payload, "slab", axis=0, tiled=True)
            if sweep == 0:
                (slots,), row_sums, to_rays, to_voxels = setup((everyone,), n_slab, (None,))
            projection = forward(slots, (everyone,), n_slab, to_rays, n_rays)
            residual = residual_of(projection, (row_sums,))
            sums = backward(slots, [residual], n_slab, to_voxels, BF16)
            parts = lax.all_to_all(
                sums.reshape(n_slab, rows, extent), "slab", split_axis=0, concat_axis=0, tiled=True)
            pieces = [jnp.sum(parts.astype(F32), axis=0)]
        volume, *rounded = update(volume, pieces, last)
        if not last:
            payload = rounded[0]
            payloads = [payload] * (1 + len(partners))
    return volume.reshape(start_volume.shape)


def solution(mesh):
    in_specs = (
        P(("scan", "slab"), None, None),
        P(("scan", "slab"), None, None),
        P(("scan", "slab"), None),
        P(("scan", "slab")),
        P(("scan", "slab")),
        P(("scan", "slab"), None),
        P(("scan", "slab"), None),
    )
    out_specs = P(("scan", "slab"), None, None)
    return jax.shard_map(shards, mesh=mesh, in_specs=in_specs, out_specs=out_specs, check_vma=False)
```

```python
import functools

import jax
import jax.numpy as jnp
from jax import lax
from jax.experimental import pallas as pl
from jax.experimental.pallas import tpu as pltpu
from jax.sharding import PartitionSpec as P

ITERS = 2
CHUNK = 16
F32 = jnp.float32
BF16 = jnp.bfloat16
I32 = jnp.int32
HIGHEST = lax.Precision.HIGHEST
VMEM = pl.BlockSpec(memory_space=pltpu.VMEM)
ANY = pl.BlockSpec(memory_space=pl.ANY)
SMEM = pl.BlockSpec(memory_space=pltpu.SMEM)
HBM = pl.BlockSpec(memory_space=pltpu.HBM)


def hat(ray, centre):
    return jnp.maximum(0.0, 1.0 - jnp.abs(ray - centre)).astype(BF16)


def row_taps(offset, slope, extent):
    shape = (offset.shape[0], extent)
    ray = lax.broadcasted_iota(I32, shape, 1).astype(F32)
    inverse = jnp.broadcast_to(1.0 / slope, shape)
    offset = jnp.broadcast_to(offset, shape)
    slope = jnp.broadcast_to(slope, shape)
    middle = jnp.floor((ray - offset) * inverse + 0.5)
    middle = jnp.minimum(jnp.maximum(middle, 1.0), extent - 2.0)
    weights = [hat(ray, offset + slope * (middle + step)) for step in (-1.0, 0.0, 1.0)]
    return middle.astype(I32), weights


def column_taps(offset, slope, extent):
    shape = (offset.shape[0], extent)
    voxel = lax.broadcasted_iota(I32, shape, 1).astype(F32)
    centre = jnp.broadcast_to(offset, shape) + jnp.broadcast_to(slope, shape) * voxel
    first = jnp.minimum(jnp.maximum(jnp.floor(centre), 0.0), extent - 2.0)
    weights = [hat(first + step, centre) for step in (0.0, 1.0)]
    return first.astype(I32), weights


def repeat_rows(values, times):
    return jnp.concatenate(
        [jnp.broadcast_to(values[row:row + 1, :], (times, values.shape[1]))
         for row in range(values.shape[0])], axis=0)


def contract_lanes(left, right):
    return lax.dot_general(
        left.astype(BF16), right.astype(BF16), (((1,), (1,)), ((), ())), preferred_element_type=F32)


def per_slot(live_ref, slots, capacity):
    targets = live_ref.shape[1]
    slot = lax.broadcasted_iota(I32, (targets, slots), 1)
    owner = lax.broadcasted_iota(I32, (targets, slots), 0)
    expand = (lax.div(slot, capacity) == owner).astype(F32)
    return jnp.dot(live_ref[...].astype(F32), expand, precision=HIGHEST, preferred_element_type=F32)


def pack_kernel(capacity, partners, *refs):
    sources, outs, loaded, arrived, packed = refs[:6], refs[6:-8], refs[-8:-2], refs[-2], refs[-1]
    copies = [
        pltpu.make_async_copy(source, ref, arrived.at[place])
        for place, (source, ref) in enumerate(zip(sources, loaded))]
    for copy in copies:
        copy.start()
    for copy in copies:
        copy.wait()
    volume_ref, offset_ref, slope_ref, voxel_ref, ray_ref, live_ref = loaded
    rows, extent = volume_ref.shape
    slots = ray_ref.shape[1]
    fields = []
    for ref in (offset_ref, slope_ref):
        left = ref[...]
        for addend in range(3):
            part = left.astype(BF16).astype(F32)
            fields.append(part)
            left = left - part
    fields.append(voxel_ref[...].astype(F32))
    fields.append(ray_ref[...].astype(F32))
    fields.append(per_slot(live_ref, slots, capacity))
    used = sum(field.shape[0] for field in fields)
    fields.append(jnp.zeros((-used % 16, slots), F32))
    fields = jnp.concatenate(fields, axis=0)
    height = fields.shape[0]
    for part in range(slots // extent):
        at = pl.ds(part * height, height)
        packed[at, :] = fields[:, part * extent:(part + 1) * extent].astype(BF16)
    me = lax.axis_index("slab").astype(I32)
    odd = sum(lax.bitwise_and(lax.shift_right_logical(me, bit), 1) for bit in range(4)) % 2
    for place, out_ref in enumerate(outs):
        out_ref[0:rows, :] = volume_ref[...].astype(BF16)
        if not partners:
            out_ref[rows:, :] = packed[...]
            continue
        distance = jnp.where(odd == 0, partners[place][0], partners[place][1])
        part = lax.div(lax.bitwise_xor(me, distance) * capacity, extent)
        out_ref[rows:, :] = packed[pl.ds(pl.multiple_of(part * height, 16), height), :]


def setup_kernel(n_payloads, members, stride, span, sizes, tiles, wanted, *refs):
    payload_refs, refs = refs[:n_payloads], refs[-(2 * len(wanted) + 10):]
    where = [(ref, index) for ref in payload_refs for index in range(ref.shape[0] // stride)]
    list_refs, row_ref, tables = refs[:len(wanted)], refs[len(wanted)], refs[len(wanted) + 1:-len(wanted) - 2]
    drafts, arrived, summed = refs[-len(wanted) - 2:-2], refs[-2], refs[-1]
    copies = [
        pltpu.make_async_copy(draft, ref, arrived.at[place])
        for place, (draft, ref) in enumerate(zip(drafts, list_refs))]
    capacity, depth, frames = sizes
    width = span * capacity
    extent = row_ref.shape[1]
    ray_tiles = row_ref.shape[0] // span
    height = -(-(7 * depth + 2) // 16) * 16
    lanes = drafts[0].shape[1]
    me = lax.axis_index("slab").astype(I32)
    parity = lax.rem(me, span)
    first_slot = (me - parity) * capacity
    part = 0 if n_payloads > 1 else lax.div(first_slot, extent)
    shift = lax.rem(extent - lax.rem(first_slot, extent), extent)

    def collect(member, lined, payload_ref, within):
        at = within * stride + tiles * frames + part * height
        raw = payload_ref[pl.ds(pl.multiple_of(at, 16), height), :].astype(F32)
        offset = (raw[0:depth] + raw[depth:2 * depth]) + raw[2 * depth:3 * depth]
        slope = (raw[3 * depth:4 * depth] + raw[4 * depth:5 * depth]) + raw[5 * depth:6 * depth]
        fields = jnp.concatenate(
            [offset, slope, raw[6 * depth:7 * depth + 2],
             jnp.zeros((16 - 3 * depth - 2, extent), F32)], axis=0)
        fields = pltpu.roll(fields, shift, axis=1)
        lane = lax.broadcasted_iota(I32, fields.shape, 1)
        fields = jnp.where(lane < width, fields, 0.0)
        if lanes > extent:
            fields = jnp.concatenate(
                [fields, jnp.zeros((fields.shape[0], lanes - extent), F32)], axis=1)
        return lined + pltpu.roll(fields, member * width, axis=1)

    lined = jnp.zeros((16, lanes), F32)
    if members <= 16:
        for member in range(members):
            lined = collect(member, lined, *where[member])
    else:
        lined = lax.fori_loop(
            0, members, lambda member, lined: collect(member, lined, payload_refs[0], member), lined)

    slot = lax.broadcasted_iota(I32, (1, lanes), 1)
    within = lax.rem(slot, width)
    target = lax.bitwise_xor(lax.div(within, capacity), parity)
    ray = lined[3 * depth:3 * depth + 1]
    count = lined[3 * depth + 1:3 * depth + 2]
    alive = jnp.logical_and(lax.rem(within, capacity).astype(F32) < count, slot < members * width)

    table = jnp.concatenate(
        [slot.astype(F32), ray, target.astype(F32), lined[2 * depth:3 * depth],
         jnp.zeros((5 - depth, lanes), F32)], axis=0)
    order = lax.broadcasted_iota(I32, (lanes, lanes), 0)
    earlier = (lax.broadcasted_iota(I32, (lanes, lanes), 1) < order).astype(F32)
    for ref, kind, copy in zip(drafts, wanted, copies):
        taken = alive if kind is None else jnp.logical_and(alive, target == kind)
        taken = taken.astype(F32)
        position = contract_lanes(jnp.broadcast_to(taken, (8, lanes)), earlier)[0:1]
        position = jnp.where(taken > 0.0, position, -1.0).astype(I32)
        choose = jnp.broadcast_to(position, (lanes, lanes)) == order
        packed = (contract_lanes(table, choose.astype(F32)) + 0.5).astype(I32)
        total = jnp.sum(taken, axis=1, keepdims=True).astype(I32)
        line = jnp.where(slot < total, packed[0:1], lanes)
        base = packed[1:2] if kind is not None else packed[1:2] + packed[2:3] * ray_tiles
        member = lax.div(packed[0:1], width) * tiles
        rows = [line, base * frames]
        rows += [(packed[3 + level:4 + level] + member) * frames for level in range(depth)]
        rows += [jnp.zeros((5 - depth, lanes), I32), jnp.broadcast_to(total, (1, lanes))]
        ref[...] = jnp.concatenate(rows, axis=0)
        copy.start()

    columns = lined.T
    step = 32
    for row in range(0, lanes, step):
        total = None
        for level in range(depth):
            offset = columns[row:row + step, level:level + 1]
            slope = columns[row:row + step, depth + level:depth + level + 1]
            middle, weights = row_taps(offset, slope, extent)
            first, pair = column_taps(offset, slope, extent)
            wide = [weight.astype(F32) for weight in weights]
            values = [middle] + wide + [first] + [weight.astype(F32) for weight in pair]
            at = level * (lanes + 8) + row
            for ref, value in zip(tables, values):
                ref[at:at + step, :] = value
            parts = (wide[0] + wide[1]) + wide[2]
            total = parts if total is None else total + parts
        summed[row:row + step, :] = total
    for ref in tables:
        blank = jnp.ones if ref.dtype == I32 else jnp.zeros
        for level in range(depth):
            at = level * (lanes + 8) + lanes
            ref[at:at + 8, :] = blank((8, extent), ref.dtype)

    tile = lax.broadcasted_iota(I32, (span * ray_tiles, lanes), 0).astype(F32)
    place = ray + (target * ray_tiles).astype(F32)
    place = jnp.where(alive, place, -1.0)
    hot = (jnp.broadcast_to(place, tile.shape) == tile).astype(F32)
    row_ref[...] = jnp.dot(hot, summed[...], precision=HIGHEST, preferred_element_type=F32)
    for copy in copies:
        copy.wait()


def column_kernel(sizes, offset_ref, slope_ref, voxel_ref, live_ref, out_ref):
    capacity, depth, frames = sizes
    tiles = out_ref.shape[0] // frames
    slots = offset_ref.shape[1]
    extent = out_ref.shape[1]
    offsets = offset_ref[...].T
    slopes = slope_ref[...].T
    within = lax.rem(lax.broadcasted_iota(I32, (1, slots), 1), capacity).astype(F32)
    alive = jnp.broadcast_to(within, (tiles, slots)) < per_slot(live_ref, slots, capacity)
    total = jnp.zeros((tiles, extent), F32)
    for level in range(depth):
        unused, pair = column_taps(
            offsets[:, level:level + 1], slopes[:, level:level + 1], extent)
        tile_of = jnp.broadcast_to(voxel_ref[level:level + 1, :], (tiles, slots))
        match = tile_of == lax.broadcasted_iota(I32, (tiles, slots), 0)
        hot = jnp.logical_and(match, alive).astype(F32).astype(BF16)
        for weight in pair:
            total += jnp.dot(hot, weight, preferred_element_type=F32)
    out_ref[...] = repeat_rows(1.0 / jnp.maximum(total, 1.0), frames)


def pick(values, index):
    numbers = lax.GatherDimensionNumbers(
        offset_dims=(), collapsed_slice_dims=(1,), start_index_map=(1,),
        operand_batching_dims=(0,), start_indices_batching_dims=(0,))
    return lax.gather(
        values, index[:, :, None], numbers, slice_sizes=(1, 1),
        mode=lax.GatherScatterMode.PROMISE_IN_BOUNDS)


def pack_pair(first, second):
    kind = jnp.int16 if first.dtype == I32 else BF16
    return jnp.concatenate([first, second], axis=0).astype(kind)


def spread(ref, row, frames):
    return ref[pl.ds(row, frames, stride=0), :]


def tile_at(start, frames):
    return pl.ds(pl.multiple_of(start, frames), frames)


def for_slots(slots, body):
    def some(step, carry):
        for place in range(CHUNK):
            body(step * CHUNK + place, place)
        return carry

    lax.fori_loop(0, lax.div(slots[7, 0] + (CHUNK - 1), CHUNK), some, 0)


def for_rows(rows, body):
    step = 128
    if rows <= 8 * step:
        for start in range(0, rows, step):
            body(pl.ds(start, step))
        return

    def some(number, carry):
        body(pl.ds(pl.multiple_of(number * step, step), step))
        return carry

    lax.fori_loop(0, rows // step, some, 0)


def forward_kernel(sizes, n_values, members, start_row, n_sums, slots, *refs):
    capacity, depth, frames = sizes
    value_refs, tables, refs = refs[:n_values], refs[n_values:n_values + 4], refs[n_values + 4:]
    start_ref = None
    if start_row is not None:
        start_ref, refs = refs[0], refs[1:]
    sum_refs, (out_ref, wide) = refs[:n_sums], refs[n_sums:]
    rows = wide.shape[0] // members
    stride = sum(ref.shape[0] for ref in value_refs) // members
    rays = out_ref.shape[0] - (sum_refs[0].shape[0] // 2 if n_sums else 0)
    line_step = tables[0].shape[0] // depth

    base = 0
    for ref in value_refs:
        def widen(member, carry, ref=ref, base=base):
            at = (base + member) * rows
            start = member * stride
            if not isinstance(member, int):
                at, start = pl.multiple_of(at, rows), pl.multiple_of(start, 16)
            wide[pl.ds(at, rows), :] = ref[pl.ds(start, rows), :].astype(F32)
            return carry

        here = ref.shape[0] // stride
        if here <= 8:
            for member in range(here):
                widen(member, 0)
        else:
            lax.fori_loop(0, here, widen, 0)
        base += here
    if start_ref is None:
        out_ref[...] = jnp.zeros_like(out_ref)
    else:
        out_ref[0:rays, :] = start_ref[start_row:start_row + rays, :]
    if n_sums:
        half = sum_refs[0].shape[0] // 2
        out_ref[rays:, :] = sum([ref[half:, :] for ref in sum_refs[1:]], sum_refs[0][half:, :])

    def one(slot, place):
        line = slots[0, slot]
        taps = []
        for start in range(0, depth, 2):
            levels = range(start, start + 2)
            values = [wide[tile_at(slots[2 + level, slot], frames), :] for level in levels]
            middles = [spread(tables[0], line + level * line_step, frames) for level in levels]
            lower = [
                pick(pack_pair(value, value), pack_pair(middle - 1, middle)).astype(F32)
                for value, middle in zip(values, middles)]
            upper = pick(
                pack_pair(*values), pack_pair(*[middle + 1 for middle in middles])).astype(F32)
            for which, pair in enumerate(lower):
                taps.append((pair[0:frames], pair[frames:2 * frames],
                             upper[which * frames:(which + 1) * frames]))
        total = None
        for level, three in enumerate(taps):
            for ref, tap in zip(tables[1:], three):
                term = spread(ref, line + level * line_step, frames) * tap
                total = term if total is None else total + term
        out_ref[tile_at(slots[1, slot], frames), :] += total.astype(BF16).astype(F32)

    for_slots(slots, one)


def residual_kernel(frames, n_own, projection_ref, sinogram_ref, *refs):
    own, refs, out_ref = refs[:n_own], refs[n_own:-1], refs[-1]
    rays = out_ref.shape[0]
    ray_tiles = rays // frames
    total = sum([ref[0:ray_tiles, :] for ref in own[1:]], own[0][0:ray_tiles, :])
    projection = projection_ref[...]
    if refs:
        projection = projection + refs[0][0:rays, :]
        total = total + refs[-1][rays:, :]
    weight = repeat_rows(1.0 / jnp.maximum(total, 1.0), frames)
    out_ref[...] = ((sinogram_ref[...].astype(F32) - projection) * weight).astype(BF16)


def backward_kernel(sizes, n_parts, has_start, split, slots, *refs):
    capacity, depth, frames = sizes
    part_refs, tables, refs = refs[:n_parts], refs[n_parts:n_parts + 3], refs[n_parts + 3:]
    start_ref = None
    if has_start:
        start_ref, refs = refs[0], refs[1:]
    outs = refs[:len(split)] if split else refs[:1]
    residual, banks = refs[len(outs)], refs[len(outs) + 1:]
    rays = part_refs[0].shape[0]
    line_step = tables[0].shape[0] // depth
    for place, ref in enumerate(part_refs):
        residual[place * rays:(place + 1) * rays, :] = ref[...].astype(F32)

    def clear(at):
        for place, bank in enumerate(banks):
            if place == 0 and has_start:
                bank[at, :] = start_ref[at, :]
            else:
                bank[at, :] = jnp.zeros((at.size, bank.shape[1]), F32)

    for_rows(banks[0].shape[0], clear)

    def one(slot, place):
        line = slots[0, slot]
        values = residual[tile_at(slots[1, slot], frames), :]
        twice = pack_pair(values, values)
        for level in range(depth):
            row = line + level * line_step
            first = spread(tables[0], row, frames)
            taps = pick(twice, pack_pair(first, first + 1)).astype(F32)
            term = (spread(tables[1], row, frames) * taps[0:frames]
                    + spread(tables[2], row, frames) * taps[frames:2 * frames])
            banks[level % len(banks)][tile_at(slots[2 + level, slot], frames), :] += term

    for_slots(slots, one)

    def total(at):
        return sum([bank[at, :] for bank in banks[1:]], banks[0][at, :])

    if split:
        for ref, members in zip(outs, split):
            rows = ref.shape[0] // len(members)
            for place, member in enumerate(members):
                ref[place * rows:(place + 1) * rows, :] = total(pl.ds(member * rows, rows)).astype(ref.dtype)
    else:
        def finish(at):
            outs[0][at, :] = total(at).astype(outs[0].dtype)

        for_rows(outs[0].shape[0], finish)


def join_kernel(*refs):
    out_ref, at = refs[-1], 0
    for ref in refs[:-1]:
        out_ref[at:at + ref.shape[0], :] = ref[...]
        at += ref.shape[0]


def combine_kernel(members, sum_ref, y_ref, *piece_refs):
    rows = piece_refs[0].shape[0]
    for place, (member, ref) in enumerate(zip(members, piece_refs)):
        mine = sum_ref[member * rows:(member + 1) * rows, :]
        ref[...] = (mine + y_ref[place * rows:(place + 1) * rows, :].astype(F32)).astype(ref.dtype)


def update_kernel(n_pieces, volume_ref, column_ref, *refs):
    back = refs[0][...]
    for ref in refs[1:n_pieces]:
        back = back + ref[...].astype(F32)
    volume = volume_ref[...] + column_ref[...] * back
    for ref in refs[n_pieces:]:
        ref[...] = volume.astype(ref.dtype)


def call(kernel, name, mib, in_specs, out_shape, *operands, scratch=()):
    one = not isinstance(out_shape, list)
    return pl.pallas_call(
        kernel,
        out_shape=out_shape,
        in_specs=in_specs,
        out_specs=VMEM if one else [
            SMEM if getattr(out, "memory_space", None) == pltpu.SMEM else VMEM for out in out_shape],
        scratch_shapes=list(scratch),
        compiler_params=pltpu.CompilerParams(vmem_limit_bytes=mib * 1024 * 1024),
        name=name,
        cost_estimate=pl.CostEstimate(flops=4 * 10**9, bytes_accessed=8 * 10**6, transcendentals=0),
    )(*operands)


def exchange(values, n_slab, distance, other_distance=None):
    far = (distance, distance if other_distance is None else other_distance)
    return lax.ppermute(
        values, "slab",
        [(device, device ^ far[device.bit_count() % 2]) for device in range(n_slab)])


def shards(sinogram, start_volume, slot_voxel, slot_ray, live_count, block_slope, block_offset):
    n_slab = lax.axis_size("slab")
    n_slots, depth = slot_voxel.shape
    capacity = n_slots // n_slab
    ray_tiles, frames, extent = sinogram.shape
    voxel_tiles = start_volume.shape[0]
    rows = voxel_tiles * frames
    sizes = (capacity, depth, frames)
    paired = n_slab == 16
    span = 2 if paired else 1
    n_bank = 2 if paired else 1
    shape = jax.ShapeDtypeStruct
    n_rays = ray_tiles * frames
    volume = start_volume.reshape(rows, extent)
    sino = sinogram.reshape(n_rays, extent)
    slots_by_depth = (block_offset.T, block_slope.T, slot_voxel.T)
    live = live_count.reshape(1, n_slab)
    height = -(-(7 * depth + 2) // 16) * 16 * (n_slots // extent)
    operands = (volume, *slots_by_depth, slot_ray.reshape(1, n_slots), live)
    partners = ((0, 0), (9, 3), (5, 9), (12, 10), (15, 15)) if paired else ()
    size = rows + height // (n_slots // extent if paired else 1)
    payloads = call(
        functools.partial(pack_kernel, capacity, partners), "pack", 16, [HBM] * 6,
        [shape((size, extent), BF16)] * max(1, len(partners)),
        *[pltpu.with_memory_space_constraint(operand, pltpu.HBM) for operand in operands],
        scratch=[pltpu.VMEM(operand.shape, operand.dtype) for operand in operands]
        + [pltpu.SemaphoreType.DMA((6,)), pltpu.VMEM((height, extent), BF16)])
    payload = payloads[0]

    def setup(payloads, members, wanted, after=None):
        lanes = -(-members * span * capacity // 128) * 128
        lines = depth * (lanes + 8)
        table = [shape((lines, extent), I32)] + [shape((lines, extent), F32)] * 3
        table += [shape((lines, extent), I32)] + [shape((lines, extent), F32)] * 2
        n = len(wanted)
        out = [pltpu.SMEM((8, lanes), I32)] * n + [shape((span * ray_tiles, extent), F32)] + table
        waits = [] if after is None else [after]
        found = call(
            functools.partial(setup_kernel, len(payloads), members,
                              sum(one.shape[0] for one in payloads) // members, span, sizes,
                              voxel_tiles, wanted),
            "setup", 24, [VMEM] * len(payloads) + [ANY] * len(waits), out, *payloads, *waits,
            scratch=[pltpu.VMEM((8, lanes), I32)] * n
            + [pltpu.SemaphoreType.DMA((n,)), pltpu.VMEM((lanes, extent), F32)])
        return found[:n], found[n], found[n + 1:n + 5], found[n + 5:]

    def forward(slots, values, members, table, n_out, start=None, start_row=None, sums=()):
        operands = [pltpu.with_memory_space_constraint(slots, pltpu.SMEM), *values, *table] + ([] if start is None else [start]) + list(sums)
        extra = ray_tiles if sums else 0
        return call(
            functools.partial(forward_kernel, sizes, len(values), members, start_row, len(sums)),
            "forward", 16 if paired else 32, [SMEM] + [VMEM] * (len(operands) - 1),
            shape((n_out + extra, extent), F32), *operands,
            scratch=[pltpu.VMEM((members * rows, extent), F32)])

    def residual_of(projection, row_sums, *sibling):
        operands = [projection, sino, *row_sums, *sibling]
        return call(
            functools.partial(residual_kernel, frames, len(row_sums)), "residual", 16,
            [VMEM] * len(operands), shape((n_rays, extent), BF16), *operands)

    def backward(slots, parts, members, table, kind, start=None, split=()):
        operands = [pltpu.with_memory_space_constraint(slots, pltpu.SMEM), *parts, *table] + ([] if start is None else [start])
        return call(
            functools.partial(backward_kernel, sizes, len(parts), start is not None, split),
            "backward", 16 if paired else 32, [SMEM] + [VMEM] * (len(operands) - 1),
            [shape((len(some) * rows, extent), each) for some, each in zip(split, kind)]
            if split else shape((members * rows, extent), kind), *operands,
            scratch=[pltpu.VMEM((len(parts) * n_rays, extent), F32)]
            + [pltpu.VMEM((members * rows, extent), F32)] * n_bank)

    def join(*parts):
        total = sum(part.shape[0] for part in parts)
        return call(join_kernel, "join", 16, [VMEM] * len(parts), shape((total, extent), BF16), *parts)

    def update(volume, pieces, last):
        out = [shape((rows, extent), F32)] + ([] if last else [shape((rows, extent), BF16)])
        return call(
            functools.partial(update_kernel, len(pieces)), "update", 16,
            [VMEM] * (2 + len(pieces)), out, volume, column_weight, *pieces)

    column_weight = call(
        functools.partial(column_kernel, sizes), "column_weight", 16, [VMEM] * 4,
        shape((rows, extent), F32), *slots_by_depth, live)

    for sweep in range(ITERS):
        last = sweep + 1 == ITERS
        if paired:
            place_1, place_2, place_3, across = [
                exchange(one, n_slab, *pair) for one, pair in zip(payloads[1:], partners[1:])]
            z_part = join(payload, place_1, place_2)
            y_part = exchange(z_part, n_slab, 3, 5)
            along_z, along_y = (z_part, place_3), (y_part, across)
            if sweep == 0:
                (z_list,), z_rows, z_forward, z_backward = setup(along_z, 4, (None,))
            both = forward(z_list, along_z, 4, z_forward, 2 * n_rays)
            if sweep == 0:
                (own_list, other_list), y_rows, y_forward, y_backward = setup(
                    along_y, 4, (0, 1), after=both)
            other = exchange(
                forward(other_list, along_y, 4, y_forward, n_rays, both, n_rays,
                        (z_rows, y_rows) if sweep == 0 else ()), n_slab, 1)
            if sweep == 0:
                first_other = other
            own = forward(own_list, along_y, 4, y_forward, n_rays, both, 0)
            residual = residual_of(own, (z_rows, y_rows), other, first_other)
            other_residual = exchange(residual, n_slab, 1)
            y_sum = backward(own_list, [residual], 4, y_backward, F32)
            far_sum, near_sum = backward(
                other_list, [other_residual], 4, y_backward, (BF16, BF16), y_sum, ((1, 3), (0, 2)))
            far_part, near_part = exchange(far_sum, n_slab, 3, 5), exchange(near_sum, n_slab, 3, 5)
            z_sum = backward(z_list, [residual, other_residual], 4, z_backward, F32)
            piece = shape((rows, extent), BF16)
            piece_1, piece_3 = call(
                functools.partial(combine_kernel, (1, 3)), "combine", 16, [VMEM] * 2,
                [piece, piece], z_sum, far_part)
            got = [exchange(piece_1, n_slab, 9, 3), exchange(piece_3, n_slab, 12, 10)]
            own_piece, piece_2 = call(
                functools.partial(combine_kernel, (0, 2)), "combine", 16, [VMEM] * 2,
                [shape((rows, extent), F32), piece], z_sum, near_part)
            pieces = [own_piece, exchange(piece_2, n_slab, 5, 9), *got]
        else:
            everyone = lax.all_gather(payload, "slab", axis=0, tiled=True)
            if sweep == 0:
                (slots,), row_sums, to_rays, to_voxels = setup((everyone,), n_slab, (None,))
            projection = forward(slots, (everyone,), n_slab, to_rays, n_rays)
            residual = residual_of(projection, (row_sums,))
            sums = backward(slots, [residual], n_slab, to_voxels, BF16)
            parts = lax.all_to_all(
                sums.reshape(n_slab, rows, extent), "slab", split_axis=0, concat_axis=0, tiled=True)
            pieces = [jnp.sum(parts.astype(F32), axis=0)]
        volume, *rounded = update(volume, pieces, last)
        if not last:
            payload = rounded[0]
            payloads = [payload] * (1 + len(partners))
    return volume.reshape(start_volume.shape)


def solution(mesh):
    in_specs = (
        P(("scan", "slab"), None, None),
        P(("scan", "slab"), None, None),
        P(("scan", "slab"), None),
        P(("scan", "slab")),
        P(("scan", "slab")),
        P(("scan", "slab"), None),
        P(("scan", "slab"), None),
    )
    out_specs = P(("scan", "slab"), None, None)
    return jax.shard_map(shards, mesh=mesh, in_specs=in_specs, out_specs=out_specs, check_vma=False)
```

```python
import functools

import jax
import jax.numpy as jnp
from jax import lax
from jax.experimental import pallas as pl
from jax.experimental.pallas import tpu as pltpu
from jax.sharding import PartitionSpec as P

ITERS = 2
CHUNK = 16
F32 = jnp.float32
BF16 = jnp.bfloat16
I32 = jnp.int32
HIGHEST = lax.Precision.HIGHEST
VMEM = pl.BlockSpec(memory_space=pltpu.VMEM)
ANY = pl.BlockSpec(memory_space=pl.ANY)
SMEM = pl.BlockSpec(memory_space=pltpu.SMEM)
HBM = pl.BlockSpec(memory_space=pltpu.HBM)


def hat(ray, centre):
    return jnp.maximum(0.0, 1.0 - jnp.abs(ray - centre)).astype(BF16)


def row_taps(offset, slope, extent):
    shape = (offset.shape[0], extent)
    ray = lax.broadcasted_iota(I32, shape, 1).astype(F32)
    inverse = jnp.broadcast_to(1.0 / slope, shape)
    offset = jnp.broadcast_to(offset, shape)
    slope = jnp.broadcast_to(slope, shape)
    middle = jnp.floor((ray - offset) * inverse + 0.5)
    middle = jnp.minimum(jnp.maximum(middle, 1.0), extent - 2.0)
    weights = [hat(ray, offset + slope * (middle + step)) for step in (-1.0, 0.0, 1.0)]
    return middle.astype(I32), weights


def column_taps(offset, slope, extent):
    shape = (offset.shape[0], extent)
    voxel = lax.broadcasted_iota(I32, shape, 1).astype(F32)
    centre = jnp.broadcast_to(offset, shape) + jnp.broadcast_to(slope, shape) * voxel
    first = jnp.minimum(jnp.maximum(jnp.floor(centre), 0.0), extent - 2.0)
    weights = [hat(first + step, centre) for step in (0.0, 1.0)]
    return first.astype(I32), weights


def repeat_rows(values, times):
    return jnp.concatenate(
        [jnp.broadcast_to(values[row:row + 1, :], (times, values.shape[1]))
         for row in range(values.shape[0])], axis=0)


def contract_lanes(left, right):
    return lax.dot_general(
        left.astype(BF16), right.astype(BF16), (((1,), (1,)), ((), ())), preferred_element_type=F32)


def per_slot(live_ref, slots, capacity):
    targets = live_ref.shape[1]
    slot = lax.broadcasted_iota(I32, (targets, slots), 1)
    owner = lax.broadcasted_iota(I32, (targets, slots), 0)
    expand = (lax.div(slot, capacity) == owner).astype(F32)
    return jnp.dot(live_ref[...].astype(F32), expand, precision=HIGHEST, preferred_element_type=F32)


def pack_kernel(capacity, partners, *refs):
    sources, outs, loaded, arrived, packed = refs[:6], refs[6:-8], refs[-8:-2], refs[-2], refs[-1]
    copies = [
        pltpu.make_async_copy(source, ref, arrived.at[place])
        for place, (source, ref) in enumerate(zip(sources, loaded))]
    for copy in copies:
        copy.start()
    for copy in copies:
        copy.wait()
    volume_ref, offset_ref, slope_ref, voxel_ref, ray_ref, live_ref = loaded
    rows, extent = volume_ref.shape
    slots = ray_ref.shape[1]
    fields = []
    for ref in (offset_ref, slope_ref):
        left = ref[...]
        for addend in range(3):
            part = left.astype(BF16).astype(F32)
            fields.append(part)
            left = left - part
    fields.append(voxel_ref[...].astype(F32))
    fields.append(ray_ref[...].astype(F32))
    fields.append(per_slot(live_ref, slots, capacity))
    used = sum(field.shape[0] for field in fields)
    fields.append(jnp.zeros((-used % 16, slots), F32))
    fields = jnp.concatenate(fields, axis=0)
    height = fields.shape[0]
    for part in range(slots // extent):
        at = pl.ds(part * height, height)
        packed[at, :] = fields[:, part * extent:(part + 1) * extent].astype(BF16)
    me = lax.axis_index("slab").astype(I32)
    odd = sum(lax.bitwise_and(lax.shift_right_logical(me, bit), 1) for bit in range(4)) % 2
    for place, out_ref in enumerate(outs):
        out_ref[0:rows, :] = volume_ref[...].astype(BF16)
        if not partners:
            out_ref[rows:, :] = packed[...]
            continue
        distance = jnp.where(odd == 0, partners[place][0], partners[place][1])
        part = lax.div(lax.bitwise_xor(me, distance) * capacity, extent)
        out_ref[rows:, :] = packed[pl.ds(pl.multiple_of(part * height, 16), height), :]


def setup_kernel(n_payloads, members, stride, span, sizes, tiles, wanted, *refs):
    payload_refs, refs = refs[:n_payloads], refs[-(2 * len(wanted) + 10):]
    where = [(ref, index) for ref in payload_refs for index in range(ref.shape[0] // stride)]
    list_refs, row_ref, tables = refs[:len(wanted)], refs[len(wanted)], refs[len(wanted) + 1:-len(wanted) - 2]
    drafts, arrived, summed = refs[-len(wanted) - 2:-2], refs[-2], refs[-1]
    copies = [
        pltpu.make_async_copy(draft, ref, arrived.at[place])
        for place, (draft, ref) in enumerate(zip(drafts, list_refs))]
    capacity, depth, frames = sizes
    width = span * capacity
    extent = row_ref.shape[1]
    ray_tiles = row_ref.shape[0] // span
    height = -(-(7 * depth + 2) // 16) * 16
    lanes = drafts[0].shape[1]
    me = lax.axis_index("slab").astype(I32)
    parity = lax.rem(me, span)
    first_slot = (me - parity) * capacity
    part = 0 if n_payloads > 1 else lax.div(first_slot, extent)
    shift = lax.rem(extent - lax.rem(first_slot, extent), extent)

    def collect(member, lined, payload_ref, within):
        at = within * stride + tiles * frames + part * height
        raw = payload_ref[pl.ds(pl.multiple_of(at, 16), height), :].astype(F32)
        offset = (raw[0:depth] + raw[depth:2 * depth]) + raw[2 * depth:3 * depth]
        slope = (raw[3 * depth:4 * depth] + raw[4 * depth:5 * depth]) + raw[5 * depth:6 * depth]
        fields = jnp.concatenate(
            [offset, slope, raw[6 * depth:7 * depth + 2],
             jnp.zeros((16 - 3 * depth - 2, extent), F32)], axis=0)
        fields = pltpu.roll(fields, shift, axis=1)
        lane = lax.broadcasted_iota(I32, fields.shape, 1)
        fields = jnp.where(lane < width, fields, 0.0)
        if lanes > extent:
            fields = jnp.concatenate(
                [fields, jnp.zeros((fields.shape[0], lanes - extent), F32)], axis=1)
        return lined + pltpu.roll(fields, member * width, axis=1)

    lined = jnp.zeros((16, lanes), F32)
    if members <= 16:
        for member in range(members):
            lined = collect(member, lined, *where[member])
    else:
        lined = lax.fori_loop(
            0, members, lambda member, lined: collect(member, lined, payload_refs[0], member), lined)

    slot = lax.broadcasted_iota(I32, (1, lanes), 1)
    within = lax.rem(slot, width)
    target = lax.bitwise_xor(lax.div(within, capacity), parity)
    ray = lined[3 * depth:3 * depth + 1]
    count = lined[3 * depth + 1:3 * depth + 2]
    alive = jnp.logical_and(lax.rem(within, capacity).astype(F32) < count, slot < members * width)

    table = jnp.concatenate(
        [slot.astype(F32), ray, target.astype(F32), lined[2 * depth:3 * depth],
         jnp.zeros((5 - depth, lanes), F32)], axis=0)
    order = lax.broadcasted_iota(I32, (lanes, lanes), 0)
    earlier = (lax.broadcasted_iota(I32, (lanes, lanes), 1) < order).astype(F32)
    for ref, kind, copy in zip(drafts, wanted, copies):
        taken = alive if kind is None else jnp.logical_and(alive, target == kind)
        taken = taken.astype(F32)
        position = contract_lanes(jnp.broadcast_to(taken, (8, lanes)), earlier)[0:1]
        position = jnp.where(taken > 0.0, position, -1.0).astype(I32)
        choose = jnp.broadcast_to(position, (lanes, lanes)) == order
        packed = (contract_lanes(table, choose.astype(F32)) + 0.5).astype(I32)
        total = jnp.sum(taken, axis=1, keepdims=True).astype(I32)
        line = jnp.where(slot < total, packed[0:1], lanes)
        base = packed[1:2] if kind is not None else packed[1:2] + packed[2:3] * ray_tiles
        member = lax.div(packed[0:1], width) * tiles
        rows = [line, base * frames]
        rows += [(packed[3 + level:4 + level] + member) * frames for level in range(depth)]
        rows += [jnp.zeros((5 - depth, lanes), I32), jnp.broadcast_to(total, (1, lanes))]
        ref[...] = jnp.concatenate(rows, axis=0)
        copy.start()

    columns = lined.T
    step = 32
    for row in range(0, lanes, step):
        total = None
        for level in range(depth):
            offset = columns[row:row + step, level:level + 1]
            slope = columns[row:row + step, depth + level:depth + level + 1]
            middle, weights = row_taps(offset, slope, extent)
            first, pair = column_taps(offset, slope, extent)
            wide = [weight.astype(F32) for weight in weights]
            values = [middle] + wide + [first] + [weight.astype(F32) for weight in pair]
            at = level * (lanes + 8) + row
            for ref, value in zip(tables, values):
                ref[at:at + step, :] = value
            parts = (wide[0] + wide[1]) + wide[2]
            total = parts if total is None else total + parts
        summed[row:row + step, :] = total
    for ref in tables:
        blank = jnp.ones if ref.dtype == I32 else jnp.zeros
        for level in range(depth):
            at = level * (lanes + 8) + lanes
            ref[at:at + 8, :] = blank((8, extent), ref.dtype)

    tile = lax.broadcasted_iota(I32, (span * ray_tiles, lanes), 0).astype(F32)
    place = ray + (target * ray_tiles).astype(F32)
    place = jnp.where(alive, place, -1.0)
    hot = (jnp.broadcast_to(place, tile.shape) == tile).astype(F32)
    row_ref[...] = jnp.dot(hot, summed[...], precision=HIGHEST, preferred_element_type=F32)
    for copy in copies:
        copy.wait()


def column_kernel(sizes, offset_ref, slope_ref, voxel_ref, live_ref, out_ref):
    capacity, depth, frames = sizes
    tiles = out_ref.shape[0] // frames
    slots = offset_ref.shape[1]
    extent = out_ref.shape[1]
    offsets = offset_ref[...].T
    slopes = slope_ref[...].T
    within = lax.rem(lax.broadcasted_iota(I32, (1, slots), 1), capacity).astype(F32)
    alive = jnp.broadcast_to(within, (tiles, slots)) < per_slot(live_ref, slots, capacity)
    total = jnp.zeros((tiles, extent), F32)
    for level in range(depth):
        unused, pair = column_taps(
            offsets[:, level:level + 1], slopes[:, level:level + 1], extent)
        tile_of = jnp.broadcast_to(voxel_ref[level:level + 1, :], (tiles, slots))
        match = tile_of == lax.broadcasted_iota(I32, (tiles, slots), 0)
        hot = jnp.logical_and(match, alive).astype(F32).astype(BF16)
        for weight in pair:
            total += jnp.dot(hot, weight, preferred_element_type=F32)
    out_ref[...] = repeat_rows(1.0 / jnp.maximum(total, 1.0), frames)


def pick(values, index):
    numbers = lax.GatherDimensionNumbers(
        offset_dims=(), collapsed_slice_dims=(1,), start_index_map=(1,),
        operand_batching_dims=(0,), start_indices_batching_dims=(0,))
    return lax.gather(
        values, index[:, :, None], numbers, slice_sizes=(1, 1),
        mode=lax.GatherScatterMode.PROMISE_IN_BOUNDS)


def pack_pair(first, second):
    kind = jnp.int16 if first.dtype == I32 else BF16
    return jnp.concatenate([first, second], axis=0).astype(kind)


def spread(ref, row, frames):
    return ref[pl.ds(row, frames, stride=0), :]


def tile_at(start, frames):
    return pl.ds(pl.multiple_of(start, frames), frames)


def for_slots(slots, body):
    def some(step, carry):
        for place in range(CHUNK):
            body(step * CHUNK + place, place)
        return carry

    lax.fori_loop(0, lax.div(slots[7, 0] + (CHUNK - 1), CHUNK), some, 0)


def for_rows(rows, body):
    step = 128
    if rows <= 8 * step:
        for start in range(0, rows, step):
            body(pl.ds(start, step))
        return

    def some(number, carry):
        body(pl.ds(pl.multiple_of(number * step, step), step))
        return carry

    lax.fori_loop(0, rows // step, some, 0)


def forward_kernel(sizes, n_values, members, start_row, n_sums, slots, *refs):
    capacity, depth, frames = sizes
    value_refs, tables, refs = refs[:n_values], refs[n_values:n_values + 4], refs[n_values + 4:]
    start_ref = None
    if start_row is not None:
        start_ref, refs = refs[0], refs[1:]
    sum_refs, (out_ref, wide, second) = refs[:n_sums], refs[n_sums:]
    rows = wide.shape[0] // members
    stride = sum(ref.shape[0] for ref in value_refs) // members
    rays = second.shape[0]
    line_step = tables[0].shape[0] // depth

    base = 0
    for ref in value_refs:
        def widen(member, carry, ref=ref, base=base):
            at = (base + member) * rows
            start = member * stride
            if not isinstance(member, int):
                at, start = pl.multiple_of(at, rows), pl.multiple_of(start, 16)
            wide[pl.ds(at, rows), :] = ref[pl.ds(start, rows), :].astype(F32)
            return carry

        here = ref.shape[0] // stride
        if here <= 8:
            for member in range(here):
                widen(member, 0)
        else:
            lax.fori_loop(0, here, widen, 0)
        base += here
    second[...] = jnp.zeros_like(second)
    if start_ref is None:
        out_ref[...] = jnp.zeros_like(out_ref)
    else:
        out_ref[0:rays, :] = start_ref[start_row:start_row + rays, :]
    if n_sums:
        half = sum_refs[0].shape[0] // 2
        out_ref[rays:, :] = sum([ref[half:, :] for ref in sum_refs[1:]], sum_refs[0][half:, :])

    def one(slot, place):
        line = slots[0, slot]
        taps = []
        for start in range(0, depth, 2):
            levels = range(start, start + 2)
            values = [wide[tile_at(slots[2 + level, slot], frames), :] for level in levels]
            middles = [spread(tables[0], line + level * line_step, frames) for level in levels]
            lower = [
                pick(pack_pair(value, value), pack_pair(middle - 1, middle)).astype(F32)
                for value, middle in zip(values, middles)]
            upper = pick(
                pack_pair(*values), pack_pair(*[middle + 1 for middle in middles])).astype(F32)
            for which, pair in enumerate(lower):
                taps.append((pair[0:frames], pair[frames:2 * frames],
                             upper[which * frames:(which + 1) * frames]))
        total = None
        for level, three in enumerate(taps):
            for ref, tap in zip(tables[1:], three):
                term = spread(ref, line + level * line_step, frames) * tap
                total = term if total is None else total + term
        projection = (out_ref, second)[place % 2]
        projection[tile_at(slots[1, slot], frames), :] += total.astype(BF16).astype(F32)

    for_slots(slots, one)
    out_ref[0:rays, :] += second[...]


def residual_kernel(frames, n_own, projection_ref, sinogram_ref, *refs):
    own, refs, out_ref = refs[:n_own], refs[n_own:-1], refs[-1]
    rays = out_ref.shape[0]
    ray_tiles = rays // frames
    total = sum([ref[0:ray_tiles, :] for ref in own[1:]], own[0][0:ray_tiles, :])
    projection = projection_ref[...]
    if refs:
        projection = projection + refs[0][0:rays, :]
        total = total + refs[-1][rays:, :]
    weight = repeat_rows(1.0 / jnp.maximum(total, 1.0), frames)
    out_ref[...] = ((sinogram_ref[...].astype(F32) - projection) * weight).astype(BF16)


def backward_kernel(sizes, n_parts, has_start, split, slots, *refs):
    capacity, depth, frames = sizes
    part_refs, tables, refs = refs[:n_parts], refs[n_parts:n_parts + 3], refs[n_parts + 3:]
    start_ref = None
    if has_start:
        start_ref, refs = refs[0], refs[1:]
    outs = refs[:len(split)] if split else refs[:1]
    residual, banks = refs[len(outs)], refs[len(outs) + 1:]
    rays = part_refs[0].shape[0]
    line_step = tables[0].shape[0] // depth
    for place, ref in enumerate(part_refs):
        residual[place * rays:(place + 1) * rays, :] = ref[...].astype(F32)

    def clear(at):
        for place, bank in enumerate(banks):
            if place == 0 and has_start:
                bank[at, :] = start_ref[at, :]
            else:
                bank[at, :] = jnp.zeros((at.size, bank.shape[1]), F32)

    for_rows(banks[0].shape[0], clear)

    def one(slot, place):
        line = slots[0, slot]
        values = residual[tile_at(slots[1, slot], frames), :]
        twice = pack_pair(values, values)
        for level in range(depth):
            row = line + level * line_step
            first = spread(tables[0], row, frames)
            taps = pick(twice, pack_pair(first, first + 1)).astype(F32)
            term = (spread(tables[1], row, frames) * taps[0:frames]
                    + spread(tables[2], row, frames) * taps[frames:2 * frames])
            banks[level % len(banks)][tile_at(slots[2 + level, slot], frames), :] += term

    for_slots(slots, one)

    def total(at):
        return sum([bank[at, :] for bank in banks[1:]], banks[0][at, :])

    if split:
        for ref, members in zip(outs, split):
            rows = ref.shape[0] // len(members)
            for place, member in enumerate(members):
                ref[place * rows:(place + 1) * rows, :] = total(pl.ds(member * rows, rows)).astype(ref.dtype)
    else:
        def finish(at):
            outs[0][at, :] = total(at).astype(outs[0].dtype)

        for_rows(outs[0].shape[0], finish)


def join_kernel(*refs):
    out_ref, at = refs[-1], 0
    for ref in refs[:-1]:
        out_ref[at:at + ref.shape[0], :] = ref[...]
        at += ref.shape[0]


def combine_kernel(members, sum_ref, y_ref, *piece_refs):
    rows = piece_refs[0].shape[0]
    for place, (member, ref) in enumerate(zip(members, piece_refs)):
        mine = sum_ref[member * rows:(member + 1) * rows, :]
        ref[...] = (mine + y_ref[place * rows:(place + 1) * rows, :].astype(F32)).astype(ref.dtype)


def update_kernel(n_pieces, volume_ref, column_ref, *refs):
    back = refs[0][...]
    for ref in refs[1:n_pieces]:
        back = back + ref[...].astype(F32)
    volume = volume_ref[...] + column_ref[...] * back
    for ref in refs[n_pieces:]:
        ref[...] = volume.astype(ref.dtype)


def call(kernel, name, mib, in_specs, out_shape, *operands, scratch=()):
    one = not isinstance(out_shape, list)
    return pl.pallas_call(
        kernel,
        out_shape=out_shape,
        in_specs=in_specs,
        out_specs=VMEM if one else [
            SMEM if getattr(out, "memory_space", None) == pltpu.SMEM else VMEM for out in out_shape],
        scratch_shapes=list(scratch),
        compiler_params=pltpu.CompilerParams(vmem_limit_bytes=mib * 1024 * 1024),
        name=name,
        cost_estimate=pl.CostEstimate(flops=4 * 10**9, bytes_accessed=8 * 10**6, transcendentals=0),
    )(*operands)


def exchange(values, n_slab, distance, other_distance=None):
    far = (distance, distance if other_distance is None else other_distance)
    return lax.ppermute(
        values, "slab",
        [(device, device ^ far[device.bit_count() % 2]) for device in range(n_slab)])


def shards(sinogram, start_volume, slot_voxel, slot_ray, live_count, block_slope, block_offset):
    n_slab = lax.axis_size("slab")
    n_slots, depth = slot_voxel.shape
    capacity = n_slots // n_slab
    ray_tiles, frames, extent = sinogram.shape
    voxel_tiles = start_volume.shape[0]
    rows = voxel_tiles * frames
    sizes = (capacity, depth, frames)
    paired = n_slab == 16
    span = 2 if paired else 1
    n_bank = 4 if paired else 1
    shape = jax.ShapeDtypeStruct
    n_rays = ray_tiles * frames
    volume = start_volume.reshape(rows, extent)
    sino = sinogram.reshape(n_rays, extent)
    slots_by_depth = (block_offset.T, block_slope.T, slot_voxel.T)
    live = live_count.reshape(1, n_slab)
    height = -(-(7 * depth + 2) // 16) * 16 * (n_slots // extent)
    operands = (volume, *slots_by_depth, slot_ray.reshape(1, n_slots), live)
    partners = ((0, 0), (9, 3), (5, 9), (12, 10), (15, 15)) if paired else ()
    size = rows + height // (n_slots // extent if paired else 1)
    payloads = call(
        functools.partial(pack_kernel, capacity, partners), "pack", 16, [HBM] * 6,
        [shape((size, extent), BF16)] * max(1, len(partners)),
        *[pltpu.with_memory_space_constraint(operand, pltpu.HBM) for operand in operands],
        scratch=[pltpu.VMEM(operand.shape, operand.dtype) for operand in operands]
        + [pltpu.SemaphoreType.DMA((6,)), pltpu.VMEM((height, extent), BF16)])
    payload = payloads[0]

    def setup(payloads, members, wanted, after=None):
        lanes = -(-members * span * capacity // 128) * 128
        lines = depth * (lanes + 8)
        table = [shape((lines, extent), I32)] + [shape((lines, extent), F32)] * 3
        table += [shape((lines, extent), I32)] + [shape((lines, extent), F32)] * 2
        n = len(wanted)
        out = [pltpu.SMEM((8, lanes), I32)] * n + [shape((span * ray_tiles, extent), F32)] + table
        waits = [] if after is None else [after]
        found = call(
            functools.partial(setup_kernel, len(payloads), members,
                              sum(one.shape[0] for one in payloads) // members, span, sizes,
                              voxel_tiles, wanted),
            "setup", 24, [VMEM] * len(payloads) + [ANY] * len(waits), out, *payloads, *waits,
            scratch=[pltpu.VMEM((8, lanes), I32)] * n
            + [pltpu.SemaphoreType.DMA((n,)), pltpu.VMEM((lanes, extent), F32)])
        return found[:n], found[n], found[n + 1:n + 5], found[n + 5:]

    def forward(slots, values, members, table, n_out, start=None, start_row=None, sums=()):
        operands = [pltpu.with_memory_space_constraint(slots, pltpu.SMEM), *values, *table] + ([] if start is None else [start]) + list(sums)
        extra = ray_tiles if sums else 0
        return call(
            functools.partial(forward_kernel, sizes, len(values), members, start_row, len(sums)),
            "forward", 16 if paired else 32, [SMEM] + [VMEM] * (len(operands) - 1),
            shape((n_out + extra, extent), F32), *operands,
            scratch=[pltpu.VMEM((members * rows, extent), F32), pltpu.VMEM((n_out, extent), F32)])

    def residual_of(projection, row_sums, *sibling):
        operands = [projection, sino, *row_sums, *sibling]
        return call(
            functools.partial(residual_kernel, frames, len(row_sums)), "residual", 16,
            [VMEM] * len(operands), shape((n_rays, extent), BF16), *operands)

    def backward(slots, parts, members, table, kind, start=None, split=()):
        operands = [pltpu.with_memory_space_constraint(slots, pltpu.SMEM), *parts, *table] + ([] if start is None else [start])
        return call(
            functools.partial(backward_kernel, sizes, len(parts), start is not None, split),
            "backward", 16 if paired else 32, [SMEM] + [VMEM] * (len(operands) - 1),
            [shape((len(some) * rows, extent), each) for some, each in zip(split, kind)]
            if split else shape((members * rows, extent), kind), *operands,
            scratch=[pltpu.VMEM((len(parts) * n_rays, extent), F32)]
            + [pltpu.VMEM((members * rows, extent), F32)] * n_bank)

    def join(*parts):
        total = sum(part.shape[0] for part in parts)
        return call(join_kernel, "join", 16, [VMEM] * len(parts), shape((total, extent), BF16), *parts)

    def update(volume, pieces, last):
        out = [shape((rows, extent), F32)] + ([] if last else [shape((rows, extent), BF16)])
        return call(
            functools.partial(update_kernel, len(pieces)), "update", 16,
            [VMEM] * (2 + len(pieces)), out, volume, column_weight, *pieces)

    column_weight = call(
        functools.partial(column_kernel, sizes), "column_weight", 16, [VMEM] * 4,
        shape((rows, extent), F32), *slots_by_depth, live)

    for sweep in range(ITERS):
        last = sweep + 1 == ITERS
        if paired:
            place_1, place_2, place_3, across = [
                exchange(one, n_slab, *pair) for one, pair in zip(payloads[1:], partners[1:])]
            z_part = join(payload, place_1, place_2)
            y_part = exchange(z_part, n_slab, 3, 5)
            along_z, along_y = (z_part, place_3), (y_part, across)
            if sweep == 0:
                (z_list,), z_rows, z_forward, z_backward = setup(along_z, 4, (None,))
            both = forward(z_list, along_z, 4, z_forward, 2 * n_rays)
            if sweep == 0:
                (own_list, other_list), y_rows, y_forward, y_backward = setup(
                    along_y, 4, (0, 1), after=both)
            other = exchange(
                forward(other_list, along_y, 4, y_forward, n_rays, both, n_rays,
                        (z_rows, y_rows) if sweep == 0 else ()), n_slab, 1)
            if sweep == 0:
                first_other = other
            own = forward(own_list, along_y, 4, y_forward, n_rays, both, 0)
            residual = residual_of(own, (z_rows, y_rows), other, first_other)
            other_residual = exchange(residual, n_slab, 1)
            y_sum = backward(own_list, [residual], 4, y_backward, F32)
            far_sum, near_sum = backward(
                other_list, [other_residual], 4, y_backward, (BF16, BF16), y_sum, ((1, 3), (0, 2)))
            far_part, near_part = exchange(far_sum, n_slab, 3, 5), exchange(near_sum, n_slab, 3, 5)
            z_sum = backward(z_list, [residual, other_residual], 4, z_backward, F32)
            piece = shape((rows, extent), BF16)
            piece_1, piece_3 = call(
                functools.partial(combine_kernel, (1, 3)), "combine", 16, [VMEM] * 2,
                [piece, piece], z_sum, far_part)
            got = [exchange(piece_1, n_slab, 9, 3), exchange(piece_3, n_slab, 12, 10)]
            own_piece, piece_2 = call(
                functools.partial(combine_kernel, (0, 2)), "combine", 16, [VMEM] * 2,
                [shape((rows, extent), F32), piece], z_sum, near_part)
            pieces = [own_piece, exchange(piece_2, n_slab, 5, 9), *got]
        else:
            everyone = lax.all_gather(payload, "slab", axis=0, tiled=True)
            if sweep == 0:
                (slots,), row_sums, to_rays, to_voxels = setup((everyone,), n_slab, (None,))
            projection = forward(slots, (everyone,), n_slab, to_rays, n_rays)
            residual = residual_of(projection, (row_sums,))
            sums = backward(slots, [residual], n_slab, to_voxels, BF16)
            parts = lax.all_to_all(
                sums.reshape(n_slab, rows, extent), "slab", split_axis=0, concat_axis=0, tiled=True)
            pieces = [jnp.sum(parts.astype(F32), axis=0)]
        volume, *rounded = update(volume, pieces, last)
        if not last:
            payload = rounded[0]
            payloads = [payload] * (1 + len(partners))
    return volume.reshape(start_volume.shape)


def solution(mesh):
    in_specs = (
        P(("scan", "slab"), None, None),
        P(("scan", "slab"), None, None),
        P(("scan", "slab"), None),
        P(("scan", "slab")),
        P(("scan", "slab")),
        P(("scan", "slab"), None),
        P(("scan", "slab"), None),
    )
    out_specs = P(("scan", "slab"), None, None)
    return jax.shard_map(shards, mesh=mesh, in_specs=in_specs, out_specs=out_specs, check_vma=False)
```
